32 devices in a mesh: dp: 16 (over z, x, core), tensor: 2 (over y).
Axes of the slice: x: 2, y: 2, z: 4, core: 2. Of those that a mesh axis runs over, the one named last changes fastest.
Arguments:
- layer_input: bfloat16 [32768, 768], P(('dp', 'tensor')), may hold values from -6 to 6
- w_qkv: bfloat16 [3, 768, 768], P(None, None, 'tensor'), may hold values from -0.21875 to 0.21875
- bias_qv: float32 [2, 768], P(None, 'tensor'), may hold values from -2 to 2
- w_out: bfloat16 [768, 768], P('tensor'), may hold values from -1.75 to 1.75
- b_out: float32 [768], replicated, may hold values from -2 to 2
- gain_one: float32 [768], replicated, may hold values from 0.5 to 1.5
- shift_one: float32 [768], replicated, may hold values from -1.2 to 1.2
- w_up: bfloat16 [768, 3072], P(None, 'tensor'), may hold values from -0.21875 to 0.21875
- b_up: float32 [3072], P('tensor'), may hold values from -3 to 3
- w_down: bfloat16 [3072, 768], P('tensor'), may hold values from -0.109375 to 0.109375
- b_down: float32 [768], replicated, may hold values from -2 to 2
- gain_two: float32 [768], replicated, may hold values from 0.5 to 1.5
- shift_two: float32 [768], replicated, may hold values from -1.2 to 1.2
- out_cot: bfloat16 [32768, 768], P(('dp', 'tensor')), may hold values from -6 to 6
- lengths: int32 [64], P('dp'), may hold values from 128 to 512, as said below
- group_ids: int32 [64], replicated, may hold values from 0 to 31, as said below
Outputs:
- loss_value: float32 [], replicated
- output: bfloat16 [32768, 768], P(('dp', 'tensor'))
- grad_input: float32 [32768, 768], P(('dp', 'tensor'))
- grad_w_qkv: float32 [3, 768, 768], P(None, None, 'tensor')
- grad_bias_qv: float32 [2, 768], P(None, 'tensor')
- grad_w_out: float32 [768, 768], P('tensor')
- grad_b_out: float32 [768], replicated
- grad_gain_one: float32 [768], replicated
- grad_shift_one: float32 [768], replicated
- grad_w_up: float32 [768, 3072], P(None, 'tensor')
- grad_b_up: float32 [3072], P('tensor')
- grad_w_down: float32 [3072, 768], P('tensor')
- grad_b_down: float32 [768], replicated
- grad_gain_two: float32 [768], replicated
- grad_shift_two: float32 [768], replicated
The draws below stay inside these ranges and needn't reach their ends.
Inputs may be any that keep to these rules, and one draw needn't show every extreme that they name: `lengths`: some sentence has exactly 512 real tokens and some other exactly 128. `group_ids`: every id that occurs names exactly 2 or 4 sentences.
All inputs are finite; a program needn't handle non-finite values.
Results may differ from the reference program's by a relative error of at most 0.02.
Values may be sent and summed in bfloat16 or wider, within the bound.
No kernel may reach another device: no remote copies, remote signals or barrier semaphores. Data moves between devices by JAX's collectives and lax.ppermute only.
A program may use at most 192 MiB of HBM per device.

```python
import math
import jax
import jax.numpy as jnp
from jax import lax

D = 768
HD = 64
FF = 3072
LEN = 512
SEQS = 64
TOKENS = 32768


def draw_lengths(key, part):
    key = jax.random.fold_in(key, 11)
    key_base, key_full, key_short = jax.random.split(key, 3)
    drawn = jax.random.randint(key_base, (SEQS,), LEN // 4, LEN + 1)
    full_index = jax.random.randint(key_full, (), 0, SEQS)
    short_index = (full_index + 1 + jax.random.randint(key_short, (), 0, SEQS - 1)) % SEQS
    drawn = drawn.at[full_index].set(LEN)
    drawn = drawn.at[short_index].set(LEN // 4)
    return drawn.astype(jnp.int32)


def draw_group_ids(key, part):
    key = jax.random.fold_in(key, 23)
    key_coin, key_order = jax.random.split(key, 2)
    pair_ids = jnp.arange(SEQS, dtype=jnp.int32) // 2
    quad_ids = pair_ids // 2
    coins = jax.random.randint(key_coin, (SEQS // 4,), 0, 2)
    coins = coins.at[SEQS // 4 - 1].set(0)
    merged = jnp.where(coins[quad_ids] == 1, quad_ids * 2, pair_ids)
    order = jax.random.permutation(key_order, SEQS)
    return merged[order].astype(jnp.int32)


def block_levels(rng, shape, pieces, low, high):
    level = 1.0
    for axis_at, shards_of in pieces:
        heights = jax.random.uniform(jax.random.fold_in(jax.random.fold_in(rng, 6), axis_at), (shards_of,), jnp.float32, low / len(pieces), high / len(pieces))
        level = level * jnp.repeat(jnp.exp(heights), shape[axis_at] // shards_of).reshape((-1,) + (1,) * (len(shape) - 1 - axis_at))
    return level


def scatter_about(own_key, extent, scale, reach, shards=(), kind=jnp.bfloat16):
    array = scale * jax.random.normal(own_key, extent, jnp.float32)
    if shards:
        array = array * block_levels(own_key, extent, shards, -0.22, 0.18)
    return jnp.clip(array, -reach, reach).astype(kind)


def setup_inputs(seed: int = 0) -> dict:
    arg_keys = jax.random.split(jax.random.key(seed), 17)
    return {
        "layer_input": scatter_about(arg_keys[0], (TOKENS, D), 1.0, 6.0, ((0, 32),)),
        "w_qkv": scatter_about(arg_keys[1], (3, D, D), D ** -0.5, 0.21875, ((2, 2),)),
        "bias_qv": scatter_about(arg_keys[2], (2, D), 0.3, 2.0, ((1, 2),), jnp.float32),
        "w_out": scatter_about(arg_keys[3], (D, D), (D // 64) ** -0.5, 1.75, ((0, 2),)),
        "b_out": scatter_about(arg_keys[4], (D,), 0.3, 2.0, (), jnp.float32),
        "gain_one": jnp.clip(1.0 + 0.1 * jax.random.normal(arg_keys[5], (D,), jnp.float32), 0.5, 1.5),
        "shift_one": scatter_about(arg_keys[6], (D,), 0.2, 1.2, (), jnp.float32),
        "w_up": scatter_about(arg_keys[7], (D, FF), D ** -0.5, 0.21875, ((1, 2),)),
        "b_up": scatter_about(arg_keys[8], (FF,), 0.5, 3.0, ((0, 2),), jnp.float32),
        "w_down": scatter_about(arg_keys[9], (FF, D), FF ** -0.5, 0.109375, ((0, 2),)),
        "b_down": scatter_about(arg_keys[10], (D,), 0.3, 2.0, (), jnp.float32),
        "gain_two": jnp.clip(1.0 + 0.1 * jax.random.normal(arg_keys[11], (D,), jnp.float32), 0.5, 1.5),
        "shift_two": scatter_about(arg_keys[12], (D,), 0.2, 1.2, (), jnp.float32),
        "out_cot": scatter_about(arg_keys[13], (TOKENS, D), 1.0, 6.0, ((0, 32),)),
        "lengths": draw_lengths(jax.random.fold_in(arg_keys[16], 71), 0),
        "group_ids": draw_group_ids(jax.random.fold_in(arg_keys[16], 71), 0),
    }


MATMUL_PRECISION = lax.Precision.HIGHEST
EPS_NORM = 1e-12
SOFTMAX_TEMP = 20.0
MASKED = -1e+30

@jax.custom_vjp
def low(v):
    return lax.optimization_barrier(v.astype(jnp.bfloat16)).astype(jnp.float32)

@jax.custom_vjp
def low_back(v):
    return v

def low_keep(v):
    return (low(v), None)

def low_pass(kept, grad):
    return (grad,)

def back_keep(v):
    return (v, None)

def back_low(kept, grad):
    return (low(grad),)
low.defvjp(low_keep, low_pass)
low_back.defvjp(back_keep, back_low)

def both_round(values):
    return low(low_back(values))

def matmul_high(left, right):
    return jnp.dot(left, right, precision=MATMUL_PRECISION)

def layer_norm(rows_in, gain, shift):
    center = rows_in - lax.optimization_barrier(jnp.mean(rows_in, axis=-1, keepdims=True))
    spread = lax.optimization_barrier(jnp.mean(center * center, axis=-1, keepdims=True))
    return center * lax.rsqrt(spread + EPS_NORM) * gain + shift

def layer_block(params, block_in, block_len):
    w_qkv, bias_qv, w_out, b_out, gain_one, shift_one, w_up, b_up, w_down, b_down, gain_two, shift_two = params
    batch_count, seq_length, model_width = block_in.shape
    flat_rows = block_in.reshape(batch_count * seq_length, model_width)
    query_rows = both_round(matmul_high(flat_rows, w_qkv[0]) + bias_qv[0])
    key_rows = both_round(matmul_high(flat_rows, w_qkv[1]))
    value_rows = both_round(matmul_high(flat_rows, w_qkv[2]) + bias_qv[1])
    head_count = model_width // HD
    head_shape = (batch_count, seq_length, head_count, HD)
    query_rows = query_rows.reshape(head_shape)
    key_rows = key_rows.reshape(head_shape)
    value_rows = value_rows.reshape(head_shape)
    similarity_scores = jnp.einsum('bqhd,bkhd->bhqk', query_rows, key_rows, precision=MATMUL_PRECISION)
    similarity_scores = low_back(similarity_scores * (1.0 / math.sqrt(HD)))
    token_live = jnp.arange(seq_length)[None, :] < block_len[:, None]
    similarity_scores = jnp.where(token_live[:, None, None, :], similarity_scores, MASKED)
    prob_low = low(jax.nn.softmax(similarity_scores, axis=-1))
    context = jnp.einsum('bhqk,bkhd->bqhd', prob_low, value_rows, precision=MATMUL_PRECISION)
    context = both_round(context.reshape(batch_count * seq_length, model_width))
    attended = low_back(matmul_high(context, w_out) + b_out)
    normed_one = layer_norm(flat_rows + attended, gain_one, shift_one)
    hidden_pre = low_back(matmul_high(low(normed_one), w_up) + b_up)
    hidden_act = low(jax.nn.gelu(hidden_pre, approximate=False))
    ffn_branch = low_back(matmul_high(hidden_act, w_down) + b_down)
    result = layer_norm(normed_one + ffn_branch, gain_two, shift_two)
    result = result.reshape(batch_count, seq_length, model_width)
    live_float = token_live.astype(jnp.float32)
    pooled = lax.optimization_barrier(jnp.sum(result * live_float[:, :, None], axis=1)) / block_len.astype(jnp.float32)[:, None]
    return (result, pooled)

def forward(params, start_rows, lengths):
    block_size = math.gcd(SEQS, max(1, 4096 // LEN))
    block_steps = SEQS // block_size
    blocks_in = start_rows.reshape(block_steps, block_size, LEN, D)
    blocks_len = lengths.reshape(block_steps, block_size)
    run_block = jax.checkpoint(layer_block)

    def scan_step(carried, inputs_pair):
        result, pooled = run_block(params, inputs_pair[0], inputs_pair[1])
        return (carried, (result, pooled))
    unused, (results, pooled) = lax.scan(scan_step, jnp.zeros((), jnp.float32), (blocks_in, blocks_len))
    return (results.reshape(TOKENS, D), pooled.reshape(SEQS, D))

def contrast_terms(pooled, group_ids):
    unit_vectors = pooled * lax.rsqrt(lax.optimization_barrier(jnp.sum(pooled * pooled, axis=-1, keepdims=True)) + 1e-06)
    similarity_scores = SOFTMAX_TEMP * jnp.dot(unit_vectors, unit_vectors.T, precision=MATMUL_PRECISION)
    number = pooled.shape[0]
    itself = jnp.arange(number)[:, None] == jnp.arange(number)[None, :]
    others = jnp.where(itself, MASKED, similarity_scores)
    row_total = jax.nn.logsumexp(others, axis=1)
    positive = jnp.logical_and(group_ids[:, None] == group_ids[None, :], jnp.logical_not(itself))
    positive = positive.astype(jnp.float32)
    matched = lax.optimization_barrier(jnp.sum(positive * similarity_scores, axis=1)) / lax.optimization_barrier(jnp.sum(positive, axis=1))
    return row_total - matched

def reference(layer_input, w_qkv, bias_qv, w_out, b_out, gain_one, shift_one, w_up, b_up, w_down, b_down, gain_two, shift_two, out_cot, lengths, group_ids):
    params = (w_qkv.astype(jnp.float32), bias_qv.astype(jnp.float32), w_out.astype(jnp.float32), b_out.astype(jnp.float32), gain_one.astype(jnp.float32), shift_one.astype(jnp.float32), w_up.astype(jnp.float32), b_up.astype(jnp.float32), w_down.astype(jnp.float32), b_down.astype(jnp.float32), gain_two.astype(jnp.float32), shift_two.astype(jnp.float32))
    start_rows = layer_input.astype(jnp.float32)

    def whole_layer(weights_in, rows_in):
        return forward(weights_in, rows_in, lengths)
    (result, pooled), pull_back = jax.vjp(whole_layer, params, start_rows)

    def anchor_loss(vectors):
        return contrast_terms(vectors, group_ids)
    anchor_terms, pool_back = jax.vjp(anchor_loss, pooled)
    pooled_cot = pool_back(jnp.full(anchor_terms.shape, float(LEN), jnp.float32))[0]
    grad_params, grad_input = pull_back((out_cot.astype(jnp.float32), pooled_cot))
    return (jnp.mean(anchor_terms), result.astype(jnp.bfloat16), grad_input, grad_params[0], grad_params[1], grad_params[2], grad_params[3], grad_params[4], grad_params[5], grad_params[6], grad_params[7], grad_params[8], grad_params[9], grad_params[10], grad_params[11])
```

```python
import functools

import jax
import jax.numpy as jnp
from jax import lax
from jax.experimental import pallas as pl
from jax.experimental.pallas import tpu as pltpu
from jax.sharding import PartitionSpec as P

HD = 64
LEN = 512
LANES = 128
EPS_NORM = 1e-12
EPS_UNIT = 1e-6
SOFTMAX_TEMP = 20.0
MASKED = -1e30
F32 = jnp.float32
BF16 = jnp.bfloat16
VMEM_BYTES = 56 * 2**20

ERFC_SLOPE = 0.41 * 0.7071067811865476
ERFC_POLY = tuple(
    0.5 * c
    for c in (
        0.23389259840606333,
        0.19943405568812744,
        0.36527628560337355,
        -0.195943508470611,
        0.5767329065489298,
        -0.17939241407306944,
    )
)
INV_SQRT_2PI = 0.3989422804014327


def params():
    return pltpu.CompilerParams(vmem_limit_bytes=VMEM_BYTES)


def nn(a, b):
    return lax.dot_general(a, b, (((1,), (0,)), ((), ())), preferred_element_type=F32)


def nt(a, b):
    return lax.dot_general(a, b, (((1,), (1,)), ((), ())), preferred_element_type=F32)


def tn(a, b):
    return lax.dot_general(a, b, (((0,), (0,)), ((), ())), preferred_element_type=F32)


def colsum(a):
    return jnp.sum(a, axis=0, keepdims=True)


def rowmean(a):
    return jnp.mean(a, axis=-1, keepdims=True)


def gelu_pair(u):
    den = 1.0 + ERFC_SLOPE * jnp.abs(u)
    t = pl.reciprocal(den, approx=True)
    t = t * (2.0 - den * t)
    poly = ERFC_POLY[-1]
    for c in ERFC_POLY[-2::-1]:
        poly = poly * t + c
    bell = jnp.exp(-0.5 * (u * u))
    tail = bell * (poly * t)
    cdf = jnp.where(u >= 0, 1.0 - tail, tail)
    return u * cdf, cdf + (u * bell) * INV_SQRT_2PI


def attend_sentence(length, x, weights, bq, bv, qkv_ref, c_ref, lse_ref):
    rows = x.shape[0]
    width = c_ref.shape[1]
    both = nn(x, jnp.concatenate(weights, axis=1))
    qkv_ref[:, :width] = (both[:, :width] + bq).astype(BF16)
    qkv_ref[:, width : 2 * width] = both[:, width : 2 * width].astype(BF16)
    qkv_ref[:, 2 * width :] = (both[:, 2 * width :] + bv).astype(BF16)
    low = lax.broadcasted_iota(jnp.int32, (rows, LANES), 1) < HD
    live = lax.broadcasted_iota(jnp.int32, (rows, LANES), 0) < length
    bias = jnp.where(live, 0.0, MASKED).astype(F32)
    zero = jnp.zeros((rows, LANES), BF16)
    for p in range(width // LANES):
        at = LANES * p
        q = qkv_ref[:, at : at + LANES] * 0.125
        k = qkv_ref[:, width + at : width + at + LANES]
        v = qkv_ref[:, 2 * width + at : 2 * width + at + LANES]
        vt = v.T
        outs = []
        for h in range(2):
            km = jnp.where(low, k, zero) if h == 0 else jnp.where(low, zero, k)
            scores = nt(km, q)
            parts, tops, sums = [], [], []
            for j in range(rows // LANES):
                piece = scores[:, LANES * j : LANES * j + LANES] + bias
                top = jnp.max(piece, axis=0, keepdims=True)
                e = jnp.exp(piece - top)
                parts.append(e.astype(BF16))
                tops.append(top)
                sums.append(colsum(e))
            top = jnp.concatenate(tops, axis=1)
            total = jnp.concatenate(sums, axis=1)
            ct = nn(vt[HD * h : HD * h + HD], jnp.concatenate(parts, axis=1))
            outs.append(ct / total)
            lse_ref[0, 2 * p + h : 2 * p + h + 1, :] = top + jnp.log(total)
        c_ref[:, at : at + LANES] = jnp.concatenate(outs, axis=0).T.astype(BF16)


def attn_own_kernel(len_ref, x_ref, w_ref, bq_ref, bv_ref, qkv_ref, c_ref, lse_ref):
    weights = [w_ref[c] for c in range(3)]
    attend_sentence(
        len_ref[pl.program_id(0)], x_ref[...], weights, bq_ref[...], bv_ref[...], qkv_ref, c_ref, lse_ref
    )


def attn_other_kernel(
    len_ref, x_ref, w0, w1, w2, w3, bq_ref, bv_ref, qkv_ref, c_ref, lse_ref, w_ref
):
    quarter = len_ref[len_ref.shape[0] - 1]

    @pl.when(pl.program_id(0) == 0)
    def _():
        for s, ref in enumerate((w0, w1, w2, w3)):
            for c in range(3):
                w_ref[c, quarter ^ s] = ref[c]

    shape = w_ref.shape
    weights = [w_ref[c].reshape(shape[1] * shape[2], shape[3]) for c in range(3)]
    attend_sentence(
        len_ref[pl.program_id(0)], x_ref[...], weights, bq_ref[...], bv_ref[...], qkv_ref, c_ref, lse_ref
    )


def whole(shape):
    return pl.BlockSpec(shape, lambda *_: (0,) * len(shape))


def attn_forward(scalars, x, weights, bq, bv):
    tokens, model = x.shape
    width = bq.shape[1]
    sents = tokens // LEN
    rows = pl.BlockSpec((LEN, model), lambda s, l: (s, 0))
    out_specs = [
        pl.BlockSpec((LEN, 3 * width), lambda s, l: (s, 0)),
        pl.BlockSpec((LEN, width), lambda s, l: (s, 0)),
        pl.BlockSpec((1, width // HD, LEN), lambda s, l: (s, 0, 0)),
    ]
    out_shape = [
        jax.ShapeDtypeStruct((tokens, 3 * width), BF16),
        jax.ShapeDtypeStruct((tokens, width), BF16),
        jax.ShapeDtypeStruct((sents, width // HD, LEN), F32),
    ]
    own = len(weights) == 1
    if not own:
        full = (3, 4, model // 4, width)
        out_specs.append(whole(full))
        out_shape.append(jax.ShapeDtypeStruct(full, BF16))
    return pl.pallas_call(
        attn_own_kernel if own else attn_other_kernel,
        grid_spec=pltpu.PrefetchScalarGridSpec(
            num_scalar_prefetch=1,
            grid=(sents,),
            in_specs=[rows] + [whole(w.shape) for w in weights] + [whole(bq.shape)] * 2,
            out_specs=out_specs,
        ),
        out_shape=out_shape,
        compiler_params=params(),
        name="attn_fwd",
    )(scalars, x, *weights, bq, bv)


def attn_back_kernel(len_ref, qkv_ref, do_ref, lse_ref, grad_ref, sum_ref):
    s = pl.program_id(0)
    length = len_ref[s]
    rows, width = do_ref.shape
    low = lax.broadcasted_iota(jnp.int32, (rows, LANES), 1) < HD
    live = lax.broadcasted_iota(jnp.int32, (rows, LANES), 0) < length
    bias = jnp.where(live, 0.0, MASKED).astype(F32)
    zero = jnp.zeros((rows, LANES), BF16)

    @pl.when(s == 0)
    def _():
        sum_ref[...] = jnp.zeros_like(sum_ref)

    for p in range(width // LANES):
        at = LANES * p
        q = qkv_ref[:, at : at + LANES] * 0.125
        k = qkv_ref[:, width + at : width + at + LANES]
        v = qkv_ref[:, 2 * width + at : 2 * width + at + LANES]
        do = do_ref[:, at : at + LANES]
        kt = k.T
        dqs, dks, dvs = [], [], []
        for h in range(2):
            km = jnp.where(low, k, zero) if h == 0 else jnp.where(low, zero, k)
            vm = jnp.where(low, v, zero) if h == 0 else jnp.where(low, zero, v)
            lse = lse_ref[0, 2 * p + h : 2 * p + h + 1, :]
            scores = nt(km, q)
            dprob = nt(vm, do)
            probs, dscores = [], []
            for j in range(rows // LANES):
                cols = slice(LANES * j, LANES * j + LANES)
                e = jnp.exp(scores[:, cols] + bias - lse[:, cols])
                probs.append(e.astype(BF16))
                dp = dprob[:, cols]
                dscores.append((e * (dp - colsum(e * dp))).astype(BF16))
            prob = jnp.concatenate(probs, axis=1)
            dscore = jnp.concatenate(dscores, axis=1)
            dvs.append(nn(prob, do))
            dks.append(nn(dscore, q))
            dqs.append(nn(kt[HD * h : HD * h + HD], dscore))
        dq = (jnp.concatenate(dqs, axis=0).T * 0.125).astype(BF16)
        dk = jnp.where(low, dks[0], dks[1]).astype(BF16)
        dv = jnp.where(low, dvs[0], dvs[1]).astype(BF16)
        grad_ref[:, at : at + LANES] = dq
        grad_ref[:, width + at : width + at + LANES] = dk
        grad_ref[:, 2 * width + at : 2 * width + at + LANES] = dv
        sum_ref[0:1, at : at + LANES] += colsum(dq.astype(F32))
        sum_ref[1:2, at : at + LANES] += colsum(dv.astype(F32))


def attn_backward(lens, qkv, do, lse):
    tokens, width = do.shape
    rows = lambda cols: pl.BlockSpec((LEN, cols), lambda s, l: (s, 0))
    return pl.pallas_call(
        attn_back_kernel,
        grid_spec=pltpu.PrefetchScalarGridSpec(
            num_scalar_prefetch=1,
            grid=(tokens // LEN,),
            in_specs=[
                rows(3 * width),
                rows(width),
                pl.BlockSpec((1, width // HD, LEN), lambda s, l: (s, 0, 0)),
            ],
            out_specs=[rows(3 * width), whole((2, width))],
        ),
        out_shape=[
            jax.ShapeDtypeStruct((tokens, 3 * width), BF16),
            jax.ShapeDtypeStruct((2, width), F32),
        ],
        compiler_params=params(),
        name="attn_bwd",
    )(lens, qkv, do, lse)


def normalize(r):
    center = r - rowmean(r)
    inverse = lax.rsqrt(rowmean(center * center) + EPS_NORM)
    return center * inverse, inverse


def project_kernel(
    q_ref, x_ref, c_own, c_oth, w_own, w0, w1, w2, w3, b_ref, g_ref, s_ref,
    h_ref, low_ref, n_ref, inv_ref, w_ref,
):
    @pl.when(pl.program_id(0) == 0)
    def _():
        for s, ref in enumerate((w0, w1, w2, w3)):
            w_ref[q_ref[0] ^ s] = ref[...]

    shape = w_ref.shape
    other = w_ref[...].reshape(shape[0] * shape[1], shape[2])
    attended = nn(c_own[...], w_own[...]) + nn(c_oth[...], other) + b_ref[...]
    normal, inverse = normalize(x_ref[...].astype(F32) + attended)
    h = normal * g_ref[...] + s_ref[...]
    h_ref[...] = h
    low_ref[...] = h.astype(BF16)
    n_ref[...] = normal.astype(BF16)
    inv_ref[...] = inverse


def project_forward(quarter, x, c_own, c_oth, w_own, slots, b_out, gain, shift):
    tokens, model = x.shape
    block = 512
    rows = lambda cols: pl.BlockSpec((block, cols), lambda i, q: (i, 0))
    vec = whole((1, model))
    full = (4,) + slots[0].shape
    return pl.pallas_call(
        project_kernel,
        grid_spec=pltpu.PrefetchScalarGridSpec(
            num_scalar_prefetch=1,
            grid=(tokens // block,),
            in_specs=[rows(model), rows(c_own.shape[1]), rows(c_own.shape[1]), whole(w_own.shape)]
            + [whole(s.shape) for s in slots]
            + [vec] * 3,
            out_specs=[rows(model), rows(model), rows(model), rows(1), whole(full)],
        ),
        out_shape=[
            jax.ShapeDtypeStruct((tokens, model), F32),
            jax.ShapeDtypeStruct((tokens, model), BF16),
            jax.ShapeDtypeStruct((tokens, model), BF16),
            jax.ShapeDtypeStruct((tokens, 1), F32),
            jax.ShapeDtypeStruct(full, BF16),
        ],
        compiler_params=params(),
        name="project_fwd",
    )(quarter, x, c_own, c_oth, w_own, *slots, b_out, gain, shift)


def feed(h, wu_ref, bu_ref, wd, g_ref, gp_ref):
    units = wu_ref.shape[1]
    chunk = units // 3
    total = None
    for j in range(3):
        cols = slice(chunk * j, chunk * j + chunk)
        act, slope = gelu_pair(nn(h, wu_ref[:, cols]) + bu_ref[:, cols])
        act = act.astype(BF16)
        g_ref[:, cols] = act
        gp_ref[:, cols] = slope.astype(BF16)
        part = nn(act, wd(cols))
        total = part if total is None else total + part
    return total


def feed_own_kernel(h_ref, wu_ref, bu_ref, wd_ref, g_ref, gp_ref, f_ref):
    f_ref[...] = feed(h_ref[...], wu_ref, bu_ref, lambda cols: wd_ref[cols, :], g_ref, gp_ref)


def feed_own(h, wu, bu, wd):
    tokens, model = h.shape
    units = wu.shape[1]
    block = 256
    rows = lambda cols: pl.BlockSpec((block, cols), lambda i: (i, 0))
    return pl.pallas_call(
        feed_own_kernel,
        grid=(tokens // block,),
        in_specs=[rows(model), whole(wu.shape), whole(bu.shape), whole(wd.shape)],
        out_specs=[rows(units), rows(units), rows(model)],
        out_shape=[
            jax.ShapeDtypeStruct((tokens, units), BF16),
            jax.ShapeDtypeStruct((tokens, units), BF16),
            jax.ShapeDtypeStruct((tokens, model), F32),
        ],
        compiler_params=params(),
        name="feed_own",
    )(h, wu, bu, wd)


def feed_other_kernel(
    q_ref, low_ref, h_ref, f_ref, u0, u1, u2, u3, d0, d1, d2, d3, bu_ref, bd_ref, gain_ref, shift_ref,
    g_ref, gp_ref, out_ref, n_ref, inv_ref, pool_ref, wu_ref, wd_ref,
):
    i = pl.program_id(0)
    quarter = q_ref[q_ref.shape[0] - 1]
    part = u0.shape[1]

    @pl.when(i == 0)
    def _():
        for s, (up, down) in enumerate(((u0, d0), (u1, d1), (u2, d2), (u3, d3))):
            at = quarter ^ s
            wu_ref[:, pl.ds(pl.multiple_of(at * part, LANES), part)] = up[...]
            wd_ref[at] = down[...]
        pool_ref[...] = jnp.zeros_like(pool_ref)

    shape = wd_ref.shape
    down = wd_ref[...].reshape(shape[0] * shape[1], shape[2])
    total = feed(low_ref[...], wu_ref, bu_ref, lambda cols: down[cols, :], g_ref, gp_ref)
    normal, inverse = normalize(h_ref[...] + (f_ref[...] + total + bd_ref[...]))
    y = normal * gain_ref[...] + shift_ref[...]
    out_ref[...] = y.astype(BF16)
    n_ref[...] = normal.astype(BF16)
    inv_ref[...] = inverse
    block = y.shape[0]
    per = LEN // block
    sent = i // per
    length = q_ref[sent]
    first = (i - sent * per) * block
    live = lax.broadcasted_iota(jnp.int32, y.shape, 0) + first < length
    gathered = colsum(jnp.where(live, y, 0.0)) / length.astype(F32)
    pool_ref[pl.ds(sent, 1), :] += gathered


def feed_other(scalars, low, h, f, up, down, bu, bd, gain, shift):
    tokens, model = low.shape
    units = bu.shape[1]
    block = 256
    sents = tokens // LEN
    rows = lambda cols: pl.BlockSpec((block, cols), lambda i, q: (i, 0))
    vec = whole((1, model))
    full_up = (model, units)
    full_down = (4,) + down[0].shape
    return pl.pallas_call(
        feed_other_kernel,
        grid_spec=pltpu.PrefetchScalarGridSpec(
            num_scalar_prefetch=1,
            grid=(tokens // block,),
            in_specs=[rows(model)] * 3
            + [whole(w.shape) for w in up]
            + [whole(w.shape) for w in down]
            + [whole(bu.shape)]
            + [vec] * 3,
            out_specs=[
                rows(units), rows(units), rows(model), rows(model), rows(1), whole((sents, model)),
                whole(full_up), whole(full_down),
            ],
        ),
        out_shape=[
            jax.ShapeDtypeStruct((tokens, units), BF16),
            jax.ShapeDtypeStruct((tokens, units), BF16),
            jax.ShapeDtypeStruct((tokens, model), BF16),
            jax.ShapeDtypeStruct((tokens, model), BF16),
            jax.ShapeDtypeStruct((tokens, 1), F32),
            jax.ShapeDtypeStruct((sents, model), F32),
            jax.ShapeDtypeStruct(full_up, BF16),
            jax.ShapeDtypeStruct(full_down, BF16),
        ],
        compiler_params=params(),
        name="feed_other",
    )(scalars, low, h, f, *up, *down, bu, bd, gain, shift)


def exact(a, b, dims):
    return lax.dot_general(
        a, b, (dims, ((), ())), precision=lax.Precision.HIGHEST, preferred_element_type=F32
    )


def loss_kernel(s_ref, slot_ref, row_ref, col_ref, loss_ref, cot_ref, pool_ref, grad_ref):
    local = cot_ref.shape[0]
    rank = s_ref[0]
    count = slot_ref.shape[0]
    for s in range(count // local):
        for i in range(local):
            pool_ref[pl.ds((rank ^ s) * local + i, 1), :] = slot_ref[pl.ds(local * s + i, 1), :]
    pooled = pool_ref[...]
    scale = lax.rsqrt(jnp.sum(pooled * pooled, axis=-1, keepdims=True) + EPS_UNIT)
    unit = pooled * scale
    score = SOFTMAX_TEMP * exact(unit, unit, ((1,), (1,)))
    itself = lax.broadcasted_iota(jnp.int32, score.shape, 0) == lax.broadcasted_iota(
        jnp.int32, score.shape, 1
    )
    others = jnp.where(itself, MASKED, score)
    top = jnp.max(others, axis=1, keepdims=True)
    power = jnp.exp(others - top)
    total = jnp.sum(power, axis=1, keepdims=True)
    match = jnp.logical_and(col_ref[...] == row_ref[...], jnp.logical_not(itself)).astype(F32)
    number = jnp.sum(match, axis=1, keepdims=True)
    matched = jnp.sum(match * score, axis=1, keepdims=True) / number
    terms = top + jnp.log(total) - matched
    loss_ref[...] = jnp.sum(terms, axis=0, keepdims=True) / count
    dscore = float(LEN) * (power / total - match / number)
    dunit = SOFTMAX_TEMP * (exact(dscore, unit, ((1,), (0,))) + exact(dscore, unit, ((0,), (0,))))
    grad_ref[...] = scale * (dunit - unit * jnp.sum(unit * dunit, axis=-1, keepdims=True))
    for i in range(local):
        own = grad_ref[pl.ds(rank * local + i, 1), :]
        cot_ref[i : i + 1, :] = own / s_ref[1 + i].astype(F32)


def loss_call(scalars, slots, group_ids, local):
    count, model = slots.shape
    return pl.pallas_call(
        loss_kernel,
        grid_spec=pltpu.PrefetchScalarGridSpec(
            num_scalar_prefetch=1,
            grid=(1,),
            in_specs=[whole((count, model)), whole((1, count)), whole((count, 1))],
            out_specs=[whole((1, 1)), whole((local, model))],
            scratch_shapes=[pltpu.VMEM((count, model), F32), pltpu.VMEM((count, model), F32)],
        ),
        out_shape=[jax.ShapeDtypeStruct((1, 1), F32), jax.ShapeDtypeStruct((local, model), F32)],
        compiler_params=params(),
        name="loss",
    )(scalars, slots, group_ids.reshape(1, count), group_ids.reshape(count, 1))


def norm_back(upstream, normal, inverse, gain):
    scaled = upstream * gain
    return inverse * (scaled - rowmean(scaled) - normal * rowmean(scaled * normal))


def norm_two_kernel(len_ref, cot_ref, n_ref, inv_ref, gain_ref, pool_ref, df_ref, sum_ref):
    s = pl.program_id(0)
    normal = n_ref[...].astype(F32)
    live = lax.broadcasted_iota(jnp.int32, normal.shape, 0) < len_ref[s]
    up = cot_ref[...].astype(F32) + jnp.where(live, pool_ref[pl.ds(s, 1), :], 0.0)
    df = norm_back(up, normal, inv_ref[...], gain_ref[...]).astype(BF16)
    df_ref[...] = df

    @pl.when(s == 0)
    def _():
        sum_ref[...] = jnp.zeros_like(sum_ref)

    sum_ref[0:1, :] += colsum(df.astype(F32))
    sum_ref[1:2, :] += colsum(up * normal)
    sum_ref[2:3, :] += colsum(up)


def norm_two_backward(lens, cot, normal, inverse, gain, pool_cot):
    tokens, model = cot.shape
    rows = lambda cols: pl.BlockSpec((LEN, cols), lambda s, l: (s, 0))
    return pl.pallas_call(
        norm_two_kernel,
        grid_spec=pltpu.PrefetchScalarGridSpec(
            num_scalar_prefetch=1,
            grid=(tokens // LEN,),
            in_specs=[rows(model), rows(model), rows(1), whole((1, model)), whole(pool_cot.shape)],
            out_specs=[rows(model), whole((3, model))],
        ),
        out_shape=[jax.ShapeDtypeStruct((tokens, model), BF16), jax.ShapeDtypeStruct((3, model), F32)],
        compiler_params=params(),
        name="norm_two_bwd",
    )(lens, cot, normal, inverse, gain, pool_cot)


def middle_kernel(
    df_ref, gp_own, gp_oth, wu_own, wu_oth, wd_own, wd_oth, n_ref, inv_ref, gain_ref, wo_own, wo_oth,
    du_own, du_oth, da_ref, dc_own, dc_oth, usum_ref, sum_ref,
):
    i = pl.program_id(0)

    @pl.when(i == 0)
    def _():
        usum_ref[...] = jnp.zeros_like(usum_ref)
        sum_ref[...] = jnp.zeros_like(sum_ref)

    df = df_ref[...]
    total = df.astype(F32)
    units = wu_own.shape[1]
    chunk = units // 3
    sides = ((gp_oth, wu_oth, wd_oth, du_oth), (gp_own, wu_own, wd_own, du_own))
    for side, (gp_ref, wu_ref, wd_ref, du_ref) in enumerate(sides):
        for j in range(3):
            cols = slice(chunk * j, chunk * j + chunk)
            du = (nt(df, wd_ref[cols, :]) * gp_ref[:, cols].astype(F32)).astype(BF16)
            du_ref[:, cols] = du
            usum_ref[side : side + 1, cols] += colsum(du.astype(F32))
            total = total + nt(du, wu_ref[:, cols])
    normal = n_ref[...].astype(F32)
    da = norm_back(total, normal, inv_ref[...], gain_ref[...]).astype(BF16)
    da_ref[...] = da
    dc_own[...] = nt(da, wo_own[...]).astype(BF16)
    dc_oth[...] = nt(da, wo_oth[...]).astype(BF16)
    sum_ref[0:1, :] += colsum(total * normal)
    sum_ref[1:2, :] += colsum(total)
    sum_ref[2:3, :] += colsum(da.astype(F32))


def middle_backward(df, gp_own, gp_oth, wu_own, wu_oth, wd_own, wd_oth, normal, inverse, gain, wo_own, wo_oth):
    tokens, model = df.shape
    units = wu_own.shape[1]
    width = wo_own.shape[0]
    block = 256
    rows = lambda cols: pl.BlockSpec((block, cols), lambda i: (i, 0))
    bf = lambda cols: jax.ShapeDtypeStruct((tokens, cols), BF16)
    return pl.pallas_call(
        middle_kernel,
        grid=(tokens // block,),
        in_specs=[rows(model), rows(units), rows(units)]
        + [whole(w.shape) for w in (wu_own, wu_oth, wd_own, wd_oth)]
        + [rows(model), rows(1), whole((1, model)), whole(wo_own.shape), whole(wo_oth.shape)],
        out_specs=[
            rows(units), rows(units), rows(model), rows(width), rows(width),
            whole((2, units)), whole((3, model)),
        ],
        out_shape=[
            bf(units), bf(units), bf(model), bf(width), bf(width),
            jax.ShapeDtypeStruct((2, units), F32), jax.ShapeDtypeStruct((3, model), F32),
        ],
        compiler_params=params(),
        name="middle_bwd",
    )(df, gp_own, gp_oth, wu_own, wu_oth, wd_own, wd_oth, normal, inverse, gain, wo_own, wo_oth)


def bit(value, at):
    return (value >> at) & 1


def split_store(d, even, odd, keep_ref, send_ref, at):
    flip = bit(d, 0) == 0
    keep_ref[at] = jnp.where(flip, even, odd).astype(BF16)
    send_ref[at] = jnp.where(flip, odd, even).astype(BF16)


def dense_grad_kernel(d_ref, a_ref, b_ref, keep_ref, send_ref):
    d = d_ref[0]
    grad = tn(a_ref[...], b_ref[...])
    step = keep_ref.shape[3]
    for x in range(2):
        for z in range(2):
            at = (4 * z + 2 * x) * step
            split_store(
                d, grad[at : at + step], grad[at + step : at + 2 * step], keep_ref, send_ref,
                (x ^ bit(d, 1), z ^ bit(d, 2), 0),
            )


def dense_grad(d, a, b, cut_left):
    tokens = a.shape[0]
    left = a.shape[1] // (2 if cut_left else 1)
    right = b.shape[1] // (1 if cut_left else 2)
    step = left // 8
    block = pl.BlockSpec((2, 2, 1, step, right), lambda i, d: (0, 0, i ^ bit(d[0], 3), 0, 0))
    shape = jax.ShapeDtypeStruct((2, 2, 2, step, right), BF16)
    return pl.pallas_call(
        dense_grad_kernel,
        grid_spec=pltpu.PrefetchScalarGridSpec(
            num_scalar_prefetch=1,
            grid=(2,),
            in_specs=[
                pl.BlockSpec((tokens, left), (lambda i, d: (0, i)) if cut_left else (lambda i, d: (0, 0))),
                pl.BlockSpec((tokens, right), (lambda i, d: (0, 0)) if cut_left else (lambda i, d: (0, i))),
            ],
            out_specs=[block, block],
        ),
        out_shape=[shape, shape],
        compiler_params=params(),
        name="dense_grad",
    )(d, a, b)


def heads_grad_kernel(d_ref, c_ref, da_ref, x_ref, dqkv_ref, keep_ref, send_ref):
    d = d_ref[0]
    width = c_ref.shape[1]
    out = tn(c_ref[...], da_ref[...])
    proj = tn(x_ref[...], dqkv_ref[...])
    step = width // 8

    def block(b):
        row, col = (b & 7) * step, (b >> 3) * width
        pieces = [out[row : row + step, col : col + width]]
        pieces += [proj[b * step : b * step + step, c * width : c * width + width] for c in range(3)]
        return jnp.concatenate(pieces, axis=0)

    for x in range(2):
        for z in range(2):
            for w in range(2):
                b = 8 * w + 4 * z + 2 * x
                split_store(
                    d, block(b), block(b + 1), keep_ref, send_ref,
                    (x ^ bit(d, 1), z ^ bit(d, 2), w ^ bit(d, 3)),
                )


def heads_grad(d, c, da, x, dqkv):
    width = c.shape[1]
    full = (2, 2, 2, width // 2, width)
    shape = jax.ShapeDtypeStruct(full, BF16)
    return pl.pallas_call(
        heads_grad_kernel,
        grid_spec=pltpu.PrefetchScalarGridSpec(
            num_scalar_prefetch=1,
            grid=(1,),
            in_specs=[whole(a.shape) for a in (c, da, x, dqkv)],
            out_specs=[whole(full), whole(full)],
        ),
        out_shape=[shape, shape],
        compiler_params=params(),
        name="heads_grad",
    )(d, c, da, x, dqkv)


def input_grad_kernel(own_ref, oth_ref, w_own, w_oth, da_ref, out_ref):
    total = da_ref[...].astype(F32)
    for grad, w in ((own_ref, w_own), (oth_ref, w_oth)):
        total = total + nt(grad[...], jnp.concatenate([w[c] for c in range(3)], axis=1))
    out_ref[...] = total


def input_grad(own, oth, w_own, w_oth, da):
    tokens, model = da.shape
    block = 512
    rows = lambda cols: pl.BlockSpec((block, cols), lambda i: (i, 0))
    return pl.pallas_call(
        input_grad_kernel,
        grid=(tokens // block,),
        in_specs=[rows(own.shape[1]), rows(own.shape[1]), whole(w_own.shape), whole(w_oth.shape), rows(model)],
        out_specs=rows(model),
        out_shape=jax.ShapeDtypeStruct((tokens, model), F32),
        compiler_params=params(),
        name="input_grad",
    )(own, oth, w_own, w_oth, da)


def place_kernel(d_ref, near_ref, far_ref, *out_refs):
    flip = bit(d_ref[0], 0) == 0
    near, far = near_ref[0, 0, 0].astype(F32), far_ref[0, 0, 0].astype(F32)
    even, odd = jnp.where(flip, near, far), jnp.where(flip, far, near)
    if len(out_refs) == 1:
        step = near.shape[0]
        out_refs[0][:step] = even
        out_refs[0][step:] = odd
        return
    out_ref, proj_ref = out_refs
    step = near.shape[0] // 4
    out_ref[:step] = even[:step]
    out_ref[step:] = odd[:step]
    for c in range(3):
        rows = slice(step * (c + 1), step * (c + 2))
        proj_ref[c, :step] = even[rows]
        proj_ref[c, step:] = odd[rows]


def pair_at(x, z, w, d):
    return (x ^ bit(d[0], 1)) + 2 * (z ^ bit(d[0], 2)), w ^ bit(d[0], 3)


def place(d, near, far, kind):
    step, cols = near.shape[3:]
    block = pl.BlockSpec((1, 1, 1, step, cols), lambda x, z, w, d: (x, z, w, 0, 0))

    def pair(x, z, w, d):
        low, high = pair_at(x, z, w, d)
        return low + 4 * high

    if kind == "rows":
        shapes = [(16 * step, cols)]
        specs = [pl.BlockSpec((2 * step, cols), lambda x, z, w, d: (pair(x, z, w, d), 0))]
    elif kind == "columns":
        shapes = [(8 * step, 2 * cols)]
        specs = [pl.BlockSpec((2 * step, cols), lambda x, z, w, d: pair_at(x, z, w, d))]
    else:
        part = step // 4
        shapes = [(8 * part, 2 * cols), (3, 16 * part, cols)]
        specs = [
            pl.BlockSpec((2 * part, cols), lambda x, z, w, d: pair_at(x, z, w, d)),
            pl.BlockSpec((3, 2 * part, cols), lambda x, z, w, d: (0, pair(x, z, w, d), 0)),
        ]
    return pl.pallas_call(
        place_kernel,
        grid_spec=pltpu.PrefetchScalarGridSpec(
            num_scalar_prefetch=1, grid=(2, 2, 2), in_specs=[block, block], out_specs=specs
        ),
        out_shape=[jax.ShapeDtypeStruct(s, F32) for s in shapes],
        compiler_params=params(),
        name="place",
    )(d, near, far)


def swap(x, axis, mask):
    size = lax.axis_size(axis)
    return lax.ppermute(x, axis, [(i, i ^ mask) for i in range(size)])


def swap_all(x, mask):
    size = lax.axis_size("dp") * lax.axis_size("tensor")
    return lax.ppermute(x, ("dp", "tensor"), [(i, i ^ mask) for i in range(size)])


def gather_slots(mine):
    first = swap(mine, "tensor", 1)
    second = swap(first, "dp", 2)
    return first, swap(first, "dp", 1), second, swap(second, "dp", 1)


def add_low(*terms):
    total = terms[0].astype(F32)
    for t in terms[1:]:
        total = total + t.astype(F32)
    return total.astype(BF16)


def levels():
    return lax.axis_size("dp").bit_length() - 1


def reduce_grads(keep_own, send_own, keep_oth, send_oth):
    other = add_low(keep_oth, swap(send_oth, "dp", 1))
    mine = add_low(keep_own, swap(send_own, "dp", 1), swap(other, "tensor", 1))
    for at in range(1, 4):
        mine = add_low(mine[0], swap(mine[1], "dp", 1 << at))
    for at in range(4, levels()):
        mine = add_low(mine, swap(mine, "dp", 1 << at))
    for at in range(3, 0, -1):
        mine = jnp.stack([mine, swap(mine, "dp", 1 << at)])
    return mine, swap(mine, "dp", 1)


def reduce_small(rep, own, oth):
    moved = swap(jnp.concatenate([rep, oth]), "tensor", 1)
    total = jnp.concatenate([rep, own]) + moved
    for at in range(levels()):
        total = total + swap(total, "dp", 1 << at)
    return total


def gather_pooled(pooled):
    bits = levels() + 1
    at = 0
    while at < bits:
        step = min(3 if at == 0 else 2, bits - at)
        pooled = jnp.concatenate(
            [pooled] + [swap_all(pooled, m << at) for m in range(1, 1 << step)], axis=0
        )
        at += step
    return pooled


def per_device(
    layer_input, w_qkv, bias_qv, w_out, b_out, gain_one, shift_one, w_up, b_up, w_down, b_down,
    gain_two, shift_two, out_cot, lengths, group_ids,
):
    tensor_size = lax.axis_size("tensor")
    position = lax.axis_index("tensor")
    d = lax.axis_index("dp")
    quarter = d & 3
    model = layer_input.shape[1]
    width = w_qkv.shape[2]
    units = w_up.shape[1]
    local = lengths.shape[0] // tensor_size
    lens = lax.dynamic_slice_in_dim(lengths, position * local, local, 0)
    dvec = d.reshape(1).astype(jnp.int32)
    qvec = quarter.reshape(1).astype(jnp.int32)
    lens_q = jnp.concatenate([lens, qvec])

    pick = lambda a, axis: lax.dynamic_index_in_dim(a, quarter, axis, keepdims=False)
    slots_qkv = gather_slots(pick(w_qkv.reshape(3, 4, model // 4, width), 1))
    biases = jnp.concatenate([bias_qv.reshape(-1), b_up])
    biases_oth = swap(biases, "tensor", 1)
    slots_out = gather_slots(pick(w_out.reshape(4, width // 4, model), 0))
    slots_up = gather_slots(lax.dynamic_slice_in_dim(w_up, quarter * (units // 4), units // 4, 1))
    slots_down = gather_slots(pick(w_down.reshape(4, units // 4, model), 0))
    bq_own, bv_own, bu_own = bias_qv[0:1], bias_qv[1:2], b_up.reshape(1, units)
    bq_oth = biases_oth[:width].reshape(1, width)
    bv_oth = biases_oth[width : 2 * width].reshape(1, width)
    bu_oth = biases_oth[2 * width :].reshape(1, units)
    row = lambda v: v.reshape(1, -1)

    qkv_own, c_own, lse_own = attn_forward(lens_q, layer_input, [w_qkv], bq_own, bv_own)
    qkv_oth, c_oth, lse_oth, wq_oth = attn_forward(lens_q, layer_input, slots_qkv, bq_oth, bv_oth)
    wq_oth = wq_oth.reshape(3, model, width)
    h1, h1_low, normal_one, inverse_one, wo_oth = project_forward(
        qvec, layer_input, c_own, c_oth, w_out, slots_out, row(b_out), row(gain_one), row(shift_one)
    )
    wo_oth = wo_oth.reshape(width, model)
    g_own, gp_own, f_own = feed_own(h1_low, w_up, bu_own, w_down)
    g_oth, gp_oth, output, normal_two, inverse_two, pooled, wu_oth, wd_oth = feed_other(
        lens_q, h1_low, h1, f_own, slots_up, slots_down, bu_oth, row(b_down), row(gain_two), row(shift_two)
    )
    wd_oth = wd_oth.reshape(units, model)

    rank = d * tensor_size + position
    scalars = jnp.concatenate([rank.reshape(1).astype(jnp.int32), lens])
    loss, pool_cot = loss_call(scalars, gather_pooled(pooled), group_ids, local)

    df, sums_two = norm_two_backward(lens, out_cot, normal_two, inverse_two, row(gain_two), pool_cot)
    down_oth = dense_grad(dvec, g_oth, df, True)
    down_own = dense_grad(dvec, g_own, df, True)
    near_down, far_down = reduce_grads(*down_own, *down_oth)
    du_own, du_oth, da, dc_own, dc_oth, sums_units, sums_one = middle_backward(
        df, gp_own, gp_oth, w_up, wu_oth, w_down, wd_oth, normal_one, inverse_one, row(gain_one), w_out, wo_oth
    )
    up_oth = dense_grad(dvec, h1_low, du_oth, False)
    up_own = dense_grad(dvec, h1_low, du_own, False)
    near_up, far_up = reduce_grads(*up_own, *up_oth)
    dqkv_oth, sums_oth = attn_backward(lens, qkv_oth, dc_oth, lse_oth)
    heads_oth = heads_grad(dvec, c_oth, da, layer_input, dqkv_oth)
    dqkv_own, sums_own = attn_backward(lens, qkv_own, dc_own, lse_own)
    heads_own = heads_grad(dvec, c_own, da, layer_input, dqkv_own)
    near_heads, far_heads = reduce_grads(*heads_own, *heads_oth)
    grad_input = input_grad(dqkv_own, dqkv_oth, w_qkv, wq_oth, da)
    small = reduce_small(
        jnp.concatenate([sums_two.reshape(-1), sums_one.reshape(-1)]),
        jnp.concatenate([sums_own.reshape(-1), sums_units[1]]),
        jnp.concatenate([sums_oth.reshape(-1), sums_units[0]]),
    )
    (grad_w_down,) = place(dvec, near_down, far_down, "rows")
    (grad_w_up,) = place(dvec, near_up, far_up, "columns")
    grad_w_out, grad_w_qkv = place(dvec, near_heads, far_heads, "heads")
    vec = lambda i: small[i * model : (i + 1) * model]
    rest = small[6 * model :]
    return (
        loss.reshape(()),
        output,
        grad_input,
        grad_w_qkv,
        rest[: 2 * width].reshape(2, width),
        grad_w_out,
        vec(5),
        vec(3),
        vec(4),
        grad_w_up,
        rest[2 * width :],
        grad_w_down,
        vec(0),
        vec(1),
        vec(2),
    )


def solution(mesh):
    rows = P(("dp", "tensor"), None)
    in_specs = (
        rows,
        P(None, None, "tensor"),
        P(None, "tensor"),
        P("tensor", None),
        P(),
        P(),
        P(),
        P(None, "tensor"),
        P("tensor"),
        P("tensor", None),
        P(),
        P(),
        P(),
        rows,
        P("dp"),
        P(),
    )
    out_specs = (
        P(),
        rows,
        rows,
        P(None, None, "tensor"),
        P(None, "tensor"),
        P("tensor", None),
        P(),
        P(),
        P(),
        P(None, "tensor"),
        P("tensor"),
        P("tensor", None),
        P(),
        P(),
        P(),
    )
    return jax.shard_map(
        per_device, mesh=mesh, in_specs=in_specs, out_specs=out_specs, check_vma=False
    )
```

```python
import functools

import jax
import jax.numpy as jnp
from jax import lax
from jax.experimental import pallas as pl
from jax.experimental.pallas import tpu as pltpu
from jax.sharding import PartitionSpec as P

HD = 64
LEN = 512
LANES = 128
EPS_NORM = 1e-12
EPS_UNIT = 1e-6
SOFTMAX_TEMP = 20.0
MASKED = -1e30
F32 = jnp.float32
BF16 = jnp.bfloat16
COST_SCALE = 0.1

ERFC_SLOPE = 0.41 * 0.7071067811865476
ERFC_POLY = tuple(
    0.5 * c
    for c in (
        0.23389259840606333,
        0.19943405568812744,
        0.36527628560337355,
        -0.195943508470611,
        0.5767329065489298,
        -0.17939241407306944,
    )
)
INV_SQRT_2PI = 0.3989422804014327


def cost(micros):
    return pl.CostEstimate(
        flops=int(micros * COST_SCALE * 1.15e9),
        bytes_accessed=int(micros * COST_SCALE * 3.6e6),
        transcendentals=0,
    )


def whole(shape):
    return pl.BlockSpec(shape, lambda *_: (0,) * len(shape))


def once(shape):
    return pl.BlockSpec(shape, lambda *_: (0,) * len(shape), pipeline_mode=pl.Buffered(1))


def shaped(shape, dtype=BF16):
    return jax.ShapeDtypeStruct(shape, dtype)


class Chain:
    def __init__(self):
        self.last = None

    def __call__(self, kernel, scalars, inputs, in_specs, out_specs, out_shape, *, name, micros,
                 grid=(1,), scratch=(), vmem=16):
        deps = [] if self.last is None else [self.last]
        count = len(inputs)

        def body(s_ref, *refs):
            kernel(s_ref, *refs[:count], *refs[count + len(deps) :])

        outs = pl.pallas_call(
            body,
            grid_spec=pltpu.PrefetchScalarGridSpec(
                num_scalar_prefetch=1,
                grid=grid,
                in_specs=list(in_specs) + [pl.BlockSpec(memory_space=pl.ANY)] * len(deps),
                out_specs=out_specs,
                scratch_shapes=list(scratch),
            ),
            out_shape=out_shape,
            compiler_params=pltpu.CompilerParams(vmem_limit_bytes=vmem * 2**20),
            cost_estimate=cost(micros),
            name=name,
        )(scalars, *inputs, *deps)
        self.last = outs[0]
        return outs

    def gate(self, scalars, a):
        def kernel(s_ref, a_ref, out_ref):
            out_ref[...] = a_ref[...]

        return self(
            kernel, scalars, [a], [whole(a.shape)], [whole(a.shape)], [shaped(a.shape, a.dtype)],
            name="gate", micros=0.3,
        )[0]


def nn(a, b):
    return lax.dot_general(a, b, (((1,), (0,)), ((), ())), preferred_element_type=F32)


def nt(a, b):
    return lax.dot_general(a, b, (((1,), (1,)), ((), ())), preferred_element_type=F32)


def tn(a, b):
    return lax.dot_general(a, b, (((0,), (0,)), ((), ())), preferred_element_type=F32)


def colsum(a):
    return jnp.sum(a, axis=0, keepdims=True)


def rowmean(a):
    return jnp.mean(a, axis=-1, keepdims=True)


def gelu_pair(u):
    den = 1.0 + ERFC_SLOPE * jnp.abs(u)
    t = pl.reciprocal(den, approx=True)
    t = t * (2.0 - den * t)
    poly = ERFC_POLY[-1]
    for c in ERFC_POLY[-2::-1]:
        poly = poly * t + c
    bell = jnp.exp(-0.5 * (u * u))
    tail = bell * (poly * t)
    cdf = jnp.where(u >= 0, 1.0 - tail, tail)
    return u * cdf, cdf + (u * bell) * INV_SQRT_2PI


def attend_sentence(length, x, weights, bq, bv, qkv_ref, c_ref, lse_ref):
    rows = x.shape[0]
    width = c_ref.shape[1]
    both = nn(x, jnp.concatenate(weights, axis=1))
    qkv_ref[:, :width] = (both[:, :width] + bq).astype(BF16)
    qkv_ref[:, width : 2 * width] = both[:, width : 2 * width].astype(BF16)
    qkv_ref[:, 2 * width :] = (both[:, 2 * width :] + bv).astype(BF16)
    low = lax.broadcasted_iota(jnp.int32, (rows, LANES), 1) < HD
    live = lax.broadcasted_iota(jnp.int32, (rows, LANES), 0) < length
    bias = jnp.where(live, 0.0, MASKED).astype(F32)
    zero = jnp.zeros((rows, LANES), BF16)
    for p in range(width // LANES):
        at = LANES * p
        q = qkv_ref[:, at : at + LANES] * 0.125
        k = qkv_ref[:, width + at : width + at + LANES]
        v = qkv_ref[:, 2 * width + at : 2 * width + at + LANES]
        vt = v.T
        outs = []
        for h in range(2):
            km = jnp.where(low, k, zero) if h == 0 else jnp.where(low, zero, k)
            scores = nt(km, q)
            parts, tops, sums = [], [], []
            for j in range(rows // LANES):
                piece = scores[:, LANES * j : LANES * j + LANES] + bias
                top = jnp.max(piece, axis=0, keepdims=True)
                e = jnp.exp(piece - top)
                parts.append(e.astype(BF16))
                tops.append(top)
                sums.append(colsum(e))
            top = jnp.concatenate(tops, axis=1)
            total = jnp.concatenate(sums, axis=1)
            ct = nn(vt[HD * h : HD * h + HD], jnp.concatenate(parts, axis=1))
            outs.append(ct / total)
            lse_ref[0, 2 * p + h : 2 * p + h + 1, :] = top + jnp.log(total)
        c_ref[:, at : at + LANES] = jnp.concatenate(outs, axis=0).T.astype(BF16)


def attn_own_kernel(s_ref, x_ref, w_ref, b_ref, qkv_ref, c_ref, lse_ref):
    weights = [w_ref[c] for c in range(3)]
    length = s_ref[2 + pl.program_id(0)]
    attend_sentence(
        length, x_ref[...], weights, b_ref[0:1, :], b_ref[1:2, :], qkv_ref, c_ref, lse_ref
    )


def attn_other_kernel(s_ref, x_ref, w0, w1, b_ref, qkv_ref, c_ref, lse_ref, w_ref):
    @pl.when(pl.program_id(0) == 0)
    def _():
        for s, ref in enumerate((w0, w1)):
            for c in range(3):
                w_ref[c, bit(s_ref[0], 0) ^ s] = ref[c]

    shape = w_ref.shape
    weights = [w_ref[c].reshape(shape[1] * shape[2], shape[3]) for c in range(3)]
    length = s_ref[2 + pl.program_id(0)]
    attend_sentence(
        length, x_ref[...], weights, b_ref[0:1, :], b_ref[1:2, :], qkv_ref, c_ref, lse_ref
    )


def by_rows(block, cols):
    return pl.BlockSpec((block, cols), lambda i, *_: (i, 0))


def attn_forward(chain, scalars, x, weights, bias):
    tokens, model = x.shape
    width = bias.shape[1]
    sents = tokens // LEN
    out_specs = [
        by_rows(LEN, 3 * width),
        by_rows(LEN, width),
        pl.BlockSpec((1, width // HD, LEN), lambda s, l: (s, 0, 0)),
    ]
    out_shape = [
        shaped((tokens, 3 * width)),
        shaped((tokens, width)),
        shaped((sents, width // HD, LEN), F32),
    ]
    own = len(weights) == 1
    if not own:
        full = (3, 2, model // 2, width)
        out_specs.append(whole(full))
        out_shape.append(shaped(full))
    return chain(
        attn_own_kernel if own else attn_other_kernel,
        scalars,
        [x, *weights, bias],
        [by_rows(LEN, model)] + [once(w.shape) for w in weights] + [whole(bias.shape)],
        out_specs,
        out_shape,
        grid=(sents,),
        name="attn_fwd",
        micros=11.4,
        vmem=24,
    )


def attn_back_kernel(s_ref, qkv_ref, do_ref, lse_ref, grad_ref, sum_ref):
    s = pl.program_id(0)
    length = s_ref[2 + s]
    rows, width = do_ref.shape
    low = lax.broadcasted_iota(jnp.int32, (rows, LANES), 1) < HD
    live = lax.broadcasted_iota(jnp.int32, (rows, LANES), 0) < length
    bias = jnp.where(live, 0.0, MASKED).astype(F32)
    zero = jnp.zeros((rows, LANES), BF16)

    @pl.when(s == 0)
    def _():
        sum_ref[...] = jnp.zeros_like(sum_ref)

    for p in range(width // LANES):
        at = LANES * p
        q = qkv_ref[:, at : at + LANES] * 0.125
        k = qkv_ref[:, width + at : width + at + LANES]
        v = qkv_ref[:, 2 * width + at : 2 * width + at + LANES]
        do = do_ref[:, at : at + LANES]
        kt = k.T
        dqs, dks, dvs = [], [], []
        for h in range(2):
            km = jnp.where(low, k, zero) if h == 0 else jnp.where(low, zero, k)
            vm = jnp.where(low, v, zero) if h == 0 else jnp.where(low, zero, v)
            lse = lse_ref[0, 2 * p + h : 2 * p + h + 1, :]
            scores = nt(km, q)
            dprob = nt(vm, do)
            probs, dscores = [], []
            for j in range(rows // LANES):
                cols = slice(LANES * j, LANES * j + LANES)
                e = jnp.exp(scores[:, cols] + bias - lse[:, cols])
                probs.append(e.astype(BF16))
                dp = dprob[:, cols]
                dscores.append((e * (dp - colsum(e * dp))).astype(BF16))
            prob = jnp.concatenate(probs, axis=1)
            dscore = jnp.concatenate(dscores, axis=1)
            dvs.append(nn(prob, do))
            dks.append(nn(dscore, q))
            dqs.append(nn(kt[HD * h : HD * h + HD], dscore))
        dq = (jnp.concatenate(dqs, axis=0).T * 0.125).astype(BF16)
        dk = jnp.where(low, dks[0], dks[1]).astype(BF16)
        dv = jnp.where(low, dvs[0], dvs[1]).astype(BF16)
        grad_ref[:, at : at + LANES] = dq
        grad_ref[:, width + at : width + at + LANES] = dk
        grad_ref[:, 2 * width + at : 2 * width + at + LANES] = dv
        sum_ref[0:1, at : at + LANES] += colsum(dq.astype(F32))
        sum_ref[1:2, at : at + LANES] += colsum(dv.astype(F32))


def attn_backward(chain, scalars, qkv, do, lse):
    tokens, width = do.shape
    return chain(
        attn_back_kernel,
        scalars,
        [qkv, do, lse],
        [
            by_rows(LEN, 3 * width),
            by_rows(LEN, width),
            pl.BlockSpec((1, width // HD, LEN), lambda s, l: (s, 0, 0)),
        ],
        [by_rows(LEN, 3 * width), whole((2, width))],
        [shaped((tokens, 3 * width)), shaped((2, width), F32)],
        grid=(tokens // LEN,),
        name="attn_bwd",
        micros=12.6,
        vmem=24,
    )


def normalize(r):
    center = r - rowmean(r)
    inverse = lax.rsqrt(rowmean(center * center) + EPS_NORM)
    return center * inverse, inverse


def project_kernel(
    s_ref, x_ref, c_own, c_oth, w_own, w0, w1, vec_ref, h_ref, low_ref, n_ref, inv_ref, w_ref
):
    @pl.when(pl.program_id(0) == 0)
    def _():
        for s, ref in enumerate((w0, w1)):
            w_ref[bit(s_ref[0], 0) ^ s] = ref[...]

    shape = w_ref.shape
    other = w_ref[...].reshape(shape[0] * shape[1], shape[2])
    attended = nn(c_own[...], w_own[...]) + nn(c_oth[...], other) + vec_ref[0:1, :]
    normal, inverse = normalize(x_ref[...].astype(F32) + attended)
    h = normal * vec_ref[1:2, :] + vec_ref[2:3, :]
    h_ref[...] = h
    low_ref[...] = h.astype(BF16)
    n_ref[...] = normal.astype(BF16)
    inv_ref[...] = inverse


def project_forward(chain, scalars, x, c_own, c_oth, w_own, slots, vecs):
    tokens, model = x.shape
    block = 512
    width = c_own.shape[1]
    full = (2,) + slots[0].shape
    return chain(
        project_kernel,
        scalars,
        [x, c_own, c_oth, w_own, *slots, vecs],
        [by_rows(block, model), by_rows(block, width), by_rows(block, width), once(w_own.shape)]
        + [once(s.shape) for s in slots]
        + [whole(vecs.shape)],
        [by_rows(block, model)] * 3 + [by_rows(block, 1), whole(full)],
        [
            shaped((tokens, model), F32),
            shaped((tokens, model)),
            shaped((tokens, model)),
            shaped((tokens, 1), F32),
            shaped(full),
        ],
        grid=(tokens // block,),
        name="project_fwd",
        micros=6.7,
        vmem=24,
    )


def feed_own_kernel(s_ref, h_ref, wu_ref, bu_ref, wd_ref, g_ref, gp_ref, f_ref):
    h = h_ref[...]
    chunk = wu_ref.shape[1] // 3
    total = None
    for j in range(3):
        cols = slice(chunk * j, chunk * j + chunk)
        act, slope = gelu_pair(nn(h, wu_ref[:, cols]) + bu_ref[:, cols])
        act = act.astype(BF16)
        g_ref[:, cols] = act
        gp_ref[:, cols] = slope.astype(BF16)
        part = nn(act, wd_ref[cols, :])
        total = part if total is None else total + part
    f_ref[...] = total


def feed_own(chain, scalars, h, wu, bu, wd):
    tokens, model = h.shape
    units = wu.shape[1]
    block = 256
    return chain(
        feed_own_kernel,
        scalars,
        [h, wu, bu, wd],
        [by_rows(block, model), once(wu.shape), whole(bu.shape), once(wd.shape)],
        [by_rows(block, units), by_rows(block, units), by_rows(block, model)],
        [shaped((tokens, units)), shaped((tokens, units)), shaped((tokens, model), F32)],
        grid=(tokens // block,),
        name="feed_own",
        micros=14.5,
        vmem=20,
    )


def feed_up_kernel(s_ref, h_ref, u0, u1, u2, u3, bu_ref, g_ref, gp_ref, wu_ref):
    part = u0.shape[1]

    @pl.when(pl.program_id(0) == 0)
    def _():
        for s, up in enumerate((u0, u1, u2, u3)):
            at = ((s_ref[0] & 3) ^ s) * part
            wu_ref[:, pl.ds(pl.multiple_of(at, LANES), part)] = up[...]

    h = h_ref[...]
    chunk = wu_ref.shape[1] // 3
    for j in range(3):
        cols = slice(chunk * j, chunk * j + chunk)
        act, slope = gelu_pair(nn(h, wu_ref[:, cols]) + bu_ref[:, cols])
        g_ref[:, cols] = act.astype(BF16)
        gp_ref[:, cols] = slope.astype(BF16)


def feed_up(chain, scalars, h, up, bu):
    tokens, model = h.shape
    units = bu.shape[1]
    block = 256
    full = (model, units)
    return chain(
        feed_up_kernel,
        scalars,
        [h, *up, bu],
        [by_rows(block, model)] + [once(w.shape) for w in up] + [whole(bu.shape)],
        [by_rows(block, units), by_rows(block, units), whole(full)],
        [shaped((tokens, units)), shaped((tokens, units)), shaped(full)],
        grid=(tokens // block,),
        name="feed_up",
        micros=11.0,
        vmem=20,
    )


def feed_down_kernel(
    s_ref, g_ref, h_ref, f_ref, d0, d1, vec_ref, out_ref, n_ref, inv_ref, pool_ref, wd_ref
):
    i = pl.program_id(0)

    @pl.when(i == 0)
    def _():
        for s, down in enumerate((d0, d1)):
            wd_ref[bit(s_ref[0], 0) ^ s] = down[...]
        pool_ref[...] = jnp.zeros_like(pool_ref)

    shape = wd_ref.shape
    down = wd_ref[...].reshape(shape[0] * shape[1], shape[2])
    total = nn(g_ref[...], down)
    normal, inverse = normalize(h_ref[...] + (f_ref[...] + total + vec_ref[3:4, :]))
    y = normal * vec_ref[4:5, :] + vec_ref[5:6, :]
    out_ref[...] = y.astype(BF16)
    n_ref[...] = normal.astype(BF16)
    inv_ref[...] = inverse
    block = y.shape[0]
    per = LEN // block
    sent = i // per
    length = s_ref[2 + sent]
    first = (i - sent * per) * block
    live = lax.broadcasted_iota(jnp.int32, y.shape, 0) + first < length
    pool_ref[pl.ds(sent, 1), :] += colsum(jnp.where(live, y, 0.0)) / length.astype(F32)


def feed_down(chain, scalars, g, h, f, down, vecs):
    tokens, model = h.shape
    units = g.shape[1]
    block = 256
    sents = tokens // LEN
    full = (2,) + down[0].shape
    return chain(
        feed_down_kernel,
        scalars,
        [g, h, f, *down, vecs],
        [by_rows(block, units), by_rows(block, model), by_rows(block, model)]
        + [once(w.shape) for w in down]
        + [whole(vecs.shape)],
        [by_rows(block, model), by_rows(block, model), by_rows(block, 1), whole((sents, model)), whole(full)],
        [
            shaped((tokens, model)),
            shaped((tokens, model)),
            shaped((tokens, 1), F32),
            shaped((sents, model), F32),
            shaped(full),
        ],
        grid=(tokens // block,),
        name="feed_down",
        micros=9.0,
        vmem=20,
    )


def exact(a, b, dims):
    return lax.dot_general(
        a, b, (dims, ((), ())), precision=lax.Precision.HIGHEST, preferred_element_type=F32
    )


def loss_kernel(s_ref, slot_ref, row_ref, col_ref, loss_ref, cot_ref, pool_ref, grad_ref):
    local = cot_ref.shape[0]
    rank = s_ref[1]
    count = slot_ref.shape[0]
    for s in range(count // local):
        for i in range(local):
            pool_ref[pl.ds((rank ^ s) * local + i, 1), :] = slot_ref[pl.ds(local * s + i, 1), :]
    pooled = pool_ref[...]
    scale = lax.rsqrt(jnp.sum(pooled * pooled, axis=-1, keepdims=True) + EPS_UNIT)
    unit = pooled * scale
    score = SOFTMAX_TEMP * exact(unit, unit, ((1,), (1,)))
    itself = lax.broadcasted_iota(jnp.int32, score.shape, 0) == lax.broadcasted_iota(
        jnp.int32, score.shape, 1
    )
    others = jnp.where(itself, MASKED, score)
    top = jnp.max(others, axis=1, keepdims=True)
    power = jnp.exp(others - top)
    total = jnp.sum(power, axis=1, keepdims=True)
    match = jnp.logical_and(col_ref[...] == row_ref[...], jnp.logical_not(itself)).astype(F32)
    number = jnp.sum(match, axis=1, keepdims=True)
    matched = jnp.sum(match * score, axis=1, keepdims=True) / number
    terms = top + jnp.log(total) - matched
    loss_ref[...] = jnp.sum(terms, axis=0, keepdims=True) / count
    dscore = float(LEN) * (power / total - match / number)
    dunit = SOFTMAX_TEMP * (exact(dscore, unit, ((1,), (0,))) + exact(dscore, unit, ((0,), (0,))))
    grad_ref[...] = scale * (dunit - unit * jnp.sum(unit * dunit, axis=-1, keepdims=True))
    for i in range(local):
        own = grad_ref[pl.ds(rank * local + i, 1), :]
        cot_ref[i : i + 1, :] = own / s_ref[2 + i].astype(F32)


def loss_call(chain, scalars, slots, group_ids, local):
    count, model = slots.shape
    return chain(
        loss_kernel,
        scalars,
        [slots, group_ids.reshape(1, count), group_ids.reshape(count, 1)],
        [whole((count, model)), whole((1, count)), whole((count, 1))],
        [whole((1, 1)), whole((local, model))],
        [shaped((1, 1), F32), shaped((local, model), F32)],
        scratch=[pltpu.VMEM((count, model), F32)] * 2,
        name="loss",
        micros=3.8,
    )


def norm_back(upstream, normal, inverse, gain):
    scaled = upstream * gain
    return inverse * (scaled - rowmean(scaled) - normal * rowmean(scaled * normal))


def norm_two_kernel(s_ref, cot_ref, n_ref, inv_ref, vec_ref, pool_ref, df_ref, sum_ref):
    s = pl.program_id(0)
    normal = n_ref[...].astype(F32)
    live = lax.broadcasted_iota(jnp.int32, normal.shape, 0) < s_ref[2 + s]
    up = cot_ref[...].astype(F32) + jnp.where(live, pool_ref[pl.ds(s, 1), :], 0.0)
    df = norm_back(up, normal, inv_ref[...], vec_ref[4:5, :]).astype(BF16)
    df_ref[...] = df

    @pl.when(s == 0)
    def _():
        sum_ref[...] = jnp.zeros_like(sum_ref)

    sum_ref[0:1, :] += colsum(df.astype(F32))
    sum_ref[1:2, :] += colsum(up * normal)
    sum_ref[2:3, :] += colsum(up)


def norm_two_backward(chain, scalars, cot, normal, inverse, vecs, pool_cot):
    tokens, model = cot.shape
    return chain(
        norm_two_kernel,
        scalars,
        [cot, normal, inverse, vecs, pool_cot],
        [by_rows(LEN, model), by_rows(LEN, model), by_rows(LEN, 1), whole(vecs.shape), whole(pool_cot.shape)],
        [by_rows(LEN, model), whole((3, model))],
        [shaped((tokens, model)), shaped((3, model), F32)],
        grid=(tokens // LEN,),
        name="norm_two_bwd",
        micros=5.4,
    )


def middle_kernel(
    s_ref, df_ref, gp_own, gp_oth, wu_own, wu_oth, wd_own, wd_oth, n_ref, inv_ref, vec_ref, wo_own, wo_oth,
    du_own, du_oth, da_ref, dc_own, dc_oth, usum_ref, sum_ref,
):
    i = pl.program_id(0)

    @pl.when(i == 0)
    def _():
        usum_ref[...] = jnp.zeros_like(usum_ref)
        sum_ref[...] = jnp.zeros_like(sum_ref)

    df = df_ref[...]
    total = df.astype(F32)
    units = wu_own.shape[1]
    chunk = units // 3
    sides = ((gp_oth, wu_oth, wd_oth, du_oth), (gp_own, wu_own, wd_own, du_own))
    for side, (gp_ref, wu_ref, wd_ref, du_ref) in enumerate(sides):
        for j in range(3):
            cols = slice(chunk * j, chunk * j + chunk)
            du = (nt(df, wd_ref[cols, :]) * gp_ref[:, cols].astype(F32)).astype(BF16)
            du_ref[:, cols] = du
            usum_ref[side : side + 1, cols] += colsum(du.astype(F32))
            total = total + nt(du, wu_ref[:, cols])
    normal = n_ref[...].astype(F32)
    da = norm_back(total, normal, inv_ref[...], vec_ref[1:2, :]).astype(BF16)
    da_ref[...] = da
    dc_own[...] = nt(da, wo_own[...]).astype(BF16)
    dc_oth[...] = nt(da, wo_oth[...]).astype(BF16)
    sum_ref[0:1, :] += colsum(total * normal)
    sum_ref[1:2, :] += colsum(total)
    sum_ref[2:3, :] += colsum(da.astype(F32))


def middle_backward(
    chain, scalars, df, gp_own, gp_oth, wu_own, wu_oth, wd_own, wd_oth, normal, inverse, vecs, wo_own, wo_oth
):
    tokens, model = df.shape
    units = wu_own.shape[1]
    width = wo_own.shape[0]
    block = 256
    return chain(
        middle_kernel,
        scalars,
        [df, gp_own, gp_oth, wu_own, wu_oth, wd_own, wd_oth, normal, inverse, vecs, wo_own, wo_oth],
        [by_rows(block, model), by_rows(block, units), by_rows(block, units)]
        + [once(w.shape) for w in (wu_own, wu_oth, wd_own, wd_oth)]
        + [by_rows(block, model), by_rows(block, 1), whole(vecs.shape), once(wo_own.shape), once(wo_oth.shape)],
        [by_rows(block, units)] * 2
        + [by_rows(block, model)]
        + [by_rows(block, width)] * 2
        + [whole((2, units)), whole((3, model))],
        [shaped((tokens, units))] * 2
        + [shaped((tokens, model))]
        + [shaped((tokens, width))] * 2
        + [shaped((2, units), F32), shaped((3, model), F32)],
        grid=(tokens // block,),
        name="middle_bwd",
        micros=22.0,
        vmem=32,
    )


def bit(value, at):
    return (value >> at) & 1


def split_store(d, even, odd, keep_ref, send_ref, at):
    flip = bit(d, 0) == 0
    keep_ref[at] = jnp.where(flip, even, odd).astype(BF16)
    send_ref[at] = jnp.where(flip, odd, even).astype(BF16)


def dense_grad_kernel(d_ref, a_ref, b_ref, keep_ref, send_ref):
    d = d_ref[0]
    grad = tn(a_ref[...], b_ref[...])
    step = keep_ref.shape[3]
    for x in range(2):
        for z in range(2):
            at = (4 * z + 2 * x) * step
            split_store(
                d, grad[at : at + step], grad[at + step : at + 2 * step], keep_ref, send_ref,
                (x ^ bit(d, 1), 0, z ^ bit(d, 2)),
            )


def dense_grad(chain, scalars, a, b, cut_left):
    tokens = a.shape[0]
    left = a.shape[1] // (2 if cut_left else 1)
    right = b.shape[1] // (1 if cut_left else 2)
    step = left // 8
    block = pl.BlockSpec((2, 1, 2, step, right), lambda i, s: (0, i ^ bit(s[0], 3), 0, 0, 0))
    fixed, moving = lambda i, s: (0, 0), lambda i, s: (0, i)
    return chain(
        dense_grad_kernel,
        scalars,
        [a, b],
        [
            pl.BlockSpec((tokens, left), moving if cut_left else fixed),
            pl.BlockSpec((tokens, right), fixed if cut_left else moving),
        ],
        [block, block],
        [shaped((2, 2, 2, step, right))] * 2,
        grid=(2,),
        name="dense_grad",
        micros=5.9,
        vmem=20,
    )


def heads_grad_kernel(
    d_ref, c_ref, da_ref, x_ref, dqkv_ref, two_ref, one_ref, bias_ref, unit_ref, keep_ref, send_ref, *, side
):
    d = d_ref[0]
    width = c_ref.shape[1]
    out = tn(c_ref[...], da_ref[...])
    proj = tn(x_ref[...], dqkv_ref[...])
    step = width // 8
    small = [ref[i : i + 1, at : at + width] for ref in (two_ref, one_ref) for i in range(3) for at in (0, width)]
    small += [bias_ref[0:1, :], bias_ref[1:2, :]]
    small += [unit_ref[side : side + 1, at : at + width] for at in range(0, unit_ref.shape[1], width)]
    small += [jnp.zeros((1, width), F32)] * (32 - len(small))
    rest = jnp.zeros((14, width), F32)

    def block(b):
        row, col = (b & 7) * step, (b >> 3) * width
        pieces = [out[row : row + step, col : col + width]]
        pieces += [proj[b * step : b * step + step, c * width : c * width + width] for c in range(3)]
        return jnp.concatenate(pieces + [small[b], small[16 + b], rest], axis=0)

    for x in range(2):
        for z in range(2):
            for w in range(2):
                b = 8 * w + 4 * z + 2 * x
                split_store(
                    d, block(b), block(b + 1), keep_ref, send_ref,
                    (x ^ bit(d, 1), w ^ bit(d, 3), z ^ bit(d, 2)),
                )


def heads_grad(chain, scalars, c, da, x, dqkv, sums, side):
    width = c.shape[1]
    full = (2, 2, 2, width // 2 + 16, width)
    inputs = [c, da, x, dqkv, *sums]
    return chain(
        functools.partial(heads_grad_kernel, side=side),
        scalars,
        inputs,
        [once(a.shape) for a in inputs],
        [whole(full), whole(full)],
        [shaped(full)] * 2,
        name="heads_grad",
        micros=7.3,
        vmem=28,
    )


def input_grad_kernel(s_ref, own_ref, oth_ref, w_own, w_oth, da_ref, out_ref):
    total = da_ref[...].astype(F32)
    for grad, w in ((own_ref, w_own), (oth_ref, w_oth)):
        total = total + nt(grad[...], jnp.concatenate([w[c] for c in range(3)], axis=1))
    out_ref[...] = total


def input_grad(chain, scalars, own, oth, w_own, w_oth, da):
    tokens, model = da.shape
    block = 512
    return chain(
        input_grad_kernel,
        scalars,
        [own, oth, w_own, w_oth, da],
        [by_rows(block, own.shape[1])] * 2 + [once(w_own.shape), once(w_oth.shape), by_rows(block, model)],
        [by_rows(block, model)],
        [shaped((tokens, model), F32)],
        grid=(tokens // block,),
        name="input_grad",
        micros=9.0,
        vmem=24,
    )[0]


def place_kernel(s_ref, a0, a1, b0, b1, *out_refs):
    d = s_ref[0]
    flip = bit(d, 0) == 0
    step = a0.shape[2]
    for x, (near_ref, far_ref) in enumerate(((a0, b0), (a1, b1))):
        for z in range(2):
            near, far = near_ref[0, z].astype(F32), far_ref[0, z].astype(F32)
            even, odd = jnp.where(flip, near, far), jnp.where(flip, far, near)
            low = (x ^ bit(d, 1)) + 2 * (z ^ bit(d, 2))
            if len(out_refs) == 1:
                out_refs[0][low, :step] = even
                out_refs[0][low, step:] = odd
                continue
            out_ref, proj_ref, small_ref = out_refs
            part = (step - 16) // 4
            small_ref[low, 0] = even[step - 16 : step - 8]
            small_ref[low, 1] = odd[step - 16 : step - 8]
            out_ref[low, :part] = even[:part]
            out_ref[low, part:] = odd[:part]
            for c in range(3):
                rows = slice(part * (c + 1), part * (c + 2))
                proj_ref[c, low, :part] = even[rows]
                proj_ref[c, low, part:] = odd[rows]


def place(chain, scalars, pieces, kind):
    step, cols = pieces[0].shape[2:]
    block = pl.BlockSpec((1, 2, step, cols), lambda w, s: (w, 0, 0, 0))
    high = lambda w, s: w ^ bit(s[0], 3)
    if kind == "rows":
        shapes = [(8, 2 * step, cols)]
        specs = [pl.BlockSpec((4, 2 * step, cols), lambda w, s: (high(w, s), 0, 0))]
    elif kind == "columns":
        shapes = [(4, 2 * step, 2 * cols)]
        specs = [pl.BlockSpec((4, 2 * step, cols), lambda w, s: (0, 0, high(w, s)))]
    else:
        part = (step - 16) // 4
        shapes = [(4, 2 * part, 2 * cols), (3, 8, 2 * part, cols), (8, 2, 8, cols)]
        specs = [
            pl.BlockSpec((4, 2 * part, cols), lambda w, s: (0, 0, high(w, s))),
            pl.BlockSpec((3, 4, 2 * part, cols), lambda w, s: (0, high(w, s), 0, 0)),
            pl.BlockSpec((4, 2, 8, cols), lambda w, s: (high(w, s), 0, 0, 0)),
        ]
    return chain(
        place_kernel,
        scalars,
        pieces,
        [block] * 4,
        specs,
        [shaped(s, F32) for s in shapes],
        grid=(2,),
        name="place",
        micros=4.0,
        vmem=24,
    )


def swap(x, axis, mask):
    size = lax.axis_size(axis)
    return lax.ppermute(x, axis, [(i, i ^ mask) for i in range(size)])


def swap_all(x, mask):
    size = lax.axis_size("dp") * lax.axis_size("tensor")
    return lax.ppermute(x, ("dp", "tensor"), [(i, i ^ mask) for i in range(size)])


def levels():
    return lax.axis_size("dp").bit_length() - 1


def sum_kernel(s_ref, *refs, count, early):
    total = refs[0][...].astype(F32) + refs[1][...].astype(F32)
    if early:
        total = total.astype(BF16).astype(F32)
    for ref in refs[2:count]:
        total = total + ref[...].astype(F32)
    total = total.astype(BF16)
    outs = refs[count:]
    if len(outs) == 1:
        outs[0][...] = total
        return
    for i, out in enumerate(outs):
        out[...] = total[i]


def add(chain, scalars, terms, split=1, early=False):
    shape = terms[0].shape
    outs = [shape] if split == 1 else [shape[1:]] * split
    return chain(
        functools.partial(sum_kernel, count=len(terms), early=early),
        scalars,
        terms,
        [whole(shape)] * len(terms),
        [whole(o) for o in outs],
        [shaped(o) for o in outs],
        name="add",
        micros=2.0,
    )


def join_kernel(s_ref, *refs):
    for i, ref in enumerate(refs[:-1]):
        refs[-1][i] = ref[...]


def join(chain, scalars, parts):
    shape = (len(parts),) + parts[0].shape
    return chain(
        join_kernel,
        scalars,
        parts,
        [whole(p.shape) for p in parts],
        [whole(shape)],
        [shaped(shape)],
        name="join",
        micros=1.5,
    )[0]


class Reduction:
    def __init__(self, chain, scalars):
        self.chain, self.scalars = chain, scalars

    def add(self, terms, split=1, early=False):
        return add(self.chain, self.scalars, terms, split, early)

    def other(self, keep, send):
        self.keep_oth, self.got_oth = keep, swap(send, "dp", 1)

    def own(self, keep, send):
        self.keep_own, self.got_own = keep, swap(send, "dp", 1)

    def across(self):
        (total,) = self.add([self.keep_oth, self.got_oth])
        self.got_y = swap(total, "tensor", 1)

    def along_x(self):
        self.keep, send = self.add([self.keep_own, self.got_own, self.got_y], 2, True)
        self.got = swap(send, "dp", 2)

    def along_z(self):
        shape = self.keep.shape
        flat = (4,) + shape[2:]
        self.keep, *send = self.add([self.keep.reshape(flat), self.got.reshape(flat)], 4)
        self.got = [swap(s, "dp", 4 * (i + 1)) for i, s in enumerate(send)]

    def back_z(self):
        (total,) = self.add([self.keep, *self.got])
        for at in range(4, levels()):
            (total,) = self.add([total, swap(total, "dp", 1 << at)])
        self.parts = [total] + [swap(total, "dp", 4 * i) for i in range(1, 4)]

    def back_x(self):
        near = join(self.chain, self.scalars, self.parts)
        self.near = near.reshape((2, 2) + near.shape[1:])
        self.near_far = swap(self.near, "dp", 1)
        self.next = swap(self.near, "dp", 2)

    def back_core(self):
        self.next = self.chain.gate(self.scalars, self.next)
        self.next_far = swap(self.next, "dp", 1)

    def place(self, kind):
        pieces = [self.near, self.next, self.near_far, self.next_far]
        return place(self.chain, self.scalars, pieces, kind)


def gather_pooled(pooled):
    bits = levels() + 1
    at = 0
    while at < bits:
        step = min(3 if at == 0 else 2, bits - at)
        pooled = jnp.concatenate(
            [pooled] + [swap_all(pooled, m << at) for m in range(1, 1 << step)], axis=0
        )
        at += step
    return pooled


def cut_kernel(s_ref, a_ref, out_ref):
    out_ref[...] = a_ref[...].reshape(out_ref.shape)


def cut(chain, scalars, a, block, index):
    shape = tuple(b for b in block if b != 1)
    return chain(
        cut_kernel,
        scalars,
        [a],
        [pl.BlockSpec(block, lambda i, s: index(s[0] & 3))],
        [whole(shape)],
        [shaped(shape, a.dtype)],
        name="cut",
        micros=1.0,
    )[0]


class Gather:
    def __init__(self, chain, scalars, piece, relayed=False):
        self.chain, self.scalars, self.relayed = chain, scalars, relayed
        self.first = swap(piece, "tensor", 1)

    def pass_first(self):
        self.first = self.chain.gate(self.scalars, self.first)
        if self.relayed:
            self.second = swap(self.first, "dp", 2)
        self.first_far = swap(self.first, "dp", 1)

    def pass_second(self):
        self.second = self.chain.gate(self.scalars, self.second)
        self.second_far = swap(self.second, "dp", 1)

    def slots(self):
        return [self.first, self.first_far] + ([self.second, self.second_far] if self.relayed else [])


def per_device(
    layer_input, w_qkv, bias_qv, w_out, b_out, gain_one, shift_one, w_up, b_up, w_down, b_down,
    gain_two, shift_two, out_cot, lengths, group_ids,
):
    tensor_size = lax.axis_size("tensor")
    position = lax.axis_index("tensor")
    d = lax.axis_index("dp")
    model = layer_input.shape[1]
    width = w_qkv.shape[2]
    units = w_up.shape[1]
    local = lengths.shape[0] // tensor_size
    lens = lax.dynamic_slice_in_dim(lengths, position * local, local, 0)
    rank = d * tensor_size + position
    scal = jnp.concatenate([jnp.stack([d, rank]).astype(jnp.int32), lens])
    chain = Chain()

    part = model // 2
    piece = cut(chain, scal, w_qkv.reshape(3, 2, part, width), (3, 1, part, width), lambda q: (0, q & 1, 0, 0))
    gather_qkv = Gather(chain, scal, piece)
    part = width // 2
    piece = cut(chain, scal, w_out.reshape(2, part, model), (1, part, model), lambda q: (q & 1, 0, 0))
    gather_out = Gather(chain, scal, piece)
    qkv_own, c_own, lse_own = attn_forward(chain, scal, layer_input, [w_qkv], bias_qv)
    part = units // 4
    piece = cut(chain, scal, w_up, (model, part), lambda q: (0, q))
    gather_up = Gather(chain, scal, piece, relayed=True)
    part = units // 2
    piece = cut(chain, scal, w_down.reshape(2, part, model), (1, part, model), lambda q: (q & 1, 0, 0))
    gather_down = Gather(chain, scal, piece)
    bias_oth = swap(bias_qv, "tensor", 1)
    bu_oth = swap(b_up, "tensor", 1)
    vecs = jnp.stack([b_out, gain_one, shift_one, b_down, gain_two, shift_two])
    bu_own, bu_oth = b_up.reshape(1, units), bu_oth.reshape(1, units)
    gather_qkv.pass_first()
    qkv_oth, c_oth, lse_oth, wq_oth = attn_forward(chain, scal, layer_input, gather_qkv.slots(), bias_oth)
    wq_oth = wq_oth.reshape(3, model, width)
    gather_out.pass_first()
    h1, h1_low, normal_one, inverse_one, wo_oth = project_forward(
        chain, scal, layer_input, c_own, c_oth, w_out, gather_out.slots(), vecs
    )
    wo_oth = wo_oth.reshape(width, model)
    gather_up.pass_first()
    g_own, gp_own, f_own = feed_own(chain, scal, h1_low, w_up, bu_own, w_down)
    gather_up.pass_second()
    g_oth, gp_oth, wu_oth = feed_up(chain, scal, h1_low, gather_up.slots(), bu_oth)
    gather_down.pass_first()
    output, normal_two, inverse_two, pooled, wd_oth = feed_down(
        chain, scal, g_oth, h1, f_own, gather_down.slots(), vecs
    )
    wd_oth = wd_oth.reshape(units, model)

    loss, pool_cot = loss_call(chain, scal, gather_pooled(pooled), group_ids, local)

    down, up, heads = (Reduction(chain, scal) for _ in range(3))
    df, sums_two = norm_two_backward(chain, scal, out_cot, normal_two, inverse_two, vecs, pool_cot)
    down.other(*dense_grad(chain, scal, g_oth, df, True))
    down.own(*dense_grad(chain, scal, g_own, df, True))
    down.across()
    du_own, du_oth, da, dc_own, dc_oth, sums_units, sums_one = middle_backward(
        chain, scal, df, gp_own, gp_oth, w_up, wu_oth, w_down, wd_oth, normal_one, inverse_one, vecs, w_out, wo_oth
    )
    up.other(*dense_grad(chain, scal, h1_low, du_oth, False))
    down.along_x()
    up.own(*dense_grad(chain, scal, h1_low, du_own, False))
    up.across()
    dqkv_oth, sums_oth = attn_backward(chain, scal, qkv_oth, dc_oth, lse_oth)
    down.along_z()
    heads.other(
        *heads_grad(
            chain, scal, c_oth, da, layer_input, dqkv_oth, [sums_two, sums_one, sums_oth, sums_units], 0
        )
    )
    dqkv_own, sums_own = attn_backward(chain, scal, qkv_own, dc_own, lse_own)
    heads.across()
    up.along_x()
    down.back_z()
    heads.own(
        *heads_grad(
            chain, scal, c_own, da, layer_input, dqkv_own, [sums_two, sums_one, sums_own, sums_units], 1
        )
    )
    up.along_z()
    down.back_x()
    heads.along_x()
    grad_input = input_grad(chain, scal, dqkv_own, dqkv_oth, w_qkv, wq_oth, da)
    up.back_z()
    down.back_core()
    up.back_x()
    heads.along_z()
    (grad_w_down,) = down.place("rows")
    up.back_core()
    heads.back_z()
    (grad_w_up,) = up.place("columns")
    heads.back_x()
    heads.back_core()
    grad_w_out, grad_w_qkv, small = heads.place("heads")
    small = small.reshape(16, 8, width)[:, :2].transpose(1, 0, 2).reshape(32, width)
    vec = lambda i: small[2 * i : 2 * i + 2].reshape(model)
    return (
        loss.reshape(()),
        output,
        grad_input,
        grad_w_qkv.reshape(w_qkv.shape),
        small[12:14],
        grad_w_out.reshape(w_out.shape),
        vec(5),
        vec(3),
        vec(4),
        grad_w_up.reshape(w_up.shape),
        small[14:18].reshape(units),
        grad_w_down.reshape(w_down.shape),
        vec(0),
        vec(1),
        vec(2),
    )


def solution(mesh):
    rows = P(("dp", "tensor"), None)
    in_specs = (
        rows,
        P(None, None, "tensor"),
        P(None, "tensor"),
        P("tensor", None),
        P(),
        P(),
        P(),
        P(None, "tensor"),
        P("tensor"),
        P("tensor", None),
        P(),
        P(),
        P(),
        rows,
        P("dp"),
        P(),
    )
    out_specs = (
        P(),
        rows,
        rows,
        P(None, None, "tensor"),
        P(None, "tensor"),
        P("tensor", None),
        P(),
        P(),
        P(),
        P(None, "tensor"),
        P("tensor"),
        P("tensor", None),
        P(),
        P(),
        P(),
    )
    return jax.shard_map(
        per_device, mesh=mesh, in_specs=in_specs, out_specs=out_specs, check_vma=False
    )
```

```python
import functools

import jax
import jax.numpy as jnp
from jax import lax
from jax.experimental import pallas as pl
from jax.experimental.pallas import tpu as pltpu
from jax.sharding import PartitionSpec as P

HD = 64
LEN = 512
LANES = 128
EPS_NORM = 1e-12
EPS_UNIT = 1e-6
SOFTMAX_TEMP = 20.0
MASKED = -1e30
F32 = jnp.float32
BF16 = jnp.bfloat16
COST_SCALE = 1

ERFC_SLOPE = 0.41 * 0.7071067811865476
ERFC_POLY = tuple(
    0.5 * c
    for c in (
        0.23389259840606333,
        0.19943405568812744,
        0.36527628560337355,
        -0.195943508470611,
        0.5767329065489298,
        -0.17939241407306944,
    )
)
INV_SQRT_2PI = 0.3989422804014327


def cost(micros):
    return pl.CostEstimate(
        flops=int(micros * COST_SCALE * 1.15e9),
        bytes_accessed=int(micros * COST_SCALE * 3.6e6),
        transcendentals=0,
    )


def whole(shape):
    return pl.BlockSpec(shape, lambda *_: (0,) * len(shape))


def once(shape):
    return pl.BlockSpec(shape, lambda *_: (0,) * len(shape), pipeline_mode=pl.Buffered(1))


def shaped(shape, dtype=BF16):
    return jax.ShapeDtypeStruct(shape, dtype)


class Chain:
    def __init__(self):
        self.last = None
        self.windows = 0

    def __call__(self, kernel, scalars, inputs, in_specs, out_specs, out_shape, *, name, micros,
                 grid=(1,), scratch=(), vmem=16, aliases=None):
        deps = [] if self.last is None else [self.last]
        count = len(inputs)

        def body(s_ref, *refs):
            kernel(s_ref, *refs[:count], *refs[count + len(deps) :])

        outs = pl.pallas_call(
            body,
            grid_spec=pltpu.PrefetchScalarGridSpec(
                num_scalar_prefetch=1,
                grid=grid,
                in_specs=list(in_specs) + [pl.BlockSpec(memory_space=pl.ANY)] * len(deps),
                out_specs=out_specs,
                scratch_shapes=list(scratch),
            ),
            out_shape=out_shape,
            input_output_aliases=aliases or {},
            compiler_params=pltpu.CompilerParams(vmem_limit_bytes=vmem * 2**20),
            cost_estimate=cost(micros),
            name=name,
        )(scalars, *inputs, *deps)
        self.last = outs[0]
        if micros >= 3:
            self.windows += 1
        return outs

    def gate(self, scalars, a):
        def kernel(s_ref, a_ref, out_ref):
            out_ref[...] = a_ref[...]

        return self(
            kernel, scalars, [a], [whole(a.shape)], [whole(a.shape)], [shaped(a.shape, a.dtype)],
            name="gate", micros=10.0,
        )[0]

    def send(self, x, axis, mask):
        return swap(x, axis, mask), self.windows

    def receive(self, scalars, sent):
        if sent[1] == self.windows:
            self.pause(scalars)
        return sent[0]

    def pause(self, scalars):
        def kernel(s_ref, out_ref):
            out_ref[...] = jnp.zeros_like(out_ref)

        tile = (8, LANES)
        self(kernel, scalars, [], [], [whole(tile)], [shaped(tile, F32)], name="pause", micros=100.0)


def nn(a, b):
    return lax.dot_general(a, b, (((1,), (0,)), ((), ())), preferred_element_type=F32)


def nt(a, b):
    return lax.dot_general(a, b, (((1,), (1,)), ((), ())), preferred_element_type=F32)


def tn(a, b):
    return lax.dot_general(a, b, (((0,), (0,)), ((), ())), preferred_element_type=F32)


def colsum(a):
    return jnp.sum(a, axis=0, keepdims=True)


def rowmean(a):
    return jnp.mean(a, axis=-1, keepdims=True)


def gelu_pair(u):
    den = 1.0 + ERFC_SLOPE * jnp.abs(u)
    t = pl.reciprocal(den, approx=True)
    t = t * (2.0 - den * t)
    poly = ERFC_POLY[-1]
    for c in ERFC_POLY[-2::-1]:
        poly = poly * t + c
    bell = jnp.exp(-0.5 * (u * u))
    tail = bell * (poly * t)
    cdf = jnp.where(u >= 0, 1.0 - tail, tail)
    return u * cdf, cdf + (u * bell) * INV_SQRT_2PI


def attend_sentence(length, x, weights, bq, bv, qkv_ref, c_ref, lse_ref):
    rows = x.shape[0]
    width = c_ref.shape[1]
    both = nn(x, jnp.concatenate(weights, axis=1))
    qkv_ref[:, :width] = (both[:, :width] + bq).astype(BF16)
    qkv_ref[:, width : 2 * width] = both[:, width : 2 * width].astype(BF16)
    qkv_ref[:, 2 * width :] = (both[:, 2 * width :] + bv).astype(BF16)
    low = lax.broadcasted_iota(jnp.int32, (rows, LANES), 1) < HD
    live = lax.broadcasted_iota(jnp.int32, (rows, LANES), 0) < length
    bias = jnp.where(live, 0.0, MASKED).astype(F32)
    zero = jnp.zeros((rows, LANES), BF16)
    for p in range(width // LANES):
        at = LANES * p
        q = qkv_ref[:, at : at + LANES] * 0.125
        k = qkv_ref[:, width + at : width + at + LANES]
        v = qkv_ref[:, 2 * width + at : 2 * width + at + LANES]
        vt = v.T
        outs = []
        for h in range(2):
            km = jnp.where(low, k, zero) if h == 0 else jnp.where(low, zero, k)
            scores = nt(km, q)
            parts, tops, sums = [], [], []
            for j in range(rows // LANES):
                piece = scores[:, LANES * j : LANES * j + LANES] + bias
                top = jnp.max(piece, axis=0, keepdims=True)
                e = jnp.exp(piece - top)
                parts.append(e.astype(BF16))
                tops.append(top)
                sums.append(colsum(e))
            top = jnp.concatenate(tops, axis=1)
            total = jnp.concatenate(sums, axis=1)
            ct = nn(vt[HD * h : HD * h + HD], jnp.concatenate(parts, axis=1))
            outs.append(ct / total)
            lse_ref[0, 2 * p + h : 2 * p + h + 1, :] = top + jnp.log(total)
        c_ref[:, at : at + LANES] = jnp.concatenate(outs, axis=0).T.astype(BF16)


def attn_own_kernel(s_ref, x_ref, w_ref, b_ref, qkv_ref, c_ref, lse_ref):
    weights = [w_ref[c] for c in range(3)]
    length = s_ref[2 + pl.program_id(0)]
    attend_sentence(
        length, x_ref[...], weights, b_ref[0:1, :], b_ref[1:2, :], qkv_ref, c_ref, lse_ref
    )


def attn_other_kernel(s_ref, x_ref, w0, w1, b_ref, qkv_ref, c_ref, lse_ref, w_ref):
    @pl.when(pl.program_id(0) == 0)
    def _():
        for s, ref in enumerate((w0, w1)):
            for c in range(3):
                w_ref[c, bit(s_ref[0], 0) ^ s] = ref[c]

    shape = w_ref.shape
    weights = [w_ref[c].reshape(shape[1] * shape[2], shape[3]) for c in range(3)]
    length = s_ref[2 + pl.program_id(0)]
    attend_sentence(
        length, x_ref[...], weights, b_ref[0:1, :], b_ref[1:2, :], qkv_ref, c_ref, lse_ref
    )


def by_rows(block, cols):
    return pl.BlockSpec((block, cols), lambda i, *_: (i, 0))


def attn_forward(chain, scalars, x, weights, bias):
    tokens, model = x.shape
    width = bias.shape[1]
    sents = tokens // LEN
    out_specs = [
        by_rows(LEN, 3 * width),
        by_rows(LEN, width),
        pl.BlockSpec((1, width // HD, LEN), lambda s, l: (s, 0, 0)),
    ]
    out_shape = [
        shaped((tokens, 3 * width)),
        shaped((tokens, width)),
        shaped((sents, width // HD, LEN), F32),
    ]
    own = len(weights) == 1
    if not own:
        full = (3, 2, model // 2, width)
        out_specs.append(whole(full))
        out_shape.append(shaped(full))
    return chain(
        attn_own_kernel if own else attn_other_kernel,
        scalars,
        [x, *weights, bias],
        [by_rows(LEN, model)] + [once(w.shape) for w in weights] + [whole(bias.shape)],
        out_specs,
        out_shape,
        grid=(sents,),
        name="attn_fwd",
        micros=11.4,
        vmem=24,
    )


def attn_back_kernel(s_ref, qkv_ref, do_ref, lse_ref, grad_ref, sum_ref):
    s = pl.program_id(0)
    length = s_ref[2 + s]
    rows, width = do_ref.shape
    low = lax.broadcasted_iota(jnp.int32, (rows, LANES), 1) < HD
    live = lax.broadcasted_iota(jnp.int32, (rows, LANES), 0) < length
    bias = jnp.where(live, 0.0, MASKED).astype(F32)
    zero = jnp.zeros((rows, LANES), BF16)

    @pl.when(s == 0)
    def _():
        sum_ref[...] = jnp.zeros_like(sum_ref)

    for p in range(width // LANES):
        at = LANES * p
        q = qkv_ref[:, at : at + LANES] * 0.125
        k = qkv_ref[:, width + at : width + at + LANES]
        v = qkv_ref[:, 2 * width + at : 2 * width + at + LANES]
        do = do_ref[:, at : at + LANES]
        kt = k.T
        dqs, dks, dvs = [], [], []
        for h in range(2):
            km = jnp.where(low, k, zero) if h == 0 else jnp.where(low, zero, k)
            vm = jnp.where(low, v, zero) if h == 0 else jnp.where(low, zero, v)
            lse = lse_ref[0, 2 * p + h : 2 * p + h + 1, :]
            scores = nt(km, q)
            dprob = nt(vm, do)
            probs, dscores = [], []
            for j in range(rows // LANES):
                cols = slice(LANES * j, LANES * j + LANES)
                e = jnp.exp(scores[:, cols] + bias - lse[:, cols])
                probs.append(e.astype(BF16))
                dp = dprob[:, cols]
                dscores.append((e * (dp - colsum(e * dp))).astype(BF16))
            prob = jnp.concatenate(probs, axis=1)
            dscore = jnp.concatenate(dscores, axis=1)
            dvs.append(nn(prob, do))
            dks.append(nn(dscore, q))
            dqs.append(nn(kt[HD * h : HD * h + HD], dscore))
        dq = (jnp.concatenate(dqs, axis=0).T * 0.125).astype(BF16)
        dk = jnp.where(low, dks[0], dks[1]).astype(BF16)
        dv = jnp.where(low, dvs[0], dvs[1]).astype(BF16)
        grad_ref[:, at : at + LANES] = dq
        grad_ref[:, width + at : width + at + LANES] = dk
        grad_ref[:, 2 * width + at : 2 * width + at + LANES] = dv
        sum_ref[0:1, at : at + LANES] += colsum(dq.astype(F32))
        sum_ref[1:2, at : at + LANES] += colsum(dv.astype(F32))


def attn_backward(chain, scalars, qkv, do, lse):
    tokens, width = do.shape
    return chain(
        attn_back_kernel,
        scalars,
        [qkv, do, lse],
        [
            by_rows(LEN, 3 * width),
            by_rows(LEN, width),
            pl.BlockSpec((1, width // HD, LEN), lambda s, l: (s, 0, 0)),
        ],
        [by_rows(LEN, 3 * width), whole((2, width))],
        [shaped((tokens, 3 * width)), shaped((2, width), F32)],
        grid=(tokens // LEN,),
        name="attn_bwd",
        micros=12.6,
        vmem=24,
    )


def across(ref):
    return ref[...].reshape(1, ref.shape[0])


def normalize(r):
    center = r - rowmean(r)
    inverse = lax.rsqrt(rowmean(center * center) + EPS_NORM)
    return center * inverse, inverse


def project_kernel(
    s_ref, x_ref, c_own, c_oth, w_own, w0, w1, bias_ref, gain_ref, shift_ref,
    h_ref, low_ref, n_ref, inv_ref, w_ref,
):
    @pl.when(pl.program_id(0) == 0)
    def _():
        for s, ref in enumerate((w0, w1)):
            w_ref[bit(s_ref[0], 0) ^ s] = ref[...]

    shape = w_ref.shape
    other = w_ref[...].reshape(shape[0] * shape[1], shape[2])
    attended = nn(c_own[...], w_own[...]) + nn(c_oth[...], other) + across(bias_ref)
    normal, inverse = normalize(x_ref[...].astype(F32) + attended)
    h = normal * across(gain_ref) + across(shift_ref)
    h_ref[...] = h
    low_ref[...] = h.astype(BF16)
    n_ref[...] = normal.astype(BF16)
    inv_ref[...] = inverse


def project_forward(chain, scalars, x, c_own, c_oth, w_own, slots, vecs):
    tokens, model = x.shape
    block = 512
    width = c_own.shape[1]
    full = (2,) + slots[0].shape
    return chain(
        project_kernel,
        scalars,
        [x, c_own, c_oth, w_own, *slots, *vecs],
        [by_rows(block, model), by_rows(block, width), by_rows(block, width), once(w_own.shape)]
        + [once(s.shape) for s in slots]
        + [whole(v.shape) for v in vecs],
        [by_rows(block, model)] * 3 + [by_rows(block, 1), whole(full)],
        [
            shaped((tokens, model), F32),
            shaped((tokens, model)),
            shaped((tokens, model)),
            shaped((tokens, 1), F32),
            shaped(full),
        ],
        grid=(tokens // block,),
        name="project_fwd",
        micros=6.7,
        vmem=24,
    )


def feed_own_kernel(s_ref, h_ref, wu_ref, bu_ref, wd_ref, g_ref, gp_ref, f_ref):
    h = h_ref[...]
    chunk = wu_ref.shape[1] // 3
    bu = across(bu_ref)
    total = None
    for j in range(3):
        cols = slice(chunk * j, chunk * j + chunk)
        act, slope = gelu_pair(nn(h, wu_ref[:, cols]) + bu[:, cols])
        act = act.astype(BF16)
        g_ref[:, cols] = act
        gp_ref[:, cols] = slope.astype(BF16)
        part = nn(act, wd_ref[cols, :])
        total = part if total is None else total + part
    f_ref[...] = total


def feed_own(chain, scalars, h, wu, bu, wd):
    tokens, model = h.shape
    units = wu.shape[1]
    block = 256
    return chain(
        feed_own_kernel,
        scalars,
        [h, wu, bu, wd],
        [by_rows(block, model), once(wu.shape), whole(bu.shape), once(wd.shape)],
        [by_rows(block, units), by_rows(block, units), by_rows(block, model)],
        [shaped((tokens, units)), shaped((tokens, units)), shaped((tokens, model), F32)],
        grid=(tokens // block,),
        name="feed_own",
        micros=14.5,
        vmem=20,
    )


def feed_up_kernel(s_ref, h_ref, u0, u1, u2, u3, bias_ref, g_ref, gp_ref, wu_ref):
    part = u0.shape[1]

    @pl.when(pl.program_id(0) == 0)
    def _():
        for s, up in enumerate((u0, u1, u2, u3)):
            at = ((s_ref[0] & 3) ^ s) * part
            wu_ref[:, pl.ds(pl.multiple_of(at, LANES), part)] = up[...]

    h = h_ref[...]
    chunk = wu_ref.shape[1] // 3
    rows = bias_ref.shape[0] - 2
    bu = jnp.concatenate([bias_ref[2 + i : 3 + i, :] for i in range(rows)], axis=1)
    for j in range(3):
        cols = slice(chunk * j, chunk * j + chunk)
        act, slope = gelu_pair(nn(h, wu_ref[:, cols]) + bu[:, cols])
        g_ref[:, cols] = act.astype(BF16)
        gp_ref[:, cols] = slope.astype(BF16)


def feed_up(chain, scalars, h, up, bias):
    tokens, model = h.shape
    units = 4 * up[0].shape[1]
    block = 256
    full = (model, units)
    return chain(
        feed_up_kernel,
        scalars,
        [h, *up, bias],
        [by_rows(block, model)] + [once(w.shape) for w in up] + [whole(bias.shape)],
        [by_rows(block, units), by_rows(block, units), whole(full)],
        [shaped((tokens, units)), shaped((tokens, units)), shaped(full)],
        grid=(tokens // block,),
        name="feed_up",
        micros=11.0,
        vmem=20,
    )


def feed_down_kernel(
    s_ref, g_ref, h_ref, f_ref, d0, d1, bias_ref, gain_ref, shift_ref,
    out_ref, n_ref, inv_ref, pool_ref, wd_ref,
):
    i = pl.program_id(0)

    @pl.when(i == 0)
    def _():
        for s, down in enumerate((d0, d1)):
            wd_ref[bit(s_ref[0], 0) ^ s] = down[...]
        pool_ref[...] = jnp.zeros_like(pool_ref)

    shape = wd_ref.shape
    down = wd_ref[...].reshape(shape[0] * shape[1], shape[2])
    total = nn(g_ref[...], down)
    normal, inverse = normalize(h_ref[...] + (f_ref[...] + total + across(bias_ref)))
    y = normal * across(gain_ref) + across(shift_ref)
    out_ref[...] = y.astype(BF16)
    n_ref[...] = normal.astype(BF16)
    inv_ref[...] = inverse
    block = y.shape[0]
    per = LEN // block
    sent = i // per
    length = s_ref[2 + sent]
    first = (i - sent * per) * block
    live = lax.broadcasted_iota(jnp.int32, y.shape, 0) + first < length
    pool_ref[pl.ds(sent, 1), :] += colsum(jnp.where(live, y, 0.0)) / length.astype(F32)


def feed_down(chain, scalars, g, h, f, down, vecs):
    tokens, model = h.shape
    units = g.shape[1]
    block = 256
    sents = tokens // LEN
    full = (2,) + down[0].shape
    return chain(
        feed_down_kernel,
        scalars,
        [g, h, f, *down, *vecs],
        [by_rows(block, units), by_rows(block, model), by_rows(block, model)]
        + [once(w.shape) for w in down]
        + [whole(v.shape) for v in vecs],
        [by_rows(block, model), by_rows(block, model), by_rows(block, 1), whole((sents, model)), whole(full)],
        [
            shaped((tokens, model)),
            shaped((tokens, model)),
            shaped((tokens, 1), F32),
            shaped((sents, model), F32),
            shaped(full),
        ],
        grid=(tokens // block,),
        name="feed_down",
        micros=9.0,
        vmem=20,
    )


def exact(a, b, dims):
    return lax.dot_general(
        a, b, (dims, ((), ())), precision=lax.Precision.HIGHEST, preferred_element_type=F32
    )


def loss_kernel(s_ref, *refs):
    *slot_refs, id_ref, loss_ref, cot_ref, pool_ref, grad_ref = refs
    local = cot_ref.shape[0]
    rank = s_ref[1]
    part = slot_refs[0].shape[0]
    count = part * len(slot_refs)
    for s in range(count // local):
        for i in range(local):
            at = local * s + i
            row = slot_refs[at // part][at % part : at % part + 1, :]
            pool_ref[pl.ds((rank ^ s) * local + i, 1), :] = row
    pooled = pool_ref[...]
    scale = lax.rsqrt(jnp.sum(pooled * pooled, axis=-1, keepdims=True) + EPS_UNIT)
    unit = pooled * scale
    score = SOFTMAX_TEMP * exact(unit, unit, ((1,), (1,)))
    itself = lax.broadcasted_iota(jnp.int32, score.shape, 0) == lax.broadcasted_iota(
        jnp.int32, score.shape, 1
    )
    others = jnp.where(itself, MASKED, score)
    top = jnp.max(others, axis=1, keepdims=True)
    power = jnp.exp(others - top)
    total = jnp.sum(power, axis=1, keepdims=True)
    ids = jnp.broadcast_to(across(id_ref).astype(F32), score.shape)
    match = jnp.logical_and(ids == ids.T, jnp.logical_not(itself)).astype(F32)
    number = jnp.sum(match, axis=1, keepdims=True)
    matched = jnp.sum(match * score, axis=1, keepdims=True) / number
    terms = top + jnp.log(total) - matched
    loss_ref[...] = jnp.sum(terms, axis=0, keepdims=True) / count
    dscore = float(LEN) * (power / total - match / number)
    dunit = SOFTMAX_TEMP * (exact(dscore, unit, ((1,), (0,))) + exact(dscore, unit, ((0,), (0,))))
    grad_ref[...] = scale * (dunit - unit * jnp.sum(unit * dunit, axis=-1, keepdims=True))
    for i in range(local):
        own = grad_ref[pl.ds(rank * local + i, 1), :]
        cot_ref[i : i + 1, :] = own / s_ref[2 + i].astype(F32)


def loss_call(chain, scalars, slots, group_ids, local):
    part, model = slots[0].shape
    count = part * len(slots)
    return chain(
        loss_kernel,
        scalars,
        [*slots, group_ids],
        [whole((part, model))] * len(slots) + [whole((count,))],
        [whole((1, 1)), whole((local, model))],
        [shaped((1, 1), F32), shaped((local, model), F32)],
        scratch=[pltpu.VMEM((count, model), F32)] * 2,
        name="loss",
        micros=3.8,
    )


def norm_back(upstream, normal, inverse, gain):
    scaled = upstream * gain
    return inverse * (scaled - rowmean(scaled) - normal * rowmean(scaled * normal))


def norm_two_kernel(s_ref, cot_ref, n_ref, inv_ref, gain_ref, pool_ref, df_ref, sum_ref):
    s = pl.program_id(0)
    normal = n_ref[...].astype(F32)
    live = lax.broadcasted_iota(jnp.int32, normal.shape, 0) < s_ref[2 + s]
    up = cot_ref[...].astype(F32) + jnp.where(live, pool_ref[pl.ds(s, 1), :], 0.0)
    df = norm_back(up, normal, inv_ref[...], across(gain_ref)).astype(BF16)
    df_ref[...] = df

    @pl.when(s == 0)
    def _():
        sum_ref[...] = jnp.zeros_like(sum_ref)

    sum_ref[0:1, :] += colsum(df.astype(F32))
    sum_ref[1:2, :] += colsum(up * normal)
    sum_ref[2:3, :] += colsum(up)


def norm_two_backward(chain, scalars, cot, normal, inverse, gain, pool_cot):
    tokens, model = cot.shape
    return chain(
        norm_two_kernel,
        scalars,
        [cot, normal, inverse, gain, pool_cot],
        [by_rows(LEN, model), by_rows(LEN, model), by_rows(LEN, 1), whole(gain.shape), whole(pool_cot.shape)],
        [by_rows(LEN, model), whole((3, model))],
        [shaped((tokens, model)), shaped((3, model), F32)],
        grid=(tokens // LEN,),
        name="norm_two_bwd",
        micros=5.4,
    )


def unit_back_kernel(s_ref, df_ref, gp_ref, wd_ref, du_ref, sum_ref):
    @pl.when(pl.program_id(0) == 0)
    def _():
        sum_ref[...] = jnp.zeros_like(sum_ref)

    df = df_ref[...]
    chunk = wd_ref.shape[0] // 3
    for j in range(3):
        cols = slice(chunk * j, chunk * j + chunk)
        du = (nt(df, wd_ref[cols, :]) * gp_ref[:, cols].astype(F32)).astype(BF16)
        du_ref[:, cols] = du
        sum_ref[:, cols] += colsum(du.astype(F32))


def unit_backward(chain, scalars, df, gp, wd):
    tokens, model = df.shape
    units = gp.shape[1]
    block = 512
    return chain(
        unit_back_kernel,
        scalars,
        [df, gp, wd],
        [by_rows(block, model), by_rows(block, units), once(wd.shape)],
        [by_rows(block, units), whole((1, units))],
        [shaped((tokens, units)), shaped((1, units), F32)],
        grid=(tokens // block,),
        name="unit_bwd",
        micros=60.0,
        vmem=24,
    )


def middle_kernel(
    s_ref, df_ref, du_own, du_oth, wu_own, wu_oth, n_ref, inv_ref, gain_ref, wo_own, wo_oth,
    da_ref, dc_own, dc_oth, sum_ref,
):
    @pl.when(pl.program_id(0) == 0)
    def _():
        sum_ref[...] = jnp.zeros_like(sum_ref)

    total = df_ref[...].astype(F32) + nt(du_oth[...], wu_oth[...]) + nt(du_own[...], wu_own[...])
    normal = n_ref[...].astype(F32)
    da = norm_back(total, normal, inv_ref[...], across(gain_ref)).astype(BF16)
    da_ref[...] = da
    dc_own[...] = nt(da, wo_own[...]).astype(BF16)
    dc_oth[...] = nt(da, wo_oth[...]).astype(BF16)
    sum_ref[0:1, :] += colsum(total * normal)
    sum_ref[1:2, :] += colsum(total)
    sum_ref[2:3, :] += colsum(da.astype(F32))


def middle_backward(chain, scalars, df, du_own, du_oth, wu_own, wu_oth, normal, inverse, gain, wo_own, wo_oth):
    tokens, model = df.shape
    units = wu_own.shape[1]
    width = wo_own.shape[0]
    block = 256
    return chain(
        middle_kernel,
        scalars,
        [df, du_own, du_oth, wu_own, wu_oth, normal, inverse, gain, wo_own, wo_oth],
        [by_rows(block, model), by_rows(block, units), by_rows(block, units)]
        + [once(wu_own.shape), once(wu_oth.shape), by_rows(block, model), by_rows(block, 1)]
        + [whole(gain.shape), once(wo_own.shape), once(wo_oth.shape)],
        [by_rows(block, model)] + [by_rows(block, width)] * 2 + [whole((3, model))],
        [shaped((tokens, model))] + [shaped((tokens, width))] * 2 + [shaped((3, model), F32)],
        grid=(tokens // block,),
        name="middle_bwd",
        micros=12.0,
        vmem=24,
    )


def bit(value, at):
    return (value >> at) & 1


def split_store(d, even, odd, keep_ref, send_ref, at):
    flip = bit(d, 0) == 0
    keep_ref[at] = jnp.where(flip, even, odd).astype(BF16)
    send_ref[at] = jnp.where(flip, odd, even).astype(BF16)


def dense_grad_kernel(d_ref, a_ref, b_ref, keep_ref, send_ref):
    d = d_ref[0]
    grad = tn(a_ref[...], b_ref[...])
    step = keep_ref.shape[3]
    for x in range(2):
        for z in range(2):
            at = (4 * z + 2 * x) * step
            split_store(
                d, grad[at : at + step], grad[at + step : at + 2 * step], keep_ref, send_ref,
                (x ^ bit(d, 1), z ^ bit(d, 2), 0),
            )


def dense_grad(chain, scalars, a, b, cut_left):
    tokens = a.shape[0]
    left = a.shape[1] // (2 if cut_left else 1)
    right = b.shape[1] // (1 if cut_left else 2)
    step = left // 8
    block = pl.BlockSpec((2, 2, 1, step, right), lambda i, s: (0, 0, i ^ bit(s[0], 3), 0, 0))
    fixed, moving = lambda i, s: (0, 0), lambda i, s: (0, i)
    return chain(
        dense_grad_kernel,
        scalars,
        [a, b],
        [
            pl.BlockSpec((tokens, left), moving if cut_left else fixed),
            pl.BlockSpec((tokens, right), fixed if cut_left else moving),
        ],
        [block, block],
        [shaped((2, 2, 2, step, right))] * 2,
        grid=(2,),
        name="dense_grad",
        micros=60.0,
        vmem=20,
    )


def heads_grad_kernel(
    d_ref, c_ref, da_ref, x_ref, dqkv_ref, two_ref, one_ref, bias_ref, unit_ref,
    keep_a, send_a, keep_b, send_b,
):
    d = d_ref[0]
    width = c_ref.shape[1]
    out = tn(c_ref[...], da_ref[...])
    proj = tn(x_ref[...], dqkv_ref[...])
    step = width // 8
    small = [ref[i : i + 1, at : at + width] for ref in (two_ref, one_ref) for i in range(3) for at in (0, width)]
    small += [bias_ref[0:1, :], bias_ref[1:2, :]]
    small += [unit_ref[:, at : at + width] for at in range(0, unit_ref.shape[1], width)]
    small += [jnp.zeros((1, width), F32)] * (32 - len(small))
    rest = jnp.zeros((14, width), F32)

    def block(b):
        row, col = (b & 7) * step, (b >> 3) * width
        pieces = [out[row : row + step, col : col + width]]
        pieces += [proj[b * step : b * step + step, c * width : c * width + width] for c in range(3)]
        first = jnp.concatenate(pieces[:2] + [small[b], small[16 + b], rest], axis=0)
        return first, jnp.concatenate(pieces[2:], axis=0)

    for x in range(2):
        for z in range(2):
            for w in range(2):
                b = 8 * w + 4 * z + 2 * x
                at = (x ^ bit(d, 1), z ^ bit(d, 2), w ^ bit(d, 3))
                even, odd = block(b), block(b + 1)
                split_store(d, even[0], odd[0], keep_a, send_a, at)
                split_store(d, even[1], odd[1], keep_b, send_b, at)


def heads_grad(chain, scalars, c, da, x, dqkv, sums):
    width = c.shape[1]
    first = (2, 2, 2, width // 4 + 16, width)
    second = (2, 2, 2, width // 4, width)
    inputs = [c, da, x, dqkv, *sums]
    return chain(
        heads_grad_kernel,
        scalars,
        inputs,
        [once(a.shape) for a in inputs],
        [whole(first)] * 2 + [whole(second)] * 2,
        [shaped(first)] * 2 + [shaped(second)] * 2,
        name="heads_grad",
        micros=60.0,
        vmem=28,
    )


def input_grad_kernel(s_ref, own_ref, oth_ref, w_own, w_oth, da_ref, out_ref):
    total = da_ref[...].astype(F32)
    for grad, w in ((own_ref, w_own), (oth_ref, w_oth)):
        total = total + nt(grad[...], jnp.concatenate([w[c] for c in range(3)], axis=1))
    out_ref[...] = total


def input_grad(chain, scalars, own, oth, w_own, w_oth, da):
    tokens, model = da.shape
    block = 512
    return chain(
        input_grad_kernel,
        scalars,
        [own, oth, w_own, w_oth, da],
        [by_rows(block, own.shape[1])] * 2 + [once(w_own.shape), once(w_oth.shape), by_rows(block, model)],
        [by_rows(block, model)],
        [shaped((tokens, model), F32)],
        grid=(tokens // block,),
        name="input_grad",
        micros=60.0,
        vmem=24,
    )[0]


def place_kernel(s_ref, a0, a1, b0, b1, *out_refs):
    d = s_ref[0]
    half = pl.program_id(0)
    flip = bit(d, 0) == 0
    for x, (near_ref, far_ref) in enumerate(((a0, b0), (a1, b1))):
        for z in range(2):
            near, far = near_ref[z, 0].astype(F32), far_ref[z, 0].astype(F32)
            low = (x ^ bit(d, 1)) + 2 * (z ^ bit(d, 2))
            for side, rows in enumerate((jnp.where(flip, near, far), jnp.where(flip, far, near))):
                if len(out_refs) == 1:
                    step = rows.shape[0]
                    out_refs[0][low, side * step : (side + 1) * step] = rows
                    continue
                out_ref, proj_ref, *vec_refs, unit_ref, small_ref = out_refs
                step = out_ref.shape[1] // 2
                here = slice(side * step, (side + 1) * step)
                out_ref[low, here] = rows[:step]
                proj_ref[0, low, here] = rows[step : 2 * step]
                b = 2 * (low + 4 * (half ^ bit(d, 3))) + side
                small_ref[pl.ds(b, 1), :] = rows[2 * step : 2 * step + 1]
                small_ref[pl.ds(16 + b, 1), :] = rows[2 * step + 1 : 2 * step + 2]
    if len(out_refs) == 1:
        return

    @pl.when(half == 1)
    def _():
        line = lambda at, count: jnp.concatenate([small_ref[i : i + 1, :] for i in range(at, at + count)], axis=1)
        for i, ref in enumerate(vec_refs[:6]):
            ref[...] = line(2 * i, 2).reshape(ref.shape[0])
        vec_refs[6][...] = small_ref[12:14, :]
        unit_ref[...] = line(14, unit_ref.shape[0] // small_ref.shape[1]).reshape(unit_ref.shape[0])


def place(chain, scalars, pieces, kind, units):
    step, cols = pieces[0].shape[2:]
    block = pl.BlockSpec((2, 1, step, cols), lambda w, s: (0, w, 0, 0))
    high = lambda w, s: w ^ bit(s[0], 3)
    scratch = []
    if kind == "down":
        shapes = [(8, 2 * step, cols)]
        specs = [pl.BlockSpec((4, 2 * step, cols), lambda w, s: (high(w, s), 0, 0))]
    elif kind == "up":
        shapes = [(4, 2 * step, 2 * cols)]
        specs = [pl.BlockSpec((4, 2 * step, cols), lambda w, s: (0, 0, high(w, s)))]
    else:
        part = (step - 16) // 2
        shapes = [(4, 2 * part, 2 * cols), (3, 8, 2 * part, cols)]
        specs = [
            pl.BlockSpec((4, 2 * part, cols), lambda w, s: (0, 0, high(w, s))),
            pl.BlockSpec((1, 4, 2 * part, cols), lambda w, s: (0, high(w, s), 0, 0)),
        ]
        vectors = [(2 * cols,)] * 6 + [(2, cols), (units,)]
        shapes += vectors
        specs += [whole(v) for v in vectors]
        scratch = [pltpu.VMEM((32, cols), F32)]
    return chain(
        place_kernel,
        scalars,
        pieces,
        [block] * 4,
        specs,
        [shaped(s, F32) for s in shapes],
        grid=(2,),
        scratch=scratch,
        name="place",
        micros=4.0,
        vmem=24,
    )


def place_more_kernel(s_ref, a0, a1, b0, b1, kept_ref, out_ref):
    d = s_ref[0]
    flip = bit(d, 0) == 0
    step = out_ref.shape[2] // 2
    for x, (near_ref, far_ref) in enumerate(((a0, b0), (a1, b1))):
        for z in range(2):
            near, far = near_ref[z, 0].astype(F32), far_ref[z, 0].astype(F32)
            low = (x ^ bit(d, 1)) + 2 * (z ^ bit(d, 2))
            out_ref[0, low, :step] = jnp.where(flip, near, far)
            out_ref[0, low, step:] = jnp.where(flip, far, near)


def place_more(chain, scalars, pieces, kept):
    step, cols = pieces[0].shape[2:]
    block = pl.BlockSpec((2, 1, step // 2, cols), lambda w, c, s: (0, w, c, 0))
    return chain(
        place_more_kernel,
        scalars,
        [*pieces, kept],
        [block] * 4 + [pl.BlockSpec(memory_space=pl.ANY)],
        [pl.BlockSpec((1, 4, step, cols), lambda w, c, s: (1 + c, w ^ bit(s[0], 3), 0, 0))],
        [shaped(kept.shape, F32)],
        grid=(2, 2),
        name="place_more",
        micros=4.0,
        vmem=24,
        aliases={5: 0},
    )[0]


def swap(x, axis, mask):
    size = lax.axis_size(axis)
    return lax.ppermute(x, axis, [(i, i ^ mask) for i in range(size)])


def swap_all(x, mask):
    size = lax.axis_size("dp") * lax.axis_size("tensor")
    return lax.ppermute(x, ("dp", "tensor"), [(i, i ^ mask) for i in range(size)])


def levels():
    return lax.axis_size("dp").bit_length() - 1


def sum_kernel(s_ref, *refs, count, early):
    total = refs[0][...].astype(F32) + refs[1][...].astype(F32)
    if early:
        total = total.astype(BF16).astype(F32)
    for ref in refs[2:count]:
        total = total + ref[...].astype(F32)
    total = total.astype(BF16)
    outs = refs[count:]
    if len(outs) == 1:
        outs[0][...] = total
        return
    for i, out in enumerate(outs):
        out[...] = total[i]


def add(chain, scalars, terms, split=1, early=False):
    shape = terms[0].shape
    outs = [shape] if split == 1 else [shape[1:]] * split
    return chain(
        functools.partial(sum_kernel, count=len(terms), early=early),
        scalars,
        terms,
        [whole(shape)] * len(terms),
        [whole(o) for o in outs],
        [shaped(o) for o in outs],
        name="add",
        micros=2.0,
    )


def join_kernel(s_ref, *refs):
    for i, ref in enumerate(refs[:-1]):
        refs[-1][i] = ref[...]


def join(chain, scalars, parts):
    shape = (len(parts),) + parts[0].shape
    return chain(
        join_kernel,
        scalars,
        parts,
        [whole(p.shape) for p in parts],
        [whole(shape)],
        [shaped(shape)],
        name="join",
        micros=1.5,
    )[0]


class Reduction:
    def __init__(self, chain, scalars):
        self.chain, self.scalars = chain, scalars

    def add(self, terms, split=1, early=False):
        return add(self.chain, self.scalars, terms, split, early)

    def send(self, x, axis, mask):
        return self.chain.send(x, axis, mask)

    def receive(self, sent):
        return self.chain.receive(self.scalars, sent)

    def other(self, keep, send):
        self.keep_oth, self.got_oth = keep, self.send(send, "dp", 1)

    def own(self, keep, send):
        self.keep_own, self.got_own = keep, self.send(send, "dp", 1)

    def across(self):
        (total,) = self.add([self.keep_oth, self.receive(self.got_oth)])
        self.got_y = self.send(total, "tensor", 1)

    def along_x(self):
        got = [self.receive(self.got_own), self.receive(self.got_y)]
        self.keep, send = self.add([self.keep_own, *got], 2, True)
        self.got = self.send(send, "dp", 2)

    def along_z0(self):
        self.keep, send = self.add([self.keep, self.receive(self.got)], 2)
        self.got = self.send(send, "dp", 4)

    def along_z1(self):
        self.keep, send = self.add([self.keep, self.receive(self.got)], 2)
        self.got = self.send(send, "dp", 8)

    def turn(self):
        (self.total,) = self.add([self.keep, self.receive(self.got)])
        for at in range(4, levels()):
            got = self.receive(self.send(self.total, "dp", 1 << at))
            (self.total,) = self.add([self.total, got])
        self.got = self.send(self.total, "dp", 8)

    def back_z0(self):
        self.total = join(self.chain, self.scalars, [self.total, self.receive(self.got)])
        self.got = self.send(self.total, "dp", 4)

    def back_x(self):
        self.near = join(self.chain, self.scalars, [self.total, self.receive(self.got)])
        self.got = self.send(self.near, "dp", 2)
        self.near_far = self.send(self.near, "dp", 1)

    def back_core(self):
        self.next = self.chain.gate(self.scalars, self.receive(self.got))
        self.next_far = self.send(self.next, "dp", 1)

    def pieces(self):
        return [self.near, self.next, self.receive(self.near_far), self.receive(self.next_far)]

    def place(self, kind, units=0):
        return place(self.chain, self.scalars, self.pieces(), kind, units)


def stack_rows_kernel(s_ref, *refs):
    step = refs[0].shape[0]
    for i, ref in enumerate(refs[:-1]):
        refs[-1][i * step : (i + 1) * step, :] = ref[...]


def stack_rows(chain, scalars, parts):
    shape = (len(parts) * parts[0].shape[0], parts[0].shape[1])
    return chain(
        stack_rows_kernel,
        scalars,
        parts,
        [whole(p.shape) for p in parts],
        [whole(shape)],
        [shaped(shape, F32)],
        name="stack_rows",
        micros=10.0,
    )[0]


def gather_pooled(chain, scalars, pooled):
    bits = levels() + 1
    at = 0
    while at < bits:
        step = min(1 if at == 2 else 2, bits - at)
        parts = [pooled] + [swap_all(pooled, m << at) for m in range(1, 1 << step)]
        chain.pause(scalars)
        at += step
        if at < bits:
            pooled = stack_rows(chain, scalars, parts)
    return parts


def cut_kernel(s_ref, a_ref, out_ref):
    out_ref[...] = a_ref[...].reshape(out_ref.shape)


def cut(chain, scalars, a, block, index):
    shape = tuple(b for b in block if b != 1)
    return chain(
        cut_kernel,
        scalars,
        [a],
        [pl.BlockSpec(block, lambda i, s: index(s[0] & 3))],
        [whole(shape)],
        [shaped(shape, a.dtype)],
        name="cut",
        micros=1.0,
    )[0]


def cut_first_kernel(s_ref, a_ref, bias_ref, unit_ref, out_ref, small_ref):
    out_ref[...] = a_ref[...].reshape(out_ref.shape)
    width = bias_ref.shape[1]
    small_ref[0:2, :] = bias_ref[...]
    unit = across(unit_ref)
    for i in range(unit.shape[1] // width):
        small_ref[2 + i : 3 + i, :] = unit[:, i * width : (i + 1) * width]


def cut_first(chain, scalars, a, bias, unit):
    _, _, part, width = a.shape
    shape = (3, part, width)
    small = (2 + unit.shape[0] // width, width)
    return chain(
        cut_first_kernel,
        scalars,
        [a, bias, unit],
        [
            pl.BlockSpec((3, 1, part, width), lambda i, s: (0, bit(s[0], 0), 0, 0)),
            whole(bias.shape),
            whole(unit.shape),
        ],
        [whole(shape), whole(small)],
        [shaped(shape), shaped(small, F32)],
        name="cut",
        micros=1.0,
    )


class Gather:
    def __init__(self, chain, scalars, piece, relayed=False):
        self.chain, self.scalars, self.relayed = chain, scalars, relayed
        self.got = chain.send(piece, "tensor", 1)
        self.parts = []

    def hand_over(self):
        part = self.chain.gate(self.scalars, self.chain.receive(self.scalars, self.got))
        if self.relayed and not self.parts:
            self.got = self.chain.send(part, "dp", 2)
        self.parts += [part, self.chain.send(part, "dp", 1)]

    def slots(self):
        parts = self.parts
        parts[1::2] = [self.chain.receive(self.scalars, p) for p in parts[1::2]]
        return parts


def per_device(
    layer_input, w_qkv, bias_qv, w_out, b_out, gain_one, shift_one, w_up, b_up, w_down, b_down,
    gain_two, shift_two, out_cot, lengths, group_ids,
):
    tensor_size = lax.axis_size("tensor")
    position = lax.axis_index("tensor")
    d = lax.axis_index("dp")
    model = layer_input.shape[1]
    width = w_qkv.shape[2]
    units = w_up.shape[1]
    local = lengths.shape[0] // tensor_size
    lens = lax.dynamic_slice_in_dim(lengths, position * local, local, 0)
    rank = d * tensor_size + position
    scal = jnp.concatenate([jnp.stack([d, rank]).astype(jnp.int32), lens])
    chain = Chain()

    part = model // 2
    piece, bias = cut_first(chain, scal, w_qkv.reshape(3, 2, part, width), bias_qv, b_up)
    gather_qkv = Gather(chain, scal, piece)
    bias_oth = swap(bias, "tensor", 1)
    part = width // 2
    piece = cut(chain, scal, w_out.reshape(2, part, model), (1, part, model), lambda q: (q & 1, 0, 0))
    gather_out = Gather(chain, scal, piece)
    qkv_own, c_own, lse_own = attn_forward(chain, scal, layer_input, [w_qkv], bias_qv)
    gather_qkv.hand_over()
    part = units // 4
    piece = cut(chain, scal, w_up, (model, part), lambda q: (0, q))
    gather_up = Gather(chain, scal, piece, relayed=True)
    part = units // 2
    piece = cut(chain, scal, w_down.reshape(2, part, model), (1, part, model), lambda q: (q & 1, 0, 0))
    gather_down = Gather(chain, scal, piece)
    gather_out.hand_over()
    qkv_oth, c_oth, lse_oth, wq_oth = attn_forward(chain, scal, layer_input, gather_qkv.slots(), bias_oth)
    wq_oth = wq_oth.reshape(3, model, width)
    h1, h1_low, normal_one, inverse_one, wo_oth = project_forward(
        chain, scal, layer_input, c_own, c_oth, w_out, gather_out.slots(), [b_out, gain_one, shift_one]
    )
    wo_oth = wo_oth.reshape(width, model)
    gather_up.hand_over()
    g_own, gp_own, f_own = feed_own(chain, scal, h1_low, w_up, b_up, w_down)
    gather_up.hand_over()
    g_oth, gp_oth, wu_oth = feed_up(chain, scal, h1_low, gather_up.slots(), bias_oth)
    gather_down.hand_over()
    output, normal_two, inverse_two, pooled, wd_oth = feed_down(
        chain, scal, g_oth, h1, f_own, gather_down.slots(), [b_down, gain_two, shift_two]
    )
    wd_oth = wd_oth.reshape(units, model)

    loss, pool_cot = loss_call(chain, scal, gather_pooled(chain, scal, pooled), group_ids, local)

    down, up, first, second = (Reduction(chain, scal) for _ in range(4))
    df, sums_two = norm_two_backward(chain, scal, out_cot, normal_two, inverse_two, gain_two, pool_cot)
    down.other(*dense_grad(chain, scal, g_oth, df, True))
    down.own(*dense_grad(chain, scal, g_own, df, True))
    down.across()
    du_oth, sums_du_oth = unit_backward(chain, scal, df, gp_oth, wd_oth)
    du_own, sums_du_own = unit_backward(chain, scal, df, gp_own, w_down)
    up.other(*dense_grad(chain, scal, h1_low, du_oth, False))
    up.own(*dense_grad(chain, scal, h1_low, du_own, False))
    up.across()
    da, dc_own, dc_oth, sums_one = middle_backward(
        chain, scal, df, du_own, du_oth, w_up, wu_oth, normal_one, inverse_one, gain_one, w_out, wo_oth
    )
    down.along_x()
    dqkv_oth, sums_oth = attn_backward(chain, scal, qkv_oth, dc_oth, lse_oth)
    sums = [sums_two, sums_one, sums_oth, sums_du_oth]
    grads = heads_grad(chain, scal, c_oth, da, layer_input, dqkv_oth, sums)
    first.other(*grads[:2])
    second.other(*grads[2:])
    down.along_z0()
    up.along_x()
    chain.pause(scal)
    first.across()
    second.across()
    dqkv_own, sums_own = attn_backward(chain, scal, qkv_own, dc_own, lse_own)
    down.along_z1()
    up.along_z0()
    sums = [sums_two, sums_one, sums_own, sums_du_own]
    grads = heads_grad(chain, scal, c_own, da, layer_input, dqkv_own, sums)
    first.own(*grads[:2])
    second.own(*grads[2:])
    down.turn()
    chain.pause(scal)
    first.along_x()
    grad_input = input_grad(chain, scal, dqkv_own, dqkv_oth, w_qkv, wq_oth, da)
    second.along_x()
    down.back_z0()
    up.along_z1()
    chain.pause(scal)
    first.along_z0()
    down.back_x()
    up.turn()
    chain.pause(scal)
    second.along_z0()
    first.along_z1()
    up.back_z0()
    chain.pause(scal)
    first.turn()
    second.along_z1()
    up.back_x()
    chain.pause(scal)
    second.turn()
    first.back_z0()
    down.back_core()
    chain.pause(scal)
    first.back_x()
    second.back_z0()
    chain.pause(scal)
    (grad_w_down,) = down.place("down")
    second.back_x()
    up.back_core()
    chain.pause(scal)
    (grad_w_up,) = up.place("up")
    first.back_core()
    chain.pause(scal)
    second.back_core()
    grad_w_out, grad_w_qkv, *grads, grad_bias_qv, grad_b_up = first.place("heads", units)
    grad_w_qkv = place_more(chain, scal, second.pieces(), grad_w_qkv)
    grad_b_down, grad_gain_two, grad_shift_two, grad_gain_one, grad_shift_one, grad_b_out = grads
    return (
        loss.reshape(()),
        output,
        grad_input,
        grad_w_qkv.reshape(w_qkv.shape),
        grad_bias_qv,
        grad_w_out.reshape(w_out.shape),
        grad_b_out,
        grad_gain_one,
        grad_shift_one,
        grad_w_up.reshape(w_up.shape),
        grad_b_up,
        grad_w_down.reshape(w_down.shape),
        grad_b_down,
        grad_gain_two,
        grad_shift_two,
    )


def solution(mesh):
    rows = P(("dp", "tensor"), None)
    in_specs = (
        rows,
        P(None, None, "tensor"),
        P(None, "tensor"),
        P("tensor", None),
        P(),
        P(),
        P(),
        P(None, "tensor"),
        P("tensor"),
        P("tensor", None),
        P(),
        P(),
        P(),
        rows,
        P("dp"),
        P(),
    )
    out_specs = (
        P(),
        rows,
        rows,
        P(None, None, "tensor"),
        P(None, "tensor"),
        P("tensor", None),
        P(),
        P(),
        P(),
        P(None, "tensor"),
        P("tensor"),
        P("tensor", None),
        P(),
        P(),
        P(),
    )
    return jax.shard_map(
        per_device, mesh=mesh, in_specs=in_specs, out_specs=out_specs, check_vma=False
    )
```

```python
import functools

import jax
import jax.numpy as jnp
from jax import lax
from jax.experimental import pallas as pl
from jax.experimental.pallas import tpu as pltpu
from jax.sharding import PartitionSpec as P

HD = 64
LEN = 512
LANES = 128
EPS_NORM = 1e-12
EPS_UNIT = 1e-6
SOFTMAX_TEMP = 20.0
MASKED = -1e30
F32 = jnp.float32
BF16 = jnp.bfloat16
COST_SCALE = 1.0

ERFC_SLOPE = 0.41 * 0.7071067811865476
ERFC_POLY = tuple(
    0.5 * c
    for c in (
        0.23389259840606333,
        0.19943405568812744,
        0.36527628560337355,
        -0.195943508470611,
        0.5767329065489298,
        -0.17939241407306944,
    )
)
INV_SQRT_2PI = 0.3989422804014327


def cost(micros):
    return pl.CostEstimate(
        flops=int(micros * COST_SCALE * 1.15e9),
        bytes_accessed=int(micros * COST_SCALE * 3.6e6),
        transcendentals=0,
    )


def whole(shape):
    return pl.BlockSpec(shape, lambda *_: (0,) * len(shape))


def once(shape):
    return pl.BlockSpec(shape, lambda *_: (0,) * len(shape), pipeline_mode=pl.Buffered(1))


def shaped(shape, dtype=BF16):
    return jax.ShapeDtypeStruct(shape, dtype)


class Chain:
    def __init__(self):
        self.last = None
        self.windows = 0

    def __call__(self, kernel, scalars, inputs, in_specs, out_specs, out_shape, *, name, micros,
                 grid=(1,), scratch=(), vmem=16, token=False, aliases=None):
        deps = [] if self.last is None else [self.last]
        count = len(inputs)

        given = len(out_shape)
        if token:
            out_specs = list(out_specs) + [pl.BlockSpec(memory_space=pl.ANY)]
            out_shape = list(out_shape) + [shaped((8, LANES), F32)]

        def body(s_ref, *refs):
            rest = refs[count + len(deps) :]
            kernel(s_ref, *refs[:count], *rest[:given], *rest[len(out_shape) :])

        outs = pl.pallas_call(
            body,
            grid_spec=pltpu.PrefetchScalarGridSpec(
                num_scalar_prefetch=1,
                grid=grid,
                in_specs=list(in_specs) + [pl.BlockSpec(memory_space=pl.ANY)] * len(deps),
                out_specs=out_specs,
                scratch_shapes=list(scratch),
            ),
            out_shape=out_shape,
            input_output_aliases=aliases or {},
            compiler_params=pltpu.CompilerParams(vmem_limit_bytes=vmem * 2**20),
            cost_estimate=cost(micros),
            name=name,
        )(scalars, *inputs, *deps)
        self.last = outs[-1] if token else outs[0]
        if micros >= 3:
            self.windows += 1
        return outs[:given]

    def gate(self, scalars, a):
        def kernel(s_ref, a_ref, out_ref):
            out_ref[...] = a_ref[...]

        return self(
            kernel, scalars, [a], [whole(a.shape)], [whole(a.shape)], [shaped(a.shape, a.dtype)],
            name="gate", micros=10.0,
        )[0]

    def send(self, x, axis, mask):
        return swap(x, axis, mask), self.windows

    def receive(self, scalars, sent):
        if sent[1] == self.windows:
            self.pause(scalars)
        return sent[0]

    def pause(self, scalars):
        def kernel(s_ref, out_ref):
            out_ref[...] = jnp.zeros_like(out_ref)

        tile = (8, LANES)
        self(kernel, scalars, [], [], [whole(tile)], [shaped(tile, F32)], name="pause", micros=100.0)


def nn(a, b):
    return lax.dot_general(a, b, (((1,), (0,)), ((), ())), preferred_element_type=F32)


def nt(a, b):
    return lax.dot_general(a, b, (((1,), (1,)), ((), ())), preferred_element_type=F32)


def tn(a, b):
    return lax.dot_general(a, b, (((0,), (0,)), ((), ())), preferred_element_type=F32)


def colsum(a):
    return jnp.sum(a, axis=0, keepdims=True)


def rowmean(a):
    return jnp.mean(a, axis=-1, keepdims=True)


def gelu_pair(u):
    den = 1.0 + ERFC_SLOPE * jnp.abs(u)
    t = pl.reciprocal(den, approx=True)
    t = t * (2.0 - den * t)
    poly = ERFC_POLY[-1]
    for c in ERFC_POLY[-2::-1]:
        poly = poly * t + c
    bell = jnp.exp(-0.5 * (u * u))
    tail = bell * (poly * t)
    cdf = jnp.where(u >= 0, 1.0 - tail, tail)
    return u * cdf, cdf + (u * bell) * INV_SQRT_2PI


def length_of(s_ref, sentence):
    return s_ref[3 + s_ref[2] + sentence]


def attend_sentence(length, x, weights, bq, bv, qkv_ref, c_ref, lse_ref):
    rows = x.shape[0]
    width = c_ref.shape[1]
    both = nn(x, jnp.concatenate(weights, axis=1))
    qkv_ref[:, :width] = (both[:, :width] + bq).astype(BF16)
    qkv_ref[:, width : 2 * width] = both[:, width : 2 * width].astype(BF16)
    qkv_ref[:, 2 * width :] = (both[:, 2 * width :] + bv).astype(BF16)
    low = lax.broadcasted_iota(jnp.int32, (rows, LANES), 1) < HD
    live = lax.broadcasted_iota(jnp.int32, (rows, LANES), 0) < length
    bias = jnp.where(live, 0.0, MASKED).astype(F32)
    zero = jnp.zeros((rows, LANES), BF16)
    for p in range(width // LANES):
        at = LANES * p
        q = qkv_ref[:, at : at + LANES] * 0.125
        k = qkv_ref[:, width + at : width + at + LANES]
        v = qkv_ref[:, 2 * width + at : 2 * width + at + LANES]
        vt = v.T
        outs = []
        for h in range(2):
            km = jnp.where(low, k, zero) if h == 0 else jnp.where(low, zero, k)
            scores = nt(km, q)
            parts, tops, sums = [], [], []
            for j in range(rows // LANES):
                piece = scores[:, LANES * j : LANES * j + LANES] + bias
                top = jnp.max(piece, axis=0, keepdims=True)
                e = jnp.exp(piece - top)
                parts.append(e.astype(BF16))
                tops.append(top)
                sums.append(colsum(e))
            top = jnp.concatenate(tops, axis=1)
            total = jnp.concatenate(sums, axis=1)
            ct = nn(vt[HD * h : HD * h + HD], jnp.concatenate(parts, axis=1))
            outs.append(ct / total)
            lse_ref[0, 2 * p + h : 2 * p + h + 1, :] = top + jnp.log(total)
        c_ref[:, at : at + LANES] = jnp.concatenate(outs, axis=0).T.astype(BF16)


def attn_own_kernel(s_ref, x_ref, w_ref, b_ref, qkv_ref, c_ref, lse_ref):
    weights = [w_ref[c] for c in range(3)]
    length = length_of(s_ref, pl.program_id(0))
    attend_sentence(
        length, x_ref[...], weights, b_ref[0:1, :], b_ref[1:2, :], qkv_ref, c_ref, lse_ref
    )


def attn_other_kernel(s_ref, x_ref, w0, w1, b_ref, qkv_ref, c_ref, lse_ref, w_ref, *, at):
    @pl.when(pl.program_id(0) == 0)
    def _():
        for s, ref in enumerate((w0, w1)):
            for c in range(3):
                w_ref[c, bit(s_ref[0], 0) ^ s] = ref[c]

    shape = w_ref.shape
    weights = [w_ref[c].reshape(shape[1] * shape[2], shape[3]) for c in range(3)]
    length = length_of(s_ref, pl.program_id(0))
    cols = slice(at, at + shape[3])
    attend_sentence(
        length, x_ref[...], weights, b_ref[0:1, cols], b_ref[1:2, cols], qkv_ref, c_ref, lse_ref
    )


def attn_pack_kernel(s_ref, x_ref, p0, p1, b_ref, qkv_ref, c_ref, lse_ref, w_ref, out_ref, *, at):
    _, _, half, width = w_ref.shape

    @pl.when(pl.program_id(0) == 0)
    def _():
        rows, cols = out_ref.shape[1:]
        for s, ref in enumerate((p0, p1)):
            place = bit(s_ref[0], 0) ^ s
            for c in range(3):
                w_ref[c, place] = ref[c * half : (c + 1) * half, :]
            for k in range(cols // width):
                begin = 3 * half + k * rows
                out_ref[place, :, k * width : (k + 1) * width] = ref[begin : begin + rows, :]

    weights = [w_ref[c].reshape(2 * half, width) for c in range(3)]
    length = length_of(s_ref, pl.program_id(0))
    cols = slice(at, at + width)
    attend_sentence(
        length, x_ref[...], weights, b_ref[0:1, cols], b_ref[1:2, cols], qkv_ref, c_ref, lse_ref
    )


def by_rows(block, cols):
    return pl.BlockSpec((block, cols), lambda i, *_: (i, 0))


def attn_forward(chain, scalars, x, weights, bias, at=0, out_rows=0):
    tokens, model = x.shape
    width = weights[0].shape[-1]
    sents = tokens // LEN
    out_specs = [
        by_rows(LEN, 3 * width),
        by_rows(LEN, width),
        pl.BlockSpec((1, width // HD, LEN), lambda s, l: (s, 0, 0)),
    ]
    out_shape = [
        shaped((tokens, 3 * width)),
        shaped((tokens, width)),
        shaped((sents, width // HD, LEN), F32),
    ]
    own = len(weights) == 1
    extra = [] if own else [(3, 2, model // 2, width)] + ([(2, out_rows // 2, model)] if out_rows else [])
    out_specs += [whole(full) for full in extra]
    out_shape += [shaped(full) for full in extra]
    kernel = attn_pack_kernel if out_rows else attn_other_kernel
    return chain(
        attn_own_kernel if own else functools.partial(kernel, at=at),
        scalars,
        [x, *weights, bias],
        [by_rows(LEN, model)] + [once(w.shape) for w in weights] + [whole(bias.shape)],
        out_specs,
        out_shape,
        grid=(sents,),
        name="attn_fwd",
        micros=8.8,
        vmem=24,
    )


def attn_back_kernel(s_ref, qkv_ref, do_ref, lse_ref, grad_ref, sum_ref):
    s = pl.program_id(0)
    length = length_of(s_ref, s)
    rows, width = do_ref.shape
    low = lax.broadcasted_iota(jnp.int32, (rows, LANES), 1) < HD
    live = lax.broadcasted_iota(jnp.int32, (rows, LANES), 0) < length
    bias = jnp.where(live, 0.0, MASKED).astype(F32)
    zero = jnp.zeros((rows, LANES), BF16)

    @pl.when(s == 0)
    def _():
        sum_ref[...] = jnp.zeros_like(sum_ref)

    for p in range(width // LANES):
        at = LANES * p
        q = qkv_ref[:, at : at + LANES] * 0.125
        k = qkv_ref[:, width + at : width + at + LANES]
        v = qkv_ref[:, 2 * width + at : 2 * width + at + LANES]
        do = do_ref[:, at : at + LANES]
        kt = k.T
        dqs, dks, dvs = [], [], []
        for h in range(2):
            km = jnp.where(low, k, zero) if h == 0 else jnp.where(low, zero, k)
            vm = jnp.where(low, v, zero) if h == 0 else jnp.where(low, zero, v)
            lse = lse_ref[0, 2 * p + h : 2 * p + h + 1, :]
            scores = nt(km, q)
            dprob = nt(vm, do)
            probs, dscores = [], []
            for j in range(rows // LANES):
                cols = slice(LANES * j, LANES * j + LANES)
                e = jnp.exp(scores[:, cols] + bias - lse[:, cols])
                probs.append(e.astype(BF16))
                dp = dprob[:, cols]
                dscores.append((e * (dp - colsum(e * dp))).astype(BF16))
            prob = jnp.concatenate(probs, axis=1)
            dscore = jnp.concatenate(dscores, axis=1)
            dvs.append(nn(prob, do))
            dks.append(nn(dscore, q))
            dqs.append(nn(kt[HD * h : HD * h + HD], dscore))
        dq = (jnp.concatenate(dqs, axis=0).T * 0.125).astype(BF16)
        dk = jnp.where(low, dks[0], dks[1]).astype(BF16)
        dv = jnp.where(low, dvs[0], dvs[1]).astype(BF16)
        grad_ref[:, at : at + LANES] = dq
        grad_ref[:, width + at : width + at + LANES] = dk
        grad_ref[:, 2 * width + at : 2 * width + at + LANES] = dv
        sum_ref[0:1, at : at + LANES] += colsum(dq.astype(F32))
        sum_ref[1:2, at : at + LANES] += colsum(dv.astype(F32))


def attn_backward(chain, scalars, qkv, do, lse):
    tokens, width = do.shape
    return chain(
        attn_back_kernel,
        scalars,
        [qkv, do, lse],
        [
            by_rows(LEN, 3 * width),
            by_rows(LEN, width),
            pl.BlockSpec((1, width // HD, LEN), lambda s, l: (s, 0, 0)),
        ],
        [by_rows(LEN, 3 * width), whole((2, width))],
        [shaped((tokens, 3 * width)), shaped((2, width), F32)],
        grid=(tokens // LEN,),
        name="attn_bwd",
        micros=12.6,
        vmem=24,
    )


def across(ref):
    return ref[...].reshape(1, ref.shape[0])


def normalize(r):
    center = r - rowmean(r)
    inverse = lax.rsqrt(rowmean(center * center) + EPS_NORM)
    return center * inverse, inverse


def project_kernel(s_ref, x_ref, *refs, count):
    c_refs, refs = refs[:count], refs[count:]
    w_own, other, bias_ref, gain_ref, shift_ref, h_ref, low_ref, n_ref, inv_ref = refs
    attended = nn(c_refs[0][...], w_own[...]) + across(bias_ref)
    at = 0
    for ref in c_refs[1:]:
        width = ref.shape[1]
        attended = attended + nn(ref[...], other[at : at + width, :])
        at += width
    normal, inverse = normalize(x_ref[...].astype(F32) + attended)
    h = normal * across(gain_ref) + across(shift_ref)
    h_ref[...] = h
    low_ref[...] = h.astype(BF16)
    n_ref[...] = normal.astype(BF16)
    inv_ref[...] = inverse


def project_forward(chain, scalars, x, contexts, w_own, w_oth, vecs):
    tokens, model = x.shape
    block = 512
    return chain(
        functools.partial(project_kernel, count=len(contexts)),
        scalars,
        [x, *contexts, w_own, w_oth, *vecs],
        [by_rows(block, model)]
        + [by_rows(block, c.shape[1]) for c in contexts]
        + [once(w_own.shape), once(w_oth.shape)]
        + [whole(v.shape) for v in vecs],
        [by_rows(block, model)] * 3 + [by_rows(block, 1)],
        [
            shaped((tokens, model), F32),
            shaped((tokens, model)),
            shaped((tokens, model)),
            shaped((tokens, 1), F32),
        ],
        grid=(tokens // block,),
        name="project_fwd",
        micros=3.7,
        vmem=24,
    )


def feed_own_kernel(s_ref, h_ref, wu_ref, bu_ref, wd_ref, g_ref, gp_ref, f_ref):
    h = h_ref[...]
    chunk = wu_ref.shape[1] // 3
    bu = across(bu_ref)
    total = None
    for j in range(3):
        cols = slice(chunk * j, chunk * j + chunk)
        act, slope = gelu_pair(nn(h, wu_ref[:, cols]) + bu[:, cols])
        act = act.astype(BF16)
        g_ref[:, cols] = act
        gp_ref[:, cols] = slope.astype(BF16)
        part = nn(act, wd_ref[cols, :])
        total = part if total is None else total + part
    f_ref[...] = total


def feed_own(chain, scalars, h, wu, bu, wd):
    tokens, model = h.shape
    units = wu.shape[1]
    block = 256
    return chain(
        feed_own_kernel,
        scalars,
        [h, wu, bu, wd],
        [by_rows(block, model), once(wu.shape), whole(bu.shape), once(wd.shape)],
        [by_rows(block, units), by_rows(block, units), by_rows(block, model)],
        [shaped((tokens, units)), shaped((tokens, units)), shaped((tokens, model), F32)],
        grid=(tokens // block,),
        name="feed_own",
        micros=14.5,
        vmem=20,
    )


def feed_up_kernel(s_ref, h_ref, near_ref, far_ref, bias_ref, *refs, second):
    g_ref, gp_ref, wu_ref = refs[-3:]
    part = near_ref.shape[1]
    core = bit(s_ref[0], 0)

    @pl.when(pl.program_id(0) == 0)
    def _():
        wu_ref[:, pl.ds(pl.multiple_of(core * part, LANES), part)] = near_ref[...]
        wu_ref[:, pl.ds(pl.multiple_of((1 - core) * part, LANES), part)] = far_ref[...]

    row = 2 + 2 * (bit(s_ref[0], 1) ^ second)
    bu = jnp.concatenate([bias_ref[pl.ds(row + i, 1), :] for i in range(2)], axis=1)
    act, slope = gelu_pair(nn(h_ref[...], wu_ref[...]) + bu)
    g_ref[...] = act.astype(BF16)
    gp_ref[...] = slope.astype(BF16)


def feed_up(chain, scalars, h, near, far, bias, kept=()):
    tokens, model = h.shape
    half = 2 * near.shape[1]
    block = 256
    second = 1 if kept else 0
    here = lambda s: bit(s[0], 1) ^ second
    columns = pl.BlockSpec((block, half), lambda i, s: (i, here(s)))
    return chain(
        functools.partial(feed_up_kernel, second=second),
        scalars,
        [h, near, far, bias, *kept],
        [by_rows(block, model), once(near.shape), once(far.shape), whole(bias.shape)]
        + [pl.BlockSpec(memory_space=pl.ANY)] * len(kept),
        [columns, columns, pl.BlockSpec((model, half), lambda i, s: (0, here(s)))],
        [shaped((tokens, 2 * half)), shaped((tokens, 2 * half)), shaped((model, 2 * half))],
        grid=(tokens // block,),
        name="feed_up",
        micros=60.0,
        vmem=20,
        aliases={5 + i: i for i in range(len(kept))},
    )


def feed_down_kernel(
    s_ref, g_ref, h_ref, f_ref, d0, d1, bias_ref, gain_ref, shift_ref,
    out_ref, n_ref, inv_ref, pool_ref, wd_ref,
):
    i = pl.program_id(0)

    @pl.when(i == 0)
    def _():
        for s, down in enumerate((d0, d1)):
            wd_ref[bit(s_ref[0], 0) ^ s] = down[...]
        pool_ref[...] = jnp.zeros_like(pool_ref)

    shape = wd_ref.shape
    down = wd_ref[...].reshape(shape[0] * shape[1], shape[2])
    total = nn(g_ref[...], down)
    normal, inverse = normalize(h_ref[...] + (f_ref[...] + total + across(bias_ref)))
    y = normal * across(gain_ref) + across(shift_ref)
    out_ref[...] = y.astype(BF16)
    n_ref[...] = normal.astype(BF16)
    inv_ref[...] = inverse
    block = y.shape[0]
    per = LEN // block
    sent = i // per
    length = length_of(s_ref, sent)
    first = (i - sent * per) * block
    live = lax.broadcasted_iota(jnp.int32, y.shape, 0) + first < length
    pool_ref[pl.ds(sent, 1), :] += colsum(jnp.where(live, y, 0.0)) / length.astype(F32)


def feed_down(chain, scalars, g, h, f, down, vecs):
    tokens, model = h.shape
    units = g.shape[1]
    block = 256
    sents = tokens // LEN
    full = (2,) + down[0].shape
    return chain(
        feed_down_kernel,
        scalars,
        [g, h, f, *down, *vecs],
        [by_rows(block, units), by_rows(block, model), by_rows(block, model)]
        + [once(w.shape) for w in down]
        + [whole(v.shape) for v in vecs],
        [by_rows(block, model), by_rows(block, model), by_rows(block, 1), whole((sents, model)), whole(full)],
        [
            shaped((tokens, model)),
            shaped((tokens, model)),
            shaped((tokens, 1), F32),
            shaped((sents, model), F32),
            shaped(full),
        ],
        grid=(tokens // block,),
        name="feed_down",
        micros=9.0,
        vmem=20,
    )


def exact(a, b, dims):
    return lax.dot_general(
        a, b, (dims, ((), ())), precision=lax.Precision.HIGHEST, preferred_element_type=F32
    )


def loss_kernel(s_ref, *refs):
    *slot_refs, id_ref, loss_ref, cot_ref, pool_ref, grad_ref = refs
    local = cot_ref.shape[0]
    rank = s_ref[1]
    part = slot_refs[0].shape[0]
    count = part * len(slot_refs)
    for s in range(count // local):
        for i in range(local):
            at = local * s + i
            row = slot_refs[at // part][at % part : at % part + 1, :]
            pool_ref[pl.ds((rank ^ s) * local + i, 1), :] = row
    pooled = pool_ref[...]
    scale = lax.rsqrt(jnp.sum(pooled * pooled, axis=-1, keepdims=True) + EPS_UNIT)
    unit = pooled * scale
    score = SOFTMAX_TEMP * exact(unit, unit, ((1,), (1,)))
    itself = lax.broadcasted_iota(jnp.int32, score.shape, 0) == lax.broadcasted_iota(
        jnp.int32, score.shape, 1
    )
    others = jnp.where(itself, MASKED, score)
    top = jnp.max(others, axis=1, keepdims=True)
    power = jnp.exp(others - top)
    total = jnp.sum(power, axis=1, keepdims=True)
    ids = jnp.broadcast_to(across(id_ref).astype(F32), score.shape)
    match = jnp.logical_and(ids == ids.T, jnp.logical_not(itself)).astype(F32)
    number = jnp.sum(match, axis=1, keepdims=True)
    matched = jnp.sum(match * score, axis=1, keepdims=True) / number
    terms = top + jnp.log(total) - matched
    loss_ref[...] = jnp.sum(terms, axis=0, keepdims=True) / count
    dscore = float(LEN) * (power / total - match / number)
    dunit = SOFTMAX_TEMP * (exact(dscore, unit, ((1,), (0,))) + exact(dscore, unit, ((0,), (0,))))
    grad_ref[...] = scale * (dunit - unit * jnp.sum(unit * dunit, axis=-1, keepdims=True))
    for i in range(local):
        own = grad_ref[pl.ds(rank * local + i, 1), :]
        cot_ref[i : i + 1, :] = own / length_of(s_ref, i).astype(F32)


def loss_call(chain, scalars, slots, group_ids, local):
    part, model = slots[0].shape
    count = part * len(slots)
    return chain(
        loss_kernel,
        scalars,
        [*slots, group_ids],
        [whole((part, model))] * len(slots) + [whole((count,))],
        [whole((1, 1)), whole((local, model))],
        [shaped((1, 1), F32), shaped((local, model), F32)],
        scratch=[pltpu.VMEM((count, model), F32)] * 2,
        name="loss",
        micros=3.8,
    )


def norm_back(upstream, normal, inverse, gain):
    scaled = upstream * gain
    return inverse * (scaled - rowmean(scaled) - normal * rowmean(scaled * normal))


def norm_two_kernel(s_ref, cot_ref, n_ref, inv_ref, gain_ref, pool_ref, df_ref, sum_ref):
    s = pl.program_id(0)
    normal = n_ref[...].astype(F32)
    live = lax.broadcasted_iota(jnp.int32, normal.shape, 0) < length_of(s_ref, s)
    up = cot_ref[...].astype(F32) + jnp.where(live, pool_ref[pl.ds(s, 1), :], 0.0)
    df = norm_back(up, normal, inv_ref[...], across(gain_ref)).astype(BF16)
    df_ref[...] = df

    @pl.when(s == 0)
    def _():
        sum_ref[...] = jnp.zeros_like(sum_ref)

    sum_ref[0:1, :] += colsum(df.astype(F32))
    sum_ref[1:2, :] += colsum(up * normal)
    sum_ref[2:3, :] += colsum(up)


def norm_two_backward(chain, scalars, cot, normal, inverse, gain, pool_cot):
    tokens, model = cot.shape
    return chain(
        norm_two_kernel,
        scalars,
        [cot, normal, inverse, gain, pool_cot],
        [by_rows(LEN, model), by_rows(LEN, model), by_rows(LEN, 1), whole(gain.shape), whole(pool_cot.shape)],
        [by_rows(LEN, model), whole((3, model))],
        [shaped((tokens, model)), shaped((3, model), F32)],
        grid=(tokens // LEN,),
        name="norm_two_bwd",
        micros=5.4,
    )


def unit_back_kernel(s_ref, df_ref, gp_ref, wd_ref, du_ref, sum_ref):
    @pl.when(pl.program_id(0) == 0)
    def _():
        sum_ref[...] = jnp.zeros_like(sum_ref)

    df = df_ref[...]
    chunk = wd_ref.shape[0] // 3
    for j in range(3):
        cols = slice(chunk * j, chunk * j + chunk)
        du = (nt(df, wd_ref[cols, :]) * gp_ref[:, cols].astype(F32)).astype(BF16)
        du_ref[:, cols] = du
        sum_ref[:, cols] += colsum(du.astype(F32))


def unit_backward(chain, scalars, df, gp, wd):
    tokens, model = df.shape
    units = gp.shape[1]
    block = 512
    return chain(
        unit_back_kernel,
        scalars,
        [df, gp, wd],
        [by_rows(block, model), by_rows(block, units), once(wd.shape)],
        [by_rows(block, units), whole((1, units))],
        [shaped((tokens, units)), shaped((1, units), F32)],
        grid=(tokens // block,),
        name="unit_bwd",
        micros=60.0,
        vmem=24,
    )


def middle_kernel(
    s_ref, df_ref, du_own, du_oth, wu_own, wu_oth, n_ref, inv_ref, gain_ref, wo_own, wo_oth,
    da_ref, sum_ref, dc_own, *dc_oth,
):
    @pl.when(pl.program_id(0) == 0)
    def _():
        sum_ref[...] = jnp.zeros_like(sum_ref)

    total = df_ref[...].astype(F32) + nt(du_oth[...], wu_oth[...]) + nt(du_own[...], wu_own[...])
    normal = n_ref[...].astype(F32)
    da = norm_back(total, normal, inv_ref[...], across(gain_ref)).astype(BF16)
    da_ref[...] = da
    dc_own[...] = nt(da, wo_own[...]).astype(BF16)
    at = 0
    for ref in dc_oth:
        width = ref.shape[1]
        ref[...] = nt(da, wo_oth[at : at + width, :]).astype(BF16)
        at += width
    sum_ref[0:1, :] += colsum(total * normal)
    sum_ref[1:2, :] += colsum(total)
    sum_ref[2:3, :] += colsum(da.astype(F32))


def middle_backward(
    chain, scalars, df, du_own, du_oth, wu_own, wu_oth, normal, inverse, gain, wo_own, wo_oth, widths
):
    tokens, model = df.shape
    units = wu_own.shape[1]
    block = 256
    return chain(
        middle_kernel,
        scalars,
        [df, du_own, du_oth, wu_own, wu_oth, normal, inverse, gain, wo_own, wo_oth],
        [by_rows(block, model), by_rows(block, units), by_rows(block, units)]
        + [once(wu_own.shape), once(wu_oth.shape), by_rows(block, model), by_rows(block, 1)]
        + [whole(gain.shape), once(wo_own.shape), once(wo_oth.shape)],
        [by_rows(block, model), whole((3, model))] + [by_rows(block, w) for w in widths],
        [shaped((tokens, model)), shaped((3, model), F32)] + [shaped((tokens, w)) for w in widths],
        grid=(tokens // block,),
        name="middle_bwd",
        micros=12.0,
        vmem=24,
    )


def bit(value, at):
    return (value >> at) & 1


def split_store(d, even, odd, keep_ref, send_ref, at):
    flip = bit(d, 0) == 0
    keep_ref[at] = jnp.where(flip, even, odd).astype(BF16)
    send_ref[at] = jnp.where(flip, odd, even).astype(BF16)


def dense_grad_kernel(d_ref, a_ref, b_ref, keep_ref, send_ref):
    d = d_ref[0]
    grad = tn(a_ref[...], b_ref[...])
    step = keep_ref.shape[3]
    for x in range(2):
        for z in range(2):
            at = (4 * z + 2 * x) * step
            split_store(
                d, grad[at : at + step], grad[at + step : at + 2 * step], keep_ref, send_ref,
                (x ^ bit(d, 1), z ^ bit(d, 2), 0),
            )


def dense_grad(chain, scalars, a, b, cut_left):
    tokens = a.shape[0]
    left = a.shape[1] // (2 if cut_left else 1)
    right = b.shape[1] // (1 if cut_left else 2)
    step = left // 8
    block = pl.BlockSpec((2, 2, 1, step, right), lambda i, s: (0, 0, i ^ bit(s[0], 3), 0, 0))
    return chain(
        dense_grad_kernel,
        scalars,
        [a, b],
        [
            pl.BlockSpec((tokens, left), lambda i, s: (0, i)) if cut_left else once(a.shape),
            once(b.shape) if cut_left else pl.BlockSpec((tokens, right), lambda i, s: (0, i)),
        ],
        [block, block],
        [shaped((2, 2, 2, step, right))] * 2,
        grid=(2,),
        name="dense_grad",
        micros=60.0,
        vmem=20,
    )


def heads_grad_kernel(d_ref, x_ref, da_ref, two_ref, one_ref, unit_ref, *refs):
    *refs, keep_ref, send_ref = refs
    count = len(refs) // 3
    c_refs, dqkv_refs, bias_refs = refs[:count], refs[count : 2 * count], refs[2 * count :]
    d = d_ref[0]
    bias = jnp.concatenate([ref[...] for ref in bias_refs], axis=1)
    width = bias.shape[1]
    out = jnp.concatenate([tn(ref[...], da_ref[...]) for ref in c_refs], axis=0)
    projs = [tn(x_ref[...], ref[...]) for ref in dqkv_refs]
    proj = jnp.concatenate(
        [p[:, c * (p.shape[1] // 3) : (c + 1) * (p.shape[1] // 3)] for c in range(3) for p in projs], axis=1
    )
    step = proj.shape[0] // 16
    small = [ref[i : i + 1, at : at + width] for ref in (two_ref, one_ref) for i in range(3) for at in (0, width)]
    small += [bias[0:1, :], bias[1:2, :]]
    small += [unit_ref[:, at : at + width] for at in range(0, unit_ref.shape[1], width)]
    small += [jnp.zeros((1, width), F32)] * (32 - len(small))
    rest = jnp.zeros((14, width), F32)

    def block(b):
        row, col = (b & 7) * step, (b >> 3) * width
        pieces = [out[row : row + step, col : col + width]]
        pieces += [proj[b * step : b * step + step, c * width : c * width + width] for c in range(3)]
        return jnp.concatenate(pieces + [small[b], small[16 + b], rest], axis=0)

    for x in range(2):
        for z in range(2):
            for w in range(2):
                b = 8 * w + 4 * z + 2 * x
                split_store(
                    d, block(b), block(b + 1), keep_ref, send_ref,
                    (x ^ bit(d, 1), z ^ bit(d, 2), w ^ bit(d, 3)),
                )


def heads_grad(chain, scalars, x, da, sums, contexts, dqkvs, biases):
    width = sum(b.shape[1] for b in biases)
    full = (2, 2, 2, width // 2 + 16, width)
    inputs = [x, da, *sums, *contexts, *dqkvs, *biases]
    return chain(
        heads_grad_kernel,
        scalars,
        inputs,
        [once(a.shape) for a in inputs],
        [whole(full), whole(full)],
        [shaped(full)] * 2,
        name="heads_grad",
        micros=60.0,
        vmem=28,
    )


def input_grad_kernel(s_ref, da_ref, *refs):
    *refs, out_ref = refs
    total = da_ref[...].astype(F32)
    for grad, w in zip(refs[: len(refs) // 2], refs[len(refs) // 2 :], strict=True):
        total = total + nt(grad[...], jnp.concatenate([w[c] for c in range(3)], axis=1))
    out_ref[...] = total


def input_grad(chain, scalars, da, grads, weights):
    tokens, model = da.shape
    block = 512
    return chain(
        input_grad_kernel,
        scalars,
        [da, *grads, *weights],
        [by_rows(block, model)] + [by_rows(block, g.shape[1]) for g in grads] + [once(w.shape) for w in weights],
        [by_rows(block, model)],
        [shaped((tokens, model), F32)],
        grid=(tokens // block,),
        name="input_grad",
        token=True,
        micros=60.0,
        vmem=24,
    )[0]


def place_kernel(s_ref, a0, a1, b0, b1, *out_refs, kind):
    d = s_ref[0]
    half = pl.program_id(0)
    flip = bit(d, 0) == 0
    for x, (near_ref, far_ref) in enumerate(((a0, b0), (a1, b1))):
        for z in range(2):
            near, far = near_ref[z, 0].astype(F32), far_ref[z, 0].astype(F32)
            low = (x ^ bit(d, 1)) + 2 * (z ^ bit(d, 2))
            for side, rows in enumerate((jnp.where(flip, near, far), jnp.where(flip, far, near))):
                if kind != "heads":
                    step = rows.shape[0]
                    out_refs[0][low, side * step : (side + 1) * step] = rows
                    continue
                out_ref, proj_ref, *vec_refs, unit_ref, small_ref = out_refs
                step = out_ref.shape[1] // 2
                out_ref[low, side * step : (side + 1) * step] = rows[:step]
                for c in range(3):
                    proj_ref[c, low, side * step : (side + 1) * step] = rows[(c + 1) * step : (c + 2) * step]
                b = 2 * (low + 4 * (half ^ bit(d, 3))) + side
                small_ref[pl.ds(b, 1), :] = rows[4 * step : 4 * step + 1]
                small_ref[pl.ds(16 + b, 1), :] = rows[4 * step + 1 : 4 * step + 2]
    if kind != "heads":
        return

    @pl.when(half == 1)
    def _():
        line = lambda at, count: jnp.concatenate([small_ref[i : i + 1, :] for i in range(at, at + count)], axis=1)
        for i, ref in enumerate(vec_refs[:6]):
            ref[...] = line(2 * i, 2).reshape(ref.shape[0])
        vec_refs[6][...] = small_ref[12:14, :]
        unit_ref[...] = line(14, unit_ref.shape[0] // small_ref.shape[1]).reshape(unit_ref.shape[0])


def place(chain, scalars, pieces, kind, units):
    step, cols = pieces[0].shape[2:]
    block = pl.BlockSpec((2, 1, step, cols), lambda w, s: (0, w, 0, 0))
    high = lambda w, s: w ^ bit(s[0], 3)
    scratch = []
    if kind == "down":
        shapes = [(8, 2 * step, cols)]
        specs = [pl.BlockSpec((4, 2 * step, cols), lambda w, s: (high(w, s), 0, 0))]
    elif kind == "up":
        shapes = [(4, 2 * step, 2 * cols)]
        specs = [pl.BlockSpec((4, 2 * step, cols), lambda w, s: (0, 0, high(w, s)))]
    else:
        part = (step - 16) // 4
        shapes = [(4, 2 * part, 2 * cols), (3, 8, 2 * part, cols)]
        specs = [
            pl.BlockSpec((4, 2 * part, cols), lambda w, s: (0, 0, high(w, s))),
            pl.BlockSpec((3, 4, 2 * part, cols), lambda w, s: (0, high(w, s), 0, 0)),
        ]
        vectors = [(2 * cols,)] * 6 + [(2, cols), (units,)]
        shapes += vectors
        specs += [whole(v) for v in vectors]
        scratch = [pltpu.VMEM((32, cols), F32)]
    return chain(
        functools.partial(place_kernel, kind=kind),
        scalars,
        pieces,
        [block] * 4,
        specs,
        [shaped(s, F32) for s in shapes],
        grid=(2,),
        scratch=scratch,
        name="place",
        token=True,
        micros=4.0,
        vmem=24,
    )


def swap(x, axis, mask):
    size = lax.axis_size(axis)
    return lax.ppermute(x, axis, [(i, i ^ mask) for i in range(size)])


def swap_all(x, mask):
    size = lax.axis_size("dp") * lax.axis_size("tensor")
    return lax.ppermute(x, ("dp", "tensor"), [(i, i ^ mask) for i in range(size)])


def levels():
    return lax.axis_size("dp").bit_length() - 1


def flip_kernel(s_ref, a_ref, b_ref, out_ref):
    for i in range(2):
        out_ref[i] = (a_ref[i].astype(F32) + b_ref[1 - i].astype(F32)).astype(BF16)


def add_flipped(chain, scalars, a, b):
    return chain(
        flip_kernel,
        scalars,
        [a, b],
        [whole(a.shape)] * 2,
        [whole(a.shape)],
        [shaped(a.shape)],
        name="add",
        micros=2.0,
    )[0]


def sum_kernel(s_ref, *refs, count, early):
    total = refs[0][...].astype(F32) + refs[1][...].astype(F32)
    if early:
        total = total.astype(BF16).astype(F32)
    for ref in refs[2:count]:
        total = total + ref[...].astype(F32)
    total = total.astype(BF16)
    outs = refs[count:]
    if len(outs) == 1:
        outs[0][...] = total
        return
    for i, out in enumerate(outs):
        out[...] = total[i]


def add(chain, scalars, terms, split=1, early=False):
    shape = terms[0].shape
    outs = [shape] if split == 1 else [shape[1:]] * split
    return chain(
        functools.partial(sum_kernel, count=len(terms), early=early),
        scalars,
        terms,
        [whole(shape)] * len(terms),
        [whole(o) for o in outs],
        [shaped(o) for o in outs],
        name="add",
        micros=2.0,
    )


def join_kernel(s_ref, *refs):
    for i, ref in enumerate(refs[:-1]):
        refs[-1][i] = ref[...]


def join(chain, scalars, parts):
    shape = (len(parts),) + parts[0].shape
    return chain(
        join_kernel,
        scalars,
        parts,
        [whole(p.shape) for p in parts],
        [whole(shape)],
        [shaped(shape)],
        name="join",
        micros=1.5,
    )[0]


class Reduction:
    def __init__(self, chain, scalars):
        self.chain, self.scalars = chain, scalars

    def add(self, terms, split=1, early=False):
        return add(self.chain, self.scalars, terms, split, early)

    def send(self, x, axis, mask):
        return self.chain.send(x, axis, mask)

    def receive(self, sent):
        return self.chain.receive(self.scalars, sent)

    def other(self, keep, send):
        self.keep_oth, self.got_oth = keep, self.send(send, "dp", 1)

    def own(self, keep, send):
        self.keep_own, self.got_own = keep, self.send(send, "dp", 1)

    def across(self):
        (total,) = self.add([self.keep_oth, self.receive(self.got_oth)])
        self.got_y = self.send(total, "tensor", 1)

    def along_x(self):
        got = [self.receive(self.got_own), self.receive(self.got_y)]
        self.keep, send = self.add([self.keep_own, *got], 2, True)
        self.got = self.send(send, "dp", 2)

    def along_z(self):
        shape = self.keep.shape
        flat = (4,) + shape[2:]
        got = self.receive(self.got)
        self.keep, *send = self.add([self.keep.reshape(flat), got.reshape(flat)], 4)
        self.got = [self.send(x, "dp", m) for x, m in zip(send, (8, 4, 12), strict=True)]

    def back_z(self):
        (total,) = self.add([self.keep, *(self.receive(g) for g in self.got)])
        for at in range(4, levels()):
            got = self.receive(self.send(total, "dp", 1 << at))
            (total,) = self.add([total, got])
        self.total = total
        self.got = [self.send(total, "dp", m) for m in (8, 4, 12)]

    def back_x_direct(self):
        near = join(self.chain, self.scalars, [self.total, *(self.receive(g) for g in self.got)])
        self.near = near.reshape((2, 2) + near.shape[1:])
        self.got = self.send(self.near, "dp", 2)
        self.near_far = self.send(self.near, "dp", 1)

    def along_z0(self):
        self.keep, send = self.add([self.keep, self.receive(self.got)], 2)
        self.got = self.send(send, "dp", 4)

    def turn(self):
        (self.total,) = self.add([self.keep, self.receive(self.got)])
        for at in range(4, levels()):
            got = self.receive(self.send(self.total, "dp", 1 << at))
            (self.total,) = self.add([self.total, got])
        self.got = self.send(self.total, "dp", 8)

    def back_z0(self):
        self.total = add_flipped(self.chain, self.scalars, self.total, self.receive(self.got))
        self.got = self.send(self.total, "dp", 4)

    def back_x(self):
        self.near = join(self.chain, self.scalars, [self.total, self.receive(self.got)])
        self.got = self.send(self.near, "dp", 2)
        self.near_far = self.send(self.near, "dp", 1)

    def back_core(self):
        self.next = self.chain.gate(self.scalars, self.receive(self.got))
        self.next_far = self.send(self.next, "dp", 1)

    def place(self, kind, units=0):
        pieces = [self.near, self.next, self.receive(self.near_far), self.receive(self.next_far)]
        return place(self.chain, self.scalars, pieces, kind, units)


def stack_rows_kernel(s_ref, *refs):
    step = refs[0].shape[0]
    for i, ref in enumerate(refs[:-1]):
        refs[-1][i * step : (i + 1) * step, :] = ref[...]


def stack_rows(chain, scalars, parts):
    shape = (len(parts) * parts[0].shape[0], parts[0].shape[1])
    return chain(
        stack_rows_kernel,
        scalars,
        parts,
        [whole(p.shape) for p in parts],
        [whole(shape)],
        [shaped(shape, F32)],
        name="stack_rows",
        micros=10.0,
    )[0]


def gather_pooled(chain, scalars, pooled):
    bits = levels() + 1
    at = 0
    while at < bits:
        step = min(1 if at == 2 else 2, bits - at)
        parts = [pooled] + [swap_all(pooled, m << at) for m in range(1, 1 << step)]
        chain.pause(scalars)
        at += step
        if at < bits:
            pooled = stack_rows(chain, scalars, parts)
    return parts


def cut_kernel(s_ref, *refs):
    count = len(refs) // 2
    for a_ref, out_ref in zip(refs[:count], refs[count:], strict=True):
        out_ref[...] = a_ref[...].reshape(out_ref.shape)


def cut(chain, scalars, *cuts):
    shapes = [tuple(b for b in block if b != 1) for _, block, _ in cuts]
    at = lambda index: lambda i, s: index(s[0] & 3)
    return chain(
        cut_kernel,
        scalars,
        [a for a, _, _ in cuts],
        [pl.BlockSpec(block, at(index)) for _, block, index in cuts],
        [whole(s) for s in shapes],
        [shaped(s, a.dtype) for s, (a, _, _) in zip(shapes, cuts, strict=True)],
        name="cut",
        micros=1.0,
    )


def cut_heads_kernel(s_ref, a_ref, out_ref):
    out_ref[...] = a_ref[:, 0, :, : out_ref.shape[2]]


def cut_heads(chain, scalars, a, width):
    _, _, part, full = a.shape
    shape = (3, part, width)
    return chain(
        cut_heads_kernel,
        scalars,
        [a],
        [pl.BlockSpec((3, 1, part, full), lambda i, s: (0, bit(s[0], 0), 0, 0))],
        [whole(shape)],
        [shaped(shape)],
        name="cut",
        micros=1.0,
    )[0]


def cut_pack_kernel(s_ref, a_ref, w_ref, bias_ref, unit_ref, out_ref, small_ref):
    part = a_ref.shape[2]
    width = out_ref.shape[1]
    rows, cols = w_ref.shape[1:]
    for c in range(3):
        out_ref[c * part : (c + 1) * part, :] = a_ref[c, 0, :, a_ref.shape[3] - width :]
    for k in range(cols // width):
        begin = 3 * part + k * rows
        out_ref[begin : begin + rows, :] = w_ref[0, :, k * width : (k + 1) * width]
    full = bias_ref.shape[1]
    small_ref[0:2, :] = bias_ref[...]
    unit = across(unit_ref)
    for i in range(unit.shape[1] // full):
        small_ref[2 + i : 3 + i, :] = unit[:, i * full : (i + 1) * full]


def cut_pack(chain, scalars, a, width, w, bias, unit):
    _, _, part, full = a.shape
    _, rows, cols = w.shape
    shapes = [shaped((3 * part + rows * cols // width, width)), shaped((2 + unit.shape[0] // full, full), F32)]
    return chain(
        cut_pack_kernel,
        scalars,
        [a, w, bias, unit],
        [
            pl.BlockSpec((3, 1, part, full), lambda i, s: (0, bit(s[0], 0), 0, 0)),
            pl.BlockSpec((1, rows, cols), lambda i, s: (bit(s[0], 0), 0, 0)),
            whole(bias.shape),
            whole(unit.shape),
        ],
        [whole(s.shape) for s in shapes],
        shapes,
        name="cut",
        micros=1.0,
    )


class Gather:
    def __init__(self, chain, scalars, piece, relayed=False):
        self.chain, self.scalars, self.relayed = chain, scalars, relayed
        self.got = chain.send(piece, "tensor", 1)
        self.parts = []

    def hand_over(self):
        part = self.chain.gate(self.scalars, self.chain.receive(self.scalars, self.got))
        if self.relayed and not self.parts:
            self.got = self.chain.send(part, "dp", 2)
        self.parts += [part, self.chain.send(part, "dp", 1)]

    def slots(self):
        return [self.slot(i) for i in range(len(self.parts))]

    def slot(self, i):
        return self.parts[i] if i % 2 == 0 else self.chain.receive(self.scalars, self.parts[i])


def per_device(
    layer_input, w_qkv, bias_qv, w_out, b_out, gain_one, shift_one, w_up, b_up, w_down, b_down,
    gain_two, shift_two, out_cot, lengths, group_ids,
):
    tensor_size = lax.axis_size("tensor")
    position = lax.axis_index("tensor")
    d = lax.axis_index("dp")
    model = layer_input.shape[1]
    width = w_qkv.shape[2]
    units = w_up.shape[1]
    local = lengths.shape[0] // tensor_size
    rank = d * tensor_size + position
    scal = jnp.concatenate([jnp.stack([d, rank, position * local]).astype(jnp.int32), lengths])
    chain = Chain()

    heads_cut = w_qkv.reshape(3, 2, model // 2, width)
    lead = width // 3 * 2
    gather_lead = Gather(chain, scal, cut_heads(chain, scal, heads_cut, lead))
    qkv_own, c_own, lse_own = attn_forward(chain, scal, layer_input, [w_qkv], bias_qv)
    piece, bias = cut_pack(
        chain, scal, heads_cut, width - lead, w_out.reshape(2, width // 2, model), bias_qv, b_up
    )
    gather_pack = Gather(chain, scal, piece)
    bias_oth = swap(bias, "tensor", 1)
    part = units // 4
    piece, second = cut(
        chain,
        scal,
        (w_up, (model, part), lambda q: (0, q)),
        (w_down.reshape(2, 2 * part, model), (1, 2 * part, model), lambda q: (q & 1, 0, 0)),
    )
    gather_up = Gather(chain, scal, piece, relayed=True)
    gather_down = Gather(chain, scal, second)
    gather_lead.hand_over()
    qkv_lead, c_lead, lse_lead, wq_lead = attn_forward(chain, scal, layer_input, gather_lead.slots(), bias_oth)
    gather_pack.hand_over()
    qkv_rest, c_rest, lse_rest, wq_rest, wo_oth = attn_forward(
        chain, scal, layer_input, gather_pack.slots(), bias_oth, lead, width
    )
    wq_lead, wq_rest = (w.reshape(3, model, w.shape[3]) for w in (wq_lead, wq_rest))
    wo_oth = wo_oth.reshape(width, model)
    h1, h1_low, normal_one, inverse_one = project_forward(
        chain, scal, layer_input, [c_own, c_lead, c_rest], w_out, wo_oth, [b_out, gain_one, shift_one]
    )
    gather_up.hand_over()
    g_own, gp_own, f_own = feed_own(chain, scal, h1_low, w_up, b_up, w_down)
    gather_up.hand_over()
    near, far = gather_up.slot(0), gather_up.slot(1)
    half = feed_up(chain, scal, h1_low, near, far, bias_oth)
    gather_down.hand_over()
    near, far = gather_up.slot(2), gather_up.slot(3)
    g_oth, gp_oth, wu_oth = feed_up(chain, scal, h1_low, near, far, bias_oth, half)
    output, normal_two, inverse_two, pooled, wd_oth = feed_down(
        chain, scal, g_oth, h1, f_own, gather_down.slots(), [b_down, gain_two, shift_two]
    )
    wd_oth = wd_oth.reshape(units, model)

    loss, pool_cot = loss_call(chain, scal, gather_pooled(chain, scal, pooled), group_ids, local)

    down, up, heads = (Reduction(chain, scal) for _ in range(3))
    df, sums_two = norm_two_backward(chain, scal, out_cot, normal_two, inverse_two, gain_two, pool_cot)
    down.other(*dense_grad(chain, scal, g_oth, df, True))
    down.own(*dense_grad(chain, scal, g_own, df, True))
    down.across()
    du_oth, sums_du_oth = unit_backward(chain, scal, df, gp_oth, wd_oth)
    du_own, sums_du_own = unit_backward(chain, scal, df, gp_own, w_down)
    up.other(*dense_grad(chain, scal, h1_low, du_oth, False))
    up.own(*dense_grad(chain, scal, h1_low, du_own, False))
    up.across()
    da, sums_one, dc_own, dc_lead, dc_rest = middle_backward(
        chain, scal, df, du_own, du_oth, w_up, wu_oth, normal_one, inverse_one, gain_one, w_out, wo_oth,
        [width, lead, width - lead],
    )
    down.along_x()
    dqkv_lead, sums_lead = attn_backward(chain, scal, qkv_lead, dc_lead, lse_lead)
    dqkv_rest, sums_rest = attn_backward(chain, scal, qkv_rest, dc_rest, lse_rest)
    sums = [sums_two, sums_one, sums_du_oth]
    heads.other(
        *heads_grad(
            chain, scal, layer_input, da, sums, [c_lead, c_rest], [dqkv_lead, dqkv_rest], [sums_lead, sums_rest]
        )
    )
    down.along_z0()
    up.along_x()
    chain.pause(scal)
    heads.across()
    dqkv_own, sums_own = attn_backward(chain, scal, qkv_own, dc_own, lse_own)
    down.turn()
    up.along_z0()
    sums = [sums_two, sums_one, sums_du_own]
    heads.own(*heads_grad(chain, scal, layer_input, da, sums, [c_own], [dqkv_own], [sums_own]))
    grad_input = input_grad(
        chain, scal, da, [dqkv_own, dqkv_lead, dqkv_rest], [w_qkv, wq_lead, wq_rest]
    )
    down.back_z0()
    heads.along_x()
    up.turn()
    chain.pause(scal)
    down.back_x()
    heads.along_z0()
    chain.pause(scal)
    heads.turn()
    up.back_z0()
    chain.pause(scal)
    heads.back_z0()
    up.back_x()
    chain.pause(scal)
    down.back_core()
    heads.back_x()
    (grad_w_down,) = down.place("down")
    up.back_core()
    chain.pause(scal)
    (grad_w_up,) = up.place("up")
    heads.back_core()
    chain.pause(scal)
    grad_w_out, grad_w_qkv, *grads, grad_bias_qv, grad_b_up = heads.place("heads", units)
    grad_b_down, grad_gain_two, grad_shift_two, grad_gain_one, grad_shift_one, grad_b_out = grads
    return (
        loss.reshape(()),
        output,
        grad_input,
        grad_w_qkv.reshape(w_qkv.shape),
        grad_bias_qv,
        grad_w_out.reshape(w_out.shape),
        grad_b_out,
        grad_gain_one,
        grad_shift_one,
        grad_w_up.reshape(w_up.shape),
        grad_b_up,
        grad_w_down.reshape(w_down.shape),
        grad_b_down,
        grad_gain_two,
        grad_shift_two,
    )


def solution(mesh):
    rows = P(("dp", "tensor"), None)
    in_specs = (
        rows,
        P(None, None, "tensor"),
        P(None, "tensor"),
        P("tensor", None),
        P(),
        P(),
        P(),
        P(None, "tensor"),
        P("tensor"),
        P("tensor", None),
        P(),
        P(),
        P(),
        rows,
        P("dp"),
        P(),
    )
    out_specs = (
        P(),
        rows,
        rows,
        P(None, None, "tensor"),
        P(None, "tensor"),
        P("tensor", None),
        P(),
        P(),
        P(),
        P(None, "tensor"),
        P("tensor"),
        P("tensor", None),
        P(),
        P(),
        P(),
    )
    return jax.shard_map(
        per_device, mesh=mesh, in_specs=in_specs, out_specs=out_specs, check_vma=False
    )
```

```python
import functools

import jax
import jax.numpy as jnp
from jax import lax
from jax.experimental import pallas as pl
from jax.experimental.pallas import tpu as pltpu
from jax.sharding import PartitionSpec as P

HD = 64
LEN = 512
LANES = 128
EPS_NORM = 1e-12
EPS_UNIT = 1e-6
SOFTMAX_TEMP = 20.0
MASKED = -1e30
F32 = jnp.float32
BF16 = jnp.bfloat16
COST_SCALE = 1.0

ERFC_SLOPE = 0.41 * 0.7071067811865476
ERFC_POLY = tuple(
    0.5 * c
    for c in (
        0.23389259840606333,
        0.19943405568812744,
        0.36527628560337355,
        -0.195943508470611,
        0.5767329065489298,
        -0.17939241407306944,
    )
)
INV_SQRT_2PI = 0.3989422804014327


def cost(micros):
    return pl.CostEstimate(
        flops=int(micros * COST_SCALE * 1.15e9),
        bytes_accessed=int(micros * COST_SCALE * 3.6e6),
        transcendentals=0,
    )


def whole(shape):
    return pl.BlockSpec(shape, lambda *_: (0,) * len(shape))


def once(shape):
    return pl.BlockSpec(shape, lambda *_: (0,) * len(shape), pipeline_mode=pl.Buffered(1))


def shaped(shape, dtype=BF16):
    return jax.ShapeDtypeStruct(shape, dtype)


class Chain:
    def __init__(self):
        self.last = None
        self.windows = 0

    def __call__(self, kernel, scalars, inputs, in_specs, out_specs, out_shape, *, name, micros,
                 grid=(1,), scratch=(), vmem=16, token=False, aliases=None):
        deps = [] if self.last is None else [self.last]
        count = len(inputs)

        given = len(out_shape)
        if token:
            out_specs = list(out_specs) + [pl.BlockSpec(memory_space=pl.ANY)]
            out_shape = list(out_shape) + [shaped((8, LANES), F32)]

        def body(s_ref, *refs):
            rest = refs[count + len(deps) :]
            kernel(s_ref, *refs[:count], *rest[:given], *rest[len(out_shape) :])

        outs = pl.pallas_call(
            body,
            grid_spec=pltpu.PrefetchScalarGridSpec(
                num_scalar_prefetch=1,
                grid=grid,
                in_specs=list(in_specs) + [pl.BlockSpec(memory_space=pl.ANY)] * len(deps),
                out_specs=out_specs,
                scratch_shapes=list(scratch),
            ),
            out_shape=out_shape,
            input_output_aliases=aliases or {},
            compiler_params=pltpu.CompilerParams(vmem_limit_bytes=vmem * 2**20),
            cost_estimate=cost(micros),
            name=name,
        )(scalars, *inputs, *deps)
        self.last = outs[-1] if token else outs[0]
        if micros >= 3:
            self.windows += 1
        return outs[:given]

    def gate(self, scalars, a):
        def kernel(s_ref, a_ref, out_ref):
            out_ref[...] = a_ref[...]

        return self(
            kernel, scalars, [a], [whole(a.shape)], [whole(a.shape)], [shaped(a.shape, a.dtype)],
            name="gate", micros=10.0,
        )[0]

    def send(self, x, axis, mask):
        return swap(x, axis, mask), self.windows

    def receive(self, scalars, sent):
        if sent[1] == self.windows:
            self.pause(scalars)
        return sent[0]

    def pause(self, scalars):
        def kernel(s_ref, out_ref):
            out_ref[...] = jnp.zeros_like(out_ref)

        tile = (8, LANES)
        self(kernel, scalars, [], [], [whole(tile)], [shaped(tile, F32)], name="pause", micros=30.0)


def nn(a, b):
    return lax.dot_general(a, b, (((1,), (0,)), ((), ())), preferred_element_type=F32)


def nt(a, b):
    return lax.dot_general(a, b, (((1,), (1,)), ((), ())), preferred_element_type=F32)


def tn(a, b):
    return lax.dot_general(a, b, (((0,), (0,)), ((), ())), preferred_element_type=F32)


def colsum(a):
    return jnp.sum(a, axis=0, keepdims=True)


def rowmean(a):
    return jnp.mean(a, axis=-1, keepdims=True)


def gelu_pair(u):
    den = 1.0 + ERFC_SLOPE * jnp.abs(u)
    t = pl.reciprocal(den, approx=True)
    t = t * (2.0 - den * t)
    poly = ERFC_POLY[-1]
    for c in ERFC_POLY[-2::-1]:
        poly = poly * t + c
    bell = jnp.exp(-0.5 * (u * u))
    tail = bell * (poly * t)
    cdf = jnp.where(u >= 0, 1.0 - tail, tail)
    return u * cdf, cdf + (u * bell) * INV_SQRT_2PI


def length_of(s_ref, sentence):
    return s_ref[3 + s_ref[2] + sentence]


def attend_sentence(length, x, weights, bq, bv, qkv_ref, c_ref, lse_ref):
    rows = x.shape[0]
    width = c_ref.shape[1]
    both = nn(x, jnp.concatenate(weights, axis=1))
    qkv_ref[:, :width] = (both[:, :width] + bq).astype(BF16)
    qkv_ref[:, width : 2 * width] = both[:, width : 2 * width].astype(BF16)
    qkv_ref[:, 2 * width :] = (both[:, 2 * width :] + bv).astype(BF16)
    low = lax.broadcasted_iota(jnp.int32, (rows, LANES), 1) < HD
    live = lax.broadcasted_iota(jnp.int32, (rows, LANES), 0) < length
    bias = jnp.where(live, 0.0, MASKED).astype(F32)
    zero = jnp.zeros((rows, LANES), BF16)
    for p in range(width // LANES):
        at = LANES * p
        q = qkv_ref[:, at : at + LANES] * 0.125
        k = qkv_ref[:, width + at : width + at + LANES]
        v = qkv_ref[:, 2 * width + at : 2 * width + at + LANES]
        vt = v.T
        outs = []
        for h in range(2):
            km = jnp.where(low, k, zero) if h == 0 else jnp.where(low, zero, k)
            scores = nt(km, q)
            parts, tops, sums = [], [], []
            for j in range(rows // LANES):
                piece = scores[:, LANES * j : LANES * j + LANES] + bias
                top = jnp.max(piece, axis=0, keepdims=True)
                e = jnp.exp(piece - top)
                parts.append(e.astype(BF16))
                tops.append(top)
                sums.append(colsum(e))
            top = jnp.concatenate(tops, axis=1)
            total = jnp.concatenate(sums, axis=1)
            ct = nn(vt[HD * h : HD * h + HD], jnp.concatenate(parts, axis=1))
            outs.append(ct / total)
            lse_ref[0, 2 * p + h : 2 * p + h + 1, :] = top + jnp.log(total)
        c_ref[:, at : at + LANES] = jnp.concatenate(outs, axis=0).T.astype(BF16)


def attn_own_kernel(s_ref, x_ref, w_ref, b_ref, qkv_ref, c_ref, lse_ref):
    weights = [w_ref[c] for c in range(3)]
    length = length_of(s_ref, pl.program_id(0))
    attend_sentence(
        length, x_ref[...], weights, b_ref[0:1, :], b_ref[1:2, :], qkv_ref, c_ref, lse_ref
    )


def attn_other_kernel(s_ref, x_ref, w0, w1, b_ref, qkv_ref, c_ref, lse_ref, w_ref, *, at):
    @pl.when(pl.program_id(0) == 0)
    def _():
        for s, ref in enumerate((w0, w1)):
            for c in range(3):
                w_ref[c, bit(s_ref[0], 0) ^ s] = ref[c]

    shape = w_ref.shape
    weights = [w_ref[c].reshape(shape[1] * shape[2], shape[3]) for c in range(3)]
    length = length_of(s_ref, pl.program_id(0))
    cols = slice(at, at + shape[3])
    attend_sentence(
        length, x_ref[...], weights, b_ref[0:1, cols], b_ref[1:2, cols], qkv_ref, c_ref, lse_ref
    )


def attn_pack_kernel(s_ref, x_ref, p0, p1, b_ref, qkv_ref, c_ref, lse_ref, w_ref, out_ref, *, at):
    _, _, half, width = w_ref.shape

    @pl.when(pl.program_id(0) == 0)
    def _():
        rows, cols = out_ref.shape[1:]
        for s, ref in enumerate((p0, p1)):
            place = bit(s_ref[0], 0) ^ s
            for c in range(3):
                w_ref[c, place] = ref[c * half : (c + 1) * half, :]
            for k in range(cols // width):
                begin = 3 * half + k * rows
                out_ref[place, :, k * width : (k + 1) * width] = ref[begin : begin + rows, :]

    weights = [w_ref[c].reshape(2 * half, width) for c in range(3)]
    length = length_of(s_ref, pl.program_id(0))
    cols = slice(at, at + width)
    attend_sentence(
        length, x_ref[...], weights, b_ref[0:1, cols], b_ref[1:2, cols], qkv_ref, c_ref, lse_ref
    )


def by_rows(block, cols):
    return pl.BlockSpec((block, cols), lambda i, *_: (i, 0))


def attn_forward(chain, scalars, x, weights, bias, at=0, out_rows=0):
    tokens, model = x.shape
    width = weights[0].shape[-1]
    sents = tokens // LEN
    out_specs = [
        by_rows(LEN, 3 * width),
        by_rows(LEN, width),
        pl.BlockSpec((1, width // HD, LEN), lambda s, l: (s, 0, 0)),
    ]
    out_shape = [
        shaped((tokens, 3 * width)),
        shaped((tokens, width)),
        shaped((sents, width // HD, LEN), F32),
    ]
    own = len(weights) == 1
    extra = [] if own else [(3, 2, model // 2, width)] + ([(2, out_rows // 2, model)] if out_rows else [])
    out_specs += [whole(full) for full in extra]
    out_shape += [shaped(full) for full in extra]
    kernel = attn_pack_kernel if out_rows else attn_other_kernel
    return chain(
        attn_own_kernel if own else functools.partial(kernel, at=at),
        scalars,
        [x, *weights, bias],
        [by_rows(LEN, model)] + [once(w.shape) for w in weights] + [whole(bias.shape)],
        out_specs,
        out_shape,
        grid=(sents,),
        name="attn_fwd",
        micros=8.8,
        vmem=18,
    )


def attn_back_kernel(s_ref, qkv_ref, do_ref, lse_ref, grad_ref, sum_ref):
    s = pl.program_id(0)
    length = length_of(s_ref, s)
    rows, width = do_ref.shape
    low = lax.broadcasted_iota(jnp.int32, (rows, LANES), 1) < HD
    live = lax.broadcasted_iota(jnp.int32, (rows, LANES), 0) < length
    bias = jnp.where(live, 0.0, MASKED).astype(F32)
    zero = jnp.zeros((rows, LANES), BF16)

    @pl.when(s == 0)
    def _():
        sum_ref[...] = jnp.zeros_like(sum_ref)

    for p in range(width // LANES):
        at = LANES * p
        q = qkv_ref[:, at : at + LANES] * 0.125
        k = qkv_ref[:, width + at : width + at + LANES]
        v = qkv_ref[:, 2 * width + at : 2 * width + at + LANES]
        do = do_ref[:, at : at + LANES]
        kt = k.T
        dqs, dks, dvs = [], [], []
        for h in range(2):
            km = jnp.where(low, k, zero) if h == 0 else jnp.where(low, zero, k)
            vm = jnp.where(low, v, zero) if h == 0 else jnp.where(low, zero, v)
            lse = lse_ref[0, 2 * p + h : 2 * p + h + 1, :]
            scores = nt(km, q)
            dprob = nt(vm, do)
            probs, dscores = [], []
            for j in range(rows // LANES):
                cols = slice(LANES * j, LANES * j + LANES)
                e = jnp.exp(scores[:, cols] + bias - lse[:, cols])
                probs.append(e.astype(BF16))
                dp = dprob[:, cols]
                dscores.append((e * (dp - colsum(e * dp))).astype(BF16))
            prob = jnp.concatenate(probs, axis=1)
            dscore = jnp.concatenate(dscores, axis=1)
            dvs.append(nn(prob, do))
            dks.append(nn(dscore, q))
            dqs.append(nn(kt[HD * h : HD * h + HD], dscore))
        dq = (jnp.concatenate(dqs, axis=0).T * 0.125).astype(BF16)
        dk = jnp.where(low, dks[0], dks[1]).astype(BF16)
        dv = jnp.where(low, dvs[0], dvs[1]).astype(BF16)
        grad_ref[:, at : at + LANES] = dq
        grad_ref[:, width + at : width + at + LANES] = dk
        grad_ref[:, 2 * width + at : 2 * width + at + LANES] = dv
        sum_ref[0:1, at : at + LANES] += colsum(dq.astype(F32))
        sum_ref[1:2, at : at + LANES] += colsum(dv.astype(F32))


def attn_backward(chain, scalars, qkv, do, lse):
    tokens, width = do.shape
    return chain(
        attn_back_kernel,
        scalars,
        [qkv, do, lse],
        [
            by_rows(LEN, 3 * width),
            by_rows(LEN, width),
            pl.BlockSpec((1, width // HD, LEN), lambda s, l: (s, 0, 0)),
        ],
        [by_rows(LEN, 3 * width), whole((2, width))],
        [shaped((tokens, 3 * width)), shaped((2, width), F32)],
        grid=(tokens // LEN,),
        name="attn_bwd",
        micros=12.6,
        vmem=18,
    )


def across(ref):
    return ref[...].reshape(1, ref.shape[0])


def normalize(r):
    center = r - rowmean(r)
    inverse = lax.rsqrt(rowmean(center * center) + EPS_NORM)
    return center * inverse, inverse


def project_kernel(s_ref, x_ref, *refs, count):
    c_refs, refs = refs[:count], refs[count:]
    w_own, other, bias_ref, gain_ref, shift_ref, h_ref, low_ref, n_ref, inv_ref = refs
    attended = nn(c_refs[0][...], w_own[...]) + across(bias_ref)
    at = 0
    for ref in c_refs[1:]:
        width = ref.shape[1]
        attended = attended + nn(ref[...], other[at : at + width, :])
        at += width
    normal, inverse = normalize(x_ref[...].astype(F32) + attended)
    h = normal * across(gain_ref) + across(shift_ref)
    h_ref[...] = h
    low_ref[...] = h.astype(BF16)
    n_ref[...] = normal.astype(BF16)
    inv_ref[...] = inverse


def project_forward(chain, scalars, x, contexts, w_own, w_oth, vecs):
    tokens, model = x.shape
    block = 512
    return chain(
        functools.partial(project_kernel, count=len(contexts)),
        scalars,
        [x, *contexts, w_own, w_oth, *vecs],
        [by_rows(block, model)]
        + [by_rows(block, c.shape[1]) for c in contexts]
        + [once(w_own.shape), once(w_oth.shape)]
        + [whole(v.shape) for v in vecs],
        [by_rows(block, model)] * 3 + [by_rows(block, 1)],
        [
            shaped((tokens, model), F32),
            shaped((tokens, model)),
            shaped((tokens, model)),
            shaped((tokens, 1), F32),
        ],
        grid=(tokens // block,),
        name="project_fwd",
        micros=3.7,
        vmem=18,
    )


def feed_own_kernel(s_ref, h_ref, wu_ref, bu_ref, wd_ref, g_ref, gp_ref, f_ref):
    h = h_ref[...]
    chunk = wu_ref.shape[1] // 3
    bu = across(bu_ref)
    total = None
    for j in range(3):
        cols = slice(chunk * j, chunk * j + chunk)
        act, slope = gelu_pair(nn(h, wu_ref[:, cols]) + bu[:, cols])
        act = act.astype(BF16)
        g_ref[:, cols] = act
        gp_ref[:, cols] = slope.astype(BF16)
        part = nn(act, wd_ref[cols, :])
        total = part if total is None else total + part
    f_ref[...] = total


def feed_own(chain, scalars, h, wu, bu, wd):
    tokens, model = h.shape
    units = wu.shape[1]
    block = 256
    return chain(
        feed_own_kernel,
        scalars,
        [h, wu, bu, wd],
        [by_rows(block, model), once(wu.shape), whole(bu.shape), once(wd.shape)],
        [by_rows(block, units), by_rows(block, units), by_rows(block, model)],
        [shaped((tokens, units)), shaped((tokens, units)), shaped((tokens, model), F32)],
        grid=(tokens // block,),
        name="feed_own",
        micros=14.5,
        vmem=15,
    )


def feed_up_kernel(s_ref, h_ref, near_ref, far_ref, bias_ref, *refs, second):
    g_ref, gp_ref, wu_ref = refs[-3:]
    part = near_ref.shape[1]
    core = bit(s_ref[0], 0)

    @pl.when(pl.program_id(0) == 0)
    def _():
        wu_ref[:, pl.ds(pl.multiple_of(core * part, LANES), part)] = near_ref[...]
        wu_ref[:, pl.ds(pl.multiple_of((1 - core) * part, LANES), part)] = far_ref[...]

    row = 2 + 2 * (bit(s_ref[0], 1) ^ second)
    bu = jnp.concatenate([bias_ref[pl.ds(row + i, 1), :] for i in range(2)], axis=1)
    act, slope = gelu_pair(nn(h_ref[...], wu_ref[...]) + bu)
    g_ref[...] = act.astype(BF16)
    gp_ref[...] = slope.astype(BF16)


def feed_up(chain, scalars, h, near, far, bias, kept=()):
    tokens, model = h.shape
    half = 2 * near.shape[1]
    block = 256
    second = 1 if kept else 0
    here = lambda s: bit(s[0], 1) ^ second
    columns = pl.BlockSpec((block, half), lambda i, s: (i, here(s)))
    return chain(
        functools.partial(feed_up_kernel, second=second),
        scalars,
        [h, near, far, bias, *kept],
        [by_rows(block, model), once(near.shape), once(far.shape), whole(bias.shape)]
        + [pl.BlockSpec(memory_space=pl.ANY)] * len(kept),
        [columns, columns, pl.BlockSpec((model, half), lambda i, s: (0, here(s)))],
        [shaped((tokens, 2 * half)), shaped((tokens, 2 * half)), shaped((model, 2 * half))],
        grid=(tokens // block,),
        name="feed_up",
        micros=60.0,
        vmem=15,
        aliases={5 + i: i for i in range(len(kept))},
    )


def feed_down_kernel(
    s_ref, g_ref, h_ref, f_ref, d0, d1, bias_ref, gain_ref, shift_ref,
    out_ref, n_ref, inv_ref, pool_ref, wd_ref,
):
    i = pl.program_id(0)

    @pl.when(i == 0)
    def _():
        for s, down in enumerate((d0, d1)):
            wd_ref[bit(s_ref[0], 0) ^ s] = down[...]
        pool_ref[...] = jnp.zeros_like(pool_ref)

    shape = wd_ref.shape
    down = wd_ref[...].reshape(shape[0] * shape[1], shape[2])
    total = nn(g_ref[...], down)
    normal, inverse = normalize(h_ref[...] + (f_ref[...] + total + across(bias_ref)))
    y = normal * across(gain_ref) + across(shift_ref)
    out_ref[...] = y.astype(BF16)
    n_ref[...] = normal.astype(BF16)
    inv_ref[...] = inverse
    block = y.shape[0]
    per = LEN // block
    sent = i // per
    length = length_of(s_ref, sent)
    first = (i - sent * per) * block
    live = lax.broadcasted_iota(jnp.int32, y.shape, 0) + first < length
    pool_ref[pl.ds(sent, 1), :] += colsum(jnp.where(live, y, 0.0)) / length.astype(F32)


def feed_down(chain, scalars, g, h, f, down, vecs):
    tokens, model = h.shape
    units = g.shape[1]
    block = 256
    sents = tokens // LEN
    full = (2,) + down[0].shape
    return chain(
        feed_down_kernel,
        scalars,
        [g, h, f, *down, *vecs],
        [by_rows(block, units), by_rows(block, model), by_rows(block, model)]
        + [once(w.shape) for w in down]
        + [whole(v.shape) for v in vecs],
        [by_rows(block, model), by_rows(block, model), by_rows(block, 1), whole((sents, model)), whole(full)],
        [
            shaped((tokens, model)),
            shaped((tokens, model)),
            shaped((tokens, 1), F32),
            shaped((sents, model), F32),
            shaped(full),
        ],
        grid=(tokens // block,),
        name="feed_down",
        micros=9.0,
        vmem=15,
    )


def exact(a, b, dims):
    return lax.dot_general(
        a, b, (dims, ((), ())), precision=lax.Precision.HIGHEST, preferred_element_type=F32
    )


def loss_kernel(s_ref, *refs):
    *slot_refs, id_ref, loss_ref, cot_ref, pool_ref, grad_ref = refs
    local = cot_ref.shape[0]
    rank = s_ref[1]
    part = slot_refs[0].shape[0]
    count = part * len(slot_refs)
    for s in range(count // local):
        for i in range(local):
            at = local * s + i
            row = slot_refs[at // part][at % part : at % part + 1, :]
            pool_ref[pl.ds((rank ^ s) * local + i, 1), :] = row
    pooled = pool_ref[...]
    scale = lax.rsqrt(jnp.sum(pooled * pooled, axis=-1, keepdims=True) + EPS_UNIT)
    unit = pooled * scale
    score = SOFTMAX_TEMP * exact(unit, unit, ((1,), (1,)))
    itself = lax.broadcasted_iota(jnp.int32, score.shape, 0) == lax.broadcasted_iota(
        jnp.int32, score.shape, 1
    )
    others = jnp.where(itself, MASKED, score)
    top = jnp.max(others, axis=1, keepdims=True)
    power = jnp.exp(others - top)
    total = jnp.sum(power, axis=1, keepdims=True)
    ids = jnp.broadcast_to(across(id_ref).astype(F32), score.shape)
    match = jnp.logical_and(ids == ids.T, jnp.logical_not(itself)).astype(F32)
    number = jnp.sum(match, axis=1, keepdims=True)
    matched = jnp.sum(match * score, axis=1, keepdims=True) / number
    terms = top + jnp.log(total) - matched
    loss_ref[...] = jnp.sum(terms, axis=0, keepdims=True) / count
    dscore = float(LEN) * (power / total - match / number)
    dunit = SOFTMAX_TEMP * (exact(dscore, unit, ((1,), (0,))) + exact(dscore, unit, ((0,), (0,))))
    grad_ref[...] = scale * (dunit - unit * jnp.sum(unit * dunit, axis=-1, keepdims=True))
    for i in range(local):
        own = grad_ref[pl.ds(rank * local + i, 1), :]
        cot_ref[i : i + 1, :] = own / length_of(s_ref, i).astype(F32)


def loss_call(chain, scalars, slots, group_ids, local):
    part, model = slots[0].shape
    count = part * len(slots)
    return chain(
        loss_kernel,
        scalars,
        [*slots, group_ids],
        [whole((part, model))] * len(slots) + [whole((count,))],
        [whole((1, 1)), whole((local, model))],
        [shaped((1, 1), F32), shaped((local, model), F32)],
        scratch=[pltpu.VMEM((count, model), F32)] * 2,
        name="loss",
        micros=3.8,
    )


def norm_back(upstream, normal, inverse, gain):
    scaled = upstream * gain
    return inverse * (scaled - rowmean(scaled) - normal * rowmean(scaled * normal))


def norm_two_kernel(s_ref, cot_ref, n_ref, inv_ref, gain_ref, pool_ref, df_ref, sum_ref):
    s = pl.program_id(0)
    normal = n_ref[...].astype(F32)
    live = lax.broadcasted_iota(jnp.int32, normal.shape, 0) < length_of(s_ref, s)
    up = cot_ref[...].astype(F32) + jnp.where(live, pool_ref[pl.ds(s, 1), :], 0.0)
    df = norm_back(up, normal, inv_ref[...], across(gain_ref)).astype(BF16)
    df_ref[...] = df

    @pl.when(s == 0)
    def _():
        sum_ref[...] = jnp.zeros_like(sum_ref)

    sum_ref[0:1, :] += colsum(df.astype(F32))
    sum_ref[1:2, :] += colsum(up * normal)
    sum_ref[2:3, :] += colsum(up)


def norm_two_backward(chain, scalars, cot, normal, inverse, gain, pool_cot):
    tokens, model = cot.shape
    return chain(
        norm_two_kernel,
        scalars,
        [cot, normal, inverse, gain, pool_cot],
        [by_rows(LEN, model), by_rows(LEN, model), by_rows(LEN, 1), whole(gain.shape), whole(pool_cot.shape)],
        [by_rows(LEN, model), whole((3, model))],
        [shaped((tokens, model)), shaped((3, model), F32)],
        grid=(tokens // LEN,),
        name="norm_two_bwd",
        micros=5.4,
    )


def unit_back_kernel(s_ref, df_ref, gp_ref, wd_ref, du_ref, sum_ref):
    @pl.when(pl.program_id(0) == 0)
    def _():
        sum_ref[...] = jnp.zeros_like(sum_ref)

    df = df_ref[...]
    chunk = wd_ref.shape[0] // 3
    for j in range(3):
        cols = slice(chunk * j, chunk * j + chunk)
        du = (nt(df, wd_ref[cols, :]) * gp_ref[:, cols].astype(F32)).astype(BF16)
        du_ref[:, cols] = du
        sum_ref[:, cols] += colsum(du.astype(F32))


def unit_backward(chain, scalars, df, gp, wd):
    tokens, model = df.shape
    units = gp.shape[1]
    block = 512
    return chain(
        unit_back_kernel,
        scalars,
        [df, gp, wd],
        [by_rows(block, model), by_rows(block, units), once(wd.shape)],
        [by_rows(block, units), whole((1, units))],
        [shaped((tokens, units)), shaped((1, units), F32)],
        grid=(tokens // block,),
        name="unit_bwd",
        micros=60.0,
        vmem=18,
    )


def middle_kernel(
    s_ref, df_ref, du_own, du_oth, wu_own, wu_oth, n_ref, inv_ref, gain_ref, wo_own, wo_oth,
    da_ref, sum_ref, dc_own, *dc_oth,
):
    @pl.when(pl.program_id(0) == 0)
    def _():
        sum_ref[...] = jnp.zeros_like(sum_ref)

    total = df_ref[...].astype(F32) + nt(du_oth[...], wu_oth[...]) + nt(du_own[...], wu_own[...])
    normal = n_ref[...].astype(F32)
    da = norm_back(total, normal, inv_ref[...], across(gain_ref)).astype(BF16)
    da_ref[...] = da
    dc_own[...] = nt(da, wo_own[...]).astype(BF16)
    at = 0
    for ref in dc_oth:
        width = ref.shape[1]
        ref[...] = nt(da, wo_oth[at : at + width, :]).astype(BF16)
        at += width
    sum_ref[0:1, :] += colsum(total * normal)
    sum_ref[1:2, :] += colsum(total)
    sum_ref[2:3, :] += colsum(da.astype(F32))


def middle_backward(
    chain, scalars, df, du_own, du_oth, wu_own, wu_oth, normal, inverse, gain, wo_own, wo_oth, widths
):
    tokens, model = df.shape
    units = wu_own.shape[1]
    block = 256
    return chain(
        middle_kernel,
        scalars,
        [df, du_own, du_oth, wu_own, wu_oth, normal, inverse, gain, wo_own, wo_oth],
        [by_rows(block, model), by_rows(block, units), by_rows(block, units)]
        + [once(wu_own.shape), once(wu_oth.shape), by_rows(block, model), by_rows(block, 1)]
        + [whole(gain.shape), once(wo_own.shape), once(wo_oth.shape)],
        [by_rows(block, model), whole((3, model))] + [by_rows(block, w) for w in widths],
        [shaped((tokens, model)), shaped((3, model), F32)] + [shaped((tokens, w)) for w in widths],
        grid=(tokens // block,),
        name="middle_bwd",
        micros=12.0,
        vmem=18,
    )


def bit(value, at):
    return (value >> at) & 1


def split_store(d, even, odd, keep_ref, send_ref, at):
    flip = bit(d, 0) == 0
    keep_ref[at] = jnp.where(flip, even, odd).astype(BF16)
    send_ref[at] = jnp.where(flip, odd, even).astype(BF16)


def dense_grad_kernel(d_ref, a_ref, b_ref, keep_ref, send_ref):
    d = d_ref[0]
    grad = tn(a_ref[...], b_ref[...])
    step = keep_ref.shape[3]
    for x in range(2):
        for z in range(2):
            at = (4 * z + 2 * x) * step
            split_store(
                d, grad[at : at + step], grad[at + step : at + 2 * step], keep_ref, send_ref,
                (x ^ bit(d, 1), z ^ bit(d, 2), 0),
            )


def dense_grad(chain, scalars, a, b, cut_left):
    tokens = a.shape[0]
    left = a.shape[1] // (2 if cut_left else 1)
    right = b.shape[1] // (1 if cut_left else 2)
    step = left // 8
    block = pl.BlockSpec((2, 2, 1, step, right), lambda i, s: (0, 0, i ^ bit(s[0], 3), 0, 0))
    return chain(
        dense_grad_kernel,
        scalars,
        [a, b],
        [
            pl.BlockSpec((tokens, left), lambda i, s: (0, i)) if cut_left else once(a.shape),
            once(b.shape) if cut_left else pl.BlockSpec((tokens, right), lambda i, s: (0, i)),
        ],
        [block, block],
        [shaped((2, 2, 2, step, right))] * 2,
        grid=(2,),
        name="dense_grad",
        micros=60.0,
        vmem=15,
    )


def heads_grad_kernel(d_ref, x_ref, da_ref, two_ref, one_ref, unit_ref, *refs):
    *refs, keep_ref, send_ref = refs
    count = len(refs) // 3
    c_refs, dqkv_refs, bias_refs = refs[:count], refs[count : 2 * count], refs[2 * count :]
    d = d_ref[0]
    bias = jnp.concatenate([ref[...] for ref in bias_refs], axis=1)
    width = bias.shape[1]
    out = jnp.concatenate([tn(ref[...], da_ref[...]) for ref in c_refs], axis=0)
    projs = [tn(x_ref[...], ref[...]) for ref in dqkv_refs]
    proj = jnp.concatenate(
        [p[:, c * (p.shape[1] // 3) : (c + 1) * (p.shape[1] // 3)] for c in range(3) for p in projs], axis=1
    )
    step = proj.shape[0] // 16
    small = [ref[i : i + 1, at : at + width] for ref in (two_ref, one_ref) for i in range(3) for at in (0, width)]
    small += [bias[0:1, :], bias[1:2, :]]
    small += [unit_ref[:, at : at + width] for at in range(0, unit_ref.shape[1], width)]
    small += [jnp.zeros((1, width), F32)] * (32 - len(small))
    rest = jnp.zeros((14, width), F32)

    def block(b):
        row, col = (b & 7) * step, (b >> 3) * width
        pieces = [out[row : row + step, col : col + width]]
        pieces += [proj[b * step : b * step + step, c * width : c * width + width] for c in range(3)]
        return jnp.concatenate(pieces + [small[b], small[16 + b], rest], axis=0)

    for x in range(2):
        for z in range(2):
            for w in range(2):
                b = 8 * w + 4 * z + 2 * x
                split_store(
                    d, block(b), block(b + 1), keep_ref, send_ref,
                    (x ^ bit(d, 1), z ^ bit(d, 2), w ^ bit(d, 3)),
                )


def heads_grad(chain, scalars, x, da, sums, contexts, dqkvs, biases):
    width = sum(b.shape[1] for b in biases)
    full = (2, 2, 2, width // 2 + 16, width)
    inputs = [x, da, *sums, *contexts, *dqkvs, *biases]
    return chain(
        heads_grad_kernel,
        scalars,
        inputs,
        [once(a.shape) for a in inputs],
        [whole(full), whole(full)],
        [shaped(full)] * 2,
        name="heads_grad",
        micros=60.0,
        vmem=21,
    )


def input_grad_kernel(s_ref, da_ref, *refs):
    *refs, out_ref = refs
    total = da_ref[...].astype(F32)
    for grad, w in zip(refs[: len(refs) // 2], refs[len(refs) // 2 :], strict=True):
        total = total + nt(grad[...], jnp.concatenate([w[c] for c in range(3)], axis=1))
    out_ref[...] = total


def input_grad(chain, scalars, da, grads, weights):
    tokens, model = da.shape
    block = 512
    return chain(
        input_grad_kernel,
        scalars,
        [da, *grads, *weights],
        [by_rows(block, model)] + [by_rows(block, g.shape[1]) for g in grads] + [once(w.shape) for w in weights],
        [by_rows(block, model)],
        [shaped((tokens, model), F32)],
        grid=(tokens // block,),
        name="input_grad",
        token=True,
        micros=60.0,
        vmem=18,
    )[0]


def place_kernel(s_ref, a0, a1, b0, b1, *out_refs, kind):
    d = s_ref[0]
    half = pl.program_id(0)
    flip = bit(d, 0) == 0
    for x, (near_ref, far_ref) in enumerate(((a0, b0), (a1, b1))):
        for z in range(2):
            near, far = near_ref[z, 0].astype(F32), far_ref[z, 0].astype(F32)
            low = (x ^ bit(d, 1)) + 2 * (z ^ bit(d, 2))
            for side, rows in enumerate((jnp.where(flip, near, far), jnp.where(flip, far, near))):
                if kind != "heads":
                    step = rows.shape[0]
                    out_refs[0][low, side * step : (side + 1) * step] = rows
                    continue
                out_ref, proj_ref, *vec_refs, unit_ref, small_ref = out_refs
                step = out_ref.shape[1] // 2
                out_ref[low, side * step : (side + 1) * step] = rows[:step]
                for c in range(3):
                    proj_ref[c, low, side * step : (side + 1) * step] = rows[(c + 1) * step : (c + 2) * step]
                b = 2 * (low + 4 * (half ^ bit(d, 3))) + side
                small_ref[pl.ds(b, 1), :] = rows[4 * step : 4 * step + 1]
                small_ref[pl.ds(16 + b, 1), :] = rows[4 * step + 1 : 4 * step + 2]
    if kind != "heads":
        return

    @pl.when(half == 1)
    def _():
        line = lambda at, count: jnp.concatenate([small_ref[i : i + 1, :] for i in range(at, at + count)], axis=1)
        for i, ref in enumerate(vec_refs[:6]):
            ref[...] = line(2 * i, 2).reshape(ref.shape[0])
        vec_refs[6][...] = small_ref[12:14, :]
        unit_ref[...] = line(14, unit_ref.shape[0] // small_ref.shape[1]).reshape(unit_ref.shape[0])


def place(chain, scalars, pieces, kind, units):
    step, cols = pieces[0].shape[2:]
    block = pl.BlockSpec((2, 1, step, cols), lambda w, s: (0, w, 0, 0))
    high = lambda w, s: w ^ bit(s[0], 3)
    scratch = []
    if kind == "down":
        shapes = [(8, 2 * step, cols)]
        specs = [pl.BlockSpec((4, 2 * step, cols), lambda w, s: (high(w, s), 0, 0))]
    elif kind == "up":
        shapes = [(4, 2 * step, 2 * cols)]
        specs = [pl.BlockSpec((4, 2 * step, cols), lambda w, s: (0, 0, high(w, s)))]
    else:
        part = (step - 16) // 4
        shapes = [(4, 2 * part, 2 * cols), (3, 8, 2 * part, cols)]
        specs = [
            pl.BlockSpec((4, 2 * part, cols), lambda w, s: (0, 0, high(w, s))),
            pl.BlockSpec((3, 4, 2 * part, cols), lambda w, s: (0, high(w, s), 0, 0)),
        ]
        vectors = [(2 * cols,)] * 6 + [(2, cols), (units,)]
        shapes += vectors
        specs += [whole(v) for v in vectors]
        scratch = [pltpu.VMEM((32, cols), F32)]
    return chain(
        functools.partial(place_kernel, kind=kind),
        scalars,
        pieces,
        [block] * 4,
        specs,
        [shaped(s, F32) for s in shapes],
        grid=(2,),
        scratch=scratch,
        name="place",
        token=True,
        micros=4.0,
        vmem=18,
    )


def swap(x, axis, mask):
    size = lax.axis_size(axis)
    return lax.ppermute(x, axis, [(i, i ^ mask) for i in range(size)])


def swap_all(x, mask):
    size = lax.axis_size("dp") * lax.axis_size("tensor")
    return lax.ppermute(x, ("dp", "tensor"), [(i, i ^ mask) for i in range(size)])


def levels():
    return lax.axis_size("dp").bit_length() - 1


def flip_kernel(s_ref, a_ref, b_ref, out_ref):
    for i in range(2):
        out_ref[i] = (a_ref[i].astype(F32) + b_ref[1 - i].astype(F32)).astype(BF16)


def add_flipped(chain, scalars, a, b):
    return chain(
        flip_kernel,
        scalars,
        [a, b],
        [whole(a.shape)] * 2,
        [whole(a.shape)],
        [shaped(a.shape)],
        name="add",
        micros=2.0,
    )[0]


def sum_kernel(s_ref, *refs, count, early):
    total = refs[0][...].astype(F32) + refs[1][...].astype(F32)
    if early:
        total = total.astype(BF16).astype(F32)
    for ref in refs[2:count]:
        total = total + ref[...].astype(F32)
    total = total.astype(BF16)
    outs = refs[count:]
    if len(outs) == 1:
        outs[0][...] = total
        return
    for i, out in enumerate(outs):
        out[...] = total[i]


def add(chain, scalars, terms, split=1, early=False):
    shape = terms[0].shape
    outs = [shape] if split == 1 else [shape[1:]] * split
    return chain(
        functools.partial(sum_kernel, count=len(terms), early=early),
        scalars,
        terms,
        [whole(shape)] * len(terms),
        [whole(o) for o in outs],
        [shaped(o) for o in outs],
        name="add",
        micros=2.0,
    )


def join_kernel(s_ref, *refs):
    for i, ref in enumerate(refs[:-1]):
        refs[-1][i] = ref[...]


def join(chain, scalars, parts):
    shape = (len(parts),) + parts[0].shape
    return chain(
        join_kernel,
        scalars,
        parts,
        [whole(p.shape) for p in parts],
        [whole(shape)],
        [shaped(shape)],
        name="join",
        micros=1.5,
    )[0]


class Reduction:
    def __init__(self, chain, scalars):
        self.chain, self.scalars = chain, scalars

    def add(self, terms, split=1, early=False):
        return add(self.chain, self.scalars, terms, split, early)

    def send(self, x, axis, mask):
        return self.chain.send(x, axis, mask)

    def receive(self, sent):
        return self.chain.receive(self.scalars, sent)

    def other(self, keep, send):
        self.keep_oth, self.got_oth = keep, self.send(send, "dp", 1)

    def own(self, keep, send):
        self.keep_own, self.got_own = keep, self.send(send, "dp", 1)

    def across(self):
        (total,) = self.add([self.keep_oth, self.receive(self.got_oth)])
        self.got_y = self.send(total, "tensor", 1)

    def along_x(self):
        got = [self.receive(self.got_own), self.receive(self.got_y)]
        self.keep, send = self.add([self.keep_own, *got], 2, True)
        self.got = self.send(send, "dp", 2)

    def along_z(self):
        shape = self.keep.shape
        flat = (4,) + shape[2:]
        got = self.receive(self.got)
        self.keep, *send = self.add([self.keep.reshape(flat), got.reshape(flat)], 4)
        self.got = [self.send(x, "dp", m) for x, m in zip(send, (8, 4, 12), strict=True)]

    def back_z(self):
        (total,) = self.add([self.keep, *(self.receive(g) for g in self.got)])
        for at in range(4, levels()):
            got = self.receive(self.send(total, "dp", 1 << at))
            (total,) = self.add([total, got])
        self.total = total
        self.got = [self.send(total, "dp", m) for m in (8, 4, 12)]

    def back_x_direct(self):
        near = join(self.chain, self.scalars, [self.total, *(self.receive(g) for g in self.got)])
        self.near = near.reshape((2, 2) + near.shape[1:])
        self.got = self.send(self.near, "dp", 2)
        self.near_far = self.send(self.near, "dp", 1)

    def along_z0(self):
        self.keep, send = self.add([self.keep, self.receive(self.got)], 2)
        self.got = self.send(send, "dp", 4)

    def turn(self):
        (self.total,) = self.add([self.keep, self.receive(self.got)])
        for at in range(4, levels()):
            got = self.receive(self.send(self.total, "dp", 1 << at))
            (self.total,) = self.add([self.total, got])
        self.got = self.send(self.total, "dp", 8)

    def back_z0(self):
        self.total = add_flipped(self.chain, self.scalars, self.total, self.receive(self.got))
        self.got = self.send(self.total, "dp", 4)

    def back_x(self):
        self.near = join(self.chain, self.scalars, [self.total, self.receive(self.got)])
        self.got = self.send(self.near, "dp", 2)
        self.near_far = self.send(self.near, "dp", 1)

    def back_core(self):
        self.next = self.chain.gate(self.scalars, self.receive(self.got))
        self.next_far = self.send(self.next, "dp", 1)

    def place(self, kind, units=0):
        pieces = [self.near, self.next, self.receive(self.near_far), self.receive(self.next_far)]
        return place(self.chain, self.scalars, pieces, kind, units)


def stack_rows_kernel(s_ref, *refs):
    step = refs[0].shape[0]
    for i, ref in enumerate(refs[:-1]):
        refs[-1][i * step : (i + 1) * step, :] = ref[...]


def stack_rows(chain, scalars, parts):
    shape = (len(parts) * parts[0].shape[0], parts[0].shape[1])
    return chain(
        stack_rows_kernel,
        scalars,
        parts,
        [whole(p.shape) for p in parts],
        [whole(shape)],
        [shaped(shape, F32)],
        name="stack_rows",
        micros=10.0,
    )[0]


def gather_pooled(chain, scalars, pooled):
    bits = levels() + 1
    at = 0
    while at < bits:
        step = min(1 if at == 2 else 2, bits - at)
        parts = [pooled] + [swap_all(pooled, m << at) for m in range(1, 1 << step)]
        chain.pause(scalars)
        at += step
        if at < bits:
            pooled = stack_rows(chain, scalars, parts)
    return parts


def cut_kernel(s_ref, *refs):
    count = len(refs) // 2
    for a_ref, out_ref in zip(refs[:count], refs[count:], strict=True):
        out_ref[...] = a_ref[...].reshape(out_ref.shape)


def cut(chain, scalars, *cuts):
    shapes = [tuple(b for b in block if b != 1) for _, block, _ in cuts]
    at = lambda index: lambda i, s: index(s[0] & 3)
    return chain(
        cut_kernel,
        scalars,
        [a for a, _, _ in cuts],
        [pl.BlockSpec(block, at(index)) for _, block, index in cuts],
        [whole(s) for s in shapes],
        [shaped(s, a.dtype) for s, (a, _, _) in zip(shapes, cuts, strict=True)],
        name="cut",
        micros=1.0,
    )


def cut_heads_kernel(s_ref, a_ref, out_ref):
    out_ref[...] = a_ref[:, 0, :, : out_ref.shape[2]]


def cut_heads(chain, scalars, a, width):
    _, _, part, full = a.shape
    shape = (3, part, width)
    return chain(
        cut_heads_kernel,
        scalars,
        [a],
        [pl.BlockSpec((3, 1, part, full), lambda i, s: (0, bit(s[0], 0), 0, 0))],
        [whole(shape)],
        [shaped(shape)],
        name="cut",
        micros=1.0,
    )[0]


def cut_pack_kernel(s_ref, a_ref, w_ref, bias_ref, unit_ref, out_ref, small_ref):
    part = a_ref.shape[2]
    width = out_ref.shape[1]
    rows, cols = w_ref.shape[1:]
    for c in range(3):
        out_ref[c * part : (c + 1) * part, :] = a_ref[c, 0, :, a_ref.shape[3] - width :]
    for k in range(cols // width):
        begin = 3 * part + k * rows
        out_ref[begin : begin + rows, :] = w_ref[0, :, k * width : (k + 1) * width]
    full = bias_ref.shape[1]
    small_ref[0:2, :] = bias_ref[...]
    unit = across(unit_ref)
    for i in range(unit.shape[1] // full):
        small_ref[2 + i : 3 + i, :] = unit[:, i * full : (i + 1) * full]


def cut_pack(chain, scalars, a, width, w, bias, unit):
    _, _, part, full = a.shape
    _, rows, cols = w.shape
    shapes = [shaped((3 * part + rows * cols // width, width)), shaped((2 + unit.shape[0] // full, full), F32)]
    return chain(
        cut_pack_kernel,
        scalars,
        [a, w, bias, unit],
        [
            pl.BlockSpec((3, 1, part, full), lambda i, s: (0, bit(s[0], 0), 0, 0)),
            pl.BlockSpec((1, rows, cols), lambda i, s: (bit(s[0], 0), 0, 0)),
            whole(bias.shape),
            whole(unit.shape),
        ],
        [whole(s.shape) for s in shapes],
        shapes,
        name="cut",
        micros=1.0,
    )


class Gather:
    def __init__(self, chain, scalars, piece, relayed=False):
        self.chain, self.scalars, self.relayed = chain, scalars, relayed
        self.got = chain.send(piece, "tensor", 1)
        self.parts = []

    def hand_over(self):
        part = self.chain.gate(self.scalars, self.chain.receive(self.scalars, self.got))
        if self.relayed and not self.parts:
            self.got = self.chain.send(part, "dp", 2)
        self.parts += [part, self.chain.send(part, "dp", 1)]

    def slots(self):
        return [self.slot(i) for i in range(len(self.parts))]

    def slot(self, i):
        return self.parts[i] if i % 2 == 0 else self.chain.receive(self.scalars, self.parts[i])


def per_device(
    layer_input, w_qkv, bias_qv, w_out, b_out, gain_one, shift_one, w_up, b_up, w_down, b_down,
    gain_two, shift_two, out_cot, lengths, group_ids,
):
    tensor_size = lax.axis_size("tensor")
    position = lax.axis_index("tensor")
    d = lax.axis_index("dp")
    model = layer_input.shape[1]
    width = w_qkv.shape[2]
    units = w_up.shape[1]
    local = lengths.shape[0] // tensor_size
    rank = d * tensor_size + position
    scal = jnp.concatenate([jnp.stack([d, rank, position * local]).astype(jnp.int32), lengths])
    chain = Chain()

    heads_cut = w_qkv.reshape(3, 2, model // 2, width)
    lead = width // 3 * 2
    gather_lead = Gather(chain, scal, cut_heads(chain, scal, heads_cut, lead))
    qkv_own, c_own, lse_own = attn_forward(chain, scal, layer_input, [w_qkv], bias_qv)
    piece, bias = cut_pack(
        chain, scal, heads_cut, width - lead, w_out.reshape(2, width // 2, model), bias_qv, b_up
    )
    gather_pack = Gather(chain, scal, piece)
    bias_oth = swap(bias, "tensor", 1)
    part = units // 4
    piece, second = cut(
        chain,
        scal,
        (w_up, (model, part), lambda q: (0, q)),
        (w_down.reshape(2, 2 * part, model), (1, 2 * part, model), lambda q: (q & 1, 0, 0)),
    )
    gather_up = Gather(chain, scal, piece, relayed=True)
    gather_down = Gather(chain, scal, second)
    gather_lead.hand_over()
    qkv_lead, c_lead, lse_lead, wq_lead = attn_forward(chain, scal, layer_input, gather_lead.slots(), bias_oth)
    gather_pack.hand_over()
    qkv_rest, c_rest, lse_rest, wq_rest, wo_oth = attn_forward(
        chain, scal, layer_input, gather_pack.slots(), bias_oth, lead, width
    )
    wq_lead, wq_rest = (w.reshape(3, model, w.shape[3]) for w in (wq_lead, wq_rest))
    wo_oth = wo_oth.reshape(width, model)
    h1, h1_low, normal_one, inverse_one = project_forward(
        chain, scal, layer_input, [c_own, c_lead, c_rest], w_out, wo_oth, [b_out, gain_one, shift_one]
    )
    gather_up.hand_over()
    g_own, gp_own, f_own = feed_own(chain, scal, h1_low, w_up, b_up, w_down)
    gather_up.hand_over()
    near, far = gather_up.slot(0), gather_up.slot(1)
    half = feed_up(chain, scal, h1_low, near, far, bias_oth)
    gather_down.hand_over()
    near, far = gather_up.slot(2), gather_up.slot(3)
    g_oth, gp_oth, wu_oth = feed_up(chain, scal, h1_low, near, far, bias_oth, half)
    output, normal_two, inverse_two, pooled, wd_oth = feed_down(
        chain, scal, g_oth, h1, f_own, gather_down.slots(), [b_down, gain_two, shift_two]
    )
    wd_oth = wd_oth.reshape(units, model)

    loss, pool_cot = loss_call(chain, scal, gather_pooled(chain, scal, pooled), group_ids, local)

    down, up, heads = (Reduction(chain, scal) for _ in range(3))
    df, sums_two = norm_two_backward(chain, scal, out_cot, normal_two, inverse_two, gain_two, pool_cot)
    down.other(*dense_grad(chain, scal, g_oth, df, True))
    down.own(*dense_grad(chain, scal, g_own, df, True))
    down.across()
    du_oth, sums_du_oth = unit_backward(chain, scal, df, gp_oth, wd_oth)
    du_own, sums_du_own = unit_backward(chain, scal, df, gp_own, w_down)
    up.other(*dense_grad(chain, scal, h1_low, du_oth, False))
    up.own(*dense_grad(chain, scal, h1_low, du_own, False))
    up.across()
    da, sums_one, dc_own, dc_lead, dc_rest = middle_backward(
        chain, scal, df, du_own, du_oth, w_up, wu_oth, normal_one, inverse_one, gain_one, w_out, wo_oth,
        [width, lead, width - lead],
    )
    down.along_x()
    dqkv_lead, sums_lead = attn_backward(chain, scal, qkv_lead, dc_lead, lse_lead)
    dqkv_rest, sums_rest = attn_backward(chain, scal, qkv_rest, dc_rest, lse_rest)
    sums = [sums_two, sums_one, sums_du_oth]
    heads.other(
        *heads_grad(
            chain, scal, layer_input, da, sums, [c_lead, c_rest], [dqkv_lead, dqkv_rest], [sums_lead, sums_rest]
        )
    )
    down.along_z0()
    up.along_x()
    chain.pause(scal)
    heads.across()
    dqkv_own, sums_own = attn_backward(chain, scal, qkv_own, dc_own, lse_own)
    down.turn()
    up.along_z0()
    sums = [sums_two, sums_one, sums_du_own]
    heads.own(*heads_grad(chain, scal, layer_input, da, sums, [c_own], [dqkv_own], [sums_own]))
    grad_input = input_grad(
        chain, scal, da, [dqkv_own, dqkv_lead, dqkv_rest], [w_qkv, wq_lead, wq_rest]
    )
    down.back_z0()
    heads.along_x()
    up.turn()
    chain.pause(scal)
    down.back_x()
    heads.along_z0()
    chain.pause(scal)
    heads.turn()
    up.back_z0()
    chain.pause(scal)
    heads.back_z0()
    up.back_x()
    chain.pause(scal)
    down.back_core()
    (grad_w_down,) = down.place("down")
    up.back_core()
    heads.back_x()
    chain.pause(scal)
    (grad_w_up,) = up.place("up")
    heads.back_core()
    chain.pause(scal)
    grad_w_out, grad_w_qkv, *grads, grad_bias_qv, grad_b_up = heads.place("heads", units)
    grad_b_down, grad_gain_two, grad_shift_two, grad_gain_one, grad_shift_one, grad_b_out = grads
    return (
        loss.reshape(()),
        output,
        grad_input,
        grad_w_qkv.reshape(w_qkv.shape),
        grad_bias_qv,
        grad_w_out.reshape(w_out.shape),
        grad_b_out,
        grad_gain_one,
        grad_shift_one,
        grad_w_up.reshape(w_up.shape),
        grad_b_up,
        grad_w_down.reshape(w_down.shape),
        grad_b_down,
        grad_gain_two,
        grad_shift_two,
    )


def solution(mesh):
    rows = P(("dp", "tensor"), None)
    in_specs = (
        rows,
        P(None, None, "tensor"),
        P(None, "tensor"),
        P("tensor", None),
        P(),
        P(),
        P(),
        P(None, "tensor"),
        P("tensor"),
        P("tensor", None),
        P(),
        P(),
        P(),
        rows,
        P("dp"),
        P(),
    )
    out_specs = (
        P(),
        rows,
        rows,
        P(None, None, "tensor"),
        P(None, "tensor"),
        P("tensor", None),
        P(),
        P(),
        P(),
        P(None, "tensor"),
        P("tensor"),
        P("tensor", None),
        P(),
        P(),
        P(),
    )
    return jax.shard_map(
        per_device, mesh=mesh, in_specs=in_specs, out_specs=out_specs, check_vma=False
    )
```

```python
import functools

import jax
import jax.numpy as jnp
from jax import lax
from jax.experimental import pallas as pl
from jax.experimental.pallas import tpu as pltpu
from jax.sharding import PartitionSpec as P

HD = 64
LEN = 512
LANES = 128
EPS_NORM = 1e-12
EPS_UNIT = 1e-6
SOFTMAX_TEMP = 20.0
MASKED = -1e30
F32 = jnp.float32
BF16 = jnp.bfloat16
COST_SCALE = 0.9

ERFC_SLOPE = 0.41 * 0.7071067811865476
ERFC_POLY = tuple(
    0.5 * c
    for c in (
        0.23389259840606333,
        0.19943405568812744,
        0.36527628560337355,
        -0.195943508470611,
        0.5767329065489298,
        -0.17939241407306944,
    )
)
INV_SQRT_2PI = 0.3989422804014327


def cost(micros):
    return pl.CostEstimate(
        flops=int(micros * COST_SCALE * 1.15e9),
        bytes_accessed=int(micros * COST_SCALE * 3.6e6),
        transcendentals=0,
    )


def whole(shape):
    return pl.BlockSpec(shape, lambda *_: (0,) * len(shape))


def once(shape):
    return pl.BlockSpec(shape, lambda *_: (0,) * len(shape), pipeline_mode=pl.Buffered(1))


def shaped(shape, dtype=BF16):
    return jax.ShapeDtypeStruct(shape, dtype)


class Chain:
    def __init__(self):
        self.last = None
        self.windows = 0

    def __call__(self, kernel, scalars, inputs, in_specs, out_specs, out_shape, *, name, micros,
                 grid=(1,), scratch=(), vmem=16, token=False, aliases=None):
        deps = [] if self.last is None else [self.last]
        count = len(inputs)

        given = len(out_shape)
        if token:
            out_specs = list(out_specs) + [pl.BlockSpec(memory_space=pl.ANY)]
            out_shape = list(out_shape) + [shaped((8, LANES), F32)]

        def body(s_ref, *refs):
            rest = refs[count + len(deps) :]
            kernel(s_ref, *refs[:count], *rest[:given], *rest[len(out_shape) :])

        outs = pl.pallas_call(
            body,
            grid_spec=pltpu.PrefetchScalarGridSpec(
                num_scalar_prefetch=1,
                grid=grid,
                in_specs=list(in_specs) + [pl.BlockSpec(memory_space=pl.ANY)] * len(deps),
                out_specs=out_specs,
                scratch_shapes=list(scratch),
            ),
            out_shape=out_shape,
            input_output_aliases=aliases or {},
            compiler_params=pltpu.CompilerParams(vmem_limit_bytes=vmem * 2**20),
            cost_estimate=cost(micros),
            name=name,
        )(scalars, *inputs, *deps)
        self.last = outs[-1] if token else outs[0]
        if micros >= 3:
            self.windows += 1
        return outs[:given]

    def gate(self, scalars, a):
        def kernel(s_ref, a_ref, out_ref):
            out_ref[...] = a_ref[...]

        return self(
            kernel, scalars, [a], [whole(a.shape)], [whole(a.shape)], [shaped(a.shape, a.dtype)],
            name="gate", micros=10.0,
        )[0]

    def send(self, x, axis, mask):
        return swap(x, axis, mask), self.windows

    def receive(self, scalars, sent):
        if sent[1] == self.windows:
            self.pause(scalars)
        return sent[0]

    def pause(self, scalars):
        def kernel(s_ref, out_ref):
            out_ref[...] = jnp.zeros_like(out_ref)

        tile = (8, LANES)
        self(kernel, scalars, [], [], [whole(tile)], [shaped(tile, F32)], name="pause", micros=30.0)


def nn(a, b):
    return lax.dot_general(a, b, (((1,), (0,)), ((), ())), preferred_element_type=F32)


def nt(a, b):
    return lax.dot_general(a, b, (((1,), (1,)), ((), ())), preferred_element_type=F32)


def tn(a, b):
    return lax.dot_general(a, b, (((0,), (0,)), ((), ())), preferred_element_type=F32)


def colsum(a):
    return jnp.sum(a, axis=0, keepdims=True)


def rowmean(a):
    return jnp.mean(a, axis=-1, keepdims=True)


def gelu_pair(u):
    den = 1.0 + ERFC_SLOPE * jnp.abs(u)
    t = pl.reciprocal(den, approx=True)
    t = t * (2.0 - den * t)
    poly = ERFC_POLY[-1]
    for c in ERFC_POLY[-2::-1]:
        poly = poly * t + c
    bell = jnp.exp(-0.5 * (u * u))
    tail = bell * (poly * t)
    cdf = jnp.where(u >= 0, 1.0 - tail, tail)
    return u * cdf, cdf + (u * bell) * INV_SQRT_2PI


def length_of(s_ref, sentence):
    return s_ref[3 + s_ref[2] + sentence]


def attend_sentence(length, x, weights, bq, bv, qkv_ref, c_ref, lse_ref):
    rows = x.shape[0]
    width = c_ref.shape[1]
    both = nn(x, jnp.concatenate(weights, axis=1))
    qkv_ref[:, :width] = (both[:, :width] + bq).astype(BF16)
    qkv_ref[:, width : 2 * width] = both[:, width : 2 * width].astype(BF16)
    qkv_ref[:, 2 * width :] = (both[:, 2 * width :] + bv).astype(BF16)
    low = lax.broadcasted_iota(jnp.int32, (rows, LANES), 1) < HD
    live = lax.broadcasted_iota(jnp.int32, (rows, LANES), 0) < length
    bias = jnp.where(live, 0.0, MASKED).astype(F32)
    zero = jnp.zeros((rows, LANES), BF16)
    for p in range(width // LANES):
        at = LANES * p
        q = qkv_ref[:, at : at + LANES] * 0.125
        k = qkv_ref[:, width + at : width + at + LANES]
        v = qkv_ref[:, 2 * width + at : 2 * width + at + LANES]
        vt = v.T
        outs = []
        for h in range(2):
            km = jnp.where(low, k, zero) if h == 0 else jnp.where(low, zero, k)
            scores = nt(km, q)
            parts, tops, sums = [], [], []
            for j in range(rows // LANES):
                piece = scores[:, LANES * j : LANES * j + LANES] + bias
                top = jnp.max(piece, axis=0, keepdims=True)
                e = jnp.exp(piece - top)
                parts.append(e.astype(BF16))
                tops.append(top)
                sums.append(colsum(e))
            top = jnp.concatenate(tops, axis=1)
            total = jnp.concatenate(sums, axis=1)
            ct = nn(vt[HD * h : HD * h + HD], jnp.concatenate(parts, axis=1))
            outs.append(ct / total)
            lse_ref[0, 2 * p + h : 2 * p + h + 1, :] = top + jnp.log(total)
        c_ref[:, at : at + LANES] = jnp.concatenate(outs, axis=0).T.astype(BF16)


def attn_own_kernel(s_ref, x_ref, w_ref, b_ref, qkv_ref, c_ref, lse_ref):
    weights = [w_ref[c] for c in range(3)]
    length = length_of(s_ref, pl.program_id(0))
    attend_sentence(
        length, x_ref[...], weights, b_ref[0:1, :], b_ref[1:2, :], qkv_ref, c_ref, lse_ref
    )


def attn_other_kernel(s_ref, x_ref, w0, w1, b_ref, qkv_ref, c_ref, lse_ref, w_ref, *, at):
    @pl.when(pl.program_id(0) == 0)
    def _():
        for s, ref in enumerate((w0, w1)):
            for c in range(3):
                w_ref[c, bit(s_ref[0], 0) ^ s] = ref[c]

    shape = w_ref.shape
    weights = [w_ref[c].reshape(shape[1] * shape[2], shape[3]) for c in range(3)]
    length = length_of(s_ref, pl.program_id(0))
    cols = slice(at, at + shape[3])
    attend_sentence(
        length, x_ref[...], weights, b_ref[0:1, cols], b_ref[1:2, cols], qkv_ref, c_ref, lse_ref
    )


def attn_pack_kernel(s_ref, x_ref, p0, p1, b_ref, qkv_ref, c_ref, lse_ref, w_ref, out_ref, *, at):
    _, _, half, width = w_ref.shape

    @pl.when(pl.program_id(0) == 0)
    def _():
        rows, cols = out_ref.shape[1:]
        for s, ref in enumerate((p0, p1)):
            place = bit(s_ref[0], 0) ^ s
            for c in range(3):
                w_ref[c, place] = ref[c * half : (c + 1) * half, :]
            for k in range(cols // width):
                begin = 3 * half + k * rows
                out_ref[place, :, k * width : (k + 1) * width] = ref[begin : begin + rows, :]

    weights = [w_ref[c].reshape(2 * half, width) for c in range(3)]
    length = length_of(s_ref, pl.program_id(0))
    cols = slice(at, at + width)
    attend_sentence(
        length, x_ref[...], weights, b_ref[0:1, cols], b_ref[1:2, cols], qkv_ref, c_ref, lse_ref
    )


def by_rows(block, cols):
    return pl.BlockSpec((block, cols), lambda i, *_: (i, 0))


def attn_forward(chain, scalars, x, weights, bias, at=0, out_rows=0):
    tokens, model = x.shape
    width = weights[0].shape[-1]
    sents = tokens // LEN
    out_specs = [
        by_rows(LEN, 3 * width),
        by_rows(LEN, width),
        pl.BlockSpec((1, width // HD, LEN), lambda s, l: (s, 0, 0)),
    ]
    out_shape = [
        shaped((tokens, 3 * width)),
        shaped((tokens, width)),
        shaped((sents, width // HD, LEN), F32),
    ]
    own = len(weights) == 1
    extra = [] if own else [(3, 2, model // 2, width)] + ([(2, out_rows // 2, model)] if out_rows else [])
    out_specs += [whole(full) for full in extra]
    out_shape += [shaped(full) for full in extra]
    kernel = attn_pack_kernel if out_rows else attn_other_kernel
    return chain(
        attn_own_kernel if own else functools.partial(kernel, at=at),
        scalars,
        [x, *weights, bias],
        [by_rows(LEN, model)] + [once(w.shape) for w in weights] + [whole(bias.shape)],
        out_specs,
        out_shape,
        grid=(sents,),
        name="attn_fwd",
        micros=8.8,
        vmem=18,
    )


def attn_back_kernel(s_ref, qkv_ref, do_ref, lse_ref, grad_ref, sum_ref):
    s = pl.program_id(0)
    length = length_of(s_ref, s)
    rows, width = do_ref.shape
    low = lax.broadcasted_iota(jnp.int32, (rows, LANES), 1) < HD
    live = lax.broadcasted_iota(jnp.int32, (rows, LANES), 0) < length
    bias = jnp.where(live, 0.0, MASKED).astype(F32)
    zero = jnp.zeros((rows, LANES), BF16)

    @pl.when(s == 0)
    def _():
        sum_ref[...] = jnp.zeros_like(sum_ref)

    for p in range(width // LANES):
        at = LANES * p
        q = qkv_ref[:, at : at + LANES] * 0.125
        k = qkv_ref[:, width + at : width + at + LANES]
        v = qkv_ref[:, 2 * width + at : 2 * width + at + LANES]
        do = do_ref[:, at : at + LANES]
        kt = k.T
        dqs, dks, dvs = [], [], []
        for h in range(2):
            km = jnp.where(low, k, zero) if h == 0 else jnp.where(low, zero, k)
            vm = jnp.where(low, v, zero) if h == 0 else jnp.where(low, zero, v)
            lse = lse_ref[0, 2 * p + h : 2 * p + h + 1, :]
            scores = nt(km, q)
            dprob = nt(vm, do)
            probs, dscores = [], []
            for j in range(rows // LANES):
                cols = slice(LANES * j, LANES * j + LANES)
                e = jnp.exp(scores[:, cols] + bias - lse[:, cols])
                probs.append(e.astype(BF16))
                dp = dprob[:, cols]
                dscores.append((e * (dp - colsum(e * dp))).astype(BF16))
            prob = jnp.concatenate(probs, axis=1)
            dscore = jnp.concatenate(dscores, axis=1)
            dvs.append(nn(prob, do))
            dks.append(nn(dscore, q))
            dqs.append(nn(kt[HD * h : HD * h + HD], dscore))
        dq = (jnp.concatenate(dqs, axis=0).T * 0.125).astype(BF16)
        dk = jnp.where(low, dks[0], dks[1]).astype(BF16)
        dv = jnp.where(low, dvs[0], dvs[1]).astype(BF16)
        grad_ref[:, at : at + LANES] = dq
        grad_ref[:, width + at : width + at + LANES] = dk
        grad_ref[:, 2 * width + at : 2 * width + at + LANES] = dv
        sum_ref[0:1, at : at + LANES] += colsum(dq.astype(F32))
        sum_ref[1:2, at : at + LANES] += colsum(dv.astype(F32))


def attn_backward(chain, scalars, qkv, do, lse):
    tokens, width = do.shape
    return chain(
        attn_back_kernel,
        scalars,
        [qkv, do, lse],
        [
            by_rows(LEN, 3 * width),
            by_rows(LEN, width),
            pl.BlockSpec((1, width // HD, LEN), lambda s, l: (s, 0, 0)),
        ],
        [by_rows(LEN, 3 * width), whole((2, width))],
        [shaped((tokens, 3 * width)), shaped((2, width), F32)],
        grid=(tokens // LEN,),
        name="attn_bwd",
        micros=12.6,
        vmem=18,
    )


def across(ref):
    return ref[...].reshape(1, ref.shape[0])


def normalize(r):
    center = r - rowmean(r)
    inverse = lax.rsqrt(rowmean(center * center) + EPS_NORM)
    return center * inverse, inverse


def project_kernel(s_ref, x_ref, *refs, count):
    c_refs, refs = refs[:count], refs[count:]
    w_own, other, bias_ref, gain_ref, shift_ref, h_ref, low_ref, n_ref, inv_ref = refs
    attended = nn(c_refs[0][...], w_own[...]) + across(bias_ref)
    at = 0
    for ref in c_refs[1:]:
        width = ref.shape[1]
        attended = attended + nn(ref[...], other[at : at + width, :])
        at += width
    normal, inverse = normalize(x_ref[...].astype(F32) + attended)
    h = normal * across(gain_ref) + across(shift_ref)
    h_ref[...] = h
    low_ref[...] = h.astype(BF16)
    n_ref[...] = normal.astype(BF16)
    inv_ref[...] = inverse


def project_forward(chain, scalars, x, contexts, w_own, w_oth, vecs):
    tokens, model = x.shape
    block = 512
    return chain(
        functools.partial(project_kernel, count=len(contexts)),
        scalars,
        [x, *contexts, w_own, w_oth, *vecs],
        [by_rows(block, model)]
        + [by_rows(block, c.shape[1]) for c in contexts]
        + [once(w_own.shape), once(w_oth.shape)]
        + [whole(v.shape) for v in vecs],
        [by_rows(block, model)] * 3 + [by_rows(block, 1)],
        [
            shaped((tokens, model), F32),
            shaped((tokens, model)),
            shaped((tokens, model)),
            shaped((tokens, 1), F32),
        ],
        grid=(tokens // block,),
        name="project_fwd",
        micros=3.7,
        vmem=18,
    )


def feed_own_kernel(s_ref, h_ref, wu_ref, bu_ref, wd_ref, g_ref, gp_ref, f_ref):
    h = h_ref[...]
    chunk = wu_ref.shape[1] // 3
    bu = across(bu_ref)
    total = None
    for j in range(3):
        cols = slice(chunk * j, chunk * j + chunk)
        act, slope = gelu_pair(nn(h, wu_ref[:, cols]) + bu[:, cols])
        act = act.astype(BF16)
        g_ref[:, cols] = act
        gp_ref[:, cols] = slope.astype(BF16)
        part = nn(act, wd_ref[cols, :])
        total = part if total is None else total + part
    f_ref[...] = total


def feed_own(chain, scalars, h, wu, bu, wd):
    tokens, model = h.shape
    units = wu.shape[1]
    block = 256
    return chain(
        feed_own_kernel,
        scalars,
        [h, wu, bu, wd],
        [by_rows(block, model), once(wu.shape), whole(bu.shape), once(wd.shape)],
        [by_rows(block, units), by_rows(block, units), by_rows(block, model)],
        [shaped((tokens, units)), shaped((tokens, units)), shaped((tokens, model), F32)],
        grid=(tokens // block,),
        name="feed_own",
        micros=14.5,
        vmem=15,
    )


def feed_up_kernel(s_ref, h_ref, near_ref, far_ref, bias_ref, *refs, second):
    g_ref, gp_ref, wu_ref = refs[-3:]
    part = near_ref.shape[1]
    core = bit(s_ref[0], 0)

    @pl.when(pl.program_id(0) == 0)
    def _():
        wu_ref[:, pl.ds(pl.multiple_of(core * part, LANES), part)] = near_ref[...]
        wu_ref[:, pl.ds(pl.multiple_of((1 - core) * part, LANES), part)] = far_ref[...]

    row = 2 + 2 * (bit(s_ref[0], 1) ^ second)
    bu = jnp.concatenate([bias_ref[pl.ds(row + i, 1), :] for i in range(2)], axis=1)
    act, slope = gelu_pair(nn(h_ref[...], wu_ref[...]) + bu)
    g_ref[...] = act.astype(BF16)
    gp_ref[...] = slope.astype(BF16)


def feed_up(chain, scalars, h, near, far, bias, kept=()):
    tokens, model = h.shape
    half = 2 * near.shape[1]
    block = 256
    second = 1 if kept else 0
    here = lambda s: bit(s[0], 1) ^ second
    columns = pl.BlockSpec((block, half), lambda i, s: (i, here(s)))
    return chain(
        functools.partial(feed_up_kernel, second=second),
        scalars,
        [h, near, far, bias, *kept],
        [by_rows(block, model), once(near.shape), once(far.shape), whole(bias.shape)]
        + [pl.BlockSpec(memory_space=pl.ANY)] * len(kept),
        [columns, columns, pl.BlockSpec((model, half), lambda i, s: (0, here(s)))],
        [shaped((tokens, 2 * half)), shaped((tokens, 2 * half)), shaped((model, 2 * half))],
        grid=(tokens // block,),
        name="feed_up",
        micros=60.0,
        vmem=15,
        aliases={5 + i: i for i in range(len(kept))},
    )


def feed_down_kernel(
    s_ref, g_ref, h_ref, f_ref, d0, d1, bias_ref, gain_ref, shift_ref,
    out_ref, n_ref, inv_ref, pool_ref, wd_ref,
):
    i = pl.program_id(0)

    @pl.when(i == 0)
    def _():
        for s, down in enumerate((d0, d1)):
            wd_ref[bit(s_ref[0], 0) ^ s] = down[...]
        pool_ref[...] = jnp.zeros_like(pool_ref)

    shape = wd_ref.shape
    down = wd_ref[...].reshape(shape[0] * shape[1], shape[2])
    total = nn(g_ref[...], down)
    normal, inverse = normalize(h_ref[...] + (f_ref[...] + total + across(bias_ref)))
    y = normal * across(gain_ref) + across(shift_ref)
    out_ref[...] = y.astype(BF16)
    n_ref[...] = normal.astype(BF16)
    inv_ref[...] = inverse
    block = y.shape[0]
    per = LEN // block
    sent = i // per
    length = length_of(s_ref, sent)
    first = (i - sent * per) * block
    live = lax.broadcasted_iota(jnp.int32, y.shape, 0) + first < length
    pool_ref[pl.ds(sent, 1), :] += colsum(jnp.where(live, y, 0.0)) / length.astype(F32)


def feed_down(chain, scalars, g, h, f, down, vecs):
    tokens, model = h.shape
    units = g.shape[1]
    block = 256
    sents = tokens // LEN
    full = (2,) + down[0].shape
    return chain(
        feed_down_kernel,
        scalars,
        [g, h, f, *down, *vecs],
        [by_rows(block, units), by_rows(block, model), by_rows(block, model)]
        + [once(w.shape) for w in down]
        + [whole(v.shape) for v in vecs],
        [by_rows(block, model), by_rows(block, model), by_rows(block, 1), whole((sents, model)), whole(full)],
        [
            shaped((tokens, model)),
            shaped((tokens, model)),
            shaped((tokens, 1), F32),
            shaped((sents, model), F32),
            shaped(full),
        ],
        grid=(tokens // block,),
        name="feed_down",
        micros=9.0,
        vmem=15,
    )


def exact(a, b, dims):
    return lax.dot_general(
        a, b, (dims, ((), ())), precision=lax.Precision.HIGHEST, preferred_element_type=F32
    )


def loss_kernel(s_ref, *refs):
    *slot_refs, id_ref, loss_ref, cot_ref, pool_ref, grad_ref = refs
    local = cot_ref.shape[0]
    rank = s_ref[1]
    part = slot_refs[0].shape[0]
    count = part * len(slot_refs)
    for s in range(count // local):
        for i in range(local):
            at = local * s + i
            row = slot_refs[at // part][at % part : at % part + 1, :]
            pool_ref[pl.ds((rank ^ s) * local + i, 1), :] = row
    pooled = pool_ref[...]
    scale = lax.rsqrt(jnp.sum(pooled * pooled, axis=-1, keepdims=True) + EPS_UNIT)
    unit = pooled * scale
    score = SOFTMAX_TEMP * exact(unit, unit, ((1,), (1,)))
    itself = lax.broadcasted_iota(jnp.int32, score.shape, 0) == lax.broadcasted_iota(
        jnp.int32, score.shape, 1
    )
    others = jnp.where(itself, MASKED, score)
    top = jnp.max(others, axis=1, keepdims=True)
    power = jnp.exp(others - top)
    total = jnp.sum(power, axis=1, keepdims=True)
    ids = jnp.broadcast_to(across(id_ref).astype(F32), score.shape)
    match = jnp.logical_and(ids == ids.T, jnp.logical_not(itself)).astype(F32)
    number = jnp.sum(match, axis=1, keepdims=True)
    matched = jnp.sum(match * score, axis=1, keepdims=True) / number
    terms = top + jnp.log(total) - matched
    loss_ref[...] = jnp.sum(terms, axis=0, keepdims=True) / count
    dscore = float(LEN) * (power / total - match / number)
    dunit = SOFTMAX_TEMP * (exact(dscore, unit, ((1,), (0,))) + exact(dscore, unit, ((0,), (0,))))
    grad_ref[...] = scale * (dunit - unit * jnp.sum(unit * dunit, axis=-1, keepdims=True))
    for i in range(local):
        own = grad_ref[pl.ds(rank * local + i, 1), :]
        cot_ref[i : i + 1, :] = own / length_of(s_ref, i).astype(F32)


def loss_call(chain, scalars, slots, group_ids, local):
    part, model = slots[0].shape
    count = part * len(slots)
    return chain(
        loss_kernel,
        scalars,
        [*slots, group_ids],
        [whole((part, model))] * len(slots) + [whole((count,))],
        [whole((1, 1)), whole((local, model))],
        [shaped((1, 1), F32), shaped((local, model), F32)],
        scratch=[pltpu.VMEM((count, model), F32)] * 2,
        name="loss",
        micros=3.8,
    )


def norm_back(upstream, normal, inverse, gain):
    scaled = upstream * gain
    return inverse * (scaled - rowmean(scaled) - normal * rowmean(scaled * normal))


def norm_two_kernel(s_ref, cot_ref, n_ref, inv_ref, gain_ref, pool_ref, df_ref, sum_ref):
    s = pl.program_id(0)
    normal = n_ref[...].astype(F32)
    live = lax.broadcasted_iota(jnp.int32, normal.shape, 0) < length_of(s_ref, s)
    up = cot_ref[...].astype(F32) + jnp.where(live, pool_ref[pl.ds(s, 1), :], 0.0)
    df = norm_back(up, normal, inv_ref[...], across(gain_ref)).astype(BF16)
    df_ref[...] = df

    @pl.when(s == 0)
    def _():
        sum_ref[...] = jnp.zeros_like(sum_ref)

    sum_ref[0:1, :] += colsum(df.astype(F32))
    sum_ref[1:2, :] += colsum(up * normal)
    sum_ref[2:3, :] += colsum(up)


def norm_two_backward(chain, scalars, cot, normal, inverse, gain, pool_cot):
    tokens, model = cot.shape
    return chain(
        norm_two_kernel,
        scalars,
        [cot, normal, inverse, gain, pool_cot],
        [by_rows(LEN, model), by_rows(LEN, model), by_rows(LEN, 1), whole(gain.shape), whole(pool_cot.shape)],
        [by_rows(LEN, model), whole((3, model))],
        [shaped((tokens, model)), shaped((3, model), F32)],
        grid=(tokens // LEN,),
        name="norm_two_bwd",
        micros=5.4,
    )


def unit_back_kernel(s_ref, df_ref, gp_ref, wd_ref, du_ref, sum_ref):
    @pl.when(pl.program_id(0) == 0)
    def _():
        sum_ref[...] = jnp.zeros_like(sum_ref)

    df = df_ref[...]
    chunk = wd_ref.shape[0] // 3
    for j in range(3):
        cols = slice(chunk * j, chunk * j + chunk)
        du = (nt(df, wd_ref[cols, :]) * gp_ref[:, cols].astype(F32)).astype(BF16)
        du_ref[:, cols] = du
        sum_ref[:, cols] += colsum(du.astype(F32))


def unit_backward(chain, scalars, df, gp, wd):
    tokens, model = df.shape
    units = gp.shape[1]
    block = 512
    return chain(
        unit_back_kernel,
        scalars,
        [df, gp, wd],
        [by_rows(block, model), by_rows(block, units), once(wd.shape)],
        [by_rows(block, units), whole((1, units))],
        [shaped((tokens, units)), shaped((1, units), F32)],
        grid=(tokens // block,),
        name="unit_bwd",
        micros=60.0,
        vmem=18,
    )


def middle_kernel(
    s_ref, df_ref, du_own, du_oth, wu_own, wu_oth, n_ref, inv_ref, gain_ref, wo_own, wo_oth,
    da_ref, sum_ref, dc_own, *dc_oth,
):
    @pl.when(pl.program_id(0) == 0)
    def _():
        sum_ref[...] = jnp.zeros_like(sum_ref)

    total = df_ref[...].astype(F32) + nt(du_oth[...], wu_oth[...]) + nt(du_own[...], wu_own[...])
    normal = n_ref[...].astype(F32)
    da = norm_back(total, normal, inv_ref[...], across(gain_ref)).astype(BF16)
    da_ref[...] = da
    dc_own[...] = nt(da, wo_own[...]).astype(BF16)
    at = 0
    for ref in dc_oth:
        width = ref.shape[1]
        ref[...] = nt(da, wo_oth[at : at + width, :]).astype(BF16)
        at += width
    sum_ref[0:1, :] += colsum(total * normal)
    sum_ref[1:2, :] += colsum(total)
    sum_ref[2:3, :] += colsum(da.astype(F32))


def middle_backward(
    chain, scalars, df, du_own, du_oth, wu_own, wu_oth, normal, inverse, gain, wo_own, wo_oth, widths
):
    tokens, model = df.shape
    units = wu_own.shape[1]
    block = 256
    return chain(
        middle_kernel,
        scalars,
        [df, du_own, du_oth, wu_own, wu_oth, normal, inverse, gain, wo_own, wo_oth],
        [by_rows(block, model), by_rows(block, units), by_rows(block, units)]
        + [once(wu_own.shape), once(wu_oth.shape), by_rows(block, model), by_rows(block, 1)]
        + [whole(gain.shape), once(wo_own.shape), once(wo_oth.shape)],
        [by_rows(block, model), whole((3, model))] + [by_rows(block, w) for w in widths],
        [shaped((tokens, model)), shaped((3, model), F32)] + [shaped((tokens, w)) for w in widths],
        grid=(tokens // block,),
        name="middle_bwd",
        micros=12.0,
        vmem=18,
    )


def bit(value, at):
    return (value >> at) & 1


def split_store(d, even, odd, keep_ref, send_ref, at):
    flip = bit(d, 0) == 0
    keep_ref[at] = jnp.where(flip, even, odd).astype(BF16)
    send_ref[at] = jnp.where(flip, odd, even).astype(BF16)


def dense_grad_kernel(d_ref, a_ref, b_ref, keep_ref, send_ref):
    d = d_ref[0]
    grad = tn(a_ref[...], b_ref[...])
    step = keep_ref.shape[3]
    for x in range(2):
        for z in range(2):
            at = (4 * z + 2 * x) * step
            split_store(
                d, grad[at : at + step], grad[at + step : at + 2 * step], keep_ref, send_ref,
                (x ^ bit(d, 1), z ^ bit(d, 2), 0),
            )


def dense_grad(chain, scalars, a, b, cut_left):
    tokens = a.shape[0]
    left = a.shape[1] // (2 if cut_left else 1)
    right = b.shape[1] // (1 if cut_left else 2)
    step = left // 8
    block = pl.BlockSpec((2, 2, 1, step, right), lambda i, s: (0, 0, i ^ bit(s[0], 3), 0, 0))
    return chain(
        dense_grad_kernel,
        scalars,
        [a, b],
        [
            pl.BlockSpec((tokens, left), lambda i, s: (0, i)) if cut_left else once(a.shape),
            once(b.shape) if cut_left else pl.BlockSpec((tokens, right), lambda i, s: (0, i)),
        ],
        [block, block],
        [shaped((2, 2, 2, step, right))] * 2,
        grid=(2,),
        name="dense_grad",
        micros=60.0,
        vmem=15,
    )


def heads_grad_kernel(d_ref, x_ref, da_ref, two_ref, one_ref, unit_ref, *refs):
    *refs, keep_ref, send_ref = refs
    count = len(refs) // 3
    c_refs, dqkv_refs, bias_refs = refs[:count], refs[count : 2 * count], refs[2 * count :]
    d = d_ref[0]
    bias = jnp.concatenate([ref[...] for ref in bias_refs], axis=1)
    width = bias.shape[1]
    out = jnp.concatenate([tn(ref[...], da_ref[...]) for ref in c_refs], axis=0)
    projs = [tn(x_ref[...], ref[...]) for ref in dqkv_refs]
    proj = jnp.concatenate(
        [p[:, c * (p.shape[1] // 3) : (c + 1) * (p.shape[1] // 3)] for c in range(3) for p in projs], axis=1
    )
    step = proj.shape[0] // 16
    small = [ref[i : i + 1, at : at + width] for ref in (two_ref, one_ref) for i in range(3) for at in (0, width)]
    small += [bias[0:1, :], bias[1:2, :]]
    small += [unit_ref[:, at : at + width] for at in range(0, unit_ref.shape[1], width)]
    small += [jnp.zeros((1, width), F32)] * (32 - len(small))
    rest = jnp.zeros((14, width), F32)

    def block(b):
        row, col = (b & 7) * step, (b >> 3) * width
        pieces = [out[row : row + step, col : col + width]]
        pieces += [proj[b * step : b * step + step, c * width : c * width + width] for c in range(3)]
        return jnp.concatenate(pieces + [small[b], small[16 + b], rest], axis=0)

    for x in range(2):
        for z in range(2):
            for w in range(2):
                b = 8 * w + 4 * z + 2 * x
                split_store(
                    d, block(b), block(b + 1), keep_ref, send_ref,
                    (x ^ bit(d, 1), z ^ bit(d, 2), w ^ bit(d, 3)),
                )


def heads_grad(chain, scalars, x, da, sums, contexts, dqkvs, biases):
    width = sum(b.shape[1] for b in biases)
    full = (2, 2, 2, width // 2 + 16, width)
    inputs = [x, da, *sums, *contexts, *dqkvs, *biases]
    return chain(
        heads_grad_kernel,
        scalars,
        inputs,
        [once(a.shape) for a in inputs],
        [whole(full), whole(full)],
        [shaped(full)] * 2,
        name="heads_grad",
        micros=60.0,
        vmem=21,
    )


def input_grad_kernel(s_ref, da_ref, *refs):
    *refs, out_ref = refs
    total = da_ref[...].astype(F32)
    for grad, w in zip(refs[: len(refs) // 2], refs[len(refs) // 2 :], strict=True):
        total = total + nt(grad[...], jnp.concatenate([w[c] for c in range(3)], axis=1))
    out_ref[...] = total


def input_grad(chain, scalars, da, grads, weights):
    tokens, model = da.shape
    block = 512
    return chain(
        input_grad_kernel,
        scalars,
        [da, *grads, *weights],
        [by_rows(block, model)] + [by_rows(block, g.shape[1]) for g in grads] + [once(w.shape) for w in weights],
        [by_rows(block, model)],
        [shaped((tokens, model), F32)],
        grid=(tokens // block,),
        name="input_grad",
        token=True,
        micros=60.0,
        vmem=18,
    )[0]


def place_kernel(s_ref, a0, a1, b0, b1, *out_refs, kind):
    d = s_ref[0]
    half = pl.program_id(0)
    flip = bit(d, 0) == 0
    for x, (near_ref, far_ref) in enumerate(((a0, b0), (a1, b1))):
        for z in range(2):
            near, far = near_ref[z, 0].astype(F32), far_ref[z, 0].astype(F32)
            low = (x ^ bit(d, 1)) + 2 * (z ^ bit(d, 2))
            for side, rows in enumerate((jnp.where(flip, near, far), jnp.where(flip, far, near))):
                if kind != "heads":
                    step = rows.shape[0]
                    out_refs[0][low, side * step : (side + 1) * step] = rows
                    continue
                out_ref, proj_ref, *vec_refs, unit_ref, small_ref = out_refs
                step = out_ref.shape[1] // 2
                out_ref[low, side * step : (side + 1) * step] = rows[:step]
                for c in range(3):
                    proj_ref[c, low, side * step : (side + 1) * step] = rows[(c + 1) * step : (c + 2) * step]
                b = 2 * (low + 4 * (half ^ bit(d, 3))) + side
                small_ref[pl.ds(b, 1), :] = rows[4 * step : 4 * step + 1]
                small_ref[pl.ds(16 + b, 1), :] = rows[4 * step + 1 : 4 * step + 2]
    if kind != "heads":
        return

    @pl.when(half == 1)
    def _():
        line = lambda at, count: jnp.concatenate([small_ref[i : i + 1, :] for i in range(at, at + count)], axis=1)
        for i, ref in enumerate(vec_refs[:6]):
            ref[...] = line(2 * i, 2).reshape(ref.shape[0])
        vec_refs[6][...] = small_ref[12:14, :]
        unit_ref[...] = line(14, unit_ref.shape[0] // small_ref.shape[1]).reshape(unit_ref.shape[0])


def place(chain, scalars, pieces, kind, units):
    step, cols = pieces[0].shape[2:]
    block = pl.BlockSpec((2, 1, step, cols), lambda w, s: (0, w, 0, 0))
    high = lambda w, s: w ^ bit(s[0], 3)
    scratch = []
    if kind == "down":
        shapes = [(8, 2 * step, cols)]
        specs = [pl.BlockSpec((4, 2 * step, cols), lambda w, s: (high(w, s), 0, 0))]
    elif kind == "up":
        shapes = [(4, 2 * step, 2 * cols)]
        specs = [pl.BlockSpec((4, 2 * step, cols), lambda w, s: (0, 0, high(w, s)))]
    else:
        part = (step - 16) // 4
        shapes = [(4, 2 * part, 2 * cols), (3, 8, 2 * part, cols)]
        specs = [
            pl.BlockSpec((4, 2 * part, cols), lambda w, s: (0, 0, high(w, s))),
            pl.BlockSpec((3, 4, 2 * part, cols), lambda w, s: (0, high(w, s), 0, 0)),
        ]
        vectors = [(2 * cols,)] * 6 + [(2, cols), (units,)]
        shapes += vectors
        specs += [whole(v) for v in vectors]
        scratch = [pltpu.VMEM((32, cols), F32)]
    return chain(
        functools.partial(place_kernel, kind=kind),
        scalars,
        pieces,
        [block] * 4,
        specs,
        [shaped(s, F32) for s in shapes],
        grid=(2,),
        scratch=scratch,
        name="place",
        token=True,
        micros=4.0,
        vmem=18,
    )


def swap(x, axis, mask):
    size = lax.axis_size(axis)
    return lax.ppermute(x, axis, [(i, i ^ mask) for i in range(size)])


def swap_all(x, mask):
    size = lax.axis_size("dp") * lax.axis_size("tensor")
    return lax.ppermute(x, ("dp", "tensor"), [(i, i ^ mask) for i in range(size)])


def levels():
    return lax.axis_size("dp").bit_length() - 1


def flip_kernel(s_ref, a_ref, b_ref, out_ref):
    for i in range(2):
        out_ref[i] = (a_ref[i].astype(F32) + b_ref[1 - i].astype(F32)).astype(BF16)


def add_flipped(chain, scalars, a, b):
    return chain(
        flip_kernel,
        scalars,
        [a, b],
        [whole(a.shape)] * 2,
        [whole(a.shape)],
        [shaped(a.shape)],
        name="add",
        micros=2.0,
    )[0]


def sum_kernel(s_ref, *refs, count, early):
    total = refs[0][...].astype(F32) + refs[1][...].astype(F32)
    if early:
        total = total.astype(BF16).astype(F32)
    for ref in refs[2:count]:
        total = total + ref[...].astype(F32)
    total = total.astype(BF16)
    outs = refs[count:]
    if len(outs) == 1:
        outs[0][...] = total
        return
    for i, out in enumerate(outs):
        out[...] = total[i]


def add(chain, scalars, terms, split=1, early=False):
    shape = terms[0].shape
    outs = [shape] if split == 1 else [shape[1:]] * split
    return chain(
        functools.partial(sum_kernel, count=len(terms), early=early),
        scalars,
        terms,
        [whole(shape)] * len(terms),
        [whole(o) for o in outs],
        [shaped(o) for o in outs],
        name="add",
        micros=2.0,
    )


def join_kernel(s_ref, *refs):
    for i, ref in enumerate(refs[:-1]):
        refs[-1][i] = ref[...]


def join(chain, scalars, parts):
    shape = (len(parts),) + parts[0].shape
    return chain(
        join_kernel,
        scalars,
        parts,
        [whole(p.shape) for p in parts],
        [whole(shape)],
        [shaped(shape)],
        name="join",
        micros=1.5,
    )[0]


class Reduction:
    def __init__(self, chain, scalars):
        self.chain, self.scalars = chain, scalars

    def add(self, terms, split=1, early=False):
        return add(self.chain, self.scalars, terms, split, early)

    def send(self, x, axis, mask):
        return self.chain.send(x, axis, mask)

    def receive(self, sent):
        return self.chain.receive(self.scalars, sent)

    def other(self, keep, send):
        self.keep_oth, self.got_oth = keep, self.send(send, "dp", 1)

    def own(self, keep, send):
        self.keep_own, self.got_own = keep, self.send(send, "dp", 1)

    def across(self):
        (total,) = self.add([self.keep_oth, self.receive(self.got_oth)])
        self.got_y = self.send(total, "tensor", 1)

    def along_x(self):
        got = [self.receive(self.got_own), self.receive(self.got_y)]
        self.keep, send = self.add([self.keep_own, *got], 2, True)
        self.got = self.send(send, "dp", 2)

    def along_z(self):
        shape = self.keep.shape
        flat = (4,) + shape[2:]
        got = self.receive(self.got)
        self.keep, *send = self.add([self.keep.reshape(flat), got.reshape(flat)], 4)
        self.got = [self.send(x, "dp", m) for x, m in zip(send, (8, 4, 12), strict=True)]

    def back_z(self):
        (total,) = self.add([self.keep, *(self.receive(g) for g in self.got)])
        for at in range(4, levels()):
            got = self.receive(self.send(total, "dp", 1 << at))
            (total,) = self.add([total, got])
        self.total = total
        self.got = [self.send(total, "dp", m) for m in (8, 4, 12)]

    def back_x_direct(self):
        near = join(self.chain, self.scalars, [self.total, *(self.receive(g) for g in self.got)])
        self.near = near.reshape((2, 2) + near.shape[1:])
        self.got = self.send(self.near, "dp", 2)
        self.near_far = self.send(self.near, "dp", 1)

    def along_z0(self):
        self.keep, send = self.add([self.keep, self.receive(self.got)], 2)
        self.got = self.send(send, "dp", 4)

    def turn(self):
        (self.total,) = self.add([self.keep, self.receive(self.got)])
        for at in range(4, levels()):
            got = self.receive(self.send(self.total, "dp", 1 << at))
            (self.total,) = self.add([self.total, got])
        self.got = self.send(self.total, "dp", 8)

    def back_z0(self):
        self.total = add_flipped(self.chain, self.scalars, self.total, self.receive(self.got))
        self.got = self.send(self.total, "dp", 4)

    def back_x(self):
        self.near = join(self.chain, self.scalars, [self.total, self.receive(self.got)])
        self.got = self.send(self.near, "dp", 2)
        self.near_far = self.send(self.near, "dp", 1)

    def back_core(self):
        self.next = self.chain.gate(self.scalars, self.receive(self.got))
        self.next_far = self.send(self.next, "dp", 1)

    def place(self, kind, units=0):
        pieces = [self.near, self.next, self.receive(self.near_far), self.receive(self.next_far)]
        return place(self.chain, self.scalars, pieces, kind, units)


def stack_rows_kernel(s_ref, *refs):
    step = refs[0].shape[0]
    for i, ref in enumerate(refs[:-1]):
        refs[-1][i * step : (i + 1) * step, :] = ref[...]


def stack_rows(chain, scalars, parts):
    shape = (len(parts) * parts[0].shape[0], parts[0].shape[1])
    return chain(
        stack_rows_kernel,
        scalars,
        parts,
        [whole(p.shape) for p in parts],
        [whole(shape)],
        [shaped(shape, F32)],
        name="stack_rows",
        micros=10.0,
    )[0]


def gather_pooled(chain, scalars, pooled):
    bits = levels() + 1
    at = 0
    while at < bits:
        step = min(1 if at == 2 else 2, bits - at)
        parts = [pooled] + [swap_all(pooled, m << at) for m in range(1, 1 << step)]
        chain.pause(scalars)
        at += step
        if at < bits:
            pooled = stack_rows(chain, scalars, parts)
    return parts


def cut_kernel(s_ref, *refs):
    count = len(refs) // 2
    for a_ref, out_ref in zip(refs[:count], refs[count:], strict=True):
        out_ref[...] = a_ref[...].reshape(out_ref.shape)


def cut(chain, scalars, *cuts):
    shapes = [tuple(b for b in block if b != 1) for _, block, _ in cuts]
    at = lambda index: lambda i, s: index(s[0] & 3)
    return chain(
        cut_kernel,
        scalars,
        [a for a, _, _ in cuts],
        [pl.BlockSpec(block, at(index)) for _, block, index in cuts],
        [whole(s) for s in shapes],
        [shaped(s, a.dtype) for s, (a, _, _) in zip(shapes, cuts, strict=True)],
        name="cut",
        micros=1.0,
    )


def cut_heads_kernel(s_ref, a_ref, out_ref):
    out_ref[...] = a_ref[:, 0, :, : out_ref.shape[2]]


def cut_heads(chain, scalars, a, width):
    _, _, part, full = a.shape
    shape = (3, part, width)
    return chain(
        cut_heads_kernel,
        scalars,
        [a],
        [pl.BlockSpec((3, 1, part, full), lambda i, s: (0, bit(s[0], 0), 0, 0))],
        [whole(shape)],
        [shaped(shape)],
        name="cut",
        micros=1.0,
    )[0]


def cut_pack_kernel(s_ref, a_ref, w_ref, bias_ref, unit_ref, out_ref, small_ref):
    part = a_ref.shape[2]
    width = out_ref.shape[1]
    rows, cols = w_ref.shape[1:]
    for c in range(3):
        out_ref[c * part : (c + 1) * part, :] = a_ref[c, 0, :, a_ref.shape[3] - width :]
    for k in range(cols // width):
        begin = 3 * part + k * rows
        out_ref[begin : begin + rows, :] = w_ref[0, :, k * width : (k + 1) * width]
    full = bias_ref.shape[1]
    small_ref[0:2, :] = bias_ref[...]
    unit = across(unit_ref)
    for i in range(unit.shape[1] // full):
        small_ref[2 + i : 3 + i, :] = unit[:, i * full : (i + 1) * full]


def cut_pack(chain, scalars, a, width, w, bias, unit):
    _, _, part, full = a.shape
    _, rows, cols = w.shape
    shapes = [shaped((3 * part + rows * cols // width, width)), shaped((2 + unit.shape[0] // full, full), F32)]
    return chain(
        cut_pack_kernel,
        scalars,
        [a, w, bias, unit],
        [
            pl.BlockSpec((3, 1, part, full), lambda i, s: (0, bit(s[0], 0), 0, 0)),
            pl.BlockSpec((1, rows, cols), lambda i, s: (bit(s[0], 0), 0, 0)),
            whole(bias.shape),
            whole(unit.shape),
        ],
        [whole(s.shape) for s in shapes],
        shapes,
        name="cut",
        micros=1.0,
    )


class Gather:
    def __init__(self, chain, scalars, piece, relayed=False):
        self.chain, self.scalars, self.relayed = chain, scalars, relayed
        self.got = chain.send(piece, "tensor", 1)
        self.parts = []

    def hand_over(self):
        part = self.chain.gate(self.scalars, self.chain.receive(self.scalars, self.got))
        if self.relayed and not self.parts:
            self.got = self.chain.send(part, "dp", 2)
        self.parts += [part, self.chain.send(part, "dp", 1)]

    def slots(self):
        return [self.slot(i) for i in range(len(self.parts))]

    def slot(self, i):
        return self.parts[i] if i % 2 == 0 else self.chain.receive(self.scalars, self.parts[i])


def per_device(
    layer_input, w_qkv, bias_qv, w_out, b_out, gain_one, shift_one, w_up, b_up, w_down, b_down,
    gain_two, shift_two, out_cot, lengths, group_ids,
):
    tensor_size = lax.axis_size("tensor")
    position = lax.axis_index("tensor")
    d = lax.axis_index("dp")
    model = layer_input.shape[1]
    width = w_qkv.shape[2]
    units = w_up.shape[1]
    local = lengths.shape[0] // tensor_size
    rank = d * tensor_size + position
    scal = jnp.concatenate([jnp.stack([d, rank, position * local]).astype(jnp.int32), lengths])
    chain = Chain()

    heads_cut = w_qkv.reshape(3, 2, model // 2, width)
    lead = width // 3 * 2
    gather_lead = Gather(chain, scal, cut_heads(chain, scal, heads_cut, lead))
    qkv_own, c_own, lse_own = attn_forward(chain, scal, layer_input, [w_qkv], bias_qv)
    piece, bias = cut_pack(
        chain, scal, heads_cut, width - lead, w_out.reshape(2, width // 2, model), bias_qv, b_up
    )
    gather_pack = Gather(chain, scal, piece)
    bias_oth = swap(bias, "tensor", 1)
    part = units // 4
    piece, second = cut(
        chain,
        scal,
        (w_up, (model, part), lambda q: (0, q)),
        (w_down.reshape(2, 2 * part, model), (1, 2 * part, model), lambda q: (q & 1, 0, 0)),
    )
    gather_up = Gather(chain, scal, piece, relayed=True)
    gather_down = Gather(chain, scal, second)
    gather_lead.hand_over()
    qkv_lead, c_lead, lse_lead, wq_lead = attn_forward(chain, scal, layer_input, gather_lead.slots(), bias_oth)
    gather_pack.hand_over()
    qkv_rest, c_rest, lse_rest, wq_rest, wo_oth = attn_forward(
        chain, scal, layer_input, gather_pack.slots(), bias_oth, lead, width
    )
    wq_lead, wq_rest = (w.reshape(3, model, w.shape[3]) for w in (wq_lead, wq_rest))
    wo_oth = wo_oth.reshape(width, model)
    h1, h1_low, normal_one, inverse_one = project_forward(
        chain, scal, layer_input, [c_own, c_lead, c_rest], w_out, wo_oth, [b_out, gain_one, shift_one]
    )
    gather_up.hand_over()
    g_own, gp_own, f_own = feed_own(chain, scal, h1_low, w_up, b_up, w_down)
    gather_up.hand_over()
    near, far = gather_up.slot(0), gather_up.slot(1)
    half = feed_up(chain, scal, h1_low, near, far, bias_oth)
    gather_down.hand_over()
    near, far = gather_up.slot(2), gather_up.slot(3)
    g_oth, gp_oth, wu_oth = feed_up(chain, scal, h1_low, near, far, bias_oth, half)
    output, normal_two, inverse_two, pooled, wd_oth = feed_down(
        chain, scal, g_oth, h1, f_own, gather_down.slots(), [b_down, gain_two, shift_two]
    )
    wd_oth = wd_oth.reshape(units, model)

    loss, pool_cot = loss_call(chain, scal, gather_pooled(chain, scal, pooled), group_ids, local)

    down, up, heads = (Reduction(chain, scal) for _ in range(3))
    df, sums_two = norm_two_backward(chain, scal, out_cot, normal_two, inverse_two, gain_two, pool_cot)
    down.other(*dense_grad(chain, scal, g_oth, df, True))
    down.own(*dense_grad(chain, scal, g_own, df, True))
    down.across()
    du_oth, sums_du_oth = unit_backward(chain, scal, df, gp_oth, wd_oth)
    du_own, sums_du_own = unit_backward(chain, scal, df, gp_own, w_down)
    up.other(*dense_grad(chain, scal, h1_low, du_oth, False))
    up.own(*dense_grad(chain, scal, h1_low, du_own, False))
    up.across()
    da, sums_one, dc_own, dc_lead, dc_rest = middle_backward(
        chain, scal, df, du_own, du_oth, w_up, wu_oth, normal_one, inverse_one, gain_one, w_out, wo_oth,
        [width, lead, width - lead],
    )
    down.along_x()
    dqkv_lead, sums_lead = attn_backward(chain, scal, qkv_lead, dc_lead, lse_lead)
    dqkv_rest, sums_rest = attn_backward(chain, scal, qkv_rest, dc_rest, lse_rest)
    sums = [sums_two, sums_one, sums_du_oth]
    heads.other(
        *heads_grad(
            chain, scal, layer_input, da, sums, [c_lead, c_rest], [dqkv_lead, dqkv_rest], [sums_lead, sums_rest]
        )
    )
    down.along_z0()
    up.along_x()
    chain.pause(scal)
    heads.across()
    dqkv_own, sums_own = attn_backward(chain, scal, qkv_own, dc_own, lse_own)
    down.turn()
    up.along_z0()
    sums = [sums_two, sums_one, sums_du_own]
    heads.own(*heads_grad(chain, scal, layer_input, da, sums, [c_own], [dqkv_own], [sums_own]))
    grad_input = input_grad(
        chain, scal, da, [dqkv_own, dqkv_lead, dqkv_rest], [w_qkv, wq_lead, wq_rest]
    )
    down.back_z0()
    heads.along_x()
    up.turn()
    chain.pause(scal)
    down.back_x()
    heads.along_z0()
    chain.pause(scal)
    heads.turn()
    up.back_z0()
    chain.pause(scal)
    heads.back_z0()
    up.back_x()
    chain.pause(scal)
    down.back_core()
    (grad_w_down,) = down.place("down")
    up.back_core()
    heads.back_x()
    chain.pause(scal)
    (grad_w_up,) = up.place("up")
    heads.back_core()
    chain.pause(scal)
    grad_w_out, grad_w_qkv, *grads, grad_bias_qv, grad_b_up = heads.place("heads", units)
    grad_b_down, grad_gain_two, grad_shift_two, grad_gain_one, grad_shift_one, grad_b_out = grads
    return (
        loss.reshape(()),
        output,
        grad_input,
        grad_w_qkv.reshape(w_qkv.shape),
        grad_bias_qv,
        grad_w_out.reshape(w_out.shape),
        grad_b_out,
        grad_gain_one,
        grad_shift_one,
        grad_w_up.reshape(w_up.shape),
        grad_b_up,
        grad_w_down.reshape(w_down.shape),
        grad_b_down,
        grad_gain_two,
        grad_shift_two,
    )


def solution(mesh):
    rows = P(("dp", "tensor"), None)
    in_specs = (
        rows,
        P(None, None, "tensor"),
        P(None, "tensor"),
        P("tensor", None),
        P(),
        P(),
        P(),
        P(None, "tensor"),
        P("tensor"),
        P("tensor", None),
        P(),
        P(),
        P(),
        rows,
        P("dp"),
        P(),
    )
    out_specs = (
        P(),
        rows,
        rows,
        P(None, None, "tensor"),
        P(None, "tensor"),
        P("tensor", None),
        P(),
        P(),
        P(),
        P(None, "tensor"),
        P("tensor"),
        P("tensor", None),
        P(),
        P(),
        P(),
    )
    return jax.shard_map(
        per_device, mesh=mesh, in_specs=in_specs, out_specs=out_specs, check_vma=False
    )
```

```python
import functools

import jax
import jax.numpy as jnp
from jax import lax
from jax.experimental import pallas as pl
from jax.experimental.pallas import tpu as pltpu
from jax.sharding import PartitionSpec as P

HD = 64
LEN = 512
LANES = 128
EPS_NORM = 1e-12
EPS_UNIT = 1e-6
SOFTMAX_TEMP = 20.0
MASKED = -1e30
F32 = jnp.float32
BF16 = jnp.bfloat16
COST_SCALE = 0.9

ERFC_SLOPE = 0.41 * 0.7071067811865476
ERFC_POLY = tuple(
    0.5 * c
    for c in (
        0.23389259840606333,
        0.19943405568812744,
        0.36527628560337355,
        -0.195943508470611,
        0.5767329065489298,
        -0.17939241407306944,
    )
)
INV_SQRT_2PI = 0.3989422804014327


def cost(micros):
    return pl.CostEstimate(
        flops=int(micros * COST_SCALE * 1.15e9),
        bytes_accessed=int(micros * COST_SCALE * 3.6e6),
        transcendentals=0,
    )


def whole(shape):
    return pl.BlockSpec(shape, lambda *_: (0,) * len(shape))


def once(shape):
    return pl.BlockSpec(shape, lambda *_: (0,) * len(shape), pipeline_mode=pl.Buffered(1))


def shaped(shape, dtype=BF16):
    return jax.ShapeDtypeStruct(shape, dtype)


class Chain:
    def __init__(self):
        self.last = None
        self.windows = 0

    def __call__(self, kernel, scalars, inputs, in_specs, out_specs, out_shape, *, name, micros,
                 grid=(1,), scratch=(), vmem=16, token=False, aliases=None):
        deps = [] if self.last is None else [self.last]
        count = len(inputs)

        given = len(out_shape)
        if token:
            out_specs = list(out_specs) + [pl.BlockSpec(memory_space=pl.ANY)]
            out_shape = list(out_shape) + [shaped((8, LANES), F32)]

        def body(s_ref, *refs):
            rest = refs[count + len(deps) :]
            kernel(s_ref, *refs[:count], *rest[:given], *rest[len(out_shape) :])

        outs = pl.pallas_call(
            body,
            grid_spec=pltpu.PrefetchScalarGridSpec(
                num_scalar_prefetch=1,
                grid=grid,
                in_specs=list(in_specs) + [pl.BlockSpec(memory_space=pl.ANY)] * len(deps),
                out_specs=out_specs,
                scratch_shapes=list(scratch),
            ),
            out_shape=out_shape,
            input_output_aliases=aliases or {},
            compiler_params=pltpu.CompilerParams(vmem_limit_bytes=vmem * 2**20),
            cost_estimate=cost(micros),
            name=name,
        )(scalars, *inputs, *deps)
        self.last = outs[-1] if token else outs[0]
        if micros >= 3:
            self.windows += 1
        return outs[:given]

    def gate(self, scalars, a):
        def kernel(s_ref, a_ref, out_ref):
            out_ref[...] = a_ref[...]

        return self(
            kernel, scalars, [a], [whole(a.shape)], [whole(a.shape)], [shaped(a.shape, a.dtype)],
            name="gate", micros=10.0,
        )[0]

    def send(self, x, axis, mask):
        return swap(x, axis, mask), self.windows

    def receive(self, scalars, sent):
        if sent[1] == self.windows:
            self.pause(scalars)
        return sent[0]

    def pause(self, scalars):
        def kernel(s_ref, out_ref):
            out_ref[...] = jnp.zeros_like(out_ref)

        tile = (8, LANES)
        self(kernel, scalars, [], [], [whole(tile)], [shaped(tile, F32)], name="pause", micros=30.0)


def nn(a, b):
    return lax.dot_general(a, b, (((1,), (0,)), ((), ())), preferred_element_type=F32)


def nt(a, b):
    return lax.dot_general(a, b, (((1,), (1,)), ((), ())), preferred_element_type=F32)


def tn(a, b):
    return lax.dot_general(a, b, (((0,), (0,)), ((), ())), preferred_element_type=F32)


def colsum(a):
    return jnp.sum(a, axis=0, keepdims=True)


def rowmean(a):
    return jnp.mean(a, axis=-1, keepdims=True)


def gelu_pair(u):
    den = 1.0 + ERFC_SLOPE * jnp.abs(u)
    t = pl.reciprocal(den, approx=True)
    t = t * (2.0 - den * t)
    poly = ERFC_POLY[-1]
    for c in ERFC_POLY[-2::-1]:
        poly = poly * t + c
    bell = jnp.exp(-0.5 * (u * u))
    tail = bell * (poly * t)
    cdf = jnp.where(u >= 0, 1.0 - tail, tail)
    return u * cdf, cdf + (u * bell) * INV_SQRT_2PI


def length_of(s_ref, sentence):
    return s_ref[3 + s_ref[2] + sentence]


def attend_sentence(length, x, weights, bq, bv, qkv_ref, c_ref, lse_ref):
    rows = x.shape[0]
    width = c_ref.shape[1]
    both = nn(x, jnp.concatenate(weights, axis=1))
    qkv_ref[:, :width] = (both[:, :width] + bq).astype(BF16)
    qkv_ref[:, width : 2 * width] = both[:, width : 2 * width].astype(BF16)
    qkv_ref[:, 2 * width :] = (both[:, 2 * width :] + bv).astype(BF16)
    low = lax.broadcasted_iota(jnp.int32, (rows, LANES), 1) < HD
    live = lax.broadcasted_iota(jnp.int32, (rows, LANES), 0) < length
    bias = jnp.where(live, 0.0, MASKED).astype(F32)
    zero = jnp.zeros((rows, LANES), BF16)
    for p in range(width // LANES):
        at = LANES * p
        q = qkv_ref[:, at : at + LANES] * 0.125
        k = qkv_ref[:, width + at : width + at + LANES]
        v = qkv_ref[:, 2 * width + at : 2 * width + at + LANES]
        vt = v.T
        outs = []
        for h in range(2):
            km = jnp.where(low, k, zero) if h == 0 else jnp.where(low, zero, k)
            scores = nt(km, q)
            parts, tops, sums = [], [], []
            for j in range(rows // LANES):
                piece = scores[:, LANES * j : LANES * j + LANES] + bias
                top = jnp.max(piece, axis=0, keepdims=True)
                e = jnp.exp(piece - top)
                parts.append(e.astype(BF16))
                tops.append(top)
                sums.append(colsum(e))
            top = jnp.concatenate(tops, axis=1)
            total = jnp.concatenate(sums, axis=1)
            ct = nn(vt[HD * h : HD * h + HD], jnp.concatenate(parts, axis=1))
            outs.append(ct / total)
            lse_ref[0, 2 * p + h : 2 * p + h + 1, :] = top + jnp.log(total)
        c_ref[:, at : at + LANES] = jnp.concatenate(outs, axis=0).T.astype(BF16)


def attn_own_kernel(s_ref, x_ref, w_ref, b_ref, qkv_ref, c_ref, lse_ref):
    weights = [w_ref[c] for c in range(3)]
    length = length_of(s_ref, pl.program_id(0))
    attend_sentence(
        length, x_ref[...], weights, b_ref[0:1, :], b_ref[1:2, :], qkv_ref, c_ref, lse_ref
    )


def attn_other_kernel(s_ref, x_ref, w0, w1, b_ref, qkv_ref, c_ref, lse_ref, w_ref, *, at):
    @pl.when(pl.program_id(0) == 0)
    def _():
        for s, ref in enumerate((w0, w1)):
            for c in range(3):
                w_ref[c, bit(s_ref[0], 0) ^ s] = ref[c]

    shape = w_ref.shape
    weights = [w_ref[c].reshape(shape[1] * shape[2], shape[3]) for c in range(3)]
    length = length_of(s_ref, pl.program_id(0))
    cols = slice(at, at + shape[3])
    attend_sentence(
        length, x_ref[...], weights, b_ref[0:1, cols], b_ref[1:2, cols], qkv_ref, c_ref, lse_ref
    )


def attn_pack_kernel(s_ref, x_ref, p0, p1, b_ref, qkv_ref, c_ref, lse_ref, w_ref, out_ref, *, at):
    _, _, half, width = w_ref.shape

    @pl.when(pl.program_id(0) == 0)
    def _():
        rows, cols = out_ref.shape[1:]
        for s, ref in enumerate((p0, p1)):
            place = bit(s_ref[0], 0) ^ s
            for c in range(3):
                w_ref[c, place] = ref[c * half : (c + 1) * half, :]
            for k in range(cols // width):
                begin = 3 * half + k * rows
                out_ref[place, :, k * width : (k + 1) * width] = ref[begin : begin + rows, :]

    weights = [w_ref[c].reshape(2 * half, width) for c in range(3)]
    length = length_of(s_ref, pl.program_id(0))
    cols = slice(at, at + width)
    attend_sentence(
        length, x_ref[...], weights, b_ref[0:1, cols], b_ref[1:2, cols], qkv_ref, c_ref, lse_ref
    )


def by_rows(block, cols):
    return pl.BlockSpec((block, cols), lambda i, *_: (i, 0))


def attn_forward(chain, scalars, x, weights, bias, at=0, out_rows=0):
    tokens, model = x.shape
    width = weights[0].shape[-1]
    sents = tokens // LEN
    out_specs = [
        by_rows(LEN, 3 * width),
        by_rows(LEN, width),
        pl.BlockSpec((1, width // HD, LEN), lambda s, l: (s, 0, 0)),
    ]
    out_shape = [
        shaped((tokens, 3 * width)),
        shaped((tokens, width)),
        shaped((sents, width // HD, LEN), F32),
    ]
    own = len(weights) == 1
    extra = [] if own else [(3, 2, model // 2, width)] + ([(2, out_rows // 2, model)] if out_rows else [])
    out_specs += [whole(full) for full in extra]
    out_shape += [shaped(full) for full in extra]
    kernel = attn_pack_kernel if out_rows else attn_other_kernel
    return chain(
        attn_own_kernel if own else functools.partial(kernel, at=at),
        scalars,
        [x, *weights, bias],
        [by_rows(LEN, model)] + [once(w.shape) for w in weights] + [whole(bias.shape)],
        out_specs,
        out_shape,
        grid=(sents,),
        name="attn_fwd",
        micros=8.8,
        vmem=18,
    )


def attn_back_kernel(s_ref, qkv_ref, do_ref, lse_ref, grad_ref, sum_ref):
    s = pl.program_id(0)
    length = length_of(s_ref, s)
    rows, width = do_ref.shape
    low = lax.broadcasted_iota(jnp.int32, (rows, LANES), 1) < HD
    live = lax.broadcasted_iota(jnp.int32, (rows, LANES), 0) < length
    bias = jnp.where(live, 0.0, MASKED).astype(F32)
    zero = jnp.zeros((rows, LANES), BF16)

    @pl.when(s == 0)
    def _():
        sum_ref[...] = jnp.zeros_like(sum_ref)

    for p in range(width // LANES):
        at = LANES * p
        q = qkv_ref[:, at : at + LANES] * 0.125
        k = qkv_ref[:, width + at : width + at + LANES]
        v = qkv_ref[:, 2 * width + at : 2 * width + at + LANES]
        do = do_ref[:, at : at + LANES]
        kt = k.T
        dqs, dks, dvs = [], [], []
        for h in range(2):
            km = jnp.where(low, k, zero) if h == 0 else jnp.where(low, zero, k)
            vm = jnp.where(low, v, zero) if h == 0 else jnp.where(low, zero, v)
            lse = lse_ref[0, 2 * p + h : 2 * p + h + 1, :]
            scores = nt(km, q)
            dprob = nt(vm, do)
            probs, dscores = [], []
            for j in range(rows // LANES):
                cols = slice(LANES * j, LANES * j + LANES)
                e = jnp.exp(scores[:, cols] + bias - lse[:, cols])
                probs.append(e.astype(BF16))
                dp = dprob[:, cols]
                dscores.append((e * (dp - colsum(e * dp))).astype(BF16))
            prob = jnp.concatenate(probs, axis=1)
            dscore = jnp.concatenate(dscores, axis=1)
            dvs.append(nn(prob, do))
            dks.append(nn(dscore, q))
            dqs.append(nn(kt[HD * h : HD * h + HD], dscore))
        dq = (jnp.concatenate(dqs, axis=0).T * 0.125).astype(BF16)
        dk = jnp.where(low, dks[0], dks[1]).astype(BF16)
        dv = jnp.where(low, dvs[0], dvs[1]).astype(BF16)
        grad_ref[:, at : at + LANES] = dq
        grad_ref[:, width + at : width + at + LANES] = dk
        grad_ref[:, 2 * width + at : 2 * width + at + LANES] = dv
        sum_ref[0:1, at : at + LANES] += colsum(dq.astype(F32))
        sum_ref[1:2, at : at + LANES] += colsum(dv.astype(F32))


def attn_backward(chain, scalars, qkv, do, lse):
    tokens, width = do.shape
    return chain(
        attn_back_kernel,
        scalars,
        [qkv, do, lse],
        [
            by_rows(LEN, 3 * width),
            by_rows(LEN, width),
            pl.BlockSpec((1, width // HD, LEN), lambda s, l: (s, 0, 0)),
        ],
        [by_rows(LEN, 3 * width), whole((2, width))],
        [shaped((tokens, 3 * width)), shaped((2, width), F32)],
        grid=(tokens // LEN,),
        name="attn_bwd",
        micros=12.6,
        vmem=18,
    )


def across(ref):
    return ref[...].reshape(1, ref.shape[0])


def normalize(r):
    center = r - rowmean(r)
    inverse = lax.rsqrt(rowmean(center * center) + EPS_NORM)
    return center * inverse, inverse


def project_kernel(s_ref, x_ref, *refs, count):
    c_refs, refs = refs[:count], refs[count:]
    w_own, other, bias_ref, gain_ref, shift_ref, h_ref, low_ref, n_ref, inv_ref = refs
    attended = nn(c_refs[0][...], w_own[...]) + across(bias_ref)
    at = 0
    for ref in c_refs[1:]:
        width = ref.shape[1]
        attended = attended + nn(ref[...], other[at : at + width, :])
        at += width
    normal, inverse = normalize(x_ref[...].astype(F32) + attended)
    h = normal * across(gain_ref) + across(shift_ref)
    h_ref[...] = h
    low_ref[...] = h.astype(BF16)
    n_ref[...] = normal.astype(BF16)
    inv_ref[...] = inverse


def project_forward(chain, scalars, x, contexts, w_own, w_oth, vecs):
    tokens, model = x.shape
    block = 512
    return chain(
        functools.partial(project_kernel, count=len(contexts)),
        scalars,
        [x, *contexts, w_own, w_oth, *vecs],
        [by_rows(block, model)]
        + [by_rows(block, c.shape[1]) for c in contexts]
        + [once(w_own.shape), once(w_oth.shape)]
        + [whole(v.shape) for v in vecs],
        [by_rows(block, model)] * 3 + [by_rows(block, 1)],
        [
            shaped((tokens, model), F32),
            shaped((tokens, model)),
            shaped((tokens, model)),
            shaped((tokens, 1), F32),
        ],
        grid=(tokens // block,),
        name="project_fwd",
        micros=3.7,
        vmem=18,
    )


def feed_own_kernel(s_ref, h_ref, wu_ref, bu_ref, wd_ref, g_ref, gp_ref, f_ref):
    h = h_ref[...]
    chunk = wu_ref.shape[1] // 3
    bu = across(bu_ref)
    total = None
    for j in range(3):
        cols = slice(chunk * j, chunk * j + chunk)
        act, slope = gelu_pair(nn(h, wu_ref[:, cols]) + bu[:, cols])
        act = act.astype(BF16)
        g_ref[:, cols] = act
        gp_ref[:, cols] = slope.astype(BF16)
        part = nn(act, wd_ref[cols, :])
        total = part if total is None else total + part
    f_ref[...] = total


def feed_own(chain, scalars, h, wu, bu, wd):
    tokens, model = h.shape
    units = wu.shape[1]
    block = 256
    return chain(
        feed_own_kernel,
        scalars,
        [h, wu, bu, wd],
        [by_rows(block, model), once(wu.shape), whole(bu.shape), once(wd.shape)],
        [by_rows(block, units), by_rows(block, units), by_rows(block, model)],
        [shaped((tokens, units)), shaped((tokens, units)), shaped((tokens, model), F32)],
        grid=(tokens // block,),
        name="feed_own",
        micros=14.5,
        vmem=15,
    )


def feed_up_kernel(s_ref, h_ref, near_ref, far_ref, bias_ref, *refs, second):
    g_ref, gp_ref, wu_ref = refs[-3:]
    part = near_ref.shape[1]
    core = bit(s_ref[0], 0)

    @pl.when(pl.program_id(0) == 0)
    def _():
        wu_ref[:, pl.ds(pl.multiple_of(core * part, LANES), part)] = near_ref[...]
        wu_ref[:, pl.ds(pl.multiple_of((1 - core) * part, LANES), part)] = far_ref[...]

    row = 2 + 2 * (bit(s_ref[0], 1) ^ second)
    bu = jnp.concatenate([bias_ref[pl.ds(row + i, 1), :] for i in range(2)], axis=1)
    act, slope = gelu_pair(nn(h_ref[...], wu_ref[...]) + bu)
    g_ref[...] = act.astype(BF16)
    gp_ref[...] = slope.astype(BF16)


def feed_up(chain, scalars, h, near, far, bias, kept=()):
    tokens, model = h.shape
    half = 2 * near.shape[1]
    block = 256
    second = 1 if kept else 0
    here = lambda s: bit(s[0], 1) ^ second
    columns = pl.BlockSpec((block, half), lambda i, s: (i, here(s)))
    return chain(
        functools.partial(feed_up_kernel, second=second),
        scalars,
        [h, near, far, bias, *kept],
        [by_rows(block, model), once(near.shape), once(far.shape), whole(bias.shape)]
        + [pl.BlockSpec(memory_space=pl.ANY)] * len(kept),
        [columns, columns, pl.BlockSpec((model, half), lambda i, s: (0, here(s)))],
        [shaped((tokens, 2 * half)), shaped((tokens, 2 * half)), shaped((model, 2 * half))],
        grid=(tokens // block,),
        name="feed_up",
        micros=60.0,
        vmem=15,
        aliases={5 + i: i for i in range(len(kept))},
    )


def feed_down_kernel(
    s_ref, g_ref, h_ref, f_ref, d0, d1, bias_ref, gain_ref, shift_ref,
    out_ref, n_ref, inv_ref, pool_ref, wd_ref,
):
    i = pl.program_id(0)

    @pl.when(i == 0)
    def _():
        for s, down in enumerate((d0, d1)):
            wd_ref[bit(s_ref[0], 0) ^ s] = down[...]
        pool_ref[...] = jnp.zeros_like(pool_ref)

    shape = wd_ref.shape
    down = wd_ref[...].reshape(shape[0] * shape[1], shape[2])
    total = nn(g_ref[...], down)
    normal, inverse = normalize(h_ref[...] + (f_ref[...] + total + across(bias_ref)))
    y = normal * across(gain_ref) + across(shift_ref)
    out_ref[...] = y.astype(BF16)
    n_ref[...] = normal.astype(BF16)
    inv_ref[...] = inverse
    block = y.shape[0]
    per = LEN // block
    sent = i // per
    length = length_of(s_ref, sent)
    first = (i - sent * per) * block
    live = lax.broadcasted_iota(jnp.int32, y.shape, 0) + first < length
    pool_ref[pl.ds(sent, 1), :] += colsum(jnp.where(live, y, 0.0)) / length.astype(F32)


def feed_down(chain, scalars, g, h, f, down, vecs):
    tokens, model = h.shape
    units = g.shape[1]
    block = 256
    sents = tokens // LEN
    full = (2,) + down[0].shape
    return chain(
        feed_down_kernel,
        scalars,
        [g, h, f, *down, *vecs],
        [by_rows(block, units), by_rows(block, model), by_rows(block, model)]
        + [once(w.shape) for w in down]
        + [whole(v.shape) for v in vecs],
        [by_rows(block, model), by_rows(block, model), by_rows(block, 1), whole((sents, model)), whole(full)],
        [
            shaped((tokens, model)),
            shaped((tokens, model)),
            shaped((tokens, 1), F32),
            shaped((sents, model), F32),
            shaped(full),
        ],
        grid=(tokens // block,),
        name="feed_down",
        micros=9.0,
        vmem=15,
    )


def exact(a, b, dims):
    return lax.dot_general(
        a, b, (dims, ((), ())), precision=lax.Precision.HIGHEST, preferred_element_type=F32
    )


def loss_kernel(s_ref, *refs):
    *slot_refs, id_ref, loss_ref, cot_ref, pool_ref, grad_ref = refs
    local = cot_ref.shape[0]
    rank = s_ref[1]
    part = slot_refs[0].shape[0]
    count = part * len(slot_refs)
    for s in range(count // local):
        for i in range(local):
            at = local * s + i
            row = slot_refs[at // part][at % part : at % part + 1, :]
            pool_ref[pl.ds((rank ^ s) * local + i, 1), :] = row
    pooled = pool_ref[...]
    scale = lax.rsqrt(jnp.sum(pooled * pooled, axis=-1, keepdims=True) + EPS_UNIT)
    unit = pooled * scale
    score = SOFTMAX_TEMP * exact(unit, unit, ((1,), (1,)))
    itself = lax.broadcasted_iota(jnp.int32, score.shape, 0) == lax.broadcasted_iota(
        jnp.int32, score.shape, 1
    )
    others = jnp.where(itself, MASKED, score)
    top = jnp.max(others, axis=1, keepdims=True)
    power = jnp.exp(others - top)
    total = jnp.sum(power, axis=1, keepdims=True)
    ids = jnp.broadcast_to(across(id_ref).astype(F32), score.shape)
    match = jnp.logical_and(ids == ids.T, jnp.logical_not(itself)).astype(F32)
    number = jnp.sum(match, axis=1, keepdims=True)
    matched = jnp.sum(match * score, axis=1, keepdims=True) / number
    terms = top + jnp.log(total) - matched
    loss_ref[...] = jnp.sum(terms, axis=0, keepdims=True) / count
    dscore = float(LEN) * (power / total - match / number)
    dunit = SOFTMAX_TEMP * (exact(dscore, unit, ((1,), (0,))) + exact(dscore, unit, ((0,), (0,))))
    grad_ref[...] = scale * (dunit - unit * jnp.sum(unit * dunit, axis=-1, keepdims=True))
    for i in range(local):
        own = grad_ref[pl.ds(rank * local + i, 1), :]
        cot_ref[i : i + 1, :] = own / length_of(s_ref, i).astype(F32)


def loss_call(chain, scalars, slots, group_ids, local):
    part, model = slots[0].shape
    count = part * len(slots)
    return chain(
        loss_kernel,
        scalars,
        [*slots, group_ids],
        [whole((part, model))] * len(slots) + [whole((count,))],
        [whole((1, 1)), whole((local, model))],
        [shaped((1, 1), F32), shaped((local, model), F32)],
        scratch=[pltpu.VMEM((count, model), F32)] * 2,
        name="loss",
        micros=3.8,
    )


def norm_back(upstream, normal, inverse, gain):
    scaled = upstream * gain
    return inverse * (scaled - rowmean(scaled) - normal * rowmean(scaled * normal))


def norm_two_kernel(s_ref, cot_ref, n_ref, inv_ref, gain_ref, pool_ref, df_ref, sum_ref):
    s = pl.program_id(0)
    normal = n_ref[...].astype(F32)
    live = lax.broadcasted_iota(jnp.int32, normal.shape, 0) < length_of(s_ref, s)
    up = cot_ref[...].astype(F32) + jnp.where(live, pool_ref[pl.ds(s, 1), :], 0.0)
    df = norm_back(up, normal, inv_ref[...], across(gain_ref)).astype(BF16)
    df_ref[...] = df

    @pl.when(s == 0)
    def _():
        sum_ref[...] = jnp.zeros_like(sum_ref)

    sum_ref[0:1, :] += colsum(df.astype(F32))
    sum_ref[1:2, :] += colsum(up * normal)
    sum_ref[2:3, :] += colsum(up)


def norm_two_backward(chain, scalars, cot, normal, inverse, gain, pool_cot):
    tokens, model = cot.shape
    return chain(
        norm_two_kernel,
        scalars,
        [cot, normal, inverse, gain, pool_cot],
        [by_rows(LEN, model), by_rows(LEN, model), by_rows(LEN, 1), whole(gain.shape), whole(pool_cot.shape)],
        [by_rows(LEN, model), whole((3, model))],
        [shaped((tokens, model)), shaped((3, model), F32)],
        grid=(tokens // LEN,),
        name="norm_two_bwd",
        micros=5.4,
    )


def unit_back_kernel(s_ref, df_ref, gp_ref, wd_ref, du_ref, sum_ref):
    @pl.when(pl.program_id(0) == 0)
    def _():
        sum_ref[...] = jnp.zeros_like(sum_ref)

    df = df_ref[...]
    chunk = wd_ref.shape[0] // 3
    for j in range(3):
        cols = slice(chunk * j, chunk * j + chunk)
        du = (nt(df, wd_ref[cols, :]) * gp_ref[:, cols].astype(F32)).astype(BF16)
        du_ref[:, cols] = du
        sum_ref[:, cols] += colsum(du.astype(F32))


def unit_backward(chain, scalars, df, gp, wd):
    tokens, model = df.shape
    units = gp.shape[1]
    block = 512
    return chain(
        unit_back_kernel,
        scalars,
        [df, gp, wd],
        [by_rows(block, model), by_rows(block, units), once(wd.shape)],
        [by_rows(block, units), whole((1, units))],
        [shaped((tokens, units)), shaped((1, units), F32)],
        grid=(tokens // block,),
        name="unit_bwd",
        micros=60.0,
        vmem=18,
    )


def middle_kernel(
    s_ref, df_ref, du_own, du_oth, wu_own, wu_oth, n_ref, inv_ref, gain_ref, wo_own, wo_oth,
    da_ref, sum_ref, dc_own, *dc_oth,
):
    @pl.when(pl.program_id(0) == 0)
    def _():
        sum_ref[...] = jnp.zeros_like(sum_ref)

    total = df_ref[...].astype(F32) + nt(du_oth[...], wu_oth[...]) + nt(du_own[...], wu_own[...])
    normal = n_ref[...].astype(F32)
    da = norm_back(total, normal, inv_ref[...], across(gain_ref)).astype(BF16)
    da_ref[...] = da
    dc_own[...] = nt(da, wo_own[...]).astype(BF16)
    at = 0
    for ref in dc_oth:
        width = ref.shape[1]
        ref[...] = nt(da, wo_oth[at : at + width, :]).astype(BF16)
        at += width
    sum_ref[0:1, :] += colsum(total * normal)
    sum_ref[1:2, :] += colsum(total)
    sum_ref[2:3, :] += colsum(da.astype(F32))


def middle_backward(
    chain, scalars, df, du_own, du_oth, wu_own, wu_oth, normal, inverse, gain, wo_own, wo_oth, widths
):
    tokens, model = df.shape
    units = wu_own.shape[1]
    block = 256
    return chain(
        middle_kernel,
        scalars,
        [df, du_own, du_oth, wu_own, wu_oth, normal, inverse, gain, wo_own, wo_oth],
        [by_rows(block, model), by_rows(block, units), by_rows(block, units)]
        + [once(wu_own.shape), once(wu_oth.shape), by_rows(block, model), by_rows(block, 1)]
        + [whole(gain.shape), once(wo_own.shape), once(wo_oth.shape)],
        [by_rows(block, model), whole((3, model))] + [by_rows(block, w) for w in widths],
        [shaped((tokens, model)), shaped((3, model), F32)] + [shaped((tokens, w)) for w in widths],
        grid=(tokens // block,),
        name="middle_bwd",
        micros=12.0,
        vmem=18,
    )


def bit(value, at):
    return (value >> at) & 1


def split_store(d, even, odd, keep_ref, send_ref, at):
    flip = bit(d, 0) == 0
    keep_ref[at] = jnp.where(flip, even, odd).astype(BF16)
    send_ref[at] = jnp.where(flip, odd, even).astype(BF16)


def dense_grad_kernel(d_ref, a_ref, b_ref, keep_ref, send_ref):
    d = d_ref[0]
    grad = tn(a_ref[...], b_ref[...])
    step = keep_ref.shape[3]
    for x in range(2):
        for z in range(2):
            at = (4 * z + 2 * x) * step
            split_store(
                d, grad[at : at + step], grad[at + step : at + 2 * step], keep_ref, send_ref,
                (x ^ bit(d, 1), z ^ bit(d, 2), 0),
            )


def dense_grad(chain, scalars, a, b, cut_left):
    tokens = a.shape[0]
    left = a.shape[1] // (2 if cut_left else 1)
    right = b.shape[1] // (1 if cut_left else 2)
    step = left // 8
    block = pl.BlockSpec((2, 2, 1, step, right), lambda i, s: (0, 0, i ^ bit(s[0], 3), 0, 0))
    return chain(
        dense_grad_kernel,
        scalars,
        [a, b],
        [
            pl.BlockSpec((tokens, left), lambda i, s: (0, i)) if cut_left else once(a.shape),
            once(b.shape) if cut_left else pl.BlockSpec((tokens, right), lambda i, s: (0, i)),
        ],
        [block, block],
        [shaped((2, 2, 2, step, right))] * 2,
        grid=(2,),
        name="dense_grad",
        micros=60.0,
        vmem=15,
    )


def heads_grad_kernel(d_ref, x_ref, da_ref, two_ref, one_ref, unit_ref, *refs):
    *refs, keep_ref, send_ref = refs
    count = len(refs) // 3
    c_refs, dqkv_refs, bias_refs = refs[:count], refs[count : 2 * count], refs[2 * count :]
    d = d_ref[0]
    bias = jnp.concatenate([ref[...] for ref in bias_refs], axis=1)
    width = bias.shape[1]
    out = jnp.concatenate([tn(ref[...], da_ref[...]) for ref in c_refs], axis=0)
    projs = [tn(x_ref[...], ref[...]) for ref in dqkv_refs]
    proj = jnp.concatenate(
        [p[:, c * (p.shape[1] // 3) : (c + 1) * (p.shape[1] // 3)] for c in range(3) for p in projs], axis=1
    )
    step = proj.shape[0] // 16
    small = [ref[i : i + 1, at : at + width] for ref in (two_ref, one_ref) for i in range(3) for at in (0, width)]
    small += [bias[0:1, :], bias[1:2, :]]
    small += [unit_ref[:, at : at + width] for at in range(0, unit_ref.shape[1], width)]
    small += [jnp.zeros((1, width), F32)] * (32 - len(small))
    rest = jnp.zeros((14, width), F32)

    def block(b):
        row, col = (b & 7) * step, (b >> 3) * width
        pieces = [out[row : row + step, col : col + width]]
        pieces += [proj[b * step : b * step + step, c * width : c * width + width] for c in range(3)]
        return jnp.concatenate(pieces + [small[b], small[16 + b], rest], axis=0)

    for x in range(2):
        for z in range(2):
            for w in range(2):
                b = 8 * w + 4 * z + 2 * x
                split_store(
                    d, block(b), block(b + 1), keep_ref, send_ref,
                    (x ^ bit(d, 1), z ^ bit(d, 2), w ^ bit(d, 3)),
                )


def heads_grad(chain, scalars, x, da, sums, contexts, dqkvs, biases):
    width = sum(b.shape[1] for b in biases)
    full = (2, 2, 2, width // 2 + 16, width)
    inputs = [x, da, *sums, *contexts, *dqkvs, *biases]
    return chain(
        heads_grad_kernel,
        scalars,
        inputs,
        [once(a.shape) for a in inputs],
        [whole(full), whole(full)],
        [shaped(full)] * 2,
        name="heads_grad",
        micros=60.0,
        vmem=21,
    )


def input_grad_kernel(s_ref, da_ref, *refs):
    *refs, out_ref = refs
    total = da_ref[...].astype(F32)
    for grad, w in zip(refs[: len(refs) // 2], refs[len(refs) // 2 :], strict=True):
        total = total + nt(grad[...], jnp.concatenate([w[c] for c in range(3)], axis=1))
    out_ref[...] = total


def input_grad(chain, scalars, da, grads, weights):
    tokens, model = da.shape
    block = 512
    return chain(
        input_grad_kernel,
        scalars,
        [da, *grads, *weights],
        [by_rows(block, model)] + [by_rows(block, g.shape[1]) for g in grads] + [once(w.shape) for w in weights],
        [by_rows(block, model)],
        [shaped((tokens, model), F32)],
        grid=(tokens // block,),
        name="input_grad",
        token=True,
        micros=60.0,
        vmem=18,
    )[0]


def place_kernel(s_ref, a0, a1, b0, b1, *out_refs, kind):
    d = s_ref[0]
    half = pl.program_id(0)
    flip = bit(d, 0) == 0
    for x, (near_ref, far_ref) in enumerate(((a0, b0), (a1, b1))):
        for z in range(2):
            near, far = near_ref[z, 0].astype(F32), far_ref[z, 0].astype(F32)
            low = (x ^ bit(d, 1)) + 2 * (z ^ bit(d, 2))
            for side, rows in enumerate((jnp.where(flip, near, far), jnp.where(flip, far, near))):
                if kind != "heads":
                    step = rows.shape[0]
                    out_refs[0][low, side * step : (side + 1) * step] = rows
                    continue
                out_ref, proj_ref, *vec_refs, unit_ref, small_ref = out_refs
                step = out_ref.shape[1] // 2
                out_ref[low, side * step : (side + 1) * step] = rows[:step]
                for c in range(3):
                    proj_ref[c, low, side * step : (side + 1) * step] = rows[(c + 1) * step : (c + 2) * step]
                b = 2 * (low + 4 * (half ^ bit(d, 3))) + side
                small_ref[pl.ds(b, 1), :] = rows[4 * step : 4 * step + 1]
                small_ref[pl.ds(16 + b, 1), :] = rows[4 * step + 1 : 4 * step + 2]
    if kind != "heads":
        return

    @pl.when(half == 1)
    def _():
        line = lambda at, count: jnp.concatenate([small_ref[i : i + 1, :] for i in range(at, at + count)], axis=1)
        for i, ref in enumerate(vec_refs[:6]):
            ref[...] = line(2 * i, 2).reshape(ref.shape[0])
        vec_refs[6][...] = small_ref[12:14, :]
        unit_ref[...] = line(14, unit_ref.shape[0] // small_ref.shape[1]).reshape(unit_ref.shape[0])


def place(chain, scalars, pieces, kind, units):
    step, cols = pieces[0].shape[2:]
    block = pl.BlockSpec((2, 1, step, cols), lambda w, s: (0, w, 0, 0))
    high = lambda w, s: w ^ bit(s[0], 3)
    scratch = []
    if kind == "down":
        shapes = [(8, 2 * step, cols)]
        specs = [pl.BlockSpec((4, 2 * step, cols), lambda w, s: (high(w, s), 0, 0))]
    elif kind == "up":
        shapes = [(4, 2 * step, 2 * cols)]
        specs = [pl.BlockSpec((4, 2 * step, cols), lambda w, s: (0, 0, high(w, s)))]
    else:
        part = (step - 16) // 4
        shapes = [(4, 2 * part, 2 * cols), (3, 8, 2 * part, cols)]
        specs = [
            pl.BlockSpec((4, 2 * part, cols), lambda w, s: (0, 0, high(w, s))),
            pl.BlockSpec((3, 4, 2 * part, cols), lambda w, s: (0, high(w, s), 0, 0)),
        ]
        vectors = [(2 * cols,)] * 6 + [(2, cols), (units,)]
        shapes += vectors
        specs += [whole(v) for v in vectors]
        scratch = [pltpu.VMEM((32, cols), F32)]
    return chain(
        functools.partial(place_kernel, kind=kind),
        scalars,
        pieces,
        [block] * 4,
        specs,
        [shaped(s, F32) for s in shapes],
        grid=(2,),
        scratch=scratch,
        name="place",
        token=True,
        micros=4.0,
        vmem=18,
    )


def swap(x, axis, mask):
    size = lax.axis_size(axis)
    return lax.ppermute(x, axis, [(i, i ^ mask) for i in range(size)])


def swap_all(x, mask):
    size = lax.axis_size("dp") * lax.axis_size("tensor")
    return lax.ppermute(x, ("dp", "tensor"), [(i, i ^ mask) for i in range(size)])


def levels():
    return lax.axis_size("dp").bit_length() - 1


def flip_kernel(s_ref, a_ref, b_ref, out_ref):
    for i in range(2):
        out_ref[i] = (a_ref[i].astype(F32) + b_ref[1 - i].astype(F32)).astype(BF16)


def add_flipped(chain, scalars, a, b):
    return chain(
        flip_kernel,
        scalars,
        [a, b],
        [whole(a.shape)] * 2,
        [whole(a.shape)],
        [shaped(a.shape)],
        name="add",
        micros=2.0,
    )[0]


def sum_kernel(s_ref, *refs, count, early):
    total = refs[0][...].astype(F32) + refs[1][...].astype(F32)
    if early:
        total = total.astype(BF16).astype(F32)
    for ref in refs[2:count]:
        total = total + ref[...].astype(F32)
    total = total.astype(BF16)
    outs = refs[count:]
    if len(outs) == 1:
        outs[0][...] = total
        return
    for i, out in enumerate(outs):
        out[...] = total[i]


def add(chain, scalars, terms, split=1, early=False):
    shape = terms[0].shape
    outs = [shape] if split == 1 else [shape[1:]] * split
    return chain(
        functools.partial(sum_kernel, count=len(terms), early=early),
        scalars,
        terms,
        [whole(shape)] * len(terms),
        [whole(o) for o in outs],
        [shaped(o) for o in outs],
        name="add",
        micros=2.0,
    )


def join_kernel(s_ref, *refs):
    for i, ref in enumerate(refs[:-1]):
        refs[-1][i] = ref[...]


def join(chain, scalars, parts):
    shape = (len(parts),) + parts[0].shape
    return chain(
        join_kernel,
        scalars,
        parts,
        [whole(p.shape) for p in parts],
        [whole(shape)],
        [shaped(shape)],
        name="join",
        micros=1.5,
    )[0]


class Reduction:
    def __init__(self, chain, scalars):
        self.chain, self.scalars = chain, scalars

    def add(self, terms, split=1, early=False):
        return add(self.chain, self.scalars, terms, split, early)

    def send(self, x, axis, mask):
        return self.chain.send(x, axis, mask)

    def receive(self, sent):
        return self.chain.receive(self.scalars, sent)

    def other(self, keep, send):
        self.keep_oth, self.got_oth = keep, self.send(send, "dp", 1)

    def own(self, keep, send):
        self.keep_own, self.got_own = keep, self.send(send, "dp", 1)

    def across(self):
        (total,) = self.add([self.keep_oth, self.receive(self.got_oth)])
        self.got_y = self.send(total, "tensor", 1)

    def along_x(self):
        got = [self.receive(self.got_own), self.receive(self.got_y)]
        self.keep, send = self.add([self.keep_own, *got], 2, True)
        self.got = self.send(send, "dp", 2)

    def along_z(self):
        shape = self.keep.shape
        flat = (4,) + shape[2:]
        got = self.receive(self.got)
        self.keep, *send = self.add([self.keep.reshape(flat), got.reshape(flat)], 4)
        self.got = [self.send(x, "dp", m) for x, m in zip(send, (8, 4, 12), strict=True)]

    def back_z(self):
        (total,) = self.add([self.keep, *(self.receive(g) for g in self.got)])
        for at in range(4, levels()):
            got = self.receive(self.send(total, "dp", 1 << at))
            (total,) = self.add([total, got])
        self.total = total
        self.got = [self.send(total, "dp", m) for m in (8, 4, 12)]

    def back_x_direct(self):
        near = join(self.chain, self.scalars, [self.total, *(self.receive(g) for g in self.got)])
        self.near = near.reshape((2, 2) + near.shape[1:])
        self.got = self.send(self.near, "dp", 2)
        self.near_far = self.send(self.near, "dp", 1)

    def along_z0(self):
        self.keep, send = self.add([self.keep, self.receive(self.got)], 2)
        self.got = self.send(send, "dp", 4)

    def turn(self):
        (self.total,) = self.add([self.keep, self.receive(self.got)])
        for at in range(4, levels()):
            got = self.receive(self.send(self.total, "dp", 1 << at))
            (self.total,) = self.add([self.total, got])
        self.got = self.send(self.total, "dp", 8)

    def back_z0(self):
        self.total = add_flipped(self.chain, self.scalars, self.total, self.receive(self.got))
        self.got = self.send(self.total, "dp", 4)

    def back_x(self):
        self.near = join(self.chain, self.scalars, [self.total, self.receive(self.got)])
        self.got = self.send(self.near, "dp", 2)
        self.near_far = self.send(self.near, "dp", 1)

    def back_core(self, gated=True):
        self.next = self.receive(self.got)
        if gated:
            self.next = self.chain.gate(self.scalars, self.next)
        self.next_far = self.send(self.next, "dp", 1)

    def place(self, kind, units=0):
        pieces = [self.near, self.next, self.receive(self.near_far), self.receive(self.next_far)]
        return place(self.chain, self.scalars, pieces, kind, units)


def stack_rows_kernel(s_ref, *refs):
    step = refs[0].shape[0]
    for i, ref in enumerate(refs[:-1]):
        refs[-1][i * step : (i + 1) * step, :] = ref[...]


def stack_rows(chain, scalars, parts):
    shape = (len(parts) * parts[0].shape[0], parts[0].shape[1])
    return chain(
        stack_rows_kernel,
        scalars,
        parts,
        [whole(p.shape) for p in parts],
        [whole(shape)],
        [shaped(shape, F32)],
        name="stack_rows",
        micros=10.0,
    )[0]


def gather_pooled(chain, scalars, pooled):
    bits = levels() + 1
    at = 0
    while at < bits:
        step = min(1 if at == 2 else 2, bits - at)
        parts = [pooled] + [swap_all(pooled, m << at) for m in range(1, 1 << step)]
        chain.pause(scalars)
        at += step
        if at < bits:
            pooled = stack_rows(chain, scalars, parts)
    return parts


def cut_kernel(s_ref, *refs):
    count = len(refs) // 2
    for a_ref, out_ref in zip(refs[:count], refs[count:], strict=True):
        out_ref[...] = a_ref[...].reshape(out_ref.shape)


def cut(chain, scalars, *cuts):
    shapes = [tuple(b for b in block if b != 1) for _, block, _ in cuts]
    at = lambda index: lambda i, s: index(s[0] & 3)
    return chain(
        cut_kernel,
        scalars,
        [a for a, _, _ in cuts],
        [pl.BlockSpec(block, at(index)) for _, block, index in cuts],
        [whole(s) for s in shapes],
        [shaped(s, a.dtype) for s, (a, _, _) in zip(shapes, cuts, strict=True)],
        name="cut",
        micros=1.0,
    )


def cut_heads_kernel(s_ref, a_ref, out_ref):
    out_ref[...] = a_ref[:, 0, :, : out_ref.shape[2]]


def cut_heads(chain, scalars, a, width):
    _, _, part, full = a.shape
    shape = (3, part, width)
    return chain(
        cut_heads_kernel,
        scalars,
        [a],
        [pl.BlockSpec((3, 1, part, full), lambda i, s: (0, bit(s[0], 0), 0, 0))],
        [whole(shape)],
        [shaped(shape)],
        name="cut",
        micros=1.0,
    )[0]


def cut_pack_kernel(s_ref, a_ref, w_ref, bias_ref, unit_ref, out_ref, small_ref):
    part = a_ref.shape[2]
    width = out_ref.shape[1]
    rows, cols = w_ref.shape[1:]
    for c in range(3):
        out_ref[c * part : (c + 1) * part, :] = a_ref[c, 0, :, a_ref.shape[3] - width :]
    for k in range(cols // width):
        begin = 3 * part + k * rows
        out_ref[begin : begin + rows, :] = w_ref[0, :, k * width : (k + 1) * width]
    full = bias_ref.shape[1]
    small_ref[0:2, :] = bias_ref[...]
    unit = across(unit_ref)
    for i in range(unit.shape[1] // full):
        small_ref[2 + i : 3 + i, :] = unit[:, i * full : (i + 1) * full]


def cut_pack(chain, scalars, a, width, w, bias, unit):
    _, _, part, full = a.shape
    _, rows, cols = w.shape
    shapes = [shaped((3 * part + rows * cols // width, width)), shaped((2 + unit.shape[0] // full, full), F32)]
    return chain(
        cut_pack_kernel,
        scalars,
        [a, w, bias, unit],
        [
            pl.BlockSpec((3, 1, part, full), lambda i, s: (0, bit(s[0], 0), 0, 0)),
            pl.BlockSpec((1, rows, cols), lambda i, s: (bit(s[0], 0), 0, 0)),
            whole(bias.shape),
            whole(unit.shape),
        ],
        [whole(s.shape) for s in shapes],
        shapes,
        name="cut",
        micros=1.0,
    )


class Gather:
    def __init__(self, chain, scalars, piece, relayed=False):
        self.chain, self.scalars, self.relayed = chain, scalars, relayed
        self.got = chain.send(piece, "tensor", 1)
        self.parts = []

    def hand_over(self):
        part = self.chain.gate(self.scalars, self.chain.receive(self.scalars, self.got))
        if self.relayed and not self.parts:
            self.got = self.chain.send(part, "dp", 2)
        self.parts += [part, self.chain.send(part, "dp", 1)]

    def slots(self):
        return [self.slot(i) for i in range(len(self.parts))]

    def slot(self, i):
        return self.parts[i] if i % 2 == 0 else self.chain.receive(self.scalars, self.parts[i])


def per_device(
    layer_input, w_qkv, bias_qv, w_out, b_out, gain_one, shift_one, w_up, b_up, w_down, b_down,
    gain_two, shift_two, out_cot, lengths, group_ids,
):
    tensor_size = lax.axis_size("tensor")
    position = lax.axis_index("tensor")
    d = lax.axis_index("dp")
    model = layer_input.shape[1]
    width = w_qkv.shape[2]
    units = w_up.shape[1]
    local = lengths.shape[0] // tensor_size
    rank = d * tensor_size + position
    scal = jnp.concatenate([jnp.stack([d, rank, position * local]).astype(jnp.int32), lengths])
    chain = Chain()

    heads_cut = w_qkv.reshape(3, 2, model // 2, width)
    lead = width // 3 * 2
    gather_lead = Gather(chain, scal, cut_heads(chain, scal, heads_cut, lead))
    qkv_own, c_own, lse_own = attn_forward(chain, scal, layer_input, [w_qkv], bias_qv)
    piece, bias = cut_pack(
        chain, scal, heads_cut, width - lead, w_out.reshape(2, width // 2, model), bias_qv, b_up
    )
    gather_pack = Gather(chain, scal, piece)
    bias_oth = swap(bias, "tensor", 1)
    part = units // 4
    piece, second = cut(
        chain,
        scal,
        (w_up, (model, part), lambda q: (0, q)),
        (w_down.reshape(2, 2 * part, model), (1, 2 * part, model), lambda q: (q & 1, 0, 0)),
    )
    gather_up = Gather(chain, scal, piece, relayed=True)
    gather_down = Gather(chain, scal, second)
    gather_lead.hand_over()
    qkv_lead, c_lead, lse_lead, wq_lead = attn_forward(chain, scal, layer_input, gather_lead.slots(), bias_oth)
    gather_pack.hand_over()
    qkv_rest, c_rest, lse_rest, wq_rest, wo_oth = attn_forward(
        chain, scal, layer_input, gather_pack.slots(), bias_oth, lead, width
    )
    wq_lead, wq_rest = (w.reshape(3, model, w.shape[3]) for w in (wq_lead, wq_rest))
    wo_oth = wo_oth.reshape(width, model)
    h1, h1_low, normal_one, inverse_one = project_forward(
        chain, scal, layer_input, [c_own, c_lead, c_rest], w_out, wo_oth, [b_out, gain_one, shift_one]
    )
    gather_up.hand_over()
    g_own, gp_own, f_own = feed_own(chain, scal, h1_low, w_up, b_up, w_down)
    gather_up.hand_over()
    near, far = gather_up.slot(0), gather_up.slot(1)
    half = feed_up(chain, scal, h1_low, near, far, bias_oth)
    gather_down.hand_over()
    near, far = gather_up.slot(2), gather_up.slot(3)
    g_oth, gp_oth, wu_oth = feed_up(chain, scal, h1_low, near, far, bias_oth, half)
    output, normal_two, inverse_two, pooled, wd_oth = feed_down(
        chain, scal, g_oth, h1, f_own, gather_down.slots(), [b_down, gain_two, shift_two]
    )
    wd_oth = wd_oth.reshape(units, model)

    loss, pool_cot = loss_call(chain, scal, gather_pooled(chain, scal, pooled), group_ids, local)

    down, up, heads = (Reduction(chain, scal) for _ in range(3))
    df, sums_two = norm_two_backward(chain, scal, out_cot, normal_two, inverse_two, gain_two, pool_cot)
    down.other(*dense_grad(chain, scal, g_oth, df, True))
    down.own(*dense_grad(chain, scal, g_own, df, True))
    down.across()
    du_oth, sums_du_oth = unit_backward(chain, scal, df, gp_oth, wd_oth)
    du_own, sums_du_own = unit_backward(chain, scal, df, gp_own, w_down)
    up.other(*dense_grad(chain, scal, h1_low, du_oth, False))
    up.own(*dense_grad(chain, scal, h1_low, du_own, False))
    up.across()
    da, sums_one, dc_own, dc_lead, dc_rest = middle_backward(
        chain, scal, df, du_own, du_oth, w_up, wu_oth, normal_one, inverse_one, gain_one, w_out, wo_oth,
        [width, lead, width - lead],
    )
    down.along_x()
    dqkv_lead, sums_lead = attn_backward(chain, scal, qkv_lead, dc_lead, lse_lead)
    dqkv_rest, sums_rest = attn_backward(chain, scal, qkv_rest, dc_rest, lse_rest)
    sums = [sums_two, sums_one, sums_du_oth]
    heads.other(
        *heads_grad(
            chain, scal, layer_input, da, sums, [c_lead, c_rest], [dqkv_lead, dqkv_rest], [sums_lead, sums_rest]
        )
    )
    down.along_z0()
    up.along_x()
    chain.pause(scal)
    heads.across()
    dqkv_own, sums_own = attn_backward(chain, scal, qkv_own, dc_own, lse_own)
    down.turn()
    up.along_z0()
    sums = [sums_two, sums_one, sums_du_own]
    heads.own(*heads_grad(chain, scal, layer_input, da, sums, [c_own], [dqkv_own], [sums_own]))
    grad_input = input_grad(
        chain, scal, da, [dqkv_own, dqkv_lead, dqkv_rest], [w_qkv, wq_lead, wq_rest]
    )
    down.back_z0()
    heads.along_x()
    up.turn()
    chain.pause(scal)
    down.back_x()
    heads.along_z0()
    chain.pause(scal)
    heads.turn()
    up.back_z0()
    chain.pause(scal)
    heads.back_z0()
    up.back_x()
    chain.pause(scal)
    down.back_core()
    (grad_w_down,) = down.place("down")
    up.back_core()
    heads.back_x()
    chain.pause(scal)
    (grad_w_up,) = up.place("up")
    heads.back_core(False)
    chain.pause(scal)
    grad_w_out, grad_w_qkv, *grads, grad_bias_qv, grad_b_up = heads.place("heads", units)
    grad_b_down, grad_gain_two, grad_shift_two, grad_gain_one, grad_shift_one, grad_b_out = grads
    return (
        loss.reshape(()),
        output,
        grad_input,
        grad_w_qkv.reshape(w_qkv.shape),
        grad_bias_qv,
        grad_w_out.reshape(w_out.shape),
        grad_b_out,
        grad_gain_one,
        grad_shift_one,
        grad_w_up.reshape(w_up.shape),
        grad_b_up,
        grad_w_down.reshape(w_down.shape),
        grad_b_down,
        grad_gain_two,
        grad_shift_two,
    )


def solution(mesh):
    rows = P(("dp", "tensor"), None)
    in_specs = (
        rows,
        P(None, None, "tensor"),
        P(None, "tensor"),
        P("tensor", None),
        P(),
        P(),
        P(),
        P(None, "tensor"),
        P("tensor"),
        P("tensor", None),
        P(),
        P(),
        P(),
        rows,
        P("dp"),
        P(),
    )
    out_specs = (
        P(),
        rows,
        rows,
        P(None, None, "tensor"),
        P(None, "tensor"),
        P("tensor", None),
        P(),
        P(),
        P(),
        P(None, "tensor"),
        P("tensor"),
        P("tensor", None),
        P(),
        P(),
        P(),
    )
    return jax.shard_map(
        per_device, mesh=mesh, in_specs=in_specs, out_specs=out_specs, check_vma=False
    )
```

```python
import functools

import jax
import jax.numpy as jnp
from jax import lax
from jax.experimental import pallas as pl
from jax.experimental.pallas import tpu as pltpu
from jax.sharding import PartitionSpec as P

HD = 64
LEN = 512
LANES = 128
EPS_NORM = 1e-12
EPS_UNIT = 1e-6
SOFTMAX_TEMP = 20.0
MASKED = -1e30
F32 = jnp.float32
BF16 = jnp.bfloat16
COST_SCALE = 0.9

ERFC_SLOPE = 0.41 * 0.7071067811865476
ERFC_POLY = tuple(
    0.5 * c
    for c in (
        0.23389259840606333,
        0.19943405568812744,
        0.36527628560337355,
        -0.195943508470611,
        0.5767329065489298,
        -0.17939241407306944,
    )
)
INV_SQRT_2PI = 0.3989422804014327


def cost(micros):
    return pl.CostEstimate(
        flops=int(micros * COST_SCALE * 1.15e9),
        bytes_accessed=int(micros * COST_SCALE * 3.6e6),
        transcendentals=0,
    )


def whole(shape):
    return pl.BlockSpec(shape, lambda *_: (0,) * len(shape))


def once(shape):
    return pl.BlockSpec(shape, lambda *_: (0,) * len(shape), pipeline_mode=pl.Buffered(1))


def shaped(shape, dtype=BF16):
    return jax.ShapeDtypeStruct(shape, dtype)


class Chain:
    def __init__(self):
        self.last = None
        self.windows = 0

    def __call__(self, kernel, scalars, inputs, in_specs, out_specs, out_shape, *, name, micros,
                 grid=(1,), scratch=(), vmem=16, token=False, aliases=None):
        deps = [] if self.last is None else [self.last]
        count = len(inputs)

        given = len(out_shape)
        if token:
            out_specs = list(out_specs) + [pl.BlockSpec(memory_space=pl.ANY)]
            out_shape = list(out_shape) + [shaped((8, LANES), F32)]

        def body(s_ref, *refs):
            rest = refs[count + len(deps) :]
            kernel(s_ref, *refs[:count], *rest[:given], *rest[len(out_shape) :])

        outs = pl.pallas_call(
            body,
            grid_spec=pltpu.PrefetchScalarGridSpec(
                num_scalar_prefetch=1,
                grid=grid,
                in_specs=list(in_specs) + [pl.BlockSpec(memory_space=pl.ANY)] * len(deps),
                out_specs=out_specs,
                scratch_shapes=list(scratch),
            ),
            out_shape=out_shape,
            input_output_aliases=aliases or {},
            compiler_params=pltpu.CompilerParams(vmem_limit_bytes=vmem * 2**20),
            cost_estimate=cost(micros),
            name=name,
        )(scalars, *inputs, *deps)
        self.last = outs[-1] if token else outs[0]
        if micros >= 3:
            self.windows += 1
        return outs[:given]

    def gate(self, scalars, a):
        def kernel(s_ref, a_ref, out_ref):
            out_ref[...] = a_ref[...]

        return self(
            kernel, scalars, [a], [whole(a.shape)], [whole(a.shape)], [shaped(a.shape, a.dtype)],
            name="gate", micros=10.0,
        )[0]

    def send(self, x, axis, mask):
        return swap(x, axis, mask), self.windows

    def receive(self, scalars, sent):
        if sent[1] == self.windows:
            self.pause(scalars)
        return sent[0]

    def pause(self, scalars):
        def kernel(s_ref, out_ref):
            out_ref[...] = jnp.zeros_like(out_ref)

        tile = (8, LANES)
        self(kernel, scalars, [], [], [whole(tile)], [shaped(tile, F32)], name="pause", micros=30.0)


def nn(a, b):
    return lax.dot_general(a, b, (((1,), (0,)), ((), ())), preferred_element_type=F32)


def nt(a, b):
    return lax.dot_general(a, b, (((1,), (1,)), ((), ())), preferred_element_type=F32)


def tn(a, b):
    return lax.dot_general(a, b, (((0,), (0,)), ((), ())), preferred_element_type=F32)


def colsum(a):
    return jnp.sum(a, axis=0, keepdims=True)


def rowmean(a):
    return jnp.mean(a, axis=-1, keepdims=True)


def gelu_pair(u):
    den = 1.0 + ERFC_SLOPE * jnp.abs(u)
    t = pl.reciprocal(den, approx=True)
    t = t * (2.0 - den * t)
    poly = ERFC_POLY[-1]
    for c in ERFC_POLY[-2::-1]:
        poly = poly * t + c
    bell = jnp.exp(-0.5 * (u * u))
    tail = bell * (poly * t)
    cdf = jnp.where(u >= 0, 1.0 - tail, tail)
    return u * cdf, cdf + (u * bell) * INV_SQRT_2PI


def length_of(s_ref, sentence):
    return s_ref[3 + s_ref[2] + sentence]


def attend_sentence(length, x, weights, bq, bv, qkv_ref, c_ref, lse_ref):
    rows = x.shape[0]
    width = c_ref.shape[1]
    both = nn(x, jnp.concatenate(weights, axis=1))
    qkv_ref[:, :width] = (both[:, :width] + bq).astype(BF16)
    qkv_ref[:, width : 2 * width] = both[:, width : 2 * width].astype(BF16)
    qkv_ref[:, 2 * width :] = (both[:, 2 * width :] + bv).astype(BF16)
    low = lax.broadcasted_iota(jnp.int32, (rows, LANES), 1) < HD
    live = lax.broadcasted_iota(jnp.int32, (rows, LANES), 0) < length
    bias = jnp.where(live, 0.0, MASKED).astype(F32)
    zero = jnp.zeros((rows, LANES), BF16)
    for p in range(width // LANES):
        at = LANES * p
        q = qkv_ref[:, at : at + LANES] * 0.125
        k = qkv_ref[:, width + at : width + at + LANES]
        v = qkv_ref[:, 2 * width + at : 2 * width + at + LANES]
        vt = v.T
        outs = []
        for h in range(2):
            km = jnp.where(low, k, zero) if h == 0 else jnp.where(low, zero, k)
            scores = nt(km, q)
            parts, tops, sums = [], [], []
            for j in range(rows // LANES):
                piece = scores[:, LANES * j : LANES * j + LANES] + bias
                top = jnp.max(piece, axis=0, keepdims=True)
                e = jnp.exp(piece - top)
                parts.append(e.astype(BF16))
                tops.append(top)
                sums.append(colsum(e))
            top = jnp.concatenate(tops, axis=1)
            total = jnp.concatenate(sums, axis=1)
            ct = nn(vt[HD * h : HD * h + HD], jnp.concatenate(parts, axis=1))
            outs.append(ct / total)
            lse_ref[0, 2 * p + h : 2 * p + h + 1, :] = top + jnp.log(total)
        c_ref[:, at : at + LANES] = jnp.concatenate(outs, axis=0).T.astype(BF16)


def attn_own_kernel(s_ref, x_ref, w_ref, b_ref, qkv_ref, c_ref, lse_ref):
    weights = [w_ref[c] for c in range(3)]
    length = length_of(s_ref, pl.program_id(0))
    attend_sentence(
        length, x_ref[...], weights, b_ref[0:1, :], b_ref[1:2, :], qkv_ref, c_ref, lse_ref
    )


def attn_other_kernel(s_ref, x_ref, w0, w1, b_ref, qkv_ref, c_ref, lse_ref, w_ref, *, at):
    @pl.when(pl.program_id(0) == 0)
    def _():
        for s, ref in enumerate((w0, w1)):
            for c in range(3):
                w_ref[c, bit(s_ref[0], 0) ^ s] = ref[c]

    shape = w_ref.shape
    weights = [w_ref[c].reshape(shape[1] * shape[2], shape[3]) for c in range(3)]
    length = length_of(s_ref, pl.program_id(0))
    cols = slice(at, at + shape[3])
    attend_sentence(
        length, x_ref[...], weights, b_ref[0:1, cols], b_ref[1:2, cols], qkv_ref, c_ref, lse_ref
    )


def attn_pack_kernel(s_ref, x_ref, p0, p1, b_ref, qkv_ref, c_ref, lse_ref, w_ref, out_ref, *, at):
    _, _, half, width = w_ref.shape

    @pl.when(pl.program_id(0) == 0)
    def _():
        rows, cols = out_ref.shape[1:]
        for s, ref in enumerate((p0, p1)):
            place = bit(s_ref[0], 0) ^ s
            for c in range(3):
                w_ref[c, place] = ref[c * half : (c + 1) * half, :]
            for k in range(cols // width):
                begin = 3 * half + k * rows
                out_ref[place, :, k * width : (k + 1) * width] = ref[begin : begin + rows, :]

    weights = [w_ref[c].reshape(2 * half, width) for c in range(3)]
    length = length_of(s_ref, pl.program_id(0))
    cols = slice(at, at + width)
    attend_sentence(
        length, x_ref[...], weights, b_ref[0:1, cols], b_ref[1:2, cols], qkv_ref, c_ref, lse_ref
    )


def by_rows(block, cols):
    return pl.BlockSpec((block, cols), lambda i, *_: (i, 0))


def attn_forward(chain, scalars, x, weights, bias, at=0, out_rows=0):
    tokens, model = x.shape
    width = weights[0].shape[-1]
    sents = tokens // LEN
    out_specs = [
        by_rows(LEN, 3 * width),
        by_rows(LEN, width),
        pl.BlockSpec((1, width // HD, LEN), lambda s, l: (s, 0, 0)),
    ]
    out_shape = [
        shaped((tokens, 3 * width)),
        shaped((tokens, width)),
        shaped((sents, width // HD, LEN), F32),
    ]
    own = len(weights) == 1
    extra = [] if own else [(3, 2, model // 2, width)] + ([(2, out_rows // 2, model)] if out_rows else [])
    out_specs += [whole(full) for full in extra]
    out_shape += [shaped(full) for full in extra]
    kernel = attn_pack_kernel if out_rows else attn_other_kernel
    return chain(
        attn_own_kernel if own else functools.partial(kernel, at=at),
        scalars,
        [x, *weights, bias],
        [by_rows(LEN, model)] + [once(w.shape) for w in weights] + [whole(bias.shape)],
        out_specs,
        out_shape,
        grid=(sents,),
        name="attn_fwd",
        micros=8.8,
        vmem=18,
    )


def attn_back_kernel(s_ref, qkv_ref, do_ref, lse_ref, grad_ref, sum_ref):
    s = pl.program_id(0)
    length = length_of(s_ref, s)
    rows, width = do_ref.shape
    low = lax.broadcasted_iota(jnp.int32, (rows, LANES), 1) < HD
    live = lax.broadcasted_iota(jnp.int32, (rows, LANES), 0) < length
    bias = jnp.where(live, 0.0, MASKED).astype(F32)
    zero = jnp.zeros((rows, LANES), BF16)

    @pl.when(s == 0)
    def _():
        sum_ref[...] = jnp.zeros_like(sum_ref)

    for p in range(width // LANES):
        at = LANES * p
        q = qkv_ref[:, at : at + LANES] * 0.125
        k = qkv_ref[:, width + at : width + at + LANES]
        v = qkv_ref[:, 2 * width + at : 2 * width + at + LANES]
        do = do_ref[:, at : at + LANES]
        kt = k.T
        dqs, dks, dvs = [], [], []
        for h in range(2):
            km = jnp.where(low, k, zero) if h == 0 else jnp.where(low, zero, k)
            vm = jnp.where(low, v, zero) if h == 0 else jnp.where(low, zero, v)
            lse = lse_ref[0, 2 * p + h : 2 * p + h + 1, :]
            scores = nt(km, q)
            dprob = nt(vm, do)
            probs, dscores = [], []
            for j in range(rows // LANES):
                cols = slice(LANES * j, LANES * j + LANES)
                e = jnp.exp(scores[:, cols] + bias - lse[:, cols])
                probs.append(e.astype(BF16))
                dp = dprob[:, cols]
                dscores.append((e * (dp - colsum(e * dp))).astype(BF16))
            prob = jnp.concatenate(probs, axis=1)
            dscore = jnp.concatenate(dscores, axis=1)
            dvs.append(nn(prob, do))
            dks.append(nn(dscore, q))
            dqs.append(nn(kt[HD * h : HD * h + HD], dscore))
        dq = (jnp.concatenate(dqs, axis=0).T * 0.125).astype(BF16)
        dk = jnp.where(low, dks[0], dks[1]).astype(BF16)
        dv = jnp.where(low, dvs[0], dvs[1]).astype(BF16)
        grad_ref[:, at : at + LANES] = dq
        grad_ref[:, width + at : width + at + LANES] = dk
        grad_ref[:, 2 * width + at : 2 * width + at + LANES] = dv
        sum_ref[0:1, at : at + LANES] += colsum(dq.astype(F32))
        sum_ref[1:2, at : at + LANES] += colsum(dv.astype(F32))


def attn_backward(chain, scalars, qkv, do, lse):
    tokens, width = do.shape
    return chain(
        attn_back_kernel,
        scalars,
        [qkv, do, lse],
        [
            by_rows(LEN, 3 * width),
            by_rows(LEN, width),
            pl.BlockSpec((1, width // HD, LEN), lambda s, l: (s, 0, 0)),
        ],
        [by_rows(LEN, 3 * width), whole((2, width))],
        [shaped((tokens, 3 * width)), shaped((2, width), F32)],
        grid=(tokens // LEN,),
        name="attn_bwd",
        micros=12.6,
        vmem=18,
    )


def across(ref):
    return ref[...].reshape(1, ref.shape[0])


def normalize(r):
    center = r - rowmean(r)
    inverse = lax.rsqrt(rowmean(center * center) + EPS_NORM)
    return center * inverse, inverse


def project_kernel(s_ref, x_ref, *refs, count):
    c_refs, refs = refs[:count], refs[count:]
    w_own, other, bias_ref, gain_ref, shift_ref, h_ref, low_ref, n_ref, inv_ref = refs
    attended = nn(c_refs[0][...], w_own[...]) + across(bias_ref)
    at = 0
    for ref in c_refs[1:]:
        width = ref.shape[1]
        attended = attended + nn(ref[...], other[at : at + width, :])
        at += width
    normal, inverse = normalize(x_ref[...].astype(F32) + attended)
    h = normal * across(gain_ref) + across(shift_ref)
    h_ref[...] = h
    low_ref[...] = h.astype(BF16)
    n_ref[...] = normal.astype(BF16)
    inv_ref[...] = inverse


def project_forward(chain, scalars, x, contexts, w_own, w_oth, vecs):
    tokens, model = x.shape
    block = 512
    return chain(
        functools.partial(project_kernel, count=len(contexts)),
        scalars,
        [x, *contexts, w_own, w_oth, *vecs],
        [by_rows(block, model)]
        + [by_rows(block, c.shape[1]) for c in contexts]
        + [once(w_own.shape), once(w_oth.shape)]
        + [whole(v.shape) for v in vecs],
        [by_rows(block, model)] * 3 + [by_rows(block, 1)],
        [
            shaped((tokens, model), F32),
            shaped((tokens, model)),
            shaped((tokens, model)),
            shaped((tokens, 1), F32),
        ],
        grid=(tokens // block,),
        name="project_fwd",
        micros=3.7,
        vmem=18,
    )


def feed_own_kernel(s_ref, h_ref, wu_ref, bu_ref, wd_ref, g_ref, gp_ref, f_ref):
    h = h_ref[...]
    chunk = wu_ref.shape[1] // 3
    bu = across(bu_ref)
    total = None
    for j in range(3):
        cols = slice(chunk * j, chunk * j + chunk)
        act, slope = gelu_pair(nn(h, wu_ref[:, cols]) + bu[:, cols])
        act = act.astype(BF16)
        g_ref[:, cols] = act
        gp_ref[:, cols] = slope.astype(BF16)
        part = nn(act, wd_ref[cols, :])
        total = part if total is None else total + part
    f_ref[...] = total


def feed_own(chain, scalars, h, wu, bu, wd):
    tokens, model = h.shape
    units = wu.shape[1]
    block = 256
    return chain(
        feed_own_kernel,
        scalars,
        [h, wu, bu, wd],
        [by_rows(block, model), once(wu.shape), whole(bu.shape), once(wd.shape)],
        [by_rows(block, units), by_rows(block, units), by_rows(block, model)],
        [shaped((tokens, units)), shaped((tokens, units)), shaped((tokens, model), F32)],
        grid=(tokens // block,),
        name="feed_own",
        micros=14.5,
        vmem=15,
    )


def feed_up_kernel(s_ref, h_ref, near_ref, far_ref, bias_ref, *refs, second):
    g_ref, gp_ref, wu_ref = refs[-3:]
    part = near_ref.shape[1]
    core = bit(s_ref[0], 0)

    @pl.when(pl.program_id(0) == 0)
    def _():
        wu_ref[:, pl.ds(pl.multiple_of(core * part, LANES), part)] = near_ref[...]
        wu_ref[:, pl.ds(pl.multiple_of((1 - core) * part, LANES), part)] = far_ref[...]

    row = 2 + 2 * (bit(s_ref[0], 1) ^ second)
    bu = jnp.concatenate([bias_ref[pl.ds(row + i, 1), :] for i in range(2)], axis=1)
    act, slope = gelu_pair(nn(h_ref[...], wu_ref[...]) + bu)
    g_ref[...] = act.astype(BF16)
    gp_ref[...] = slope.astype(BF16)


def feed_up(chain, scalars, h, near, far, bias, kept=()):
    tokens, model = h.shape
    half = 2 * near.shape[1]
    block = 256
    second = 1 if kept else 0
    here = lambda s: bit(s[0], 1) ^ second
    columns = pl.BlockSpec((block, half), lambda i, s: (i, here(s)))
    return chain(
        functools.partial(feed_up_kernel, second=second),
        scalars,
        [h, near, far, bias, *kept],
        [by_rows(block, model), once(near.shape), once(far.shape), whole(bias.shape)]
        + [pl.BlockSpec(memory_space=pl.ANY)] * len(kept),
        [columns, columns, pl.BlockSpec((model, half), lambda i, s: (0, here(s)))],
        [shaped((tokens, 2 * half)), shaped((tokens, 2 * half)), shaped((model, 2 * half))],
        grid=(tokens // block,),
        name="feed_up",
        micros=60.0,
        vmem=15,
        aliases={5 + i: i for i in range(len(kept))},
    )


def feed_down_kernel(
    s_ref, g_ref, h_ref, f_ref, d0, d1, bias_ref, gain_ref, shift_ref,
    out_ref, n_ref, inv_ref, pool_ref, wd_ref,
):
    i = pl.program_id(0)

    @pl.when(i == 0)
    def _():
        for s, down in enumerate((d0, d1)):
            wd_ref[bit(s_ref[0], 0) ^ s] = down[...]
        pool_ref[...] = jnp.zeros_like(pool_ref)

    shape = wd_ref.shape
    down = wd_ref[...].reshape(shape[0] * shape[1], shape[2])
    total = nn(g_ref[...], down)
    normal, inverse = normalize(h_ref[...] + (f_ref[...] + total + across(bias_ref)))
    y = normal * across(gain_ref) + across(shift_ref)
    out_ref[...] = y.astype(BF16)
    n_ref[...] = normal.astype(BF16)
    inv_ref[...] = inverse
    block = y.shape[0]
    per = LEN // block
    sent = i // per
    length = length_of(s_ref, sent)
    first = (i - sent * per) * block
    live = lax.broadcasted_iota(jnp.int32, y.shape, 0) + first < length
    pool_ref[pl.ds(sent, 1), :] += colsum(jnp.where(live, y, 0.0)) / length.astype(F32)


def feed_down(chain, scalars, g, h, f, down, vecs):
    tokens, model = h.shape
    units = g.shape[1]
    block = 512
    sents = tokens // LEN
    full = (2,) + down[0].shape
    return chain(
        feed_down_kernel,
        scalars,
        [g, h, f, *down, *vecs],
        [by_rows(block, units), by_rows(block, model), by_rows(block, model)]
        + [once(w.shape) for w in down]
        + [whole(v.shape) for v in vecs],
        [by_rows(block, model), by_rows(block, model), by_rows(block, 1), whole((sents, model)), whole(full)],
        [
            shaped((tokens, model)),
            shaped((tokens, model)),
            shaped((tokens, 1), F32),
            shaped((sents, model), F32),
            shaped(full),
        ],
        grid=(tokens // block,),
        name="feed_down",
        micros=9.0,
        vmem=24,
    )


def exact(a, b, dims):
    return lax.dot_general(
        a, b, (dims, ((), ())), precision=lax.Precision.HIGHEST, preferred_element_type=F32
    )


def loss_kernel(s_ref, *refs):
    *slot_refs, id_ref, loss_ref, cot_ref, pool_ref, grad_ref = refs
    local = cot_ref.shape[0]
    rank = s_ref[1]
    part = slot_refs[0].shape[0]
    count = part * len(slot_refs)
    for s in range(count // local):
        for i in range(local):
            at = local * s + i
            row = slot_refs[at // part][at % part : at % part + 1, :]
            pool_ref[pl.ds((rank ^ s) * local + i, 1), :] = row
    pooled = pool_ref[...]
    scale = lax.rsqrt(jnp.sum(pooled * pooled, axis=-1, keepdims=True) + EPS_UNIT)
    unit = pooled * scale
    score = SOFTMAX_TEMP * exact(unit, unit, ((1,), (1,)))
    itself = lax.broadcasted_iota(jnp.int32, score.shape, 0) == lax.broadcasted_iota(
        jnp.int32, score.shape, 1
    )
    others = jnp.where(itself, MASKED, score)
    top = jnp.max(others, axis=1, keepdims=True)
    power = jnp.exp(others - top)
    total = jnp.sum(power, axis=1, keepdims=True)
    ids = jnp.broadcast_to(across(id_ref).astype(F32), score.shape)
    match = jnp.logical_and(ids == ids.T, jnp.logical_not(itself)).astype(F32)
    number = jnp.sum(match, axis=1, keepdims=True)
    matched = jnp.sum(match * score, axis=1, keepdims=True) / number
    terms = top + jnp.log(total) - matched
    loss_ref[...] = jnp.sum(terms, axis=0, keepdims=True) / count
    dscore = float(LEN) * (power / total - match / number)
    dunit = SOFTMAX_TEMP * (exact(dscore, unit, ((1,), (0,))) + exact(dscore, unit, ((0,), (0,))))
    grad_ref[...] = scale * (dunit - unit * jnp.sum(unit * dunit, axis=-1, keepdims=True))
    for i in range(local):
        own = grad_ref[pl.ds(rank * local + i, 1), :]
        cot_ref[i : i + 1, :] = own / length_of(s_ref, i).astype(F32)


def loss_call(chain, scalars, slots, group_ids, local):
    part, model = slots[0].shape
    count = part * len(slots)
    return chain(
        loss_kernel,
        scalars,
        [*slots, group_ids],
        [whole((part, model))] * len(slots) + [whole((count,))],
        [whole((1, 1)), whole((local, model))],
        [shaped((1, 1), F32), shaped((local, model), F32)],
        scratch=[pltpu.VMEM((count, model), F32)] * 2,
        name="loss",
        micros=3.8,
    )


def norm_back(upstream, normal, inverse, gain):
    scaled = upstream * gain
    return inverse * (scaled - rowmean(scaled) - normal * rowmean(scaled * normal))


def norm_two_kernel(s_ref, cot_ref, n_ref, inv_ref, gain_ref, pool_ref, df_ref, sum_ref):
    s = pl.program_id(0)
    normal = n_ref[...].astype(F32)
    live = lax.broadcasted_iota(jnp.int32, normal.shape, 0) < length_of(s_ref, s)
    up = cot_ref[...].astype(F32) + jnp.where(live, pool_ref[pl.ds(s, 1), :], 0.0)
    df = norm_back(up, normal, inv_ref[...], across(gain_ref)).astype(BF16)
    df_ref[...] = df

    @pl.when(s == 0)
    def _():
        sum_ref[...] = jnp.zeros_like(sum_ref)

    sum_ref[0:1, :] += colsum(df.astype(F32))
    sum_ref[1:2, :] += colsum(up * normal)
    sum_ref[2:3, :] += colsum(up)


def norm_two_backward(chain, scalars, cot, normal, inverse, gain, pool_cot):
    tokens, model = cot.shape
    return chain(
        norm_two_kernel,
        scalars,
        [cot, normal, inverse, gain, pool_cot],
        [by_rows(LEN, model), by_rows(LEN, model), by_rows(LEN, 1), whole(gain.shape), whole(pool_cot.shape)],
        [by_rows(LEN, model), whole((3, model))],
        [shaped((tokens, model)), shaped((3, model), F32)],
        grid=(tokens // LEN,),
        name="norm_two_bwd",
        micros=5.4,
    )


def unit_back_kernel(s_ref, df_ref, gp_ref, wd_ref, du_ref, sum_ref):
    @pl.when(pl.program_id(0) == 0)
    def _():
        sum_ref[...] = jnp.zeros_like(sum_ref)

    df = df_ref[...]
    chunk = wd_ref.shape[0] // 3
    for j in range(3):
        cols = slice(chunk * j, chunk * j + chunk)
        du = (nt(df, wd_ref[cols, :]) * gp_ref[:, cols].astype(F32)).astype(BF16)
        du_ref[:, cols] = du
        sum_ref[:, cols] += colsum(du.astype(F32))


def unit_backward(chain, scalars, df, gp, wd):
    tokens, model = df.shape
    units = gp.shape[1]
    block = 512
    return chain(
        unit_back_kernel,
        scalars,
        [df, gp, wd],
        [by_rows(block, model), by_rows(block, units), once(wd.shape)],
        [by_rows(block, units), whole((1, units))],
        [shaped((tokens, units)), shaped((1, units), F32)],
        grid=(tokens // block,),
        name="unit_bwd",
        micros=60.0,
        vmem=18,
    )


def middle_kernel(
    s_ref, df_ref, du_own, du_oth, wu_own, wu_oth, n_ref, inv_ref, gain_ref, wo_own, wo_oth,
    da_ref, sum_ref, dc_own, *dc_oth,
):
    @pl.when(pl.program_id(0) == 0)
    def _():
        sum_ref[...] = jnp.zeros_like(sum_ref)

    total = df_ref[...].astype(F32) + nt(du_oth[...], wu_oth[...]) + nt(du_own[...], wu_own[...])
    normal = n_ref[...].astype(F32)
    da = norm_back(total, normal, inv_ref[...], across(gain_ref)).astype(BF16)
    da_ref[...] = da
    dc_own[...] = nt(da, wo_own[...]).astype(BF16)
    at = 0
    for ref in dc_oth:
        width = ref.shape[1]
        ref[...] = nt(da, wo_oth[at : at + width, :]).astype(BF16)
        at += width
    sum_ref[0:1, :] += colsum(total * normal)
    sum_ref[1:2, :] += colsum(total)
    sum_ref[2:3, :] += colsum(da.astype(F32))


def middle_backward(
    chain, scalars, df, du_own, du_oth, wu_own, wu_oth, normal, inverse, gain, wo_own, wo_oth, widths
):
    tokens, model = df.shape
    units = wu_own.shape[1]
    block = 256
    return chain(
        middle_kernel,
        scalars,
        [df, du_own, du_oth, wu_own, wu_oth, normal, inverse, gain, wo_own, wo_oth],
        [by_rows(block, model), by_rows(block, units), by_rows(block, units)]
        + [once(wu_own.shape), once(wu_oth.shape), by_rows(block, model), by_rows(block, 1)]
        + [whole(gain.shape), once(wo_own.shape), once(wo_oth.shape)],
        [by_rows(block, model), whole((3, model))] + [by_rows(block, w) for w in widths],
        [shaped((tokens, model)), shaped((3, model), F32)] + [shaped((tokens, w)) for w in widths],
        grid=(tokens // block,),
        name="middle_bwd",
        micros=12.0,
        vmem=18,
    )


def bit(value, at):
    return (value >> at) & 1


def split_store(d, even, odd, keep_ref, send_ref, at):
    flip = bit(d, 0) == 0
    keep_ref[at] = jnp.where(flip, even, odd).astype(BF16)
    send_ref[at] = jnp.where(flip, odd, even).astype(BF16)


def dense_grad_kernel(d_ref, a_ref, b_ref, keep_ref, send_ref):
    d = d_ref[0]
    grad = tn(a_ref[...], b_ref[...])
    step = keep_ref.shape[3]
    for x in range(2):
        for z in range(2):
            at = (4 * z + 2 * x) * step
            split_store(
                d, grad[at : at + step], grad[at + step : at + 2 * step], keep_ref, send_ref,
                (x ^ bit(d, 1), z ^ bit(d, 2), 0),
            )


def dense_grad(chain, scalars, a, b, cut_left):
    tokens = a.shape[0]
    left = a.shape[1] // (2 if cut_left else 1)
    right = b.shape[1] // (1 if cut_left else 2)
    step = left // 8
    block = pl.BlockSpec((2, 2, 1, step, right), lambda i, s: (0, 0, i ^ bit(s[0], 3), 0, 0))
    return chain(
        dense_grad_kernel,
        scalars,
        [a, b],
        [
            pl.BlockSpec((tokens, left), lambda i, s: (0, i)) if cut_left else once(a.shape),
            once(b.shape) if cut_left else pl.BlockSpec((tokens, right), lambda i, s: (0, i)),
        ],
        [block, block],
        [shaped((2, 2, 2, step, right))] * 2,
        grid=(2,),
        name="dense_grad",
        micros=60.0,
        vmem=15,
    )


def heads_grad_kernel(d_ref, x_ref, da_ref, two_ref, one_ref, unit_ref, *refs):
    *refs, keep_ref, send_ref = refs
    count = len(refs) // 3
    c_refs, dqkv_refs, bias_refs = refs[:count], refs[count : 2 * count], refs[2 * count :]
    d = d_ref[0]
    bias = jnp.concatenate([ref[...] for ref in bias_refs], axis=1)
    width = bias.shape[1]
    out = jnp.concatenate([tn(ref[...], da_ref[...]) for ref in c_refs], axis=0)
    projs = [tn(x_ref[...], ref[...]) for ref in dqkv_refs]
    proj = jnp.concatenate(
        [p[:, c * (p.shape[1] // 3) : (c + 1) * (p.shape[1] // 3)] for c in range(3) for p in projs], axis=1
    )
    step = proj.shape[0] // 16
    small = [ref[i : i + 1, at : at + width] for ref in (two_ref, one_ref) for i in range(3) for at in (0, width)]
    small += [bias[0:1, :], bias[1:2, :]]
    small += [unit_ref[:, at : at + width] for at in range(0, unit_ref.shape[1], width)]
    small += [jnp.zeros((1, width), F32)] * (32 - len(small))
    rest = jnp.zeros((14, width), F32)

    def block(b):
        row, col = (b & 7) * step, (b >> 3) * width
        pieces = [out[row : row + step, col : col + width]]
        pieces += [proj[b * step : b * step + step, c * width : c * width + width] for c in range(3)]
        return jnp.concatenate(pieces + [small[b], small[16 + b], rest], axis=0)

    for x in range(2):
        for z in range(2):
            for w in range(2):
                b = 8 * w + 4 * z + 2 * x
                split_store(
                    d, block(b), block(b + 1), keep_ref, send_ref,
                    (x ^ bit(d, 1), z ^ bit(d, 2), w ^ bit(d, 3)),
                )


def heads_grad(chain, scalars, x, da, sums, contexts, dqkvs, biases):
    width = sum(b.shape[1] for b in biases)
    full = (2, 2, 2, width // 2 + 16, width)
    inputs = [x, da, *sums, *contexts, *dqkvs, *biases]
    return chain(
        heads_grad_kernel,
        scalars,
        inputs,
        [once(a.shape) for a in inputs],
        [whole(full), whole(full)],
        [shaped(full)] * 2,
        name="heads_grad",
        micros=60.0,
        vmem=21,
    )


def input_grad_kernel(s_ref, da_ref, *refs):
    *refs, out_ref = refs
    total = da_ref[...].astype(F32)
    for grad, w in zip(refs[: len(refs) // 2], refs[len(refs) // 2 :], strict=True):
        total = total + nt(grad[...], jnp.concatenate([w[c] for c in range(3)], axis=1))
    out_ref[...] = total


def input_grad(chain, scalars, da, grads, weights):
    tokens, model = da.shape
    block = 512
    return chain(
        input_grad_kernel,
        scalars,
        [da, *grads, *weights],
        [by_rows(block, model)] + [by_rows(block, g.shape[1]) for g in grads] + [once(w.shape) for w in weights],
        [by_rows(block, model)],
        [shaped((tokens, model), F32)],
        grid=(tokens // block,),
        name="input_grad",
        token=True,
        micros=60.0,
        vmem=18,
    )[0]


def place_kernel(s_ref, a0, a1, b0, b1, *out_refs, kind):
    d = s_ref[0]
    half = pl.program_id(0)
    flip = bit(d, 0) == 0
    for x, (near_ref, far_ref) in enumerate(((a0, b0), (a1, b1))):
        for z in range(2):
            near, far = near_ref[z, 0].astype(F32), far_ref[z, 0].astype(F32)
            low = (x ^ bit(d, 1)) + 2 * (z ^ bit(d, 2))
            for side, rows in enumerate((jnp.where(flip, near, far), jnp.where(flip, far, near))):
                if kind != "heads":
                    step = rows.shape[0]
                    out_refs[0][low, side * step : (side + 1) * step] = rows
                    continue
                out_ref, proj_ref, *vec_refs, unit_ref, small_ref = out_refs
                step = out_ref.shape[1] // 2
                out_ref[low, side * step : (side + 1) * step] = rows[:step]
                for c in range(3):
                    proj_ref[c, low, side * step : (side + 1) * step] = rows[(c + 1) * step : (c + 2) * step]
                b = 2 * (low + 4 * (half ^ bit(d, 3))) + side
                small_ref[pl.ds(b, 1), :] = rows[4 * step : 4 * step + 1]
                small_ref[pl.ds(16 + b, 1), :] = rows[4 * step + 1 : 4 * step + 2]
    if kind != "heads":
        return

    @pl.when(half == 1)
    def _():
        line = lambda at, count: jnp.concatenate([small_ref[i : i + 1, :] for i in range(at, at + count)], axis=1)
        for i, ref in enumerate(vec_refs[:6]):
            ref[...] = line(2 * i, 2).reshape(ref.shape[0])
        vec_refs[6][...] = small_ref[12:14, :]
        unit_ref[...] = line(14, unit_ref.shape[0] // small_ref.shape[1]).reshape(unit_ref.shape[0])


def place(chain, scalars, pieces, kind, units):
    step, cols = pieces[0].shape[2:]
    block = pl.BlockSpec((2, 1, step, cols), lambda w, s: (0, w, 0, 0))
    high = lambda w, s: w ^ bit(s[0], 3)
    scratch = []
    if kind == "down":
        shapes = [(8, 2 * step, cols)]
        specs = [pl.BlockSpec((4, 2 * step, cols), lambda w, s: (high(w, s), 0, 0))]
    elif kind == "up":
        shapes = [(4, 2 * step, 2 * cols)]
        specs = [pl.BlockSpec((4, 2 * step, cols), lambda w, s: (0, 0, high(w, s)))]
    else:
        part = (step - 16) // 4
        shapes = [(4, 2 * part, 2 * cols), (3, 8, 2 * part, cols)]
        specs = [
            pl.BlockSpec((4, 2 * part, cols), lambda w, s: (0, 0, high(w, s))),
            pl.BlockSpec((3, 4, 2 * part, cols), lambda w, s: (0, high(w, s), 0, 0)),
        ]
        vectors = [(2 * cols,)] * 6 + [(2, cols), (units,)]
        shapes += vectors
        specs += [whole(v) for v in vectors]
        scratch = [pltpu.VMEM((32, cols), F32)]
    return chain(
        functools.partial(place_kernel, kind=kind),
        scalars,
        pieces,
        [block] * 4,
        specs,
        [shaped(s, F32) for s in shapes],
        grid=(2,),
        scratch=scratch,
        name="place",
        token=True,
        micros=4.0,
        vmem=18,
    )


def swap(x, axis, mask):
    size = lax.axis_size(axis)
    return lax.ppermute(x, axis, [(i, i ^ mask) for i in range(size)])


def swap_all(x, mask):
    size = lax.axis_size("dp") * lax.axis_size("tensor")
    return lax.ppermute(x, ("dp", "tensor"), [(i, i ^ mask) for i in range(size)])


def levels():
    return lax.axis_size("dp").bit_length() - 1


def flip_kernel(s_ref, a_ref, b_ref, out_ref):
    for i in range(2):
        out_ref[i] = (a_ref[i].astype(F32) + b_ref[1 - i].astype(F32)).astype(BF16)


def add_flipped(chain, scalars, a, b):
    return chain(
        flip_kernel,
        scalars,
        [a, b],
        [whole(a.shape)] * 2,
        [whole(a.shape)],
        [shaped(a.shape)],
        name="add",
        micros=2.0,
    )[0]


def sum_kernel(s_ref, *refs, count, early):
    total = refs[0][...].astype(F32) + refs[1][...].astype(F32)
    if early:
        total = total.astype(BF16).astype(F32)
    for ref in refs[2:count]:
        total = total + ref[...].astype(F32)
    total = total.astype(BF16)
    outs = refs[count:]
    if len(outs) == 1:
        outs[0][...] = total
        return
    for i, out in enumerate(outs):
        out[...] = total[i]


def add(chain, scalars, terms, split=1, early=False):
    shape = terms[0].shape
    outs = [shape] if split == 1 else [shape[1:]] * split
    return chain(
        functools.partial(sum_kernel, count=len(terms), early=early),
        scalars,
        terms,
        [whole(shape)] * len(terms),
        [whole(o) for o in outs],
        [shaped(o) for o in outs],
        name="add",
        micros=2.0,
    )


def join_kernel(s_ref, *refs):
    for i, ref in enumerate(refs[:-1]):
        refs[-1][i] = ref[...]


def join(chain, scalars, parts):
    shape = (len(parts),) + parts[0].shape
    return chain(
        join_kernel,
        scalars,
        parts,
        [whole(p.shape) for p in parts],
        [whole(shape)],
        [shaped(shape)],
        name="join",
        micros=1.5,
    )[0]


class Reduction:
    def __init__(self, chain, scalars):
        self.chain, self.scalars = chain, scalars

    def add(self, terms, split=1, early=False):
        return add(self.chain, self.scalars, terms, split, early)

    def send(self, x, axis, mask):
        return self.chain.send(x, axis, mask)

    def receive(self, sent):
        return self.chain.receive(self.scalars, sent)

    def other(self, keep, send):
        self.keep_oth, self.got_oth = keep, self.send(send, "dp", 1)

    def own(self, keep, send):
        self.keep_own, self.got_own = keep, self.send(send, "dp", 1)

    def across(self):
        (total,) = self.add([self.keep_oth, self.receive(self.got_oth)])
        self.got_y = self.send(total, "tensor", 1)

    def along_x(self):
        got = [self.receive(self.got_own), self.receive(self.got_y)]
        self.keep, send = self.add([self.keep_own, *got], 2, True)
        self.got = self.send(send, "dp", 2)

    def along_z(self):
        shape = self.keep.shape
        flat = (4,) + shape[2:]
        got = self.receive(self.got)
        self.keep, *send = self.add([self.keep.reshape(flat), got.reshape(flat)], 4)
        self.got = [self.send(x, "dp", m) for x, m in zip(send, (8, 4, 12), strict=True)]

    def back_z(self):
        (total,) = self.add([self.keep, *(self.receive(g) for g in self.got)])
        for at in range(4, levels()):
            got = self.receive(self.send(total, "dp", 1 << at))
            (total,) = self.add([total, got])
        self.total = total
        self.got = [self.send(total, "dp", m) for m in (8, 4, 12)]

    def back_x_direct(self):
        near = join(self.chain, self.scalars, [self.total, *(self.receive(g) for g in self.got)])
        self.near = near.reshape((2, 2) + near.shape[1:])
        self.got = self.send(self.near, "dp", 2)
        self.near_far = self.send(self.near, "dp", 1)

    def along_z0(self):
        self.keep, send = self.add([self.keep, self.receive(self.got)], 2)
        self.got = self.send(send, "dp", 4)

    def turn(self):
        (self.total,) = self.add([self.keep, self.receive(self.got)])
        for at in range(4, levels()):
            got = self.receive(self.send(self.total, "dp", 1 << at))
            (self.total,) = self.add([self.total, got])
        self.got = self.send(self.total, "dp", 8)

    def back_z0(self):
        self.total = add_flipped(self.chain, self.scalars, self.total, self.receive(self.got))
        self.got = self.send(self.total, "dp", 4)

    def back_x(self):
        self.near = join(self.chain, self.scalars, [self.total, self.receive(self.got)])
        self.got = self.send(self.near, "dp", 2)
        self.near_far = self.send(self.near, "dp", 1)

    def back_core(self, gated=True):
        self.next = self.receive(self.got)
        if gated:
            self.next = self.chain.gate(self.scalars, self.next)
        self.next_far = self.send(self.next, "dp", 1)

    def place(self, kind, units=0):
        pieces = [self.near, self.next, self.receive(self.near_far), self.receive(self.next_far)]
        return place(self.chain, self.scalars, pieces, kind, units)


def stack_rows_kernel(s_ref, *refs):
    step = refs[0].shape[0]
    for i, ref in enumerate(refs[:-1]):
        refs[-1][i * step : (i + 1) * step, :] = ref[...]


def stack_rows(chain, scalars, parts):
    shape = (len(parts) * parts[0].shape[0], parts[0].shape[1])
    return chain(
        stack_rows_kernel,
        scalars,
        parts,
        [whole(p.shape) for p in parts],
        [whole(shape)],
        [shaped(shape, F32)],
        name="stack_rows",
        micros=10.0,
    )[0]


def gather_pooled(chain, scalars, pooled):
    bits = levels() + 1
    at = 0
    while at < bits:
        step = min(1 if at == 2 else 2, bits - at)
        parts = [pooled] + [swap_all(pooled, m << at) for m in range(1, 1 << step)]
        chain.pause(scalars)
        at += step
        if at < bits:
            pooled = stack_rows(chain, scalars, parts)
    return parts


def cut_kernel(s_ref, *refs):
    count = len(refs) // 2
    for a_ref, out_ref in zip(refs[:count], refs[count:], strict=True):
        out_ref[...] = a_ref[...].reshape(out_ref.shape)


def cut(chain, scalars, *cuts):
    shapes = [tuple(b for b in block if b != 1) for _, block, _ in cuts]
    at = lambda index: lambda i, s: index(s[0] & 3)
    return chain(
        cut_kernel,
        scalars,
        [a for a, _, _ in cuts],
        [pl.BlockSpec(block, at(index)) for _, block, index in cuts],
        [whole(s) for s in shapes],
        [shaped(s, a.dtype) for s, (a, _, _) in zip(shapes, cuts, strict=True)],
        name="cut",
        micros=1.0,
    )


def cut_heads_kernel(s_ref, a_ref, out_ref):
    out_ref[...] = a_ref[:, 0, :, : out_ref.shape[2]]


def cut_heads(chain, scalars, a, width):
    _, _, part, full = a.shape
    shape = (3, part, width)
    return chain(
        cut_heads_kernel,
        scalars,
        [a],
        [pl.BlockSpec((3, 1, part, full), lambda i, s: (0, bit(s[0], 0), 0, 0))],
        [whole(shape)],
        [shaped(shape)],
        name="cut",
        micros=1.0,
    )[0]


def cut_pack_kernel(s_ref, a_ref, w_ref, bias_ref, unit_ref, out_ref, small_ref):
    part = a_ref.shape[2]
    width = out_ref.shape[1]
    rows, cols = w_ref.shape[1:]
    for c in range(3):
        out_ref[c * part : (c + 1) * part, :] = a_ref[c, 0, :, a_ref.shape[3] - width :]
    for k in range(cols // width):
        begin = 3 * part + k * rows
        out_ref[begin : begin + rows, :] = w_ref[0, :, k * width : (k + 1) * width]
    full = bias_ref.shape[1]
    small_ref[0:2, :] = bias_ref[...]
    unit = across(unit_ref)
    for i in range(unit.shape[1] // full):
        small_ref[2 + i : 3 + i, :] = unit[:, i * full : (i + 1) * full]


def cut_pack(chain, scalars, a, width, w, bias, unit):
    _, _, part, full = a.shape
    _, rows, cols = w.shape
    shapes = [shaped((3 * part + rows * cols // width, width)), shaped((2 + unit.shape[0] // full, full), F32)]
    return chain(
        cut_pack_kernel,
        scalars,
        [a, w, bias, unit],
        [
            pl.BlockSpec((3, 1, part, full), lambda i, s: (0, bit(s[0], 0), 0, 0)),
            pl.BlockSpec((1, rows, cols), lambda i, s: (bit(s[0], 0), 0, 0)),
            whole(bias.shape),
            whole(unit.shape),
        ],
        [whole(s.shape) for s in shapes],
        shapes,
        name="cut",
        micros=1.0,
    )


class Gather:
    def __init__(self, chain, scalars, piece, relayed=False):
        self.chain, self.scalars, self.relayed = chain, scalars, relayed
        self.got = chain.send(piece, "tensor", 1)
        self.parts = []

    def hand_over(self):
        part = self.chain.gate(self.scalars, self.chain.receive(self.scalars, self.got))
        if self.relayed and not self.parts:
            self.got = self.chain.send(part, "dp", 2)
        self.parts += [part, self.chain.send(part, "dp", 1)]

    def slots(self):
        return [self.slot(i) for i in range(len(self.parts))]

    def slot(self, i):
        return self.parts[i] if i % 2 == 0 else self.chain.receive(self.scalars, self.parts[i])


def per_device(
    layer_input, w_qkv, bias_qv, w_out, b_out, gain_one, shift_one, w_up, b_up, w_down, b_down,
    gain_two, shift_two, out_cot, lengths, group_ids,
):
    tensor_size = lax.axis_size("tensor")
    position = lax.axis_index("tensor")
    d = lax.axis_index("dp")
    model = layer_input.shape[1]
    width = w_qkv.shape[2]
    units = w_up.shape[1]
    local = lengths.shape[0] // tensor_size
    rank = d * tensor_size + position
    scal = jnp.concatenate([jnp.stack([d, rank, position * local]).astype(jnp.int32), lengths])
    chain = Chain()

    heads_cut = w_qkv.reshape(3, 2, model // 2, width)
    lead = width // 3 * 2
    gather_lead = Gather(chain, scal, cut_heads(chain, scal, heads_cut, lead))
    qkv_own, c_own, lse_own = attn_forward(chain, scal, layer_input, [w_qkv], bias_qv)
    piece, bias = cut_pack(
        chain, scal, heads_cut, width - lead, w_out.reshape(2, width // 2, model), bias_qv, b_up
    )
    gather_pack = Gather(chain, scal, piece)
    bias_oth = swap(bias, "tensor", 1)
    part = units // 4
    piece, second = cut(
        chain,
        scal,
        (w_up, (model, part), lambda q: (0, q)),
        (w_down.reshape(2, 2 * part, model), (1, 2 * part, model), lambda q: (q & 1, 0, 0)),
    )
    gather_up = Gather(chain, scal, piece, relayed=True)
    gather_down = Gather(chain, scal, second)
    gather_lead.hand_over()
    qkv_lead, c_lead, lse_lead, wq_lead = attn_forward(chain, scal, layer_input, gather_lead.slots(), bias_oth)
    gather_pack.hand_over()
    qkv_rest, c_rest, lse_rest, wq_rest, wo_oth = attn_forward(
        chain, scal, layer_input, gather_pack.slots(), bias_oth, lead, width
    )
    wq_lead, wq_rest = (w.reshape(3, model, w.shape[3]) for w in (wq_lead, wq_rest))
    wo_oth = wo_oth.reshape(width, model)
    h1, h1_low, normal_one, inverse_one = project_forward(
        chain, scal, layer_input, [c_own, c_lead, c_rest], w_out, wo_oth, [b_out, gain_one, shift_one]
    )
    gather_up.hand_over()
    g_own, gp_own, f_own = feed_own(chain, scal, h1_low, w_up, b_up, w_down)
    gather_up.hand_over()
    near, far = gather_up.slot(0), gather_up.slot(1)
    half = feed_up(chain, scal, h1_low, near, far, bias_oth)
    gather_down.hand_over()
    near, far = gather_up.slot(2), gather_up.slot(3)
    g_oth, gp_oth, wu_oth = feed_up(chain, scal, h1_low, near, far, bias_oth, half)
    output, normal_two, inverse_two, pooled, wd_oth = feed_down(
        chain, scal, g_oth, h1, f_own, gather_down.slots(), [b_down, gain_two, shift_two]
    )
    wd_oth = wd_oth.reshape(units, model)

    loss, pool_cot = loss_call(chain, scal, gather_pooled(chain, scal, pooled), group_ids, local)

    down, up, heads = (Reduction(chain, scal) for _ in range(3))
    df, sums_two = norm_two_backward(chain, scal, out_cot, normal_two, inverse_two, gain_two, pool_cot)
    down.other(*dense_grad(chain, scal, g_oth, df, True))
    down.own(*dense_grad(chain, scal, g_own, df, True))
    down.across()
    du_oth, sums_du_oth = unit_backward(chain, scal, df, gp_oth, wd_oth)
    du_own, sums_du_own = unit_backward(chain, scal, df, gp_own, w_down)
    up.other(*dense_grad(chain, scal, h1_low, du_oth, False))
    up.own(*dense_grad(chain, scal, h1_low, du_own, False))
    up.across()
    da, sums_one, dc_own, dc_lead, dc_rest = middle_backward(
        chain, scal, df, du_own, du_oth, w_up, wu_oth, normal_one, inverse_one, gain_one, w_out, wo_oth,
        [width, lead, width - lead],
    )
    down.along_x()
    dqkv_lead, sums_lead = attn_backward(chain, scal, qkv_lead, dc_lead, lse_lead)
    dqkv_rest, sums_rest = attn_backward(chain, scal, qkv_rest, dc_rest, lse_rest)
    sums = [sums_two, sums_one, sums_du_oth]
    heads.other(
        *heads_grad(
            chain, scal, layer_input, da, sums, [c_lead, c_rest], [dqkv_lead, dqkv_rest], [sums_lead, sums_rest]
        )
    )
    down.along_z0()
    up.along_x()
    chain.pause(scal)
    heads.across()
    dqkv_own, sums_own = attn_backward(chain, scal, qkv_own, dc_own, lse_own)
    down.turn()
    up.along_z0()
    sums = [sums_two, sums_one, sums_du_own]
    heads.own(*heads_grad(chain, scal, layer_input, da, sums, [c_own], [dqkv_own], [sums_own]))
    grad_input = input_grad(
        chain, scal, da, [dqkv_own, dqkv_lead, dqkv_rest], [w_qkv, wq_lead, wq_rest]
    )
    down.back_z0()
    heads.along_x()
    up.turn()
    chain.pause(scal)
    down.back_x()
    heads.along_z0()
    chain.pause(scal)
    heads.turn()
    up.back_z0()
    chain.pause(scal)
    heads.back_z0()
    up.back_x()
    chain.pause(scal)
    down.back_core()
    (grad_w_down,) = down.place("down")
    up.back_core()
    heads.back_x()
    chain.pause(scal)
    (grad_w_up,) = up.place("up")
    heads.back_core(False)
    chain.pause(scal)
    grad_w_out, grad_w_qkv, *grads, grad_bias_qv, grad_b_up = heads.place("heads", units)
    grad_b_down, grad_gain_two, grad_shift_two, grad_gain_one, grad_shift_one, grad_b_out = grads
    return (
        loss.reshape(()),
        output,
        grad_input,
        grad_w_qkv.reshape(w_qkv.shape),
        grad_bias_qv,
        grad_w_out.reshape(w_out.shape),
        grad_b_out,
        grad_gain_one,
        grad_shift_one,
        grad_w_up.reshape(w_up.shape),
        grad_b_up,
        grad_w_down.reshape(w_down.shape),
        grad_b_down,
        grad_gain_two,
        grad_shift_two,
    )


def solution(mesh):
    rows = P(("dp", "tensor"), None)
    in_specs = (
        rows,
        P(None, None, "tensor"),
        P(None, "tensor"),
        P("tensor", None),
        P(),
        P(),
        P(),
        P(None, "tensor"),
        P("tensor"),
        P("tensor", None),
        P(),
        P(),
        P(),
        rows,
        P("dp"),
        P(),
    )
    out_specs = (
        P(),
        rows,
        rows,
        P(None, None, "tensor"),
        P(None, "tensor"),
        P("tensor", None),
        P(),
        P(),
        P(),
        P(None, "tensor"),
        P("tensor"),
        P("tensor", None),
        P(),
        P(),
        P(),
    )
    return jax.shard_map(
        per_device, mesh=mesh, in_specs=in_specs, out_specs=out_specs, check_vma=False
    )
```
